32 devices in a mesh: groups: 1, role: 2 (over core), ep: 8 (over z, y), tp: 2 (over x).
Axes of the slice: x: 2, y: 2, z: 4, core: 2. Of those that a mesh axis runs over, the one named last changes fastest.
Arguments:
- tokens: bfloat16 [2048, 2048], P(('groups', 'role', 'ep'), 'tp'), may hold values from -6 to 6
- out_grad: bfloat16 [2048, 2048], P(('groups', 'role', 'ep'), 'tp'), may hold values from -6 to 6
- routes: int32 [2048, 8], P(('groups', 'role', 'ep')), may hold values from 0 to 15, all different within a row; in each aligned block of 128 rows (0 to 127, 128 to 255, ...) at most 72 rows name the same one
- probs: bfloat16 [2048, 8], P(('groups', 'role', 'ep')), may hold values from 0.049804688 to 1
- w_gate: bfloat16 [16, 2048, 768], P(('role', 'ep'), None, 'tp'), may hold values from -0.125 to 0.125
- w_up: bfloat16 [16, 2048, 768], P(('role', 'ep'), None, 'tp'), may hold values from -0.125 to 0.125
- w_down: bfloat16 [16, 768, 2048], P(('role', 'ep'), 'tp'), may hold values from -0.21875 to 0.21875
Outputs:
- d_tokens: bfloat16 [2048, 2048], P(('groups', 'role', 'ep'), 'tp')
- d_probs: float32 [2048, 8], P(('groups', 'role', 'ep'))
- d_w_gate: bfloat16 [16, 2048, 768], P(('groups', 'role', 'ep'), None, 'tp')
- d_w_up: bfloat16 [16, 2048, 768], P(('groups', 'role', 'ep'), None, 'tp')
- d_w_down: bfloat16 [16, 768, 2048], P(('groups', 'role', 'ep'), 'tp')
The draws below stay inside these ranges and needn't reach their ends.
Inputs may be any that keep to these rules, and one draw needn't show every extreme that they name: `routes`: in each aligned block of 128 rows (the tokens of one index of role and ep) no expert is named by more than 72 rows, a bound that some block reaches.
All inputs are finite; a program needn't handle non-finite values.
Results may differ from the reference program's by a relative error of at most 0.012.
Values may be sent and summed in bfloat16 or wider, within the bound.
No kernel may reach another device: no remote copies, remote signals or barrier semaphores. Data moves between devices by JAX's collectives and lax.ppermute only.
A program may use at most 128 MiB of HBM per device.

```python
import math
import jax
import jax.numpy as jnp
import numpy as np
from jax import lax

D = 2048
HIDDEN_SIZE = 768
TOP = 8
TOK_DEV = 128
EXPERTS = 16
CAP = 72
TOKENS = 2048
N_TP = 2


def levels(rng, dims, cuts, smallest, largest):
    loudness = 1.0
    for position, parts in cuts:
        heights = jax.random.uniform(jax.random.fold_in(jax.random.fold_in(rng, 6), position), (parts,), jnp.float32, smallest / len(cuts), largest / len(cuts))
        loudness = loudness * jnp.repeat(jnp.exp(heights), dims[position] // parts).reshape((-1,) + (1,) * (len(dims) - 1 - position))
    return loudness


def routed_block(rng, own, number, rows, amount, top, bound, lean):
    ranking = jax.random.permutation(rng, amount)
    crowded, usual = load_shares(amount, rows * top, bound, lean, True), load_shares(amount, rows * top, bound, lean, False)
    places = jnp.arange(amount)

    def named(lengths, rotation):
        used = int((lengths > 0).sum())
        fixed = max(1, used // 4)
        moved = fixed + (places - fixed + rotation * (used - fixed)) % max(1, amount - fixed)
        return jnp.zeros((amount,), jnp.int32).at[ranking[jnp.where(places < fixed, places, moved)]].set(jnp.asarray(lengths, jnp.int32))

    lengths = jnp.where(number % 4 == 0, named(crowded, number // 4), named(usual, number - number // 4 - 1))
    mixed = jax.random.permutation(jax.random.fold_in(own, 3), amount)
    giver, taker = mixed[0:amount // 2 * 2:2], mixed[1:amount // 2 * 2:2]
    room = jnp.minimum(lengths[giver] - 1, bound - lengths[taker]) // 2
    room = jnp.where((giver == ranking[0]) | (taker == ranking[0]) | (lengths[taker] == 0), 0, jnp.maximum(room, 0))
    moved = jax.random.randint(jax.random.fold_in(own, 4), (amount // 2,), 0, 1 << 20) % (room + 1)
    lengths = lengths.at[giver].add(-moved).at[taker].add(moved)
    labels = jnp.searchsorted(jnp.cumsum(lengths), jnp.arange(rows * top), side="right").astype(jnp.int32)
    table = labels.reshape(top, rows).T
    table = table[jax.random.permutation(jax.random.fold_in(own, 1), rows)]
    rotation = jax.random.randint(jax.random.fold_in(own, 2), (rows, 1), 0, top)
    return jnp.take_along_axis(table, (jnp.arange(top)[None, :] + rotation) % top, axis=1)


def load_shares(amount, total, bound, lean, full):
    loads = [(1 << 20) // math.isqrt(standing ** lean) + 1 for standing in range(1, amount + 1)]
    largest = bound if full else min(bound, max(-(-total // amount), total * loads[0] // sum(loads)))
    least = 1 if total - largest >= amount - 1 else 0
    holding, surplus = [largest] + [least] * (amount - 1), total - largest - least * (amount - 1)
    while surplus > 0:
        candidates = [i for i in range(1, amount) if holding[i] < largest] or [i for i in range(1, amount) if holding[i] < bound]
        pool, budget = sum([loads[i] for i in candidates]), surplus
        for i in candidates:
            addition = min(bound - holding[i], max(1, budget * loads[i] // pool), surplus)
            holding[i] = holding[i] + addition
            surplus = surplus - addition
    return np.array(holding)


def gaussian(stream_key, dims, scale, reach, cuts=(), held_as=jnp.bfloat16):
    result = scale * jax.random.normal(stream_key, dims, jnp.float32)
    if cuts:
        result = result * levels(stream_key, dims, cuts, -0.22, 0.18)
    return jnp.clip(result, -reach, reach).astype(held_as)


def setup_inputs(seed: int = 0, part: int = 0) -> dict:
    splits = jax.random.split(jax.random.key(seed), 8)
    own_keys = jax.random.split(jax.random.fold_in(splits[7], part), 8)
    tokens = gaussian(own_keys[0], (TOKENS, D), 1.0, 6.0, ((0, 16), (1, 2)))
    out_grad = gaussian(own_keys[1], (TOKENS, D), 1.0, 6.0, ((0, 16), (1, 2)))
    routes_keys = jax.random.split(jax.random.fold_in(own_keys[2], 1), TOKENS // TOK_DEV)
    routes_turns = jax.random.permutation(jax.random.fold_in(own_keys[2], 3), TOKENS // TOK_DEV)
    routes = jax.vmap(lambda own, number: routed_block(jax.random.fold_in(own_keys[2], 2), own, number, TOK_DEV, EXPERTS, TOP, CAP, 2))(routes_keys, routes_turns).reshape((TOKENS, TOP))
    probs = jnp.clip(jnp.exp(math.log(1.0) - 2.9996462 * jax.random.uniform(own_keys[3], (TOKENS, TOP), jnp.float32) ** levels(own_keys[3], (TOKENS, TOP), ((0, 16),), -0.2, 0.2)), 0.049804688, 1.0).astype(jnp.bfloat16)
    w_gate = gaussian(splits[4], (EXPERTS, D, HIDDEN_SIZE), D ** -0.5, 0.125, ((0, 16), (2, 2)))
    w_up = gaussian(splits[5], (EXPERTS, D, HIDDEN_SIZE), D ** -0.5, 0.125, ((0, 16), (2, 2)))
    w_down = gaussian(splits[6], (EXPERTS, HIDDEN_SIZE, D), HIDDEN_SIZE ** -0.5, 0.21875, ((0, 16), (1, 2)))
    return {"tokens": tokens, "out_grad": out_grad, "routes": routes, "probs": probs, "w_gate": w_gate, "w_up": w_up, "w_down": w_down}


HIGHEST_PRECISION = lax.Precision.HIGHEST


def reference(tokens, out_grad, routes, probs, w_gate, w_up, w_down):
    total_rows = tokens.shape[0]
    width_full = tokens.shape[1]
    blocks = total_rows // TOK_DEV
    length = TOK_DEV * TOP
    routes_block = routes.reshape(blocks, length)
    onehot = (routes_block[:, :, None] == jnp.arange(EXPERTS, dtype=jnp.int32)[None, None, :]).astype(jnp.int32)
    before = jnp.cumsum(onehot, axis=1) - onehot
    slot_index = jnp.sum(before * onehot, axis=2).reshape(-1).astype(jnp.int32)
    owner_ids = routes_block.reshape(-1).astype(jnp.int32)
    source = jnp.repeat(jnp.arange(blocks, dtype=jnp.int32), length)
    entries = jnp.arange(blocks * length, dtype=jnp.int32)
    slot_table = jnp.full((EXPERTS, blocks, CAP), blocks * length, jnp.int32)
    slot_table = slot_table.at[owner_ids, source, slot_index].set(entries)
    padded_x = jnp.concatenate([tokens.astype(jnp.float32), jnp.zeros((1, width_full), jnp.float32)], 0)
    padded_g = jnp.concatenate([out_grad.astype(jnp.float32), jnp.zeros((1, width_full), jnp.float32)], 0)
    padded_p = jnp.concatenate([probs.reshape(-1).astype(jnp.float32), jnp.zeros((1,), jnp.float32)], 0)
    hidden_size = w_gate.shape[2]
    part_size = hidden_size // N_TP

    def expert(carried, inputs):
        d_tok, d_prob = carried
        table_rows, gate_weight, up_weight, down_weight = inputs
        entry_index = table_rows.reshape(-1)
        token_index = entry_index // TOP
        rows_x = padded_x[token_index]
        rows_g = padded_g[token_index]
        weight_p = padded_p[entry_index][:, None]
        gate_f = gate_weight.astype(jnp.float32)
        up_f = up_weight.astype(jnp.float32)
        down_f = down_weight.astype(jnp.float32)
        gate_rows = jnp.dot(rows_x, gate_f, precision=HIGHEST_PRECISION)
        up_rows = jnp.dot(rows_x, up_f, precision=HIGHEST_PRECISION)
        sigmoid_gate = jax.nn.sigmoid(gate_rows)
        activated = gate_rows * sigmoid_gate
        hidden = activated * up_rows
        back_rows = jnp.dot(rows_g, down_f.T, precision=HIGHEST_PRECISION)
        scores = jnp.sum(hidden * back_rows, axis=1)
        hidden_grad = weight_p * back_rows
        d_gate_rows = (hidden_grad * up_rows * sigmoid_gate * (1.0 + gate_rows * (1.0 - sigmoid_gate))).astype(jnp.bfloat16)
        d_up_rows = (hidden_grad * activated).astype(jnp.bfloat16)
        scaled = (weight_p * hidden).astype(jnp.bfloat16)
        d_gate_rows, d_up_rows, scaled = lax.optimization_barrier((d_gate_rows, d_up_rows, scaled))
        d_gate_f = d_gate_rows.astype(jnp.float32)
        d_up_f = d_up_rows.astype(jnp.float32)
        grad_down = jnp.dot(scaled.astype(jnp.float32).T, rows_g, precision=HIGHEST_PRECISION).astype(jnp.bfloat16)
        grad_gate = jnp.dot(rows_x.T, d_gate_f, precision=HIGHEST_PRECISION).astype(jnp.bfloat16)
        grad_up = jnp.dot(rows_x.T, d_up_f, precision=HIGHEST_PRECISION).astype(jnp.bfloat16)
        row_count = entry_index.shape[0]
        gate_blocks = d_gate_f.reshape(row_count, N_TP, part_size)
        up_blocks = d_up_f.reshape(row_count, N_TP, part_size)
        gate_split = gate_f.reshape(width_full, N_TP, part_size)
        up_split = up_f.reshape(width_full, N_TP, part_size)
        pieces = jnp.einsum("rbh,dbh->rbd", gate_blocks, gate_split, precision=HIGHEST_PRECISION)
        pieces = pieces + jnp.einsum("rbh,dbh->rbd", up_blocks, up_split, precision=HIGHEST_PRECISION)
        pieces = lax.optimization_barrier(pieces.astype(jnp.bfloat16)).astype(jnp.float32)
        route_grad = lax.optimization_barrier(jnp.sum(pieces, axis=1).astype(jnp.bfloat16)).astype(jnp.float32)
        d_tok = d_tok.at[token_index].add(route_grad)
        d_prob = d_prob.at[entry_index].add(scores)
        return (d_tok, d_prob), (grad_gate, grad_up, grad_down)

    start = (jnp.zeros((total_rows + 1, width_full), jnp.float32), jnp.zeros((blocks * length + 1,), jnp.float32))
    (d_tok, d_prob), (grads_gate, grads_up, grads_down) = lax.scan(expert, start, (slot_table, w_gate, w_up, w_down))
    d_tokens = d_tok[:total_rows].astype(jnp.bfloat16)
    d_probs = d_prob[:blocks * length].reshape(total_rows, TOP)
    return (d_tokens, d_probs, grads_gate, grads_up, grads_down)
```

```python
import math

import jax
import jax.numpy as jnp
from jax import lax
from jax.experimental import pallas as pl
from jax.experimental.pallas import tpu as pltpu
from jax.sharding import PartitionSpec as P


def pad_rows(array):
    return jnp.concatenate([array, jnp.zeros((1, array.shape[1]), array.dtype)], 0)


def routed_device(tokens, out_grad, routes, probs, w_gate, w_up, w_down):
    owners = lax.axis_size(("role", "ep"))
    tok_rows, top_count = routes.shape
    width_full = w_gate.shape[1]
    part_width = w_gate.shape[2]
    capacity = min(tok_rows, tok_rows * top_count * 9 // (8 * owners))
    entry_total = tok_rows * top_count
    routes_flat = routes.reshape(-1)
    onehot = (routes_flat[:, None] == jnp.arange(owners, dtype=jnp.int32)[None, :]).astype(
        jnp.int32
    )
    before = jnp.cumsum(onehot, axis=0) - onehot
    slot_index = jnp.sum(before * onehot, axis=1)
    target = routes_flat * capacity + slot_index
    row_count = owners * capacity
    entry_of_slot = (
        jnp.full((row_count,), entry_total, jnp.int32)
        .at[target]
        .set(jnp.arange(entry_total, dtype=jnp.int32))
    )
    token_of_slot = entry_of_slot // top_count
    padded_prob = jnp.concatenate([probs.reshape(-1), jnp.zeros((1,), probs.dtype)], 0)
    send_prob = padded_prob[entry_of_slot].reshape(owners, capacity)
    send_x = pad_rows(tokens)[token_of_slot]
    send_g = pad_rows(out_grad)[token_of_slot]
    slice_x, slice_g, recv_p = (
        lax.all_to_all(
            send_x.reshape(owners, capacity, tokens.shape[1]),
            ("role", "ep"),
            split_axis=0,
            concat_axis=0,
            tiled=True,
        ),
        lax.all_to_all(
            send_g.reshape(owners, capacity, tokens.shape[1]),
            ("role", "ep"),
            split_axis=0,
            concat_axis=0,
            tiled=True,
        ),
        lax.all_to_all(send_prob, ("role", "ep"), split_axis=0, concat_axis=0, tiled=True),
    )
    recv_x, recv_g = (
        lax.all_gather(slice_x, "tp", axis=2, tiled=True),
        lax.all_gather(slice_g, "tp", axis=2, tiled=True),
    )
    rows_x = recv_x.reshape(row_count, width_full)
    rows_g = recv_g.reshape(row_count, width_full)
    weight_p = recv_p.reshape(row_count, 1).astype(jnp.float32)
    gate_up = jnp.concatenate([w_gate[0], w_up[0]], 1)
    down_shard = w_down[0]
    both_rows = jnp.dot(rows_x, gate_up, preferred_element_type=jnp.float32)
    gate_rows = both_rows[:, :part_width]
    up_rows = both_rows[:, part_width:]
    sigmoid_gate = jax.nn.sigmoid(gate_rows)
    activated = gate_rows * sigmoid_gate
    hidden = activated * up_rows
    back_rows = lax.dot_general(
        rows_g, down_shard, (((1,), (1,)), ((), ())), preferred_element_type=jnp.float32
    )
    scores = lax.psum(jnp.sum(hidden * back_rows, axis=1), "tp")
    hidden_grad = weight_p * back_rows
    d_gate_rows = (
        hidden_grad * up_rows * sigmoid_gate * (1.0 + gate_rows * (1.0 - sigmoid_gate))
    ).astype(jnp.bfloat16)
    d_up_rows = (hidden_grad * activated).astype(jnp.bfloat16)
    d_both = jnp.concatenate([d_gate_rows, d_up_rows], 1)
    scaled = (weight_p * hidden).astype(jnp.bfloat16)
    grad_down = lax.dot_general(
        scaled, rows_g, (((0,), (0,)), ((), ())), preferred_element_type=jnp.float32
    )
    grad_both = lax.dot_general(
        rows_x, d_both, (((0,), (0,)), ((), ())), preferred_element_type=jnp.float32
    )
    grad_gate = grad_both[:, :part_width]
    grad_up = grad_both[:, part_width:]
    partial_low = lax.dot_general(
        d_both, gate_up, (((1,), (1,)), ((), ())), preferred_element_type=jnp.float32
    ).astype(jnp.bfloat16)
    home_s = lax.all_to_all(
        scores.reshape(owners, capacity), ("role", "ep"), split_axis=0, concat_axis=0, tiled=True
    )
    summed = lax.psum_scatter(
        partial_low.reshape(owners, capacity, width_full), "tp", scatter_dimension=2, tiled=True
    ).astype(jnp.float32)
    summed_low = summed.astype(jnp.bfloat16)
    home_x = lax.all_to_all(summed_low, ("role", "ep"), split_axis=0, concat_axis=0, tiled=True)
    slice_width = summed.shape[2]
    route_rows = home_x.reshape(row_count, slice_width).astype(jnp.float32)
    d_tok = (
        jnp.zeros((tok_rows + 1, slice_width), jnp.float32)
        .at[token_of_slot]
        .add(route_rows)[:tok_rows]
    )
    d_probs = home_s.reshape(-1)[target].reshape(tok_rows, top_count)
    return (
        d_tok.astype(jnp.bfloat16),
        d_probs,
        grad_gate.astype(jnp.bfloat16)[None],
        grad_up.astype(jnp.bfloat16)[None],
        grad_down.astype(jnp.bfloat16)[None],
    )


def slot_capacity(tok_rows, top_count, owners):
    return min(tok_rows, tok_rows * top_count * 9 // (8 * owners))


def rows_kernel(x_ref, g_ref, p_ref, wg_ref, wu_ref, wd_ref, both_ref, scaled_ref, score_ref, piece_ref, wgu):
    part = wg_ref.shape[2]
    half = x_ref.shape[2]

    @pl.when(pl.program_id(0) == 0)
    def _():
        wgu[:, :part] = wg_ref[0]
        wgu[:, part:] = wu_ref[0]

    rows = jnp.dot(x_ref[0], wgu[:half], preferred_element_type=jnp.float32)
    rows = rows + jnp.dot(x_ref[1], wgu[half:], preferred_element_type=jnp.float32)
    wd = wd_ref[0]
    back = lax.dot_general(g_ref[0], wd[:, :half], (((1,), (1,)), ((), ())), preferred_element_type=jnp.float32)
    back = back + lax.dot_general(g_ref[1], wd[:, half:], (((1,), (1,)), ((), ())), preferred_element_type=jnp.float32)
    gate, up = rows[:, :part], rows[:, part:]
    sig = jax.nn.sigmoid(gate)
    act = gate * sig
    hidden = act * up
    score_ref[...] = jnp.sum(hidden * back, axis=1, keepdims=True)
    prob = p_ref[...]
    hgrad = prob * back
    both_ref[:, :part] = (hgrad * up * sig * (1.0 + gate * (1.0 - sig))).astype(jnp.bfloat16)
    both_ref[:, part:] = (hgrad * act).astype(jnp.bfloat16)
    scaled_ref[...] = (prob * hidden).astype(jnp.bfloat16)
    both = both_ref[...]
    piece_ref[0] = lax.dot_general(both, wgu[:half], (((1,), (1,)), ((), ())), preferred_element_type=jnp.float32).astype(jnp.bfloat16)
    piece_ref[1] = lax.dot_general(both, wgu[half:], (((1,), (1,)), ((), ())), preferred_element_type=jnp.float32).astype(jnp.bfloat16)


def rows_call(x_all, g_all, prob, w_gate, w_up, w_down):
    tp, total, half = x_all.shape
    part = w_gate.shape[2]
    width = w_gate.shape[1]
    step = math.gcd(total, 256)
    grid = (total // step,)
    moving = pl.BlockSpec((tp, step, half), lambda i: (0, i, 0))
    return pl.pallas_call(
        rows_kernel,
        grid=grid,
        in_specs=[
            moving,
            moving,
            pl.BlockSpec((step, 1), lambda i: (i, 0)),
            pl.BlockSpec((1, width, part), lambda i: (0, 0, 0)),
            pl.BlockSpec((1, width, part), lambda i: (0, 0, 0)),
            pl.BlockSpec((1, part, width), lambda i: (0, 0, 0)),
        ],
        out_specs=[
            pl.BlockSpec((step, 2 * part), lambda i: (i, 0)),
            pl.BlockSpec((step, part), lambda i: (i, 0)),
            pl.BlockSpec((step, 1), lambda i: (i, 0)),
            moving,
        ],
        out_shape=[
            jax.ShapeDtypeStruct((total, 2 * part), jnp.bfloat16),
            jax.ShapeDtypeStruct((total, part), jnp.bfloat16),
            jax.ShapeDtypeStruct((total, 1), jnp.float32),
            jax.ShapeDtypeStruct((tp, total, half), jnp.bfloat16),
        ],
        scratch_shapes=[pltpu.VMEM((width, 2 * part), jnp.bfloat16)],
        compiler_params=pltpu.CompilerParams(vmem_limit_bytes=48 << 20),
        cost_estimate=pl.CostEstimate(flops=10 * total * width * part, bytes_accessed=6 * total * width * 2, transcendentals=total * part),
        name="rows",
    )(x_all, g_all, prob, w_gate, w_up, w_down)


def grads_kernel(x_ref, g_ref, both_ref, scaled_ref, dg_ref, du_ref, dd_ref):
    part = scaled_ref.shape[1]
    both = lax.dot_general(x_ref[0], both_ref[...], (((0,), (0,)), ((), ())), preferred_element_type=jnp.float32)
    dg_ref[0] = both[:, :part].astype(jnp.bfloat16)
    du_ref[0] = both[:, part:].astype(jnp.bfloat16)
    dd_ref[0] = lax.dot_general(scaled_ref[...], g_ref[0], (((0,), (0,)), ((), ())), preferred_element_type=jnp.float32).astype(jnp.bfloat16)


def grads_call(x_all, g_all, both, scaled):
    tp, total, half = x_all.shape
    part = scaled.shape[1]
    width = tp * half
    step = math.gcd(half, 256)
    per = half // step
    moving = pl.BlockSpec((1, total, step), lambda i: (i // per, 0, i % per))
    return pl.pallas_call(
        grads_kernel,
        grid=(width // step,),
        in_specs=[
            moving,
            moving,
            pl.BlockSpec((total, 2 * part), lambda i: (0, 0)),
            pl.BlockSpec((total, part), lambda i: (0, 0)),
        ],
        out_specs=[
            pl.BlockSpec((1, step, part), lambda i: (0, i, 0)),
            pl.BlockSpec((1, step, part), lambda i: (0, i, 0)),
            pl.BlockSpec((1, part, step), lambda i: (0, 0, i)),
        ],
        out_shape=[
            jax.ShapeDtypeStruct((1, width, part), jnp.bfloat16),
            jax.ShapeDtypeStruct((1, width, part), jnp.bfloat16),
            jax.ShapeDtypeStruct((1, part, width), jnp.bfloat16),
        ],
        compiler_params=pltpu.CompilerParams(vmem_limit_bytes=48 << 20),
        cost_estimate=pl.CostEstimate(flops=6 * total * width * part, bytes_accessed=6 * total * width, transcendentals=0),
        name="grads",
    )(x_all, g_all, both, scaled)


def dense_device(tokens, out_grad, routes, probs, w_gate, w_up, w_down):
    everyone = ("tp", "role", "ep")
    owners = lax.axis_size(("role", "ep"))
    tp = lax.axis_size("tp")
    me = lax.axis_index(("role", "ep"))
    tok_rows, half = tokens.shape
    total = owners * tok_rows
    chosen = routes[:, :, None] == jnp.arange(owners, dtype=jnp.int32)
    table = jnp.sum(jnp.where(chosen, probs[:, :, None].astype(jnp.float32), 0.0), axis=1)
    table_all = lax.all_gather(table.astype(jnp.bfloat16), ("role", "ep"), axis=0, tiled=True)
    prob = lax.dynamic_slice(table_all, (0, me), (total, 1)).astype(jnp.float32)
    x_all = lax.all_gather(tokens, everyone, axis=0, tiled=True).reshape(tp, total, half)
    g_all = lax.all_gather(out_grad, everyone, axis=0, tiled=True).reshape(tp, total, half)
    both, scaled, score, piece = rows_call(x_all, g_all, prob, w_gate, w_up, w_down)
    d_tok = lax.psum_scatter(piece.reshape(tp * total, half), everyone, scatter_dimension=0, tiled=True)
    scores = lax.all_gather(score.reshape(1, total), everyone, axis=0, tiled=True)
    d_gate, d_up, d_down = grads_call(x_all, g_all, both, scaled)
    home = lax.dynamic_slice(scores.reshape(tp, owners, total), (0, 0, me * tok_rows), (tp, owners, tok_rows))
    home = jnp.sum(home, axis=0).T
    d_probs = jnp.sum(jnp.where(chosen, home[:, None, :], 0.0), axis=2)
    return d_tok, d_probs, d_gate, d_up, d_down


def per_device(tokens, out_grad, routes, probs, w_gate, w_up, w_down):
    owners = lax.axis_size(("role", "ep"))
    tok_rows, top_count = routes.shape
    if 2 * slot_capacity(tok_rows, top_count, owners) >= tok_rows:
        return dense_device(tokens, out_grad, routes, probs, w_gate, w_up, w_down)
    return routed_device(tokens, out_grad, routes, probs, w_gate, w_up, w_down)


def solution(mesh):
    in_specs = (
        P(("groups", "role", "ep"), "tp"),
        P(("groups", "role", "ep"), "tp"),
        P(("groups", "role", "ep"), None),
        P(("groups", "role", "ep"), None),
        P(("role", "ep"), None, "tp"),
        P(("role", "ep"), None, "tp"),
        P(("role", "ep"), "tp", None),
    )
    out_specs = (
        P(("groups", "role", "ep"), "tp"),
        P(("groups", "role", "ep"), None),
        P(("groups", "role", "ep"), None, "tp"),
        P(("groups", "role", "ep"), None, "tp"),
        P(("groups", "role", "ep"), "tp", None),
    )
    return jax.shard_map(
        per_device, mesh=mesh, in_specs=in_specs, out_specs=out_specs, check_vma=False
    )
```

```python
import functools
import math

import jax
import jax.numpy as jnp
from jax import lax
from jax.experimental import pallas as pl
from jax.experimental.pallas import tpu as pltpu
from jax.sharding import PartitionSpec as P


def pad_rows(array):
    return jnp.concatenate([array, jnp.zeros((1, array.shape[1]), array.dtype)], 0)


def routed_device(tokens, out_grad, routes, probs, w_gate, w_up, w_down):
    owners = lax.axis_size(("role", "ep"))
    tok_rows, top_count = routes.shape
    width_full = w_gate.shape[1]
    part_width = w_gate.shape[2]
    capacity = min(tok_rows, tok_rows * top_count * 9 // (8 * owners))
    entry_total = tok_rows * top_count
    routes_flat = routes.reshape(-1)
    onehot = (routes_flat[:, None] == jnp.arange(owners, dtype=jnp.int32)[None, :]).astype(
        jnp.int32
    )
    before = jnp.cumsum(onehot, axis=0) - onehot
    slot_index = jnp.sum(before * onehot, axis=1)
    target = routes_flat * capacity + slot_index
    row_count = owners * capacity
    entry_of_slot = (
        jnp.full((row_count,), entry_total, jnp.int32)
        .at[target]
        .set(jnp.arange(entry_total, dtype=jnp.int32))
    )
    token_of_slot = entry_of_slot // top_count
    padded_prob = jnp.concatenate([probs.reshape(-1), jnp.zeros((1,), probs.dtype)], 0)
    send_prob = padded_prob[entry_of_slot].reshape(owners, capacity)
    send_x = pad_rows(tokens)[token_of_slot]
    send_g = pad_rows(out_grad)[token_of_slot]
    slice_x, slice_g, recv_p = (
        lax.all_to_all(
            send_x.reshape(owners, capacity, tokens.shape[1]),
            ("role", "ep"),
            split_axis=0,
            concat_axis=0,
            tiled=True,
        ),
        lax.all_to_all(
            send_g.reshape(owners, capacity, tokens.shape[1]),
            ("role", "ep"),
            split_axis=0,
            concat_axis=0,
            tiled=True,
        ),
        lax.all_to_all(send_prob, ("role", "ep"), split_axis=0, concat_axis=0, tiled=True),
    )
    recv_x, recv_g = (
        lax.all_gather(slice_x, "tp", axis=2, tiled=True),
        lax.all_gather(slice_g, "tp", axis=2, tiled=True),
    )
    rows_x = recv_x.reshape(row_count, width_full)
    rows_g = recv_g.reshape(row_count, width_full)
    weight_p = recv_p.reshape(row_count, 1).astype(jnp.float32)
    gate_up = jnp.concatenate([w_gate[0], w_up[0]], 1)
    down_shard = w_down[0]
    both_rows = jnp.dot(rows_x, gate_up, preferred_element_type=jnp.float32)
    gate_rows = both_rows[:, :part_width]
    up_rows = both_rows[:, part_width:]
    sigmoid_gate = jax.nn.sigmoid(gate_rows)
    activated = gate_rows * sigmoid_gate
    hidden = activated * up_rows
    back_rows = lax.dot_general(
        rows_g, down_shard, (((1,), (1,)), ((), ())), preferred_element_type=jnp.float32
    )
    scores = lax.psum(jnp.sum(hidden * back_rows, axis=1), "tp")
    hidden_grad = weight_p * back_rows
    d_gate_rows = (
        hidden_grad * up_rows * sigmoid_gate * (1.0 + gate_rows * (1.0 - sigmoid_gate))
    ).astype(jnp.bfloat16)
    d_up_rows = (hidden_grad * activated).astype(jnp.bfloat16)
    d_both = jnp.concatenate([d_gate_rows, d_up_rows], 1)
    scaled = (weight_p * hidden).astype(jnp.bfloat16)
    grad_down = lax.dot_general(
        scaled, rows_g, (((0,), (0,)), ((), ())), preferred_element_type=jnp.float32
    )
    grad_both = lax.dot_general(
        rows_x, d_both, (((0,), (0,)), ((), ())), preferred_element_type=jnp.float32
    )
    grad_gate = grad_both[:, :part_width]
    grad_up = grad_both[:, part_width:]
    partial_low = lax.dot_general(
        d_both, gate_up, (((1,), (1,)), ((), ())), preferred_element_type=jnp.float32
    ).astype(jnp.bfloat16)
    home_s = lax.all_to_all(
        scores.reshape(owners, capacity), ("role", "ep"), split_axis=0, concat_axis=0, tiled=True
    )
    summed = lax.psum_scatter(
        partial_low.reshape(owners, capacity, width_full), "tp", scatter_dimension=2, tiled=True
    ).astype(jnp.float32)
    summed_low = summed.astype(jnp.bfloat16)
    home_x = lax.all_to_all(summed_low, ("role", "ep"), split_axis=0, concat_axis=0, tiled=True)
    slice_width = summed.shape[2]
    route_rows = home_x.reshape(row_count, slice_width).astype(jnp.float32)
    d_tok = (
        jnp.zeros((tok_rows + 1, slice_width), jnp.float32)
        .at[token_of_slot]
        .add(route_rows)[:tok_rows]
    )
    d_probs = home_s.reshape(-1)[target].reshape(tok_rows, top_count)
    return (
        d_tok.astype(jnp.bfloat16),
        d_probs,
        grad_gate.astype(jnp.bfloat16)[None],
        grad_up.astype(jnp.bfloat16)[None],
        grad_down.astype(jnp.bfloat16)[None],
    )


def slot_capacity(tok_rows, top_count, owners):
    return min(tok_rows, tok_rows * top_count * 9 // (8 * owners))


def rows_kernel(
    tp_ref, x_ref, g_ref, p_ref, wg0, wg1, wu0, wu1, wd0, wd1, both_ref, scaled_ref, score_ref, keep_ref, send_ref, wgu
):
    part = wg0.shape[2]
    half = x_ref.shape[2]

    @pl.when(pl.program_id(0) == 0)
    def _():
        wgu[:half, :part] = wg0[0]
        wgu[:half, part:] = wu0[0]
        wgu[half:, :part] = wg1[0]
        wgu[half:, part:] = wu1[0]

    rows = jnp.dot(x_ref[0], wgu[:half], preferred_element_type=jnp.float32)
    rows = rows + jnp.dot(x_ref[1], wgu[half:], preferred_element_type=jnp.float32)
    back = lax.dot_general(g_ref[0], wd0[0], (((1,), (1,)), ((), ())), preferred_element_type=jnp.float32)
    back = back + lax.dot_general(g_ref[1], wd1[0], (((1,), (1,)), ((), ())), preferred_element_type=jnp.float32)
    gate, up = rows[:, :part], rows[:, part:]
    sig = jax.nn.sigmoid(gate)
    act = gate * sig
    hidden = act * up
    score_ref[...] = jnp.sum(hidden * back, axis=1, keepdims=True)
    prob = p_ref[...]
    hgrad = prob * back
    both_ref[:, :part] = (hgrad * up * sig * (1.0 + gate * (1.0 - sig))).astype(jnp.bfloat16)
    both_ref[:, part:] = (hgrad * act).astype(jnp.bfloat16)
    scaled_ref[...] = (prob * hidden).astype(jnp.bfloat16)
    both = both_ref[...]
    for index in range(2):
        low = lax.dot_general(
            both, wgu[index * half : (index + 1) * half], (((1,), (1,)), ((), ())), preferred_element_type=jnp.float32
        ).astype(jnp.bfloat16)

        @pl.when(pl.program_id(0) == 0)
        def _(low=low, index=index):
            keep_ref[index] = low

        @pl.when(pl.program_id(0) == 1)
        def _(low=low, index=index):
            send_ref[index] = low


def rows_call(which, x_rows, g_rows, prob, w_gate, w_up, w_down):
    _, total, half = x_rows.shape
    _, width, part = w_gate.shape
    step = total // 2
    moving = pl.BlockSpec((2, step, half), lambda i, w: (0, i, 0))
    fixed = pl.BlockSpec((2, step, half), lambda i, w: (0, 0, 0))
    own_in = pl.BlockSpec((1, half, part), lambda i, w: (0, w[0], 0))
    far_in = pl.BlockSpec((1, half, part), lambda i, w: (0, 1 - w[0], 0))
    own_out = pl.BlockSpec((1, part, half), lambda i, w: (0, 0, w[0]))
    far_out = pl.BlockSpec((1, part, half), lambda i, w: (0, 0, 1 - w[0]))
    return pl.pallas_call(
        rows_kernel,
        grid_spec=pltpu.PrefetchScalarGridSpec(
            num_scalar_prefetch=1,
            grid=(2,),
            in_specs=[
                moving,
                moving,
                pl.BlockSpec((step, 1), lambda i, w: (i, 0)),
                own_in,
                far_in,
                own_in,
                far_in,
                own_out,
                far_out,
            ],
            out_specs=[
                pl.BlockSpec((step, 2 * part), lambda i, w: (i, 0)),
                pl.BlockSpec((step, part), lambda i, w: (i, 0)),
                pl.BlockSpec((step, 1), lambda i, w: (i, 0)),
                fixed,
                fixed,
            ],
            scratch_shapes=[pltpu.VMEM((width, 2 * part), jnp.bfloat16)],
        ),
        out_shape=[
            jax.ShapeDtypeStruct((total, 2 * part), jnp.bfloat16),
            jax.ShapeDtypeStruct((total, part), jnp.bfloat16),
            jax.ShapeDtypeStruct((total, 1), jnp.float32),
            jax.ShapeDtypeStruct((2, step, half), jnp.bfloat16),
            jax.ShapeDtypeStruct((2, step, half), jnp.bfloat16),
        ],
        compiler_params=pltpu.CompilerParams(vmem_limit_bytes=48 << 20),
        cost_estimate=pl.CostEstimate(
            flops=10 * total * width * part, bytes_accessed=6 * total * width + 6 * width * part, transcendentals=total * part
        ),
        name="rows",
    )(which, x_rows, g_rows, prob, w_gate, w_gate, w_up, w_up, w_down, w_down)


def grads_kernel(count, tp_ref, *refs):
    x_refs, g_refs = refs[:count], refs[count : 2 * count]
    both_refs, scaled_refs = refs[2 * count : 3 * count], refs[3 * count : 4 * count]
    dg_ref, du_ref, dd_ref = refs[4 * count :]
    part = scaled_refs[0].shape[1]
    both, down = None, None
    for x_ref, g_ref, both_ref, scaled_ref in zip(x_refs, g_refs, both_refs, scaled_refs):
        term = lax.dot_general(x_ref[0], both_ref[...], (((0,), (0,)), ((), ())), preferred_element_type=jnp.float32)
        both = term if both is None else both + term
        term = lax.dot_general(scaled_ref[...], g_ref[0], (((0,), (0,)), ((), ())), preferred_element_type=jnp.float32)
        down = term if down is None else down + term
    dg_ref[0] = both[:, :part].astype(jnp.bfloat16)
    du_ref[0] = both[:, part:].astype(jnp.bfloat16)
    dd_ref[0] = down.astype(jnp.bfloat16)


def grads_call(which, x_parts, g_parts, both_parts, scaled_parts):
    count = len(x_parts)
    _, total, half = x_parts[0].shape
    part = scaled_parts[0].shape[1]
    width = 2 * half
    step = math.gcd(half, 256)
    per = half // step

    def place(i, w):
        return jnp.where(i < per, w[0], 1 - w[0]) * per + i % per

    moving = pl.BlockSpec((1, total, step), lambda i, w: (i // per, 0, i % per))
    return pl.pallas_call(
        functools.partial(grads_kernel, count),
        grid_spec=pltpu.PrefetchScalarGridSpec(
            num_scalar_prefetch=1,
            grid=(width // step,),
            in_specs=[moving] * (2 * count)
            + [pl.BlockSpec((total, 2 * part), lambda i, w: (0, 0))] * count
            + [pl.BlockSpec((total, part), lambda i, w: (0, 0))] * count,
            out_specs=[
                pl.BlockSpec((1, step, part), lambda i, w: (0, place(i, w), 0)),
                pl.BlockSpec((1, step, part), lambda i, w: (0, place(i, w), 0)),
                pl.BlockSpec((1, part, step), lambda i, w: (0, 0, place(i, w))),
            ],
        ),
        out_shape=[
            jax.ShapeDtypeStruct((1, width, part), jnp.bfloat16),
            jax.ShapeDtypeStruct((1, width, part), jnp.bfloat16),
            jax.ShapeDtypeStruct((1, part, width), jnp.bfloat16),
        ],
        compiler_params=pltpu.CompilerParams(vmem_limit_bytes=48 << 20),
        cost_estimate=pl.CostEstimate(
            flops=6 * count * total * width * part, bytes_accessed=6 * count * total * width, transcendentals=0
        ),
        name="grads",
    )(which, *x_parts, *g_parts, *both_parts, *scaled_parts)


def dense_device(tokens, out_grad, routes, probs, w_gate, w_up, w_down):
    owners = lax.axis_size(("role", "ep"))
    ep = lax.axis_size("ep")
    n_y = 2
    n_z = ep // n_y
    tok_rows, half = tokens.shape
    me = lax.axis_index(("role", "ep"))
    role, place, which = lax.axis_index("role"), lax.axis_index("ep"), lax.axis_index("tp")
    my_z, my_y = place // n_y, place % n_y

    def over_x(array):
        return lax.ppermute(array, "tp", [(0, 1), (1, 0)])

    def over_role(array):
        return lax.ppermute(array, "role", [(0, 1), (1, 0)])

    def over_y(array):
        return lax.ppermute(array, "ep", [(i, i + 1 - 2 * (i % n_y)) for i in range(ep)])

    def over_z(array, shift):
        return lax.ppermute(array, "ep", [(i, (i + shift * n_y) % ep) for i in range(ep)])

    steps = jnp.arange(n_z)[:, None, None]
    source = (role + jnp.arange(2)[None, :, None]) % 2 * ep + (my_z - steps) % n_z * n_y + (my_y + jnp.arange(n_y)) % n_y
    source = source.reshape(-1)

    chosen = routes[:, :, None] == jnp.arange(owners, dtype=jnp.int32)
    table = jnp.sum(jnp.where(chosen, probs[:, :, None].astype(jnp.float32), 0.0), axis=1)
    table_all = lax.all_gather(table.astype(jnp.bfloat16).T, ("role", "ep"), axis=0)
    prob = lax.dynamic_slice(table_all, (0, me, 0), (owners, 1, tok_rows)).reshape(owners, tok_rows)
    prob = prob[source].astype(jnp.float32).reshape(n_z, 2 * n_y * tok_rows, 1)

    x_own, g_own = tokens, jnp.stack([out_grad, over_x(out_grad)])
    x_parts, g_parts = [], []
    for step in range(n_z):
        if step:
            x_own, g_own = over_z(x_own, 1), over_z(g_own, 1)
        pair = jnp.concatenate([x_own, over_y(x_own)], 0)
        full = jnp.stack([pair, over_x(pair)])
        x_parts.append(jnp.concatenate([full, over_role(full)], 1))
        full = jnp.concatenate([g_own, over_y(g_own)], 1)
        g_parts.append(jnp.concatenate([full, over_role(full)], 1))

    which_ref = which.reshape(1).astype(jnp.int32)
    both_parts, scaled_parts, scores, homeward = [], [], [], []
    for step in range(n_z):
        both, scaled, score, keep, send = rows_call(
            which_ref, x_parts[step], g_parts[step], prob[step], w_gate, w_up, w_down
        )
        both_parts.append(both)
        scaled_parts.append(scaled)
        scores.append(score)
        total = keep.astype(jnp.float32) + over_role(send).astype(jnp.float32)
        total = total[0] + over_x(total[1].astype(jnp.bfloat16)).astype(jnp.float32)
        total = total[:tok_rows] + over_y(total[tok_rows:].astype(jnp.bfloat16)).astype(jnp.float32)
        homeward.append(over_z(total.astype(jnp.bfloat16), -step).astype(jnp.float32) if step else total)
    d_tok = sum(homeward[1:], homeward[0]).astype(jnp.bfloat16)
    d_gate, d_up, d_down = grads_call(which_ref, x_parts, g_parts, both_parts, scaled_parts)

    mine = jnp.concatenate(scores, 0).reshape(owners, tok_rows)
    placed = (jnp.arange(owners)[:, None] == source[None, :]).astype(jnp.float32)
    mine = jnp.sum(placed[:, :, None] * mine[None], axis=1)
    scores = lax.all_gather(mine, ("tp", "role", "ep"), axis=0)
    home = lax.dynamic_slice(scores, (0, me, 0), (2 * owners, 1, tok_rows)).reshape(2, owners, tok_rows)
    home = jnp.sum(home, axis=0).T
    d_probs = jnp.sum(jnp.where(chosen, home[:, None, :], 0.0), axis=2)
    return d_tok, d_probs, d_gate, d_up, d_down


def per_device(tokens, out_grad, routes, probs, w_gate, w_up, w_down):
    owners = lax.axis_size(("role", "ep"))
    tok_rows, top_count = routes.shape
    paired = lax.axis_size("tp") == 2 and lax.axis_size("role") == 2 and lax.axis_size("ep") % 2 == 0
    if paired and 2 * slot_capacity(tok_rows, top_count, owners) >= tok_rows:
        return dense_device(tokens, out_grad, routes, probs, w_gate, w_up, w_down)
    return routed_device(tokens, out_grad, routes, probs, w_gate, w_up, w_down)


def solution(mesh):
    in_specs = (
        P(("groups", "role", "ep"), "tp"),
        P(("groups", "role", "ep"), "tp"),
        P(("groups", "role", "ep"), None),
        P(("groups", "role", "ep"), None),
        P(("role", "ep"), None, "tp"),
        P(("role", "ep"), None, "tp"),
        P(("role", "ep"), "tp", None),
    )
    out_specs = (
        P(("groups", "role", "ep"), "tp"),
        P(("groups", "role", "ep"), None),
        P(("groups", "role", "ep"), None, "tp"),
        P(("groups", "role", "ep"), None, "tp"),
        P(("groups", "role", "ep"), "tp", None),
    )
    return jax.shard_map(
        per_device, mesh=mesh, in_specs=in_specs, out_specs=out_specs, check_vma=False
    )
```

```python
import functools
import math

import jax
import jax.numpy as jnp
from jax import lax
from jax.experimental import pallas as pl
from jax.experimental.pallas import tpu as pltpu
from jax.sharding import PartitionSpec as P


def pad_rows(array):
    return jnp.concatenate([array, jnp.zeros((1, array.shape[1]), array.dtype)], 0)


def routed_device(tokens, out_grad, routes, probs, w_gate, w_up, w_down):
    owners = lax.axis_size(("role", "ep"))
    tok_rows, top_count = routes.shape
    width_full = w_gate.shape[1]
    part_width = w_gate.shape[2]
    capacity = min(tok_rows, tok_rows * top_count * 9 // (8 * owners))
    entry_total = tok_rows * top_count
    routes_flat = routes.reshape(-1)
    onehot = (routes_flat[:, None] == jnp.arange(owners, dtype=jnp.int32)[None, :]).astype(
        jnp.int32
    )
    before = jnp.cumsum(onehot, axis=0) - onehot
    slot_index = jnp.sum(before * onehot, axis=1)
    target = routes_flat * capacity + slot_index
    row_count = owners * capacity
    entry_of_slot = (
        jnp.full((row_count,), entry_total, jnp.int32)
        .at[target]
        .set(jnp.arange(entry_total, dtype=jnp.int32))
    )
    token_of_slot = entry_of_slot // top_count
    padded_prob = jnp.concatenate([probs.reshape(-1), jnp.zeros((1,), probs.dtype)], 0)
    send_prob = padded_prob[entry_of_slot].reshape(owners, capacity)
    send_x = pad_rows(tokens)[token_of_slot]
    send_g = pad_rows(out_grad)[token_of_slot]
    slice_x, slice_g, recv_p = (
        lax.all_to_all(
            send_x.reshape(owners, capacity, tokens.shape[1]),
            ("role", "ep"),
            split_axis=0,
            concat_axis=0,
            tiled=True,
        ),
        lax.all_to_all(
            send_g.reshape(owners, capacity, tokens.shape[1]),
            ("role", "ep"),
            split_axis=0,
            concat_axis=0,
            tiled=True,
        ),
        lax.all_to_all(send_prob, ("role", "ep"), split_axis=0, concat_axis=0, tiled=True),
    )
    recv_x, recv_g = (
        lax.all_gather(slice_x, "tp", axis=2, tiled=True),
        lax.all_gather(slice_g, "tp", axis=2, tiled=True),
    )
    rows_x = recv_x.reshape(row_count, width_full)
    rows_g = recv_g.reshape(row_count, width_full)
    weight_p = recv_p.reshape(row_count, 1).astype(jnp.float32)
    gate_up = jnp.concatenate([w_gate[0], w_up[0]], 1)
    down_shard = w_down[0]
    both_rows = jnp.dot(rows_x, gate_up, preferred_element_type=jnp.float32)
    gate_rows = both_rows[:, :part_width]
    up_rows = both_rows[:, part_width:]
    sigmoid_gate = jax.nn.sigmoid(gate_rows)
    activated = gate_rows * sigmoid_gate
    hidden = activated * up_rows
    back_rows = lax.dot_general(
        rows_g, down_shard, (((1,), (1,)), ((), ())), preferred_element_type=jnp.float32
    )
    scores = lax.psum(jnp.sum(hidden * back_rows, axis=1), "tp")
    hidden_grad = weight_p * back_rows
    d_gate_rows = (
        hidden_grad * up_rows * sigmoid_gate * (1.0 + gate_rows * (1.0 - sigmoid_gate))
    ).astype(jnp.bfloat16)
    d_up_rows = (hidden_grad * activated).astype(jnp.bfloat16)
    d_both = jnp.concatenate([d_gate_rows, d_up_rows], 1)
    scaled = (weight_p * hidden).astype(jnp.bfloat16)
    grad_down = lax.dot_general(
        scaled, rows_g, (((0,), (0,)), ((), ())), preferred_element_type=jnp.float32
    )
    grad_both = lax.dot_general(
        rows_x, d_both, (((0,), (0,)), ((), ())), preferred_element_type=jnp.float32
    )
    grad_gate = grad_both[:, :part_width]
    grad_up = grad_both[:, part_width:]
    partial_low = lax.dot_general(
        d_both, gate_up, (((1,), (1,)), ((), ())), preferred_element_type=jnp.float32
    ).astype(jnp.bfloat16)
    home_s = lax.all_to_all(
        scores.reshape(owners, capacity), ("role", "ep"), split_axis=0, concat_axis=0, tiled=True
    )
    summed = lax.psum_scatter(
        partial_low.reshape(owners, capacity, width_full), "tp", scatter_dimension=2, tiled=True
    ).astype(jnp.float32)
    summed_low = summed.astype(jnp.bfloat16)
    home_x = lax.all_to_all(summed_low, ("role", "ep"), split_axis=0, concat_axis=0, tiled=True)
    slice_width = summed.shape[2]
    route_rows = home_x.reshape(row_count, slice_width).astype(jnp.float32)
    d_tok = (
        jnp.zeros((tok_rows + 1, slice_width), jnp.float32)
        .at[token_of_slot]
        .add(route_rows)[:tok_rows]
    )
    d_probs = home_s.reshape(-1)[target].reshape(tok_rows, top_count)
    return (
        d_tok.astype(jnp.bfloat16),
        d_probs,
        grad_gate.astype(jnp.bfloat16)[None],
        grad_up.astype(jnp.bfloat16)[None],
        grad_down.astype(jnp.bfloat16)[None],
    )


def slot_capacity(tok_rows, top_count, owners):
    return min(tok_rows, tok_rows * top_count * 9 // (8 * owners))


def weights_kernel(tp_ref, wg_ref, wu_ref, wd_ref, both_ref, down_ref):
    part = wg_ref.shape[2]
    both_ref[:, :part] = wg_ref[0]
    both_ref[:, part:] = wu_ref[0]
    down_ref[...] = wd_ref[0]


def weights_call(which, w_gate, w_up, w_down):
    _, width, part = w_gate.shape
    half = width // 2

    def place(i, w):
        return (i + w[0]) % 2

    return pl.pallas_call(
        weights_kernel,
        grid_spec=pltpu.PrefetchScalarGridSpec(
            num_scalar_prefetch=1,
            grid=(2,),
            in_specs=[
                pl.BlockSpec((1, half, part), lambda i, w: (0, place(i, w), 0)),
                pl.BlockSpec((1, half, part), lambda i, w: (0, place(i, w), 0)),
                pl.BlockSpec((1, part, half), lambda i, w: (0, 0, place(i, w))),
            ],
            out_specs=[
                pl.BlockSpec((half, 2 * part), lambda i, w: (i, 0)),
                pl.BlockSpec((part, half), lambda i, w: (0, i)),
            ],
        ),
        out_shape=[
            jax.ShapeDtypeStruct((width, 2 * part), jnp.bfloat16),
            jax.ShapeDtypeStruct((part, width), jnp.bfloat16),
        ],
        compiler_params=pltpu.CompilerParams(vmem_limit_bytes=24 << 20),
        cost_estimate=pl.CostEstimate(flops=0, bytes_accessed=12 * width * part, transcendentals=0),
        name="weights",
    )(which, w_gate, w_up, w_down)


def rows_kernel(slots, slot_ref, p_ref, wgu_ref, wd_ref, *refs):
    x_in, g_in = refs[:4], refs[4:8]
    refs = refs[len(refs) - 11 :]
    xc_ref, gc_ref, both_ref, scaled_ref, score_ref, keep_ref, send_ref, x_all, g_all, x_sems, g_sems = refs
    half = x_all.shape[3]
    tok = g_in[0].shape[1]
    part = scaled_ref.shape[1]

    x_copies = [pltpu.make_async_copy(x_in[i], x_all.at[i // 2, i % 2], x_sems.at[i]) for i in range(4)]
    g_copies = [
        pltpu.make_async_copy(g_in[i], g_all.at[i // 2, :, pl.ds(i % 2 * tok, tok)], g_sems.at[i]) for i in range(4)
    ]
    for copy in x_copies + g_copies:
        copy.start()

    def pick(a, b, dims):
        return lax.dot_general(a, b, (dims, ((), ())), preferred_element_type=jnp.float32)

    number = lax.broadcasted_iota(jnp.int32, (slots, 2 * tok), 0)
    picks = [(number == slot_ref[core : core + 1, :]).astype(jnp.float32) for core in range(2)]
    picks_low = [item.astype(jnp.bfloat16) for item in picks]
    prob = jnp.concatenate(
        [jnp.sum(picks[core] * p_ref[core : core + 1, :], axis=1, keepdims=True) for core in range(2)], 0
    )
    for core in range(2):
        x_copies[2 * core].wait()
        x_copies[2 * core + 1].wait()
        for side in range(2):
            xc_ref[core * slots : (core + 1) * slots, side * half : (side + 1) * half] = pick(
                picks_low[core], x_all[core, side], ((1,), (0,))
            ).astype(jnp.bfloat16)
    rows = pick(xc_ref[...], wgu_ref[...], ((1,), (0,)))
    for core in range(2):
        g_copies[2 * core].wait()
        g_copies[2 * core + 1].wait()
        for side in range(2):
            gc_ref[core * slots : (core + 1) * slots, side * half : (side + 1) * half] = pick(
                picks_low[core], g_all[core, side], ((1,), (0,))
            ).astype(jnp.bfloat16)
    back = pick(gc_ref[...], wd_ref[...], ((1,), (1,)))
    gate, up = rows[:, :part], rows[:, part:]
    sig = jax.nn.sigmoid(gate)
    act = gate * sig
    hidden = act * up
    score = jnp.sum(hidden * back, axis=1, keepdims=True)
    for core in range(2):
        score_ref[core : core + 1, :] = jnp.sum(
            picks[core] * score[core * slots : (core + 1) * slots], axis=0, keepdims=True
        )
    hgrad = prob * back
    both_ref[:, :part] = (hgrad * up * sig * (1.0 + gate * (1.0 - sig))).astype(jnp.bfloat16)
    both_ref[:, part:] = (hgrad * act).astype(jnp.bfloat16)
    scaled_ref[...] = (prob * hidden).astype(jnp.bfloat16)
    for side in range(2):
        low = pick(both_ref[...], wgu_ref[side * half : (side + 1) * half, :], ((1,), (1,))).astype(jnp.bfloat16)
        for core, out_ref in ((1, send_ref), (0, keep_ref)):
            out_ref[side] = pick(picks_low[core], low[core * slots : (core + 1) * slots], ((0,), (0,))).astype(jnp.bfloat16)


def rows_call(step, steps, slots, slot, prob, both_w, down_w, x_in, g_in, held):
    pair, half = x_in[0].shape
    width, part = 2 * half, down_w.shape[0]
    loose = pl.BlockSpec(memory_space=pl.ANY)
    rows = 2 * slots
    widths = (width, width, 2 * part, part)
    return pl.pallas_call(
        functools.partial(rows_kernel, slots),
        grid=(1,),
        in_specs=[
            pl.BlockSpec((2, pair), lambda i: (0, 0)),
            pl.BlockSpec((2, pair), lambda i: (0, 0)),
            pl.BlockSpec((width, 2 * part), lambda i: (0, 0)),
            pl.BlockSpec((part, width), lambda i: (0, 0)),
        ]
        + [loose] * (8 + len(held)),
        out_specs=[pl.BlockSpec((rows, size), lambda i: (step, 0)) for size in widths]
        + [pl.BlockSpec((2, pair), lambda i: (0, 0))]
        + [pl.BlockSpec((2, pair, half), lambda i: (0, 0, 0))] * 2,
        out_shape=[jax.ShapeDtypeStruct((steps * rows, size), jnp.bfloat16) for size in widths]
        + [jax.ShapeDtypeStruct((2, pair), jnp.float32)]
        + [jax.ShapeDtypeStruct((2, pair, half), jnp.bfloat16)] * 2,
        scratch_shapes=[
            pltpu.VMEM((2, 2, pair, half), jnp.bfloat16),
            pltpu.VMEM((2, 2, pair, half), jnp.bfloat16),
            pltpu.SemaphoreType.DMA((4,)),
            pltpu.SemaphoreType.DMA((4,)),
        ],
        input_output_aliases={12 + i: i for i in range(len(held))},
        compiler_params=pltpu.CompilerParams(vmem_limit_bytes=40 << 20),
        cost_estimate=pl.CostEstimate(
            flops=10 * rows * width * part + 12 * rows * pair * width,
            bytes_accessed=8 * 2 * pair * width + 6 * width * part,
            transcendentals=rows * part,
        ),
        name="rows",
    )(slot, prob, both_w, down_w, *x_in, *g_in, *held)


def grads_kernel(tp_ref, x_ref, g_ref, both_ref, scaled_ref, dg_ref, du_ref, dd_ref):
    part = scaled_ref.shape[1]
    both = lax.dot_general(x_ref[...], both_ref[...], (((0,), (0,)), ((), ())), preferred_element_type=jnp.float32)
    dg_ref[0] = both[:, :part].astype(jnp.bfloat16)
    du_ref[0] = both[:, part:].astype(jnp.bfloat16)
    down = lax.dot_general(scaled_ref[...], g_ref[...], (((0,), (0,)), ((), ())), preferred_element_type=jnp.float32)
    dd_ref[0] = down.astype(jnp.bfloat16)


def grads_call(which, x_rows, g_rows, both, scaled):
    total, width = x_rows.shape
    part = scaled.shape[1]
    step = math.gcd(width // 2, 256)
    per = width // 2 // step

    def place(i, w):
        return (i + w[0] * per) % (2 * per)

    moving = pl.BlockSpec((total, step), lambda i, w: (0, i))
    return pl.pallas_call(
        grads_kernel,
        grid_spec=pltpu.PrefetchScalarGridSpec(
            num_scalar_prefetch=1,
            grid=(width // step,),
            in_specs=[
                moving,
                moving,
                pl.BlockSpec((total, 2 * part), lambda i, w: (0, 0)),
                pl.BlockSpec((total, part), lambda i, w: (0, 0)),
            ],
            out_specs=[
                pl.BlockSpec((1, step, part), lambda i, w: (0, place(i, w), 0)),
                pl.BlockSpec((1, step, part), lambda i, w: (0, place(i, w), 0)),
                pl.BlockSpec((1, part, step), lambda i, w: (0, 0, place(i, w))),
            ],
        ),
        out_shape=[
            jax.ShapeDtypeStruct((1, width, part), jnp.bfloat16),
            jax.ShapeDtypeStruct((1, width, part), jnp.bfloat16),
            jax.ShapeDtypeStruct((1, part, width), jnp.bfloat16),
        ],
        compiler_params=pltpu.CompilerParams(vmem_limit_bytes=40 << 20),
        cost_estimate=pl.CostEstimate(flops=6 * total * width * part, bytes_accessed=6 * total * width, transcendentals=0),
        name="grads",
    )(which, x_rows, g_rows, both, scaled)


def dense_device(tokens, out_grad, routes, probs, w_gate, w_up, w_down):
    owners = lax.axis_size(("role", "ep"))
    ep = lax.axis_size("ep")
    n_y = 2
    n_z = ep // n_y
    tok_rows, half = tokens.shape
    capacity = slot_capacity(tok_rows, routes.shape[1], owners)
    slots = -(-n_y * capacity // 16) * 16
    me = lax.axis_index(("role", "ep"))
    role, place, which = lax.axis_index("role"), lax.axis_index("ep"), lax.axis_index("tp")
    my_z, my_y = place // n_y, place % n_y

    def over_x(array):
        return lax.ppermute(array, "tp", [(0, 1), (1, 0)])

    def over_role(array):
        return lax.ppermute(array, "role", [(0, 1), (1, 0)])

    def over_y(array):
        return lax.ppermute(array, "ep", [(i, i + 1 - 2 * (i % n_y)) for i in range(ep)])

    def over_z(array, shift):
        return lax.ppermute(array, "ep", [(i, (i + shift * n_y) % ep) for i in range(ep)])

    chosen = routes[:, :, None] == jnp.arange(owners, dtype=jnp.int32)
    table = jnp.sum(jnp.where(chosen, probs[:, :, None].astype(jnp.float32) + 1.0, 0.0), axis=1) - 1.0
    table = table.astype(jnp.bfloat16).T
    tables = jnp.stack([table] + [over_z(table, step) for step in range(1, n_z)])
    tables = jnp.stack([tables, over_y(tables)], 1)
    tables = jnp.stack([tables, over_role(tables)], 1)
    prob = lax.dynamic_slice_in_dim(tables, me, 1, 3)[:, :, :, 0].astype(jnp.float32)
    routed = prob >= 0.0
    before = jnp.tril(jnp.ones((tok_rows, tok_rows), jnp.bfloat16), -1).T
    slot = jnp.dot(routed.astype(jnp.bfloat16), before, preferred_element_type=jnp.float32).astype(jnp.int32)
    slot = jnp.where(routed, slot + capacity * jnp.arange(n_y, dtype=jnp.int32)[:, None], -1)
    slot = slot.reshape(n_z, 2, n_y * tok_rows)
    prob = prob.reshape(n_z, 2, n_y * tok_rows)

    which_ref = which.reshape(1).astype(jnp.int32)
    both_w, down_w = weights_call(which_ref, w_gate, w_up, w_down)

    x_own, g_own = tokens, jnp.stack([out_grad, over_x(out_grad)])
    x_parts, g_parts = [], []
    for step in range(n_z):
        if step:
            x_own, g_own = over_z(x_own, 1), over_z(g_own, 1)
        pair = jnp.concatenate([x_own, over_y(x_own)], 0)
        far = over_x(pair)
        x_parts.append((pair, far, over_role(pair), over_role(far)))
        far = over_y(g_own)
        g_parts.append((g_own, far, over_role(g_own), over_role(far)))

    held, scores, homeward = (), [], []
    for step in range(n_z):
        *held, score, keep, send = rows_call(
            step, n_z, slots, slot[step], prob[step], both_w, down_w, x_parts[step], g_parts[step], held
        )
        scores.append(score)
        total = keep.astype(jnp.float32) + over_role(send).astype(jnp.float32)
        total = total[0] + over_x(total[1].astype(jnp.bfloat16)).astype(jnp.float32)
        total = total[:tok_rows] + over_y(total[tok_rows:].astype(jnp.bfloat16)).astype(jnp.float32)
        homeward.append(over_z(total.astype(jnp.bfloat16), -step).astype(jnp.float32) if step else total)
    d_tok = sum(homeward[1:], homeward[0]).astype(jnp.bfloat16)
    d_gate, d_up, d_down = grads_call(which_ref, *held)

    mine = jnp.stack(scores).reshape(n_z, 2, n_y, tok_rows)
    mine = mine + over_x(mine)
    mine = jnp.stack([mine[:, 0], over_role(mine[:, 1])])
    mine = jnp.stack([mine[:, :, 0], over_y(mine[:, :, 1])])
    mine = jnp.stack([mine[:, :, 0]] + [over_z(mine[:, :, step], -step) for step in range(1, n_z)])
    steps = jnp.arange(n_z)[:, None, None]
    source = (role + jnp.arange(2)) % 2 * ep + (my_z + steps) % n_z * n_y + ((my_y + jnp.arange(n_y)) % n_y)[:, None]
    picked = routes[:, :, None] == source.reshape(-1)
    d_probs = jnp.sum(jnp.where(picked, mine.reshape(owners, tok_rows).T[:, None, :], 0.0), axis=2)
    return d_tok, d_probs, d_gate, d_up, d_down


def per_device(tokens, out_grad, routes, probs, w_gate, w_up, w_down):
    owners = lax.axis_size(("role", "ep"))
    tok_rows, top_count = routes.shape
    paired = lax.axis_size("tp") == 2 and lax.axis_size("role") == 2 and lax.axis_size("ep") % 2 == 0
    if paired and 2 * slot_capacity(tok_rows, top_count, owners) >= tok_rows:
        return dense_device(tokens, out_grad, routes, probs, w_gate, w_up, w_down)
    return routed_device(tokens, out_grad, routes, probs, w_gate, w_up, w_down)


def solution(mesh):
    in_specs = (
        P(("groups", "role", "ep"), "tp"),
        P(("groups", "role", "ep"), "tp"),
        P(("groups", "role", "ep"), None),
        P(("groups", "role", "ep"), None),
        P(("role", "ep"), None, "tp"),
        P(("role", "ep"), None, "tp"),
        P(("role", "ep"), "tp", None),
    )
    out_specs = (
        P(("groups", "role", "ep"), "tp"),
        P(("groups", "role", "ep"), None),
        P(("groups", "role", "ep"), None, "tp"),
        P(("groups", "role", "ep"), None, "tp"),
        P(("groups", "role", "ep"), "tp", None),
    )
    return jax.shard_map(
        per_device, mesh=mesh, in_specs=in_specs, out_specs=out_specs, check_vma=False
    )
```

```python
import functools
import math

import jax
import jax.numpy as jnp
from jax import lax
from jax.experimental import pallas as pl
from jax.experimental.pallas import tpu as pltpu
from jax.sharding import PartitionSpec as P


def pad_rows(array):
    return jnp.concatenate([array, jnp.zeros((1, array.shape[1]), array.dtype)], 0)


def routed_device(tokens, out_grad, routes, probs, w_gate, w_up, w_down):
    owners = lax.axis_size(("role", "ep"))
    tok_rows, top_count = routes.shape
    width_full = w_gate.shape[1]
    part_width = w_gate.shape[2]
    capacity = min(tok_rows, tok_rows * top_count * 9 // (8 * owners))
    entry_total = tok_rows * top_count
    routes_flat = routes.reshape(-1)
    onehot = (routes_flat[:, None] == jnp.arange(owners, dtype=jnp.int32)[None, :]).astype(
        jnp.int32
    )
    before = jnp.cumsum(onehot, axis=0) - onehot
    slot_index = jnp.sum(before * onehot, axis=1)
    target = routes_flat * capacity + slot_index
    row_count = owners * capacity
    entry_of_slot = (
        jnp.full((row_count,), entry_total, jnp.int32)
        .at[target]
        .set(jnp.arange(entry_total, dtype=jnp.int32))
    )
    token_of_slot = entry_of_slot // top_count
    padded_prob = jnp.concatenate([probs.reshape(-1), jnp.zeros((1,), probs.dtype)], 0)
    send_prob = padded_prob[entry_of_slot].reshape(owners, capacity)
    send_x = pad_rows(tokens)[token_of_slot]
    send_g = pad_rows(out_grad)[token_of_slot]
    slice_x, slice_g, recv_p = (
        lax.all_to_all(
            send_x.reshape(owners, capacity, tokens.shape[1]),
            ("role", "ep"),
            split_axis=0,
            concat_axis=0,
            tiled=True,
        ),
        lax.all_to_all(
            send_g.reshape(owners, capacity, tokens.shape[1]),
            ("role", "ep"),
            split_axis=0,
            concat_axis=0,
            tiled=True,
        ),
        lax.all_to_all(send_prob, ("role", "ep"), split_axis=0, concat_axis=0, tiled=True),
    )
    recv_x, recv_g = (
        lax.all_gather(slice_x, "tp", axis=2, tiled=True),
        lax.all_gather(slice_g, "tp", axis=2, tiled=True),
    )
    rows_x = recv_x.reshape(row_count, width_full)
    rows_g = recv_g.reshape(row_count, width_full)
    weight_p = recv_p.reshape(row_count, 1).astype(jnp.float32)
    gate_up = jnp.concatenate([w_gate[0], w_up[0]], 1)
    down_shard = w_down[0]
    both_rows = jnp.dot(rows_x, gate_up, preferred_element_type=jnp.float32)
    gate_rows = both_rows[:, :part_width]
    up_rows = both_rows[:, part_width:]
    sigmoid_gate = jax.nn.sigmoid(gate_rows)
    activated = gate_rows * sigmoid_gate
    hidden = activated * up_rows
    back_rows = lax.dot_general(
        rows_g, down_shard, (((1,), (1,)), ((), ())), preferred_element_type=jnp.float32
    )
    scores = lax.psum(jnp.sum(hidden * back_rows, axis=1), "tp")
    hidden_grad = weight_p * back_rows
    d_gate_rows = (
        hidden_grad * up_rows * sigmoid_gate * (1.0 + gate_rows * (1.0 - sigmoid_gate))
    ).astype(jnp.bfloat16)
    d_up_rows = (hidden_grad * activated).astype(jnp.bfloat16)
    d_both = jnp.concatenate([d_gate_rows, d_up_rows], 1)
    scaled = (weight_p * hidden).astype(jnp.bfloat16)
    grad_down = lax.dot_general(
        scaled, rows_g, (((0,), (0,)), ((), ())), preferred_element_type=jnp.float32
    )
    grad_both = lax.dot_general(
        rows_x, d_both, (((0,), (0,)), ((), ())), preferred_element_type=jnp.float32
    )
    grad_gate = grad_both[:, :part_width]
    grad_up = grad_both[:, part_width:]
    partial_low = lax.dot_general(
        d_both, gate_up, (((1,), (1,)), ((), ())), preferred_element_type=jnp.float32
    ).astype(jnp.bfloat16)
    home_s = lax.all_to_all(
        scores.reshape(owners, capacity), ("role", "ep"), split_axis=0, concat_axis=0, tiled=True
    )
    summed = lax.psum_scatter(
        partial_low.reshape(owners, capacity, width_full), "tp", scatter_dimension=2, tiled=True
    ).astype(jnp.float32)
    summed_low = summed.astype(jnp.bfloat16)
    home_x = lax.all_to_all(summed_low, ("role", "ep"), split_axis=0, concat_axis=0, tiled=True)
    slice_width = summed.shape[2]
    route_rows = home_x.reshape(row_count, slice_width).astype(jnp.float32)
    d_tok = (
        jnp.zeros((tok_rows + 1, slice_width), jnp.float32)
        .at[token_of_slot]
        .add(route_rows)[:tok_rows]
    )
    d_probs = home_s.reshape(-1)[target].reshape(tok_rows, top_count)
    return (
        d_tok.astype(jnp.bfloat16),
        d_probs,
        grad_gate.astype(jnp.bfloat16)[None],
        grad_up.astype(jnp.bfloat16)[None],
        grad_down.astype(jnp.bfloat16)[None],
    )


def slot_capacity(tok_rows, top_count, owners):
    return min(tok_rows, tok_rows * top_count * 9 // (8 * owners))


def weights_kernel(tp_ref, wg_ref, wu_ref, wd_ref, both_ref, down_ref):
    part = wg_ref.shape[2]
    both_ref[:, :part] = wg_ref[0]
    both_ref[:, part:] = wu_ref[0]
    down_ref[...] = wd_ref[0]


def weights_call(which, w_gate, w_up, w_down):
    _, width, part = w_gate.shape
    half = width // 2

    def place(i, w):
        return (i + w[0]) % 2

    return pl.pallas_call(
        weights_kernel,
        grid_spec=pltpu.PrefetchScalarGridSpec(
            num_scalar_prefetch=1,
            grid=(2,),
            in_specs=[
                pl.BlockSpec((1, half, part), lambda i, w: (0, place(i, w), 0)),
                pl.BlockSpec((1, half, part), lambda i, w: (0, place(i, w), 0)),
                pl.BlockSpec((1, part, half), lambda i, w: (0, 0, place(i, w))),
            ],
            out_specs=[
                pl.BlockSpec((half, 2 * part), lambda i, w: (i, 0)),
                pl.BlockSpec((part, half), lambda i, w: (0, i)),
            ],
        ),
        out_shape=[
            jax.ShapeDtypeStruct((width, 2 * part), jnp.bfloat16),
            jax.ShapeDtypeStruct((part, width), jnp.bfloat16),
        ],
        compiler_params=pltpu.CompilerParams(vmem_limit_bytes=24 << 20),
        cost_estimate=pl.CostEstimate(flops=0, bytes_accessed=12 * width * part, transcendentals=0),
        name="weights",
    )(which, w_gate, w_up, w_down)


def rows_kernel(step, y_first, slots, slot_ref, p_ref, *refs):
    weights_in, units_in, refs = refs[:4], refs[4:8], refs[len(refs) - 21 :]
    outs, refs = refs[:4], refs[4:]
    score_ref, keep_ref, send_ref, x_all, g_all, wgu0, wgu1, wd0, wd1, xc, gc, both, scaled, piece = refs[:14]
    unit_sems, weight_sems, out_sems = refs[14:]
    half, tok = x_all.shape[2], x_all.shape[1] // 2
    part = scaled.shape[1]
    wgu, wd = (wgu0, wgu1), (wd0, wd1)

    x_copies, g_copies = [], []
    for index, unit in enumerate(units_in):
        rows = pl.ds(index // 2 * tok, tok)
        x_copies.append(pltpu.make_async_copy(unit.at[pl.ds(0, tok)], x_all.at[index % 2, rows], unit_sems.at[0, index]))
        g_copies.append(pltpu.make_async_copy(unit.at[pl.ds(tok, tok)], g_all.at[index % 2, rows], unit_sems.at[1, index]))
    weight_copies = [
        pltpu.make_async_copy(source, target, weight_sems.at[index])
        for index, (source, target) in enumerate(zip(weights_in, (wgu0, wgu1, wd0, wd1)))
    ]
    for copy in x_copies + weight_copies[:2] + g_copies + weight_copies[2:]:
        copy.start()
    leaving = []

    def leave(source, target):
        copy = pltpu.make_async_copy(source, target, out_sems.at[len(leaving)])
        copy.start()
        leaving.append(copy)

    def leave_rows(held, target):
        for expert in range(2):
            leave(held.at[pl.ds(expert * slots, slots)], target.at[expert, pl.ds(step * slots, slots)])

    def dot(a, b, dims):
        return lax.dot_general(a, b, (dims, ((), ())), preferred_element_type=jnp.float32)

    number = lax.broadcasted_iota(jnp.int32, (slots, 2 * tok), 0)
    picks = [(number == slot_ref[expert : expert + 1, :]).astype(jnp.float32) for expert in range(2)]
    prob = [jnp.sum(picks[e] * p_ref[e : e + 1, :], axis=1, keepdims=True) for e in range(2)]
    low_picks = [item.astype(jnp.bfloat16) for item in picks]
    all_picks = jnp.concatenate(low_picks, 0)
    spans = [slice(expert * slots, (expert + 1) * slots) for expert in range(2)]
    sides = [slice(side * half, (side + 1) * half) for side in range(2)]
    for copy in x_copies:
        copy.wait()
    for side in range(2):
        xc[:, sides[side]] = dot(all_picks, x_all[side], ((1,), (0,))).astype(jnp.bfloat16)
    leave_rows(xc, outs[0])
    rows = []
    for expert in range(2):
        weight_copies[expert].wait()
        rows.append(dot(xc[spans[expert], :], wgu[expert][...], ((1,), (0,))))
    for copy in g_copies:
        copy.wait()
    for side in range(2):
        gc[:, sides[side]] = dot(all_picks, g_all[side], ((1,), (0,))).astype(jnp.bfloat16)
    leave_rows(gc, outs[1])
    for expert in range(2):
        weight_copies[2 + expert].wait()
        back = dot(gc[spans[expert], :], wd[expert][...], ((1,), (1,)))
        gate, up = rows[expert][:, :part], rows[expert][:, part:]
        sig = jax.nn.sigmoid(gate)
        act = gate * sig
        hidden = act * up
        score = jnp.sum(hidden * back, axis=1, keepdims=True)
        score_ref[expert : expert + 1, :] = jnp.sum(picks[expert] * score, axis=0, keepdims=True)
        hgrad = prob[expert] * back
        both[spans[expert], :part] = (hgrad * up * sig * (1.0 + gate * (1.0 - sig))).astype(jnp.bfloat16)
        both[spans[expert], part:] = (hgrad * act).astype(jnp.bfloat16)
        scaled[spans[expert], :] = (prob[expert] * hidden).astype(jnp.bfloat16)
    leave_rows(both, outs[2])
    leave_rows(scaled, outs[3])
    for side in (1, 0):
        total = None
        for expert in range(2):
            low = dot(both[spans[expert], :], wgu[expert][sides[side], :], ((1,), (1,))).astype(jnp.bfloat16)
            term = dot(low_picks[expert], low, ((0,), (0,)))
            total = term if total is None else total + term
        piece[side] = total.astype(jnp.bfloat16)
        for y in range(2):
            first, second = (y, side) if y_first else (side, y)
            leave(piece.at[side, pl.ds(y * tok, tok)], (send_ref if first else keep_ref).at[second])
    for copy in leaving:
        copy.wait()


def rows_call(step, steps, slots, slot, prob, weights, units, held):
    pair, half = units[0].shape
    part, width = weights[2].shape
    loose = pl.BlockSpec(memory_space=pl.ANY)
    widths = (width, width, 2 * part, part)
    return pl.pallas_call(
        functools.partial(rows_kernel, step, step % 2 == 1, slots),
        grid=(1,),
        in_specs=[pl.BlockSpec((2, pair), lambda i: (0, 0))] * 2 + [loose] * (8 + len(held)),
        out_specs=[loose] * 4 + [pl.BlockSpec((2, pair), lambda i: (0, 0))] + [loose] * 2,
        out_shape=[jax.ShapeDtypeStruct((2, steps * slots, size), jnp.bfloat16) for size in widths]
        + [jax.ShapeDtypeStruct((2, pair), jnp.float32)]
        + [jax.ShapeDtypeStruct((2, pair // 2, half), jnp.bfloat16)] * 2,
        scratch_shapes=[pltpu.VMEM((2, pair, half), jnp.bfloat16)] * 2
        + [pltpu.VMEM((width, 2 * part), jnp.bfloat16)] * 2
        + [pltpu.VMEM((part, width), jnp.bfloat16)] * 2
        + [pltpu.VMEM((2 * slots, size), jnp.bfloat16) for size in widths]
        + [
            pltpu.VMEM((2, pair, half), jnp.bfloat16),
            pltpu.SemaphoreType.DMA((2, 4)),
            pltpu.SemaphoreType.DMA((4,)),
            pltpu.SemaphoreType.DMA((12,)),
        ],
        input_output_aliases={10 + i: i for i in range(len(held))},
        compiler_params=pltpu.CompilerParams(vmem_limit_bytes=56 << 20),
        cost_estimate=pl.CostEstimate(
            flops=20 * slots * width * part + 12 * slots * pair * width,
            bytes_accessed=8 * pair * width + 12 * width * part,
            transcendentals=2 * slots * part,
        ),
        name="rows",
    )(slot, prob, *weights, *units, *held)


def grads_kernel(first, tp_ref, x_ref, g_ref, both_ref, scaled_ref, *refs):
    part = scaled_ref.shape[2]
    dims = (((0,), (0,)), ((), ()))
    both = lax.dot_general(x_ref[0], both_ref[0], dims, preferred_element_type=jnp.float32)
    down = lax.dot_general(scaled_ref[0], g_ref[0], dims, preferred_element_type=jnp.float32)
    if first:
        refs[0][...] = both.astype(jnp.bfloat16)
        refs[1][...] = down.astype(jnp.bfloat16)
        return
    more_both, more_down, dg_ref, du_ref, dd_ref = refs
    both = both + more_both[...].astype(jnp.float32)
    dg_ref[0] = both[:, :part].astype(jnp.bfloat16)
    du_ref[0] = both[:, part:].astype(jnp.bfloat16)
    dd_ref[0] = (down + more_down[...].astype(jnp.float32)).astype(jnp.bfloat16)


def grads_call(which, expert, x_rows, g_rows, both, scaled, more=()):
    _, total, width = x_rows.shape
    part = scaled.shape[2]
    step = math.gcd(width // 2, 256)
    per = width // 2 // step

    def place(i, w):
        return (i + w[0] * per) % (2 * per)

    moving = pl.BlockSpec((1, total, step), lambda i, w: (expert, 0, i))
    passing = [
        pl.BlockSpec((step, 2 * part), lambda i, w: (i, 0)),
        pl.BlockSpec((part, step), lambda i, w: (0, i)),
    ]
    if more:
        out_specs = [
            pl.BlockSpec((1, step, part), lambda i, w: (0, place(i, w), 0)),
            pl.BlockSpec((1, step, part), lambda i, w: (0, place(i, w), 0)),
            pl.BlockSpec((1, part, step), lambda i, w: (0, 0, place(i, w))),
        ]
        shapes = [(1, width, part), (1, width, part), (1, part, width)]
    else:
        out_specs = passing
        shapes = [(width, 2 * part), (part, width)]
    return pl.pallas_call(
        functools.partial(grads_kernel, not more),
        grid_spec=pltpu.PrefetchScalarGridSpec(
            num_scalar_prefetch=1,
            grid=(width // step,),
            in_specs=[
                moving,
                moving,
                pl.BlockSpec((1, total, 2 * part), lambda i, w: (expert, 0, 0)),
                pl.BlockSpec((1, total, part), lambda i, w: (expert, 0, 0)),
            ]
            + (passing if more else []),
            out_specs=out_specs,
        ),
        out_shape=[jax.ShapeDtypeStruct(shape, jnp.bfloat16) for shape in shapes],
        compiler_params=pltpu.CompilerParams(vmem_limit_bytes=40 << 20),
        cost_estimate=pl.CostEstimate(flops=6 * total * width * part, bytes_accessed=6 * total * width, transcendentals=0),
        name="grads",
    )(which, x_rows, g_rows, both, scaled, *more)


def dense_device(tokens, out_grad, routes, probs, w_gate, w_up, w_down):
    owners = lax.axis_size(("role", "ep"))
    ep = lax.axis_size("ep")
    n_y = 2
    n_z = ep // n_y
    tok_rows, half = tokens.shape
    capacity = slot_capacity(tok_rows, routes.shape[1], owners)
    slots = -(-n_y * capacity // 16) * 16
    role, place, which = lax.axis_index("role"), lax.axis_index("ep"), lax.axis_index("tp")
    my_z, my_y = place // n_y, place % n_y

    def over_x(array):
        return lax.ppermute(array, "tp", [(0, 1), (1, 0)])

    def over_role(array):
        return lax.ppermute(array, "role", [(0, 1), (1, 0)])

    def over_y(array):
        return lax.ppermute(array, "ep", [(i, i + 1 - 2 * (i % n_y)) for i in range(ep)])

    def over_z(array, shift):
        return lax.ppermute(array, "ep", [(i, (i + shift * n_y) % ep) for i in range(ep)])

    units = {(0, 0, 0): jnp.concatenate([tokens, out_grad], 0)}
    for z in range(n_z):
        if z:
            units[z, 0, 0] = over_z(units[z - 1, 0, 0], 1)
        units[z, 1, 0] = over_y(units[z, 0, 0])
        units[z, 0, 1] = over_x(units[z, 0, 0])
        if z == 0:
            units[z, 1, 1] = over_x(units[z, 1, 0])
        elif z < n_z - 1:
            units[z, 1, 1] = over_z(units[z - 1, 1, 1], 1)
        else:
            units[z, 1, 1] = over_y(units[z, 0, 1])

    which_ref = which.reshape(1).astype(jnp.int32)
    both_w, down_w = weights_call(which_ref, w_gate, w_up, w_down)
    weights = (both_w, over_role(both_w), down_w, over_role(down_w))

    chosen = routes[:, :, None] == jnp.arange(owners, dtype=jnp.int32)
    table = jnp.sum(jnp.where(chosen, probs[:, :, None].astype(jnp.float32) + 1.0, 0.0), axis=1) - 1.0
    table = table.astype(jnp.bfloat16).T
    tables = jnp.stack([table, over_y(table)])
    tables = jnp.stack([tables] + [over_z(tables, step) for step in range(1, n_z)])
    tables = tables.reshape(n_z, n_y, 2, ep, tok_rows)
    prob = lax.dynamic_slice_in_dim(tables, place, 1, 3)[:, :, :, 0].astype(jnp.float32)
    prob = jnp.where(role == 0, prob, prob[:, :, ::-1])
    routed = prob >= 0.0
    before = jnp.triu(jnp.ones((tok_rows, tok_rows), jnp.bfloat16), 1)
    slot = jnp.dot(routed.astype(jnp.bfloat16), before, preferred_element_type=jnp.float32).astype(jnp.int32)
    slot = jnp.where(routed, slot + capacity * jnp.arange(n_y, dtype=jnp.int32)[:, None, None], -1)
    slot = slot.transpose(0, 2, 1, 3).reshape(n_z, 2, n_y * tok_rows)
    prob = prob.transpose(0, 2, 1, 3).reshape(n_z, 2, n_y * tok_rows)

    def add(a, b):
        return a.astype(jnp.float32) + b.astype(jnp.float32)

    held, scores, homeward = (), [], []
    for z in range(n_z):
        four = [units[z, y, x] for y in range(2) for x in range(2)]
        *held, score, keep, send = rows_call(z, n_z, slots, slot[z], prob[z], weights, four, held)
        scores.append(score)
        go_first, go_second = (over_y, over_x) if z % 2 else (over_x, over_y)
        recv = go_first(send)
        recv_next = go_second(add(keep[1], recv[1]).astype(jnp.bfloat16))
        total = add(add(keep[0], recv[0]), recv_next)
        homeward.append(over_z(total.astype(jnp.bfloat16), -z).astype(jnp.float32) if z else total)
    d_tok = sum(homeward[1:], homeward[0]).astype(jnp.bfloat16)
    more = grads_call(which_ref, 1, *held)
    d_gate, d_up, d_down = grads_call(which_ref, 0, *held, [over_role(item) for item in more])

    mine = jnp.stack(scores).reshape(n_z, 2, n_y, tok_rows)
    mine = mine + over_x(mine)
    mine = jnp.stack([mine[:, :, 0], over_y(mine[:, :, 1])])
    mine = jnp.stack([mine[:, 0]] + [over_z(mine[:, step], -step) for step in range(1, n_z)])
    steps = jnp.arange(n_z)[:, None, None]
    source = (my_z + steps) % n_z * n_y + ((my_y + jnp.arange(n_y)) % n_y)[:, None] + (role + jnp.arange(2)) % 2 * ep
    picked = routes[:, :, None] == source.reshape(-1)
    d_probs = jnp.sum(jnp.where(picked, mine.reshape(owners, tok_rows).T[:, None, :], 0.0), axis=2)
    return d_tok, d_probs, d_gate, d_up, d_down


def per_device(tokens, out_grad, routes, probs, w_gate, w_up, w_down):
    owners = lax.axis_size(("role", "ep"))
    tok_rows, top_count = routes.shape
    paired = lax.axis_size("tp") == 2 and lax.axis_size("role") == 2 and lax.axis_size("ep") % 2 == 0
    if paired and 2 * slot_capacity(tok_rows, top_count, owners) >= tok_rows:
        return dense_device(tokens, out_grad, routes, probs, w_gate, w_up, w_down)
    return routed_device(tokens, out_grad, routes, probs, w_gate, w_up, w_down)


def solution(mesh):
    in_specs = (
        P(("groups", "role", "ep"), "tp"),
        P(("groups", "role", "ep"), "tp"),
        P(("groups", "role", "ep"), None),
        P(("groups", "role", "ep"), None),
        P(("role", "ep"), None, "tp"),
        P(("role", "ep"), None, "tp"),
        P(("role", "ep"), "tp", None),
    )
    out_specs = (
        P(("groups", "role", "ep"), "tp"),
        P(("groups", "role", "ep"), None),
        P(("groups", "role", "ep"), None, "tp"),
        P(("groups", "role", "ep"), None, "tp"),
        P(("groups", "role", "ep"), "tp", None),
    )
    return jax.shard_map(
        per_device, mesh=mesh, in_specs=in_specs, out_specs=out_specs, check_vma=False
    )
```

```python
import functools
import math

import jax
import jax.numpy as jnp
from jax import lax
from jax.experimental import pallas as pl
from jax.experimental.pallas import tpu as pltpu
from jax.sharding import PartitionSpec as P


def pad_rows(array):
    return jnp.concatenate([array, jnp.zeros((1, array.shape[1]), array.dtype)], 0)


def routed_device(tokens, out_grad, routes, probs, w_gate, w_up, w_down):
    owners = lax.axis_size(("role", "ep"))
    tok_rows, top_count = routes.shape
    width_full = w_gate.shape[1]
    part_width = w_gate.shape[2]
    capacity = min(tok_rows, tok_rows * top_count * 9 // (8 * owners))
    entry_total = tok_rows * top_count
    routes_flat = routes.reshape(-1)
    onehot = (routes_flat[:, None] == jnp.arange(owners, dtype=jnp.int32)[None, :]).astype(
        jnp.int32
    )
    before = jnp.cumsum(onehot, axis=0) - onehot
    slot_index = jnp.sum(before * onehot, axis=1)
    target = routes_flat * capacity + slot_index
    row_count = owners * capacity
    entry_of_slot = (
        jnp.full((row_count,), entry_total, jnp.int32)
        .at[target]
        .set(jnp.arange(entry_total, dtype=jnp.int32))
    )
    token_of_slot = entry_of_slot // top_count
    padded_prob = jnp.concatenate([probs.reshape(-1), jnp.zeros((1,), probs.dtype)], 0)
    send_prob = padded_prob[entry_of_slot].reshape(owners, capacity)
    send_x = pad_rows(tokens)[token_of_slot]
    send_g = pad_rows(out_grad)[token_of_slot]
    slice_x, slice_g, recv_p = (
        lax.all_to_all(
            send_x.reshape(owners, capacity, tokens.shape[1]),
            ("role", "ep"),
            split_axis=0,
            concat_axis=0,
            tiled=True,
        ),
        lax.all_to_all(
            send_g.reshape(owners, capacity, tokens.shape[1]),
            ("role", "ep"),
            split_axis=0,
            concat_axis=0,
            tiled=True,
        ),
        lax.all_to_all(send_prob, ("role", "ep"), split_axis=0, concat_axis=0, tiled=True),
    )
    recv_x, recv_g = (
        lax.all_gather(slice_x, "tp", axis=2, tiled=True),
        lax.all_gather(slice_g, "tp", axis=2, tiled=True),
    )
    rows_x = recv_x.reshape(row_count, width_full)
    rows_g = recv_g.reshape(row_count, width_full)
    weight_p = recv_p.reshape(row_count, 1).astype(jnp.float32)
    gate_up = jnp.concatenate([w_gate[0], w_up[0]], 1)
    down_shard = w_down[0]
    both_rows = jnp.dot(rows_x, gate_up, preferred_element_type=jnp.float32)
    gate_rows = both_rows[:, :part_width]
    up_rows = both_rows[:, part_width:]
    sigmoid_gate = jax.nn.sigmoid(gate_rows)
    activated = gate_rows * sigmoid_gate
    hidden = activated * up_rows
    back_rows = lax.dot_general(
        rows_g, down_shard, (((1,), (1,)), ((), ())), preferred_element_type=jnp.float32
    )
    scores = lax.psum(jnp.sum(hidden * back_rows, axis=1), "tp")
    hidden_grad = weight_p * back_rows
    d_gate_rows = (
        hidden_grad * up_rows * sigmoid_gate * (1.0 + gate_rows * (1.0 - sigmoid_gate))
    ).astype(jnp.bfloat16)
    d_up_rows = (hidden_grad * activated).astype(jnp.bfloat16)
    d_both = jnp.concatenate([d_gate_rows, d_up_rows], 1)
    scaled = (weight_p * hidden).astype(jnp.bfloat16)
    grad_down = lax.dot_general(
        scaled, rows_g, (((0,), (0,)), ((), ())), preferred_element_type=jnp.float32
    )
    grad_both = lax.dot_general(
        rows_x, d_both, (((0,), (0,)), ((), ())), preferred_element_type=jnp.float32
    )
    grad_gate = grad_both[:, :part_width]
    grad_up = grad_both[:, part_width:]
    partial_low = lax.dot_general(
        d_both, gate_up, (((1,), (1,)), ((), ())), preferred_element_type=jnp.float32
    ).astype(jnp.bfloat16)
    home_s = lax.all_to_all(
        scores.reshape(owners, capacity), ("role", "ep"), split_axis=0, concat_axis=0, tiled=True
    )
    summed = lax.psum_scatter(
        partial_low.reshape(owners, capacity, width_full), "tp", scatter_dimension=2, tiled=True
    ).astype(jnp.float32)
    summed_low = summed.astype(jnp.bfloat16)
    home_x = lax.all_to_all(summed_low, ("role", "ep"), split_axis=0, concat_axis=0, tiled=True)
    slice_width = summed.shape[2]
    route_rows = home_x.reshape(row_count, slice_width).astype(jnp.float32)
    d_tok = (
        jnp.zeros((tok_rows + 1, slice_width), jnp.float32)
        .at[token_of_slot]
        .add(route_rows)[:tok_rows]
    )
    d_probs = home_s.reshape(-1)[target].reshape(tok_rows, top_count)
    return (
        d_tok.astype(jnp.bfloat16),
        d_probs,
        grad_gate.astype(jnp.bfloat16)[None],
        grad_up.astype(jnp.bfloat16)[None],
        grad_down.astype(jnp.bfloat16)[None],
    )


def slot_capacity(tok_rows, top_count, owners):
    return min(tok_rows, tok_rows * top_count * 9 // (8 * owners))


LOOSE = pl.BlockSpec(memory_space=pl.ANY)


def weights_kernel(tp_ref, wg_ref, wu_ref, wd_ref, *refs):
    both_ref, down_ref = refs[-2:]
    part = wg_ref.shape[2]
    both_ref[:, :part] = wg_ref[0]
    both_ref[:, part:] = wu_ref[0]
    down_ref[...] = wd_ref[0]


def weights_call(which, w_gate, w_up, w_down, after):
    _, width, part = w_gate.shape
    half = width // 2

    def place(i, w):
        return (i + w[0]) % 2

    return pl.pallas_call(
        weights_kernel,
        grid_spec=pltpu.PrefetchScalarGridSpec(
            num_scalar_prefetch=1,
            grid=(2,),
            in_specs=[
                pl.BlockSpec((1, half, part), lambda i, w: (0, place(i, w), 0)),
                pl.BlockSpec((1, half, part), lambda i, w: (0, place(i, w), 0)),
                pl.BlockSpec((1, part, half), lambda i, w: (0, 0, place(i, w))),
            ]
            + [LOOSE] * len(after),
            out_specs=[
                pl.BlockSpec((half, 2 * part), lambda i, w: (i, 0)),
                pl.BlockSpec((part, half), lambda i, w: (0, i)),
            ],
        ),
        out_shape=[
            jax.ShapeDtypeStruct((width, 2 * part), jnp.bfloat16),
            jax.ShapeDtypeStruct((part, width), jnp.bfloat16),
        ],
        compiler_params=pltpu.CompilerParams(vmem_limit_bytes=56 << 20),
        cost_estimate=pl.CostEstimate(flops=0, bytes_accessed=12 * width * part, transcendentals=0),
        name="weights",
    )(which, w_gate, w_up, w_down, *after)


def rows_kernel(places, modes, capacity, slots, where_ref, *refs):
    count = len(places)
    weights_in, units_in, refs = refs[:4], refs[4 : 4 + 4 * count], refs[len(refs) - 19 - 2 * count :]
    outs, keeps, sends, refs = refs[:4], refs[4 : 4 + count], refs[4 + count : 4 + 2 * count], refs[4 + 2 * count :]
    x_all, g_all, tables, wgu0, wgu1, wd0, wd1, xc, gc, both, scaled, piece, unit_sems, weight_sems = refs[:14]
    out_sems = refs[14]
    half, tok = x_all.shape[3], x_all.shape[2] // 2
    part = scaled.shape[2]
    owners = tables.shape[2]
    wgu, wd = (wgu0, wgu1), (wd0, wd1)

    x_copies, g_copies, t_copies = [], [], []
    for index, unit in enumerate(units_in):
        chunk, y, x = index // 4, index // 2 % 2, index % 2
        rows = pl.ds(y * tok, tok)
        x_copies.append(pltpu.make_async_copy(unit.at[pl.ds(0, tok)], x_all.at[chunk, x, rows], unit_sems.at[0, index]))
        g_copies.append(pltpu.make_async_copy(unit.at[pl.ds(tok, tok)], g_all.at[chunk, x, rows], unit_sems.at[1, index]))
        if x == 0:
            table = unit.at[pl.ds(2 * tok, owners), pl.ds(0, tok)]
            t_copies.append(pltpu.make_async_copy(table, tables.at[chunk, y], unit_sems.at[2, index]))
    weight_copies = [
        pltpu.make_async_copy(source, target, weight_sems.at[index])
        for index, (source, target) in enumerate(zip(weights_in, (wgu0, wgu1, wd0, wd1)))
    ]
    for copy in t_copies + x_copies + weight_copies[:2] + g_copies + weight_copies[2:]:
        copy.start()
    leaving = []

    def leave(source, target):
        copy = pltpu.make_async_copy(source, target, out_sems.at[len(leaving)])
        copy.start()
        leaving.append(copy)

    def leave_rows(held, target):
        for expert in range(2):
            for chunk, place in enumerate(places):
                source = held.at[expert, pl.ds(chunk * slots, slots)]
                leave(source, target.at[expert, pl.ds(place * slots, slots)])

    def dot(a, b, dims):
        return lax.dot_general(a, b, (dims, ((), ())), preferred_element_type=jnp.float32)

    for copy in t_copies:
        copy.wait()
    earlier = lax.broadcasted_iota(jnp.int32, (tok, tok), 0) < lax.broadcasted_iota(jnp.int32, (tok, tok), 1)
    earlier = earlier.astype(jnp.bfloat16)
    number = lax.broadcasted_iota(jnp.int32, (slots, tok), 0).astype(jnp.float32)
    names = lax.broadcasted_iota(jnp.int32, (owners, tok), 0)
    picks, low_picks, probs = {}, {}, {}
    for chunk in range(count):
        found = []
        for y in range(2):
            table = tables[chunk, y].astype(jnp.float32)
            rank = dot((table >= 0.0).astype(jnp.bfloat16), earlier, ((1,), (0,))) + float(y * capacity)
            found.append((table, jnp.where(table >= 0.0, rank, -1.0)))
        for expert in range(2):
            mine = names == where_ref[expert]
            halves, prob = [], None
            for table, rank in found:
                weight = jnp.sum(jnp.where(mine, table, 0.0), axis=0, keepdims=True)
                slot = jnp.sum(jnp.where(mine, rank, 0.0), axis=0, keepdims=True)
                halves.append((number == slot).astype(jnp.float32))
                term = jnp.sum(halves[-1] * weight, axis=1, keepdims=True)
                prob = term if prob is None else prob + term
            picks[chunk, expert] = halves
            low_picks[chunk, expert] = jnp.concatenate(halves, 1).astype(jnp.bfloat16)
            probs[chunk, expert] = prob
    spans = [pl.ds(chunk * slots, slots) for chunk in range(count)]
    sides = [slice(side * half, (side + 1) * half) for side in range(2)]

    def gather(copies, source, target):
        for chunk in range(count):
            for copy in copies[4 * chunk : 4 * chunk + 4]:
                copy.wait()
            both_picks = jnp.concatenate([low_picks[chunk, expert] for expert in range(2)], 0)
            for side in range(2):
                rows = dot(both_picks, source[chunk, side], ((1,), (0,))).astype(jnp.bfloat16)
                for expert in range(2):
                    target[expert, spans[chunk], sides[side]] = rows[expert * slots : (expert + 1) * slots]

    gather(x_copies, x_all, xc)
    leave_rows(xc, outs[0])
    rows = []
    for expert in range(2):
        weight_copies[expert].wait()
        rows.append(dot(xc[expert], wgu[expert][...], ((1,), (0,))))
    gather(g_copies, g_all, gc)
    leave_rows(gc, outs[1])
    scores = []
    for expert in range(2):
        weight_copies[2 + expert].wait()
        back = dot(gc[expert], wd[expert][...], ((1,), (1,)))
        gate, up = rows[expert][:, :part], rows[expert][:, part:]
        sig = jax.nn.sigmoid(gate)
        act = gate * sig
        hidden = act * up
        scores.append(jnp.sum(hidden * back, axis=1, keepdims=True))
        prob = jnp.concatenate([probs[chunk, expert] for chunk in range(count)], 0)
        hgrad = prob * back
        both[expert, :, :part] = (hgrad * up * sig * (1.0 + gate * (1.0 - sig))).astype(jnp.bfloat16)
        both[expert, :, part:] = (hgrad * act).astype(jnp.bfloat16)
        scaled[expert] = (prob * hidden).astype(jnp.bfloat16)
    leave_rows(both, outs[2])
    leave_rows(scaled, outs[3])

    names = lax.broadcasted_iota(jnp.int32, (owners, half), 0)
    column = lax.broadcasted_iota(jnp.int32, (owners, half), 1) // (2 * tok)
    for chunk in range(count):
        for y in range(2):
            extra = jnp.zeros((owners, half), jnp.float32)
            for expert in range(2):
                part_scores = scores[expert][chunk * slots : (chunk + 1) * slots]
                line = jnp.sum(picks[chunk, expert][y] * part_scores, axis=0, keepdims=True)
                high = line.astype(jnp.bfloat16).astype(jnp.float32)
                line = jnp.concatenate([high, line - high] * (half // (2 * tok)), 1)
                extra = extra + jnp.where((names == where_ref[expert]) & (column == where_ref[2]), line, 0.0)
            for side in range(2):
                piece[chunk, side, y, tok:] = extra.astype(jnp.bfloat16)
    for side in (1, 0):
        low = [
            dot(both[expert], wgu[expert][sides[side], :], ((1,), (1,))).astype(jnp.bfloat16) for expert in range(2)
        ]
        for chunk in range(count):
            total = None
            for expert in range(2):
                term = dot(low_picks[chunk, expert], low[expert][chunk * slots : (chunk + 1) * slots], ((0,), (0,)))
                total = term if total is None else total + term
            for y in range(2):
                piece[chunk, side, y, :tok] = total[y * tok : (y + 1) * tok].astype(jnp.bfloat16)
                first, second = (y, side) if modes[chunk] else (side, y)
                leave(piece.at[chunk, side, y], (sends if first else keeps)[chunk].at[second])
    for copy in leaving:
        copy.wait()


def rows_call(places, modes, steps, owners, capacity, slots, where, weights, units, held):
    count = len(places)
    tok, half = (units[0].shape[0] - owners) // 2, units[0].shape[1]
    part, width = weights[2].shape
    widths = (width, width, 2 * part, part)
    packet = (2, tok + owners, half)
    return pl.pallas_call(
        functools.partial(rows_kernel, places, modes, capacity, slots),
        grid_spec=pltpu.PrefetchScalarGridSpec(
            num_scalar_prefetch=1,
            grid=(1,),
            in_specs=[LOOSE] * (4 + len(units) + len(held)),
            out_specs=[LOOSE] * (4 + 2 * count),
            scratch_shapes=[pltpu.VMEM((count, 2, 2 * tok, half), jnp.bfloat16)] * 2
            + [pltpu.VMEM((count, 2, owners, tok), jnp.bfloat16)]
            + [pltpu.VMEM((width, 2 * part), jnp.bfloat16)] * 2
            + [pltpu.VMEM((part, width), jnp.bfloat16)] * 2
            + [pltpu.VMEM((2, count * slots, size), jnp.bfloat16) for size in widths]
            + [
                pltpu.VMEM((count, 2) + packet, jnp.bfloat16),
                pltpu.SemaphoreType.DMA((3, 4 * count)),
                pltpu.SemaphoreType.DMA((4,)),
                pltpu.SemaphoreType.DMA((12 * count,)),
            ],
        ),
        out_shape=[jax.ShapeDtypeStruct((2, steps * slots, size), jnp.bfloat16) for size in widths]
        + [jax.ShapeDtypeStruct(packet, jnp.bfloat16)] * (2 * count),
        input_output_aliases={5 + len(units) + i: i for i in range(len(held))},
        compiler_params=pltpu.CompilerParams(vmem_limit_bytes=56 << 20),
        cost_estimate=pl.CostEstimate(
            flops=count * (20 * slots * width * part + 24 * slots * tok * width),
            bytes_accessed=count * 16 * tok * width + 12 * width * part,
            transcendentals=2 * count * slots * part,
        ),
        name="rows",
    )(where, *weights, *units, *held)


def grads_kernel(first, tp_ref, x_ref, g_ref, both_ref, scaled_ref, *refs):
    flipped = refs[-1]
    part = scaled_ref.shape[2]

    @pl.when(pl.program_id(0) == 0)
    def _():
        flipped[...] = scaled_ref[0].T

    both = lax.dot_general(x_ref[0], both_ref[0], (((0,), (0,)), ((), ())), preferred_element_type=jnp.float32)
    down = jnp.dot(flipped[...], g_ref[0], preferred_element_type=jnp.float32)
    if first:
        both_out, down_out = refs[-3:-1]
        both_out[...] = both.astype(jnp.bfloat16)
        down_out[...] = down.astype(jnp.bfloat16)
        return
    more_both, more_down = refs[:2]
    dg_ref, du_ref, dd_ref = refs[-4:-1]
    both = both + more_both[...].astype(jnp.float32)
    dg_ref[0] = both[:, :part].astype(jnp.bfloat16)
    du_ref[0] = both[:, part:].astype(jnp.bfloat16)
    dd_ref[0] = (down + more_down[...].astype(jnp.float32)).astype(jnp.bfloat16)


def grads_call(which, expert, x_rows, g_rows, both, scaled, more, after):
    _, total, width = x_rows.shape
    part = scaled.shape[2]
    step = math.gcd(width // 2, 512)
    per = width // 2 // step

    def place(i, w):
        return (i + w[0] * per) % (2 * per)

    moving = pl.BlockSpec((1, total, step), lambda i, w: (expert, 0, i))
    passing = [
        pl.BlockSpec((step, 2 * part), lambda i, w: (i, 0)),
        pl.BlockSpec((part, step), lambda i, w: (0, i)),
    ]
    if more:
        out_specs = [
            pl.BlockSpec((1, step, part), lambda i, w: (0, place(i, w), 0)),
            pl.BlockSpec((1, step, part), lambda i, w: (0, place(i, w), 0)),
            pl.BlockSpec((1, part, step), lambda i, w: (0, 0, place(i, w))),
        ]
        shapes = [(1, width, part), (1, width, part), (1, part, width)]
    else:
        out_specs = passing
        shapes = [(width, 2 * part), (part, width)]
    return pl.pallas_call(
        functools.partial(grads_kernel, not more),
        grid_spec=pltpu.PrefetchScalarGridSpec(
            num_scalar_prefetch=1,
            grid=(width // step,),
            in_specs=[
                moving,
                moving,
                pl.BlockSpec((1, total, 2 * part), lambda i, w: (expert, 0, 0)),
                pl.BlockSpec((1, total, part), lambda i, w: (expert, 0, 0)),
            ]
            + (passing if more else [])
            + [LOOSE] * len(after),
            out_specs=out_specs,
            scratch_shapes=[pltpu.VMEM((part, total), jnp.bfloat16)],
        ),
        out_shape=[jax.ShapeDtypeStruct(shape, jnp.bfloat16) for shape in shapes],
        compiler_params=pltpu.CompilerParams(vmem_limit_bytes=56 << 20),
        cost_estimate=pl.CostEstimate(flops=6 * total * width * part, bytes_accessed=6 * total * width, transcendentals=0),
        name="grads",
    )(which, x_rows, g_rows, both, scaled, *more, *after)


def dense_device(tokens, out_grad, routes, probs, w_gate, w_up, w_down):
    owners = lax.axis_size(("role", "ep"))
    ep = lax.axis_size("ep")
    n_y = 2
    n_z = ep // n_y
    tok_rows, half = tokens.shape
    capacity = slot_capacity(tok_rows, routes.shape[1], owners)
    slots = -(-n_y * capacity // 16) * 16
    role, place, which = lax.axis_index("role"), lax.axis_index("ep"), lax.axis_index("tp")

    def over_x(array):
        return lax.ppermute(array, "tp", [(0, 1), (1, 0)])

    def over_role(array):
        return lax.ppermute(array, "role", [(0, 1), (1, 0)])

    def over_y(array):
        return lax.ppermute(array, "ep", [(i, i + 1 - 2 * (i % n_y)) for i in range(ep)])

    def over_z(array, shift):
        return lax.ppermute(array, "ep", [(i, (i + shift * n_y) % ep) for i in range(ep)])

    chosen = routes[:, :, None] == jnp.arange(owners, dtype=jnp.int32)
    table = jnp.sum(jnp.where(chosen, probs[:, :, None].astype(jnp.float32) + 1.0, 0.0), axis=1) - 1.0
    table = jnp.pad(table.astype(jnp.bfloat16).T, ((0, 0), (0, half - tok_rows)))
    units = {(0, 0, 0): jnp.concatenate([tokens, out_grad, table], 0)}
    last = n_z - 1
    for z in range(n_z):
        if z:
            back = 0 if z in (1, last) else z - 1
            shift = -1 if z == last and z > 1 else 1
            units[z, 0, 0] = over_z(units[back, 0, 0], shift)
        units[z, 1, 0] = over_y(units[z, 0, 0])
        units[z, 0, 1] = over_x(units[z, 0, 0])
        if z == 0:
            units[z, 1, 1] = over_x(units[z, 1, 0])
        elif z in (1, last):
            units[z, 1, 1] = over_z(units[0, 1, 1], shift)
        else:
            units[z, 1, 1] = over_y(units[z, 0, 1])

    which_ref = which.reshape(1).astype(jnp.int32)
    both_w, down_w = weights_call(which_ref, w_gate, w_up, w_down, [units[1, 0, 0], units[0, 1, 0], units[0, 0, 1]])
    weights = (both_w, over_role(both_w), down_w, over_role(down_w))
    where = jnp.stack([role * ep + place, (1 - role) * ep + place, which]).astype(jnp.int32)

    def add(a, b):
        return a.astype(jnp.float32) + b.astype(jnp.float32)

    held, homeward, early, late = (), [], [], []
    for group in (range(0, n_z, 2), range(1, n_z, 2)):
        modes = [index % 2 for index in range(len(group))]
        four = [units[z, y, x] for z in group for y in range(2) for x in range(2)]
        packets = rows_call(group, modes, n_z, owners, capacity, slots, where, weights, four, held)
        held, packets = packets[:4], packets[4:]
        for index, z in enumerate(group):
            keep, send = packets[index], packets[len(group) + index]
            go_first, go_second = (over_y, over_x) if modes[index] else (over_x, over_y)
            recv = go_first(send)
            recv_next = go_second(add(keep[1], recv[1]).astype(jnp.bfloat16))
            (late if group[0] else early).append(recv)
            if not group[0]:
                late.append(recv_next)
            total = add(add(keep[0], recv[0]), recv_next)
            homeward.append(over_z(total.astype(jnp.bfloat16), -z).astype(jnp.float32) if z else total)
    home = sum(homeward[1:], homeward[0])
    d_tok = home[:tok_rows].astype(jnp.bfloat16)
    more = grads_call(which_ref, 1, *held, [], early)
    d_gate, d_up, d_down = grads_call(which_ref, 0, *held, [over_role(item) for item in more], late)
    score = jnp.sum(home[tok_rows:, : 4 * tok_rows].reshape(owners, 4, tok_rows), axis=1).T
    d_probs = jnp.sum(jnp.where(chosen, score[:, None, :], 0.0), axis=2)
    return d_tok, d_probs, d_gate, d_up, d_down


def per_device(tokens, out_grad, routes, probs, w_gate, w_up, w_down):
    owners = lax.axis_size(("role", "ep"))
    tok_rows, top_count = routes.shape
    paired = lax.axis_size("tp") == 2 and lax.axis_size("role") == 2 and lax.axis_size("ep") % 4 == 0
    if paired and 2 * slot_capacity(tok_rows, top_count, owners) >= tok_rows:
        return dense_device(tokens, out_grad, routes, probs, w_gate, w_up, w_down)
    return routed_device(tokens, out_grad, routes, probs, w_gate, w_up, w_down)


def solution(mesh):
    in_specs = (
        P(("groups", "role", "ep"), "tp"),
        P(("groups", "role", "ep"), "tp"),
        P(("groups", "role", "ep"), None),
        P(("groups", "role", "ep"), None),
        P(("role", "ep"), None, "tp"),
        P(("role", "ep"), None, "tp"),
        P(("role", "ep"), "tp", None),
    )
    out_specs = (
        P(("groups", "role", "ep"), "tp"),
        P(("groups", "role", "ep"), None),
        P(("groups", "role", "ep"), None, "tp"),
        P(("groups", "role", "ep"), None, "tp"),
        P(("groups", "role", "ep"), "tp", None),
    )
    return jax.shard_map(
        per_device, mesh=mesh, in_specs=in_specs, out_specs=out_specs, check_vma=False
    )
```

```python
import functools
import math

import jax
import jax.numpy as jnp
from jax import lax
from jax.experimental import pallas as pl
from jax.experimental.pallas import tpu as pltpu
from jax.sharding import PartitionSpec as P


def pad_rows(array):
    return jnp.concatenate([array, jnp.zeros((1, array.shape[1]), array.dtype)], 0)


def routed_device(tokens, out_grad, routes, probs, w_gate, w_up, w_down):
    owners = lax.axis_size(("role", "ep"))
    tok_rows, top_count = routes.shape
    width_full = w_gate.shape[1]
    part_width = w_gate.shape[2]
    capacity = min(tok_rows, tok_rows * top_count * 9 // (8 * owners))
    entry_total = tok_rows * top_count
    routes_flat = routes.reshape(-1)
    onehot = (routes_flat[:, None] == jnp.arange(owners, dtype=jnp.int32)[None, :]).astype(
        jnp.int32
    )
    before = jnp.cumsum(onehot, axis=0) - onehot
    slot_index = jnp.sum(before * onehot, axis=1)
    target = routes_flat * capacity + slot_index
    row_count = owners * capacity
    entry_of_slot = (
        jnp.full((row_count,), entry_total, jnp.int32)
        .at[target]
        .set(jnp.arange(entry_total, dtype=jnp.int32))
    )
    token_of_slot = entry_of_slot // top_count
    padded_prob = jnp.concatenate([probs.reshape(-1), jnp.zeros((1,), probs.dtype)], 0)
    send_prob = padded_prob[entry_of_slot].reshape(owners, capacity)
    send_x = pad_rows(tokens)[token_of_slot]
    send_g = pad_rows(out_grad)[token_of_slot]
    slice_x, slice_g, recv_p = (
        lax.all_to_all(
            send_x.reshape(owners, capacity, tokens.shape[1]),
            ("role", "ep"),
            split_axis=0,
            concat_axis=0,
            tiled=True,
        ),
        lax.all_to_all(
            send_g.reshape(owners, capacity, tokens.shape[1]),
            ("role", "ep"),
            split_axis=0,
            concat_axis=0,
            tiled=True,
        ),
        lax.all_to_all(send_prob, ("role", "ep"), split_axis=0, concat_axis=0, tiled=True),
    )
    recv_x, recv_g = (
        lax.all_gather(slice_x, "tp", axis=2, tiled=True),
        lax.all_gather(slice_g, "tp", axis=2, tiled=True),
    )
    rows_x = recv_x.reshape(row_count, width_full)
    rows_g = recv_g.reshape(row_count, width_full)
    weight_p = recv_p.reshape(row_count, 1).astype(jnp.float32)
    gate_up = jnp.concatenate([w_gate[0], w_up[0]], 1)
    down_shard = w_down[0]
    both_rows = jnp.dot(rows_x, gate_up, preferred_element_type=jnp.float32)
    gate_rows = both_rows[:, :part_width]
    up_rows = both_rows[:, part_width:]
    sigmoid_gate = jax.nn.sigmoid(gate_rows)
    activated = gate_rows * sigmoid_gate
    hidden = activated * up_rows
    back_rows = lax.dot_general(
        rows_g, down_shard, (((1,), (1,)), ((), ())), preferred_element_type=jnp.float32
    )
    scores = lax.psum(jnp.sum(hidden * back_rows, axis=1), "tp")
    hidden_grad = weight_p * back_rows
    d_gate_rows = (
        hidden_grad * up_rows * sigmoid_gate * (1.0 + gate_rows * (1.0 - sigmoid_gate))
    ).astype(jnp.bfloat16)
    d_up_rows = (hidden_grad * activated).astype(jnp.bfloat16)
    d_both = jnp.concatenate([d_gate_rows, d_up_rows], 1)
    scaled = (weight_p * hidden).astype(jnp.bfloat16)
    grad_down = lax.dot_general(
        scaled, rows_g, (((0,), (0,)), ((), ())), preferred_element_type=jnp.float32
    )
    grad_both = lax.dot_general(
        rows_x, d_both, (((0,), (0,)), ((), ())), preferred_element_type=jnp.float32
    )
    grad_gate = grad_both[:, :part_width]
    grad_up = grad_both[:, part_width:]
    partial_low = lax.dot_general(
        d_both, gate_up, (((1,), (1,)), ((), ())), preferred_element_type=jnp.float32
    ).astype(jnp.bfloat16)
    home_s = lax.all_to_all(
        scores.reshape(owners, capacity), ("role", "ep"), split_axis=0, concat_axis=0, tiled=True
    )
    summed = lax.psum_scatter(
        partial_low.reshape(owners, capacity, width_full), "tp", scatter_dimension=2, tiled=True
    ).astype(jnp.float32)
    summed_low = summed.astype(jnp.bfloat16)
    home_x = lax.all_to_all(summed_low, ("role", "ep"), split_axis=0, concat_axis=0, tiled=True)
    slice_width = summed.shape[2]
    route_rows = home_x.reshape(row_count, slice_width).astype(jnp.float32)
    d_tok = (
        jnp.zeros((tok_rows + 1, slice_width), jnp.float32)
        .at[token_of_slot]
        .add(route_rows)[:tok_rows]
    )
    d_probs = home_s.reshape(-1)[target].reshape(tok_rows, top_count)
    return (
        d_tok.astype(jnp.bfloat16),
        d_probs,
        grad_gate.astype(jnp.bfloat16)[None],
        grad_up.astype(jnp.bfloat16)[None],
        grad_down.astype(jnp.bfloat16)[None],
    )


def slot_capacity(tok_rows, top_count, owners):
    return min(tok_rows, tok_rows * top_count * 9 // (8 * owners))


LOOSE = pl.BlockSpec(memory_space=pl.ANY)


def weights_kernel(tp_ref, wg_ref, wu_ref, wd_ref, *refs):
    both_ref, down_ref = refs[-2:]
    part = wg_ref.shape[2]
    both_ref[:, :part] = wg_ref[0]
    both_ref[:, part:] = wu_ref[0]
    down_ref[...] = wd_ref[0]


def weights_call(which, w_gate, w_up, w_down, after):
    _, width, part = w_gate.shape
    half = width // 2

    def place(i, w):
        return (i + w[0]) % 2

    return pl.pallas_call(
        weights_kernel,
        grid_spec=pltpu.PrefetchScalarGridSpec(
            num_scalar_prefetch=1,
            grid=(2,),
            in_specs=[
                pl.BlockSpec((1, half, part), lambda i, w: (0, place(i, w), 0)),
                pl.BlockSpec((1, half, part), lambda i, w: (0, place(i, w), 0)),
                pl.BlockSpec((1, part, half), lambda i, w: (0, 0, place(i, w))),
            ]
            + [LOOSE] * len(after),
            out_specs=[
                pl.BlockSpec((half, 2 * part), lambda i, w: (i, 0)),
                pl.BlockSpec((part, half), lambda i, w: (0, i)),
            ],
        ),
        out_shape=[
            jax.ShapeDtypeStruct((width, 2 * part), jnp.bfloat16),
            jax.ShapeDtypeStruct((part, width), jnp.bfloat16),
        ],
        compiler_params=pltpu.CompilerParams(vmem_limit_bytes=56 << 20),
        cost_estimate=pl.CostEstimate(flops=0, bytes_accessed=12 * width * part, transcendentals=0),
        name="weights",
    )(which, w_gate, w_up, w_down, *after)


def rows_kernel(count, modes, capacity, slots, where_ref, *refs):
    weights_in, x_in, g_in = refs[:4], refs[4 : 4 + 4 * count], refs[4 + 4 * count : 4 + 8 * count]
    refs = refs[len(refs) - 17 - 2 * count :]
    outs, keeps, sends, refs = refs[:2], refs[2 : 2 + count], refs[2 + count : 2 + 2 * count], refs[2 + 2 * count :]
    x_all, g_all, tables, wgu0, wgu1, wd0, wd1, xc, gc, both, scaled, piece, unit_sems, weight_sems = refs[:14]
    out_sems = refs[14]
    half, tok = x_all.shape[3], x_all.shape[2] // 2
    part = scaled.shape[2]
    owners = tables.shape[2]
    wgu, wd = (wgu0, wgu1), (wd0, wd1)

    x_copies, g_copies, t_copies = [], [], []
    for index, (x_unit, g_unit) in enumerate(zip(x_in, g_in)):
        chunk, y, x = index // 4, index // 2 % 2, index % 2
        rows = pl.ds(y * tok, tok)
        x_copies.append(pltpu.make_async_copy(x_unit.at[pl.ds(0, tok)], x_all.at[chunk, x, rows], unit_sems.at[0, index]))
        g_copies.append(pltpu.make_async_copy(g_unit, g_all.at[chunk, x, rows], unit_sems.at[1, index]))
        if x == 0:
            table = x_unit.at[pl.ds(tok, owners), pl.ds(0, tok)]
            t_copies.append(pltpu.make_async_copy(table, tables.at[chunk, y], unit_sems.at[2, index]))
    weight_copies = [
        pltpu.make_async_copy(source, target, weight_sems.at[index])
        for index, (source, target) in enumerate(zip(weights_in, (wgu0, wgu1, wd0, wd1)))
    ]
    for copy in t_copies + x_copies + weight_copies[:2] + g_copies + weight_copies[2:]:
        copy.start()
    leaving = []

    def leave(source, target):
        copy = pltpu.make_async_copy(source, target, out_sems.at[len(leaving)])
        copy.start()
        leaving.append(copy)

    def leave_rows(held, start):
        for expert in range(2):
            leave(held.at[expert], outs[expert].at[:, pl.ds(start, held.shape[2])])

    def dot(a, b, dims):
        return lax.dot_general(a, b, (dims, ((), ())), preferred_element_type=jnp.float32)

    for copy in t_copies:
        copy.wait()
    earlier = lax.broadcasted_iota(jnp.int32, (tok, tok), 0) < lax.broadcasted_iota(jnp.int32, (tok, tok), 1)
    earlier = earlier.astype(jnp.bfloat16)
    number = lax.broadcasted_iota(jnp.int32, (slots, tok), 0).astype(jnp.float32)
    names = lax.broadcasted_iota(jnp.int32, (owners, tok), 0)
    picks, low_picks, probs = {}, {}, {}
    for chunk in range(count):
        found = []
        for y in range(2):
            table = tables[chunk, y].astype(jnp.float32)
            rank = dot((table >= 0.0).astype(jnp.bfloat16), earlier, ((1,), (0,))) + float(y * capacity)
            found.append((table, jnp.where(table >= 0.0, rank, -1.0)))
        for expert in range(2):
            mine = names == where_ref[expert]
            halves, prob = [], None
            for table, rank in found:
                weight = jnp.sum(jnp.where(mine, table, 0.0), axis=0, keepdims=True)
                slot = jnp.sum(jnp.where(mine, rank, 0.0), axis=0, keepdims=True)
                halves.append((number == slot).astype(jnp.float32))
                term = jnp.sum(halves[-1] * weight, axis=1, keepdims=True)
                prob = term if prob is None else prob + term
            picks[chunk, expert] = halves
            low_picks[chunk, expert] = jnp.concatenate(halves, 1).astype(jnp.bfloat16)
            probs[chunk, expert] = prob
    spans = [pl.ds(chunk * slots, slots) for chunk in range(count)]
    sides = [slice(side * half, (side + 1) * half) for side in range(2)]

    def gather(copies, source, target):
        for chunk in range(count):
            for copy in copies[4 * chunk : 4 * chunk + 4]:
                copy.wait()
            both_picks = jnp.concatenate([low_picks[chunk, expert] for expert in range(2)], 0)
            for side in range(2):
                rows = dot(both_picks, source[chunk, side], ((1,), (0,))).astype(jnp.bfloat16)
                for expert in range(2):
                    target[expert, spans[chunk], sides[side]] = rows[expert * slots : (expert + 1) * slots]

    gather(x_copies, x_all, xc)
    leave_rows(xc, 0)
    rows = []
    for expert in range(2):
        weight_copies[expert].wait()
        rows.append(dot(xc[expert], wgu[expert][...], ((1,), (0,))))
    gather(g_copies, g_all, gc)
    leave_rows(gc, 2 * half)
    scores = []
    for expert in range(2):
        weight_copies[2 + expert].wait()
        back = dot(gc[expert], wd[expert][...], ((1,), (1,)))
        gate, up = rows[expert][:, :part], rows[expert][:, part:]
        sig = jax.nn.sigmoid(gate)
        act = gate * sig
        hidden = act * up
        scores.append(jnp.sum(hidden * back, axis=1, keepdims=True))
        prob = jnp.concatenate([probs[chunk, expert] for chunk in range(count)], 0)
        hgrad = prob * back
        both[expert, :, :part] = (hgrad * up * sig * (1.0 + gate * (1.0 - sig))).astype(jnp.bfloat16)
        both[expert, :, part:] = (hgrad * act).astype(jnp.bfloat16)
        scaled[expert] = (prob * hidden).astype(jnp.bfloat16)
    leave_rows(both, 4 * half)
    leave_rows(scaled, 4 * half + 2 * part)

    names = lax.broadcasted_iota(jnp.int32, (owners, half), 0)
    column = lax.broadcasted_iota(jnp.int32, (owners, half), 1) // (2 * tok)
    for chunk in range(count):
        for y in range(2):
            extra = jnp.zeros((owners, half), jnp.float32)
            for expert in range(2):
                part_scores = scores[expert][chunk * slots : (chunk + 1) * slots]
                line = jnp.sum(picks[chunk, expert][y] * part_scores, axis=0, keepdims=True)
                high = line.astype(jnp.bfloat16).astype(jnp.float32)
                line = jnp.concatenate([high, line - high] * (half // (2 * tok)), 1)
                extra = extra + jnp.where((names == where_ref[expert]) & (column == where_ref[2]), line, 0.0)
            for side in range(2):
                piece[chunk, side, y, tok:] = extra.astype(jnp.bfloat16)
    for side in (1, 0):
        low = [
            dot(both[expert], wgu[expert][sides[side], :], ((1,), (1,))).astype(jnp.bfloat16) for expert in range(2)
        ]
        for chunk in range(count):
            total = None
            for expert in range(2):
                term = dot(low_picks[chunk, expert], low[expert][chunk * slots : (chunk + 1) * slots], ((0,), (0,)))
                total = term if total is None else total + term
            for y in range(2):
                piece[chunk, side, y, :tok] = total[y * tok : (y + 1) * tok].astype(jnp.bfloat16)
                first, second = (y, side) if modes[chunk] else (side, y)
                leave(piece.at[chunk, side, y], (sends if first else keeps)[chunk].at[second])
    for copy in leaving:
        copy.wait()


def rows_call(modes, owners, capacity, slots, where, weights, units, after):
    count = len(modes)
    tok, half = units[-1].shape
    part, width = weights[2].shape
    widths = (width, width, 2 * part, part)
    packet = (2, tok + owners, half)
    return pl.pallas_call(
        functools.partial(rows_kernel, count, modes, capacity, slots),
        grid_spec=pltpu.PrefetchScalarGridSpec(
            num_scalar_prefetch=1,
            grid=(1,),
            in_specs=[LOOSE] * (4 + len(units) + len(after)),
            out_specs=[LOOSE] * (2 + 2 * count),
            scratch_shapes=[pltpu.VMEM((count, 2, 2 * tok, half), jnp.bfloat16)] * 2
            + [pltpu.VMEM((count, 2, owners, tok), jnp.bfloat16)]
            + [pltpu.VMEM((width, 2 * part), jnp.bfloat16)] * 2
            + [pltpu.VMEM((part, width), jnp.bfloat16)] * 2
            + [pltpu.VMEM((2, count * slots, size), jnp.bfloat16) for size in widths]
            + [
                pltpu.VMEM((count, 2) + packet, jnp.bfloat16),
                pltpu.SemaphoreType.DMA((3, 4 * count)),
                pltpu.SemaphoreType.DMA((4,)),
                pltpu.SemaphoreType.DMA((8 + 4 * count,)),
            ],
        ),
        out_shape=[jax.ShapeDtypeStruct((count * slots, sum(widths)), jnp.bfloat16)] * 2
        + [jax.ShapeDtypeStruct(packet, jnp.bfloat16)] * (2 * count),
        compiler_params=pltpu.CompilerParams(vmem_limit_bytes=56 << 20),
        cost_estimate=pl.CostEstimate(
            flops=count * (20 * slots * width * part + 24 * slots * tok * width),
            bytes_accessed=count * 16 * tok * width + 12 * width * part,
            transcendentals=2 * count * slots * part,
        ),
        name="rows",
    )(where, *weights, *units, *after)


def grads_kernel(count, wide, deep, blocks, tp_ref, *refs):
    sources, outs = refs[:count], refs[count:-4]
    wide_all, deep_all, wide_sems, deep_sems = refs[-4:]
    rows = sources[0].shape[0]
    size = wide_all.shape[2]
    block = pl.program_id(0)

    def copies(column):
        return [
            pltpu.make_async_copy(
                source.at[:, pl.ds(wide + column * size, size)],
                wide_all.at[column, pl.ds(index * rows, rows)],
                wide_sems.at[column, index],
            )
            for index, source in enumerate(sources)
        ]

    @pl.when(block == 0)
    def _():
        deep_copies = [
            pltpu.make_async_copy(
                source.at[:, pl.ds(deep, deep_all.shape[1])], deep_all.at[pl.ds(index * rows, rows)], deep_sems.at[index]
            )
            for index, source in enumerate(sources)
        ]
        for copy in deep_copies:
            copy.start()
        for column in range(blocks):
            for copy in copies(column):
                copy.start()
        for copy in deep_copies:
            copy.wait()

    for column in range(blocks):

        @pl.when(block == column)
        def _(column=column):
            for copy in copies(column):
                copy.wait()

    dims = (((0,), (0,)), ((), ()))
    if len(outs) == 2:
        part = outs[0].shape[2]
        both = lax.dot_general(wide_all[block], deep_all[...], dims, preferred_element_type=jnp.float32)
        outs[0][0] = both[:, :part].astype(jnp.bfloat16)
        outs[1][0] = both[:, part:].astype(jnp.bfloat16)
    else:
        down = lax.dot_general(deep_all[...], wide_all[block], dims, preferred_element_type=jnp.float32)
        outs[0][0] = down.astype(jnp.bfloat16)


def grads_call(which, packed, width, part, down):
    rows, count = packed[0].shape[0], len(packed)
    step = math.gcd(width // 2, 512)
    per = width // 2 // step
    deep = part if down else 2 * part

    def place(i, w):
        return (i + w[0] * per) % (2 * per)

    if down:
        specs = [pl.BlockSpec((1, part, step), lambda i, w: (0, 0, place(i, w)))]
        shapes = [(1, part, width)]
    else:
        specs = [pl.BlockSpec((1, step, part), lambda i, w: (0, place(i, w), 0))] * 2
        shapes = [(1, width, part)] * 2
    starts = (width, 2 * width + 2 * part) if down else (0, 2 * width)
    return pl.pallas_call(
        functools.partial(grads_kernel, count, *starts, 2 * per),
        grid_spec=pltpu.PrefetchScalarGridSpec(
            num_scalar_prefetch=1,
            grid=(2 * per,),
            in_specs=[LOOSE] * count,
            out_specs=specs,
            scratch_shapes=[
                pltpu.VMEM((2 * per, count * rows, step), jnp.bfloat16),
                pltpu.VMEM((count * rows, deep), jnp.bfloat16),
                pltpu.SemaphoreType.DMA((2 * per, count)),
                pltpu.SemaphoreType.DMA((count,)),
            ],
        ),
        out_shape=[jax.ShapeDtypeStruct(shape, jnp.bfloat16) for shape in shapes],
        compiler_params=pltpu.CompilerParams(vmem_limit_bytes=56 << 20),
        cost_estimate=pl.CostEstimate(
            flops=2 * count * rows * width * deep, bytes_accessed=2 * count * rows * (width + deep), transcendentals=0
        ),
        name="grads",
    )(which, *packed)


def dense_device(tokens, out_grad, routes, probs, w_gate, w_up, w_down):
    owners = lax.axis_size(("role", "ep"))
    ep = lax.axis_size("ep")
    n_y = 2
    n_z = ep // n_y
    tok_rows, half = tokens.shape
    capacity = slot_capacity(tok_rows, routes.shape[1], owners)
    slots = -(-n_y * capacity // 16) * 16
    role, place, which = lax.axis_index("role"), lax.axis_index("ep"), lax.axis_index("tp")

    def over_x(array):
        return lax.ppermute(array, "tp", [(0, 1), (1, 0)])

    def over_role(array):
        return lax.ppermute(array, "role", [(0, 1), (1, 0)])

    def over_y(array):
        return lax.ppermute(array, "ep", [(i, i + 1 - 2 * (i % n_y)) for i in range(ep)])

    def over_z(array, shift):
        return lax.ppermute(array, "ep", [(i, (i + shift * n_y) % ep) for i in range(ep)])

    chosen = routes[:, :, None] == jnp.arange(owners, dtype=jnp.int32)
    table = jnp.sum(jnp.where(chosen, probs[:, :, None].astype(jnp.float32) + 1.0, 0.0), axis=1) - 1.0
    table = jnp.pad(table.astype(jnp.bfloat16).T, ((0, 0), (0, half - tok_rows)))
    last = n_z - 1
    routes_in = []
    for z in range(n_z):
        shift = -1 if z == last and z > 1 else 1
        if z:
            routes_in.append(((z, 0, 0), (0 if z in (1, last) else z - 1, 0, 0), functools.partial(over_z, shift=shift)))
        routes_in.append(((z, 1, 0), (z, 0, 0), over_y))
        routes_in.append(((z, 0, 1), (z, 0, 0), over_x))
        if z == 0:
            routes_in.append(((z, 1, 1), (z, 1, 0), over_x))
        elif z in (1, last):
            routes_in.append(((z, 1, 1), (0, 1, 1), functools.partial(over_z, shift=shift)))
        else:
            routes_in.append(((z, 1, 1), (z, 0, 1), over_y))
    routes_in.sort(key=lambda item: (item[0][0] % 2 if item[2] in (over_x, over_y) else 0, sum(item[0][1:])))

    rounds, waiting, there = [], list(routes_in), {(0, 0, 0)}
    while waiting:
        moves = {}
        for item in waiting:
            axis = item[2] if item[2] in (over_x, over_y) else over_z
            if item[1] in there and axis not in moves:
                moves[axis] = item
        rounds.append(list(moves.values()))
        there |= {item[0] for item in rounds[-1]}
        waiting = [item for item in waiting if item[0] not in there]

    units = {("x", 0, 0, 0): jnp.concatenate([tokens, table], 0), ("g", 0, 0, 0): out_grad}
    settled, flying = dict(units), {}
    for moves in rounds:
        for name in ("x", "g"):
            arrived = {(name,) + target: move(settled[(name,) + source]) for target, source, move in moves}
            units.update(arrived)
            settled.update(flying)
            names = list(settled)
            settled = dict(zip(names, lax.optimization_barrier([settled[item] for item in names])))
            flying = arrived

    which_ref = which.reshape(1).astype(jnp.int32)
    first = [units[("x",) + item[0]] for item in rounds[1]]
    both_w, down_w = weights_call(which_ref, w_gate, w_up, w_down, first)
    weights = (both_w, over_role(both_w), down_w, over_role(down_w))
    where = jnp.stack([role * ep + place, (1 - role) * ep + place, which]).astype(jnp.int32)

    def add(a, b):
        return a.astype(jnp.float32) + b.astype(jnp.float32)

    def tied(values, others):
        return lax.optimization_barrier((list(values), list(others)))[0]

    width, part = both_w.shape[0], down_w.shape[0]
    packed, flown, homeward, done = [], [], [], []
    for turn, group in enumerate((range(0, n_z, 2), range(1, n_z, 2))):
        modes = [index % 2 for index in range(len(group))]
        eight = [units[name, z, y, x] for name in ("x", "g") for z in group for y in range(2) for x in range(2)]
        mine, other, *packets = rows_call(modes, owners, capacity, slots, where, weights, eight, packed[:1])
        keeps, sends = packets[: len(group)], packets[len(group) :]
        if turn:
            mine, other, *sends = tied([mine, other] + sends, flown[0])
        packed += [mine, over_role(other)]
        firsts = [over_y(send) if mode else over_x(send) for mode, send in zip(modes, sends)]
        if turn:
            done += grads_call(which_ref, packed, width, part, False)
            firsts = tied(firsts, flown[1] + done)
        sends = [add(keep[1], first[1]).astype(jnp.bfloat16) for keep, first in zip(keeps, firsts)]
        seconds = [over_x(send) if mode else over_y(send) for mode, send in zip(modes, sends)]
        if turn:
            done += grads_call(which_ref, packed, width, part, True)
            seconds = tied(seconds, homeward[1:] + done)
        totals = [add(add(keep[0], first[0]), second) for keep, first, second in zip(keeps, firsts, seconds)]
        sends = [total.astype(jnp.bfloat16) for total in totals]
        thirds = [over_z(send, -z) if z else total for z, send, total in zip(group, sends, totals)]
        homeward += thirds
        flown += [firsts, seconds]
    home = sum(item.astype(jnp.float32) for item in homeward)
    d_tok = home[:tok_rows].astype(jnp.bfloat16)
    d_gate, d_up, d_down = done
    score = jnp.sum(home[tok_rows:, : 4 * tok_rows].reshape(owners, 4, tok_rows), axis=1).T
    d_probs = jnp.sum(jnp.where(chosen, score[:, None, :], 0.0), axis=2)
    return d_tok, d_probs, d_gate, d_up, d_down


def per_device(tokens, out_grad, routes, probs, w_gate, w_up, w_down):
    owners = lax.axis_size(("role", "ep"))
    tok_rows, top_count = routes.shape
    paired = lax.axis_size("tp") == 2 and lax.axis_size("role") == 2 and lax.axis_size("ep") % 4 == 0
    if paired and 2 * slot_capacity(tok_rows, top_count, owners) >= tok_rows:
        return dense_device(tokens, out_grad, routes, probs, w_gate, w_up, w_down)
    return routed_device(tokens, out_grad, routes, probs, w_gate, w_up, w_down)


def solution(mesh):
    in_specs = (
        P(("groups", "role", "ep"), "tp"),
        P(("groups", "role", "ep"), "tp"),
        P(("groups", "role", "ep"), None),
        P(("groups", "role", "ep"), None),
        P(("role", "ep"), None, "tp"),
        P(("role", "ep"), None, "tp"),
        P(("role", "ep"), "tp", None),
    )
    out_specs = (
        P(("groups", "role", "ep"), "tp"),
        P(("groups", "role", "ep"), None),
        P(("groups", "role", "ep"), None, "tp"),
        P(("groups", "role", "ep"), None, "tp"),
        P(("groups", "role", "ep"), "tp", None),
    )
    return jax.shard_map(
        per_device, mesh=mesh, in_specs=in_specs, out_specs=out_specs, check_vma=False
    )
```

```python
import functools
import math

import jax
import jax.numpy as jnp
from jax import lax
from jax.experimental import pallas as pl
from jax.experimental.pallas import tpu as pltpu
from jax.sharding import PartitionSpec as P


def pad_rows(array):
    return jnp.concatenate([array, jnp.zeros((1, array.shape[1]), array.dtype)], 0)


def routed_device(tokens, out_grad, routes, probs, w_gate, w_up, w_down):
    owners = lax.axis_size(("role", "ep"))
    tok_rows, top_count = routes.shape
    width_full = w_gate.shape[1]
    part_width = w_gate.shape[2]
    capacity = min(tok_rows, tok_rows * top_count * 9 // (8 * owners))
    entry_total = tok_rows * top_count
    routes_flat = routes.reshape(-1)
    onehot = (routes_flat[:, None] == jnp.arange(owners, dtype=jnp.int32)[None, :]).astype(
        jnp.int32
    )
    before = jnp.cumsum(onehot, axis=0) - onehot
    slot_index = jnp.sum(before * onehot, axis=1)
    target = routes_flat * capacity + slot_index
    row_count = owners * capacity
    entry_of_slot = (
        jnp.full((row_count,), entry_total, jnp.int32)
        .at[target]
        .set(jnp.arange(entry_total, dtype=jnp.int32))
    )
    token_of_slot = entry_of_slot // top_count
    padded_prob = jnp.concatenate([probs.reshape(-1), jnp.zeros((1,), probs.dtype)], 0)
    send_prob = padded_prob[entry_of_slot].reshape(owners, capacity)
    send_x = pad_rows(tokens)[token_of_slot]
    send_g = pad_rows(out_grad)[token_of_slot]
    slice_x, slice_g, recv_p = (
        lax.all_to_all(
            send_x.reshape(owners, capacity, tokens.shape[1]),
            ("role", "ep"),
            split_axis=0,
            concat_axis=0,
            tiled=True,
        ),
        lax.all_to_all(
            send_g.reshape(owners, capacity, tokens.shape[1]),
            ("role", "ep"),
            split_axis=0,
            concat_axis=0,
            tiled=True,
        ),
        lax.all_to_all(send_prob, ("role", "ep"), split_axis=0, concat_axis=0, tiled=True),
    )
    recv_x, recv_g = (
        lax.all_gather(slice_x, "tp", axis=2, tiled=True),
        lax.all_gather(slice_g, "tp", axis=2, tiled=True),
    )
    rows_x = recv_x.reshape(row_count, width_full)
    rows_g = recv_g.reshape(row_count, width_full)
    weight_p = recv_p.reshape(row_count, 1).astype(jnp.float32)
    gate_up = jnp.concatenate([w_gate[0], w_up[0]], 1)
    down_shard = w_down[0]
    both_rows = jnp.dot(rows_x, gate_up, preferred_element_type=jnp.float32)
    gate_rows = both_rows[:, :part_width]
    up_rows = both_rows[:, part_width:]
    sigmoid_gate = jax.nn.sigmoid(gate_rows)
    activated = gate_rows * sigmoid_gate
    hidden = activated * up_rows
    back_rows = lax.dot_general(
        rows_g, down_shard, (((1,), (1,)), ((), ())), preferred_element_type=jnp.float32
    )
    scores = lax.psum(jnp.sum(hidden * back_rows, axis=1), "tp")
    hidden_grad = weight_p * back_rows
    d_gate_rows = (
        hidden_grad * up_rows * sigmoid_gate * (1.0 + gate_rows * (1.0 - sigmoid_gate))
    ).astype(jnp.bfloat16)
    d_up_rows = (hidden_grad * activated).astype(jnp.bfloat16)
    d_both = jnp.concatenate([d_gate_rows, d_up_rows], 1)
    scaled = (weight_p * hidden).astype(jnp.bfloat16)
    grad_down = lax.dot_general(
        scaled, rows_g, (((0,), (0,)), ((), ())), preferred_element_type=jnp.float32
    )
    grad_both = lax.dot_general(
        rows_x, d_both, (((0,), (0,)), ((), ())), preferred_element_type=jnp.float32
    )
    grad_gate = grad_both[:, :part_width]
    grad_up = grad_both[:, part_width:]
    partial_low = lax.dot_general(
        d_both, gate_up, (((1,), (1,)), ((), ())), preferred_element_type=jnp.float32
    ).astype(jnp.bfloat16)
    home_s = lax.all_to_all(
        scores.reshape(owners, capacity), ("role", "ep"), split_axis=0, concat_axis=0, tiled=True
    )
    summed = lax.psum_scatter(
        partial_low.reshape(owners, capacity, width_full), "tp", scatter_dimension=2, tiled=True
    ).astype(jnp.float32)
    summed_low = summed.astype(jnp.bfloat16)
    home_x = lax.all_to_all(summed_low, ("role", "ep"), split_axis=0, concat_axis=0, tiled=True)
    slice_width = summed.shape[2]
    route_rows = home_x.reshape(row_count, slice_width).astype(jnp.float32)
    d_tok = (
        jnp.zeros((tok_rows + 1, slice_width), jnp.float32)
        .at[token_of_slot]
        .add(route_rows)[:tok_rows]
    )
    d_probs = home_s.reshape(-1)[target].reshape(tok_rows, top_count)
    return (
        d_tok.astype(jnp.bfloat16),
        d_probs,
        grad_gate.astype(jnp.bfloat16)[None],
        grad_up.astype(jnp.bfloat16)[None],
        grad_down.astype(jnp.bfloat16)[None],
    )


def slot_capacity(tok_rows, top_count, owners):
    return min(tok_rows, tok_rows * top_count * 9 // (8 * owners))


LOOSE = pl.BlockSpec(memory_space=pl.ANY)


def weights_kernel(tp_ref, wg_ref, wu_ref, wd_ref, both_ref, down_ref):
    part = wg_ref.shape[2]
    both_ref[:, :part] = wg_ref[0]
    both_ref[:, part:] = wu_ref[0]
    down_ref[...] = wd_ref[0]


def weights_call(which, w_gate, w_up, w_down):
    _, width, part = w_gate.shape
    half = width // 2

    def place(i, w):
        return (i + w[0]) % 2

    return pl.pallas_call(
        weights_kernel,
        grid_spec=pltpu.PrefetchScalarGridSpec(
            num_scalar_prefetch=1,
            grid=(2,),
            in_specs=[
                pl.BlockSpec((1, half, part), lambda i, w: (0, place(i, w), 0)),
                pl.BlockSpec((1, half, part), lambda i, w: (0, place(i, w), 0)),
                pl.BlockSpec((1, part, half), lambda i, w: (0, 0, place(i, w))),
            ],
            out_specs=[
                pl.BlockSpec((half, 2 * part), lambda i, w: (i, 0)),
                pl.BlockSpec((part, half), lambda i, w: (0, i)),
            ],
        ),
        out_shape=[
            jax.ShapeDtypeStruct((width, 2 * part), jnp.bfloat16),
            jax.ShapeDtypeStruct((part, width), jnp.bfloat16),
        ],
        compiler_params=pltpu.CompilerParams(vmem_limit_bytes=62 << 20),
        cost_estimate=pl.CostEstimate(flops=0, bytes_accessed=12 * width * part, transcendentals=0),
        name="weights",
    )(which, w_gate, w_up, w_down)


def rows_kernel(count, modes, capacity, slots, where_ref, *refs):
    weights_in, units_in = refs[:4], refs[4 : 4 + 4 * count]
    refs = refs[len(refs) - 17 - 2 * count :]
    outs, keeps, sends, refs = refs[:2], refs[2 : 2 + count], refs[2 + count : 2 + 2 * count], refs[2 + 2 * count :]
    x_all, g_all, tables, wgu0, wgu1, wd0, wd1, xc, gc, both, scaled, piece, unit_sems, weight_sems = refs[:14]
    out_sems = refs[14]
    half, tok = x_all.shape[3], x_all.shape[2] // 2
    part = scaled.shape[2]
    owners = tables.shape[2]
    wgu, wd = (wgu0, wgu1), (wd0, wd1)

    x_copies, g_copies, t_copies = [], [], []
    for index, unit in enumerate(units_in):
        chunk, y, x = index // 4, index // 2 % 2, index % 2
        rows = pl.ds(y * tok, tok)
        x_copies.append(pltpu.make_async_copy(unit.at[pl.ds(0, tok)], x_all.at[chunk, x, rows], unit_sems.at[0, index]))
        g_copies.append(pltpu.make_async_copy(unit.at[pl.ds(tok, tok)], g_all.at[chunk, x, rows], unit_sems.at[1, index]))
        if x == 0:
            table = unit.at[pl.ds(2 * tok, owners), pl.ds(0, tok)]
            t_copies.append(pltpu.make_async_copy(table, tables.at[chunk, y], unit_sems.at[2, index]))
    weight_copies = [
        pltpu.make_async_copy(source, target, weight_sems.at[index])
        for index, (source, target) in enumerate(zip(weights_in, (wgu0, wgu1, wd0, wd1)))
    ]
    for copy in t_copies + x_copies + weight_copies[:2] + g_copies + weight_copies[2:]:
        copy.start()
    leaving = []

    def leave(source, target):
        copy = pltpu.make_async_copy(source, target, out_sems.at[len(leaving)])
        copy.start()
        leaving.append(copy)

    def leave_rows(held, start):
        for expert in range(2):
            leave(held.at[expert], outs[expert].at[:, pl.ds(start, held.shape[2])])

    def dot(a, b, dims):
        return lax.dot_general(a, b, (dims, ((), ())), preferred_element_type=jnp.float32)

    for copy in t_copies:
        copy.wait()
    earlier = lax.broadcasted_iota(jnp.int32, (tok, tok), 0) < lax.broadcasted_iota(jnp.int32, (tok, tok), 1)
    earlier = earlier.astype(jnp.bfloat16)
    number = lax.broadcasted_iota(jnp.int32, (slots, tok), 0).astype(jnp.float32)
    names = lax.broadcasted_iota(jnp.int32, (owners, tok), 0)
    picks, low_picks, probs = {}, {}, {}
    for chunk in range(count):
        found = []
        for y in range(2):
            table = tables[chunk, y].astype(jnp.float32)
            rank = dot((table >= 0.0).astype(jnp.bfloat16), earlier, ((1,), (0,))) + float(y * capacity)
            found.append((table, jnp.where(table >= 0.0, rank, -1.0)))
        for expert in range(2):
            mine = names == where_ref[expert]
            halves, prob = [], None
            for table, rank in found:
                weight = jnp.sum(jnp.where(mine, table, 0.0), axis=0, keepdims=True)
                slot = jnp.sum(jnp.where(mine, rank, 0.0), axis=0, keepdims=True)
                halves.append((number == slot).astype(jnp.float32))
                term = jnp.sum(halves[-1] * weight, axis=1, keepdims=True)
                prob = term if prob is None else prob + term
            picks[chunk, expert] = halves
            low_picks[chunk, expert] = jnp.concatenate(halves, 1).astype(jnp.bfloat16)
            probs[chunk, expert] = prob
    spans = [pl.ds(chunk * slots, slots) for chunk in range(count)]
    sides = [slice(side * half, (side + 1) * half) for side in range(2)]

    def gather(copies, source, target):
        for chunk in range(count):
            for copy in copies[4 * chunk : 4 * chunk + 4]:
                copy.wait()
            both_picks = jnp.concatenate([low_picks[chunk, expert] for expert in range(2)], 0)
            for side in range(2):
                rows = dot(both_picks, source[chunk, side], ((1,), (0,))).astype(jnp.bfloat16)
                for expert in range(2):
                    target[expert, spans[chunk], sides[side]] = rows[expert * slots : (expert + 1) * slots]

    gather(x_copies, x_all, xc)
    leave_rows(xc, 0)
    rows = []
    for expert in range(2):
        weight_copies[expert].wait()
        rows.append(dot(xc[expert], wgu[expert][...], ((1,), (0,))))
    gather(g_copies, g_all, gc)
    leave_rows(gc, 2 * half)
    scores = []
    for expert in range(2):
        weight_copies[2 + expert].wait()
        back = dot(gc[expert], wd[expert][...], ((1,), (1,)))
        gate, up = rows[expert][:, :part], rows[expert][:, part:]
        sig = jax.nn.sigmoid(gate)
        act = gate * sig
        hidden = act * up
        scores.append(jnp.sum(hidden * back, axis=1, keepdims=True))
        prob = jnp.concatenate([probs[chunk, expert] for chunk in range(count)], 0)
        hgrad = prob * back
        both[expert, :, :part] = (hgrad * up * sig * (1.0 + gate * (1.0 - sig))).astype(jnp.bfloat16)
        both[expert, :, part:] = (hgrad * act).astype(jnp.bfloat16)
        scaled[expert] = (prob * hidden).astype(jnp.bfloat16)
    leave_rows(both, 4 * half)
    leave_rows(scaled, 4 * half + 2 * part)

    names = lax.broadcasted_iota(jnp.int32, (owners, half), 0)
    column = lax.broadcasted_iota(jnp.int32, (owners, half), 1) // (2 * tok)
    for chunk in range(count):
        for y in range(2):
            extra = jnp.zeros((owners, half), jnp.float32)
            for expert in range(2):
                part_scores = scores[expert][chunk * slots : (chunk + 1) * slots]
                line = jnp.sum(picks[chunk, expert][y] * part_scores, axis=0, keepdims=True)
                high = line.astype(jnp.bfloat16).astype(jnp.float32)
                line = jnp.concatenate([high, line - high] * (half // (2 * tok)), 1)
                extra = extra + jnp.where((names == where_ref[expert]) & (column == where_ref[2]), line, 0.0)
            for side in range(2):
                piece[chunk, side, y, tok:] = extra.astype(jnp.bfloat16)
    for side in (1, 0):
        low = [
            dot(both[expert], wgu[expert][sides[side], :], ((1,), (1,))).astype(jnp.bfloat16) for expert in range(2)
        ]
        for chunk in range(count):
            total = None
            for expert in range(2):
                term = dot(low_picks[chunk, expert], low[expert][chunk * slots : (chunk + 1) * slots], ((0,), (0,)))
                total = term if total is None else total + term
            for y in range(2):
                piece[chunk, side, y, :tok] = total[y * tok : (y + 1) * tok].astype(jnp.bfloat16)
                first, second = (y, side) if modes[chunk] else (side, y)
                leave(piece.at[chunk, side, y], (sends if first else keeps)[chunk].at[second])
    for copy in leaving:
        copy.wait()


def rows_call(modes, owners, capacity, slots, where, weights, units, after):
    count = len(modes)
    tok, half = (units[0].shape[0] - owners) // 2, units[0].shape[1]
    part, width = weights[2].shape
    widths = (width, width, 2 * part, part)
    packet = (2, tok + owners, half)
    return pl.pallas_call(
        functools.partial(rows_kernel, count, modes, capacity, slots),
        grid_spec=pltpu.PrefetchScalarGridSpec(
            num_scalar_prefetch=1,
            grid=(1,),
            in_specs=[LOOSE] * (4 + len(units) + len(after)),
            out_specs=[LOOSE] * (2 + 2 * count),
            scratch_shapes=[pltpu.VMEM((count, 2, 2 * tok, half), jnp.bfloat16)] * 2
            + [pltpu.VMEM((count, 2, owners, tok), jnp.bfloat16)]
            + [pltpu.VMEM((width, 2 * part), jnp.bfloat16)] * 2
            + [pltpu.VMEM((part, width), jnp.bfloat16)] * 2
            + [pltpu.VMEM((2, count * slots, size), jnp.bfloat16) for size in widths]
            + [
                pltpu.VMEM((count, 2) + packet, jnp.bfloat16),
                pltpu.SemaphoreType.DMA((3, 4 * count)),
                pltpu.SemaphoreType.DMA((4,)),
                pltpu.SemaphoreType.DMA((8 + 4 * count,)),
            ],
        ),
        out_shape=[jax.ShapeDtypeStruct((count * slots, sum(widths)), jnp.bfloat16)] * 2
        + [jax.ShapeDtypeStruct(packet, jnp.bfloat16)] * (2 * count),
        compiler_params=pltpu.CompilerParams(vmem_limit_bytes=62 << 20),
        cost_estimate=pl.CostEstimate(
            flops=count * (20 * slots * width * part + 24 * slots * tok * width),
            bytes_accessed=count * 16 * tok * width + 12 * width * part,
            transcendentals=2 * count * slots * part,
        ),
        name="rows",
    )(where, *weights, *units, *after)


def grads_kernel(count, wide, deep, blocks, tp_ref, *refs):
    sources, outs = refs[:count], refs[count:-4]
    wide_all, deep_all, wide_sems, deep_sems = refs[-4:]
    rows = sources[0].shape[0]
    size = wide_all.shape[2]
    block = pl.program_id(0)

    def copies(column):
        return [
            pltpu.make_async_copy(
                source.at[:, pl.ds(wide + column * size, size)],
                wide_all.at[column, pl.ds(index * rows, rows)],
                wide_sems.at[column, index],
            )
            for index, source in enumerate(sources)
        ]

    @pl.when(block == 0)
    def _():
        deep_copies = [
            pltpu.make_async_copy(
                source.at[:, pl.ds(deep, deep_all.shape[1])], deep_all.at[pl.ds(index * rows, rows)], deep_sems.at[index]
            )
            for index, source in enumerate(sources)
        ]
        for copy in deep_copies:
            copy.start()
        for column in range(blocks):
            for copy in copies(column):
                copy.start()
        for copy in deep_copies:
            copy.wait()

    for column in range(blocks):

        @pl.when(block == column)
        def _(column=column):
            for copy in copies(column):
                copy.wait()

    dims = (((0,), (0,)), ((), ()))
    if len(outs) == 2:
        part = outs[0].shape[2]
        both = lax.dot_general(wide_all[block], deep_all[...], dims, preferred_element_type=jnp.float32)
        outs[0][0] = both[:, :part].astype(jnp.bfloat16)
        outs[1][0] = both[:, part:].astype(jnp.bfloat16)
    else:
        down = lax.dot_general(deep_all[...], wide_all[block], dims, preferred_element_type=jnp.float32)
        outs[0][0] = down.astype(jnp.bfloat16)


def grads_call(which, packed, width, part, down):
    rows, count = packed[0].shape[0], len(packed)
    step = math.gcd(width // 2, 512)
    per = width // 2 // step
    deep = part if down else 2 * part

    def place(i, w):
        return (i + w[0] * per) % (2 * per)

    if down:
        specs = [pl.BlockSpec((1, part, step), lambda i, w: (0, 0, place(i, w)))]
        shapes = [(1, part, width)]
    else:
        specs = [pl.BlockSpec((1, step, part), lambda i, w: (0, place(i, w), 0))] * 2
        shapes = [(1, width, part)] * 2
    starts = (width, 2 * width + 2 * part) if down else (0, 2 * width)
    return pl.pallas_call(
        functools.partial(grads_kernel, count, *starts, 2 * per),
        grid_spec=pltpu.PrefetchScalarGridSpec(
            num_scalar_prefetch=1,
            grid=(2 * per,),
            in_specs=[LOOSE] * count,
            out_specs=specs,
            scratch_shapes=[
                pltpu.VMEM((2 * per, count * rows, step), jnp.bfloat16),
                pltpu.VMEM((count * rows, deep), jnp.bfloat16),
                pltpu.SemaphoreType.DMA((2 * per, count)),
                pltpu.SemaphoreType.DMA((count,)),
            ],
        ),
        out_shape=[jax.ShapeDtypeStruct(shape, jnp.bfloat16) for shape in shapes],
        compiler_params=pltpu.CompilerParams(vmem_limit_bytes=24 << 20),
        cost_estimate=pl.CostEstimate(
            flops=2 * count * rows * width * deep, bytes_accessed=2 * count * rows * (width + deep), transcendentals=0
        ),
        name="grads",
    )(which, *packed)


def dense_device(tokens, out_grad, routes, probs, w_gate, w_up, w_down):
    owners = lax.axis_size(("role", "ep"))
    ep = lax.axis_size("ep")
    n_y = 2
    n_z = ep // n_y
    tok_rows, half = tokens.shape
    capacity = slot_capacity(tok_rows, routes.shape[1], owners)
    slots = -(-n_y * capacity // 16) * 16
    role, place, which = lax.axis_index("role"), lax.axis_index("ep"), lax.axis_index("tp")

    def over_x(array):
        return lax.ppermute(array, "tp", [(0, 1), (1, 0)])

    def over_role(array):
        return lax.ppermute(array, "role", [(0, 1), (1, 0)])

    def over_y(array):
        return lax.ppermute(array, "ep", [(i, i + 1 - 2 * (i % n_y)) for i in range(ep)])

    def over_z(array, shift):
        return lax.ppermute(array, "ep", [(i, (i + shift * n_y) % ep) for i in range(ep)])

    def tied(values, others):
        return lax.optimization_barrier((list(values), list(others)))[0]

    chosen = routes[:, :, None] == jnp.arange(owners, dtype=jnp.int32)
    table = jnp.sum(jnp.where(chosen, probs[:, :, None].astype(jnp.float32) + 1.0, 0.0), axis=1) - 1.0
    table = jnp.pad(table.astype(jnp.bfloat16).T, ((0, 0), (0, half - tok_rows)))
    last = n_z - 1
    routes_in = []
    for z in range(n_z):
        shift = -1 if z == last and z > 1 else 1
        if z:
            routes_in.append(((z, 0, 0), (0 if z in (1, last) else z - 1, 0, 0), functools.partial(over_z, shift=shift)))
        routes_in.append(((z, 1, 0), (z, 0, 0), over_y))
        routes_in.append(((z, 0, 1), (z, 0, 0), over_x))
        if z == 0:
            routes_in.append(((z, 1, 1), (z, 1, 0), over_x))
        elif z in (1, last):
            routes_in.append(((z, 1, 1), (0, 1, 1), functools.partial(over_z, shift=shift)))
        else:
            routes_in.append(((z, 1, 1), (z, 0, 1), over_y))
    routes_in.sort(key=lambda item: (item[0][0] % 2 if item[2] in (over_x, over_y) else 0, sum(item[0][1:])))

    rounds, waiting, there = [], list(routes_in), {(0, 0, 0)}
    while waiting:
        moves = {}
        for item in waiting:
            axis = item[2] if item[2] in (over_x, over_y) else over_z
            if item[1] in there and axis not in moves:
                moves[axis] = item
        rounds.append(list(moves.values()))
        there |= {item[0] for item in rounds[-1]}
        waiting = [item for item in waiting if item[0] not in there]

    which_ref = which.reshape(1).astype(jnp.int32)
    both_w, down_w = weights_call(which_ref, w_gate, w_up, w_down)
    units = {(0, 0, 0): jnp.concatenate([tokens, out_grad, table], 0)}
    settled, extra, weights = dict(units), [both_w, down_w], ()
    for moves in rounds:
        arrived = {target: move(settled[source]) for target, source, move in moves}
        units.update(arrived)
        settled.update(arrived)
        names = list(settled)
        settled = dict(zip(names, tied([settled[item] for item in names], extra)))
        if extra:
            both_w, down_w = tied(extra, arrived.values())
            weights, extra = (both_w, over_role(both_w), down_w, over_role(down_w)), []

    where = jnp.stack([role * ep + place, (1 - role) * ep + place, which]).astype(jnp.int32)

    def add(a, b):
        return a.astype(jnp.float32) + b.astype(jnp.float32)

    width, part = both_w.shape[0], down_w.shape[0]
    packed, flown, homeward, done = [], [], [], []
    for turn, group in enumerate((range(0, n_z, 2), range(1, n_z, 2))):
        modes = [index % 2 for index in range(len(group))]
        four = [units[z, y, x] for z in group for y in range(2) for x in range(2)]
        mine, other, *packets = rows_call(modes, owners, capacity, slots, where, weights, four, packed[:1])
        keeps, sends = packets[: len(group)], packets[len(group) :]
        if turn:
            mine, other, *sends = tied([mine, other] + sends, flown[0])
        packed += [mine, over_role(other)]
        firsts = [over_y(send) if mode else over_x(send) for mode, send in zip(modes, sends)]
        if turn:
            done += grads_call(which_ref, packed, width, part, False)
            firsts = tied(firsts, flown[1] + done)
        sends = [add(keep[1], first[1]).astype(jnp.bfloat16) for keep, first in zip(keeps, firsts)]
        seconds = [over_x(send) if mode else over_y(send) for mode, send in zip(modes, sends)]
        if turn:
            done += grads_call(which_ref, packed, width, part, True)
            seconds = tied(seconds, homeward[1:] + done)
        totals = [add(add(keep[0], first[0]), second) for keep, first, second in zip(keeps, firsts, seconds)]
        sends = [total.astype(jnp.bfloat16) for total in totals]
        thirds = [over_z(send, -z) if z else total for z, send, total in zip(group, sends, totals)]
        homeward += thirds
        flown += [firsts, seconds]
    home = sum(item.astype(jnp.float32) for item in homeward)
    d_tok = home[:tok_rows].astype(jnp.bfloat16)
    d_gate, d_up, d_down = done
    score = jnp.sum(home[tok_rows:, : 4 * tok_rows].reshape(owners, 4, tok_rows), axis=1).T
    d_probs = jnp.sum(jnp.where(chosen, score[:, None, :], 0.0), axis=2)
    return d_tok, d_probs, d_gate, d_up, d_down


def per_device(tokens, out_grad, routes, probs, w_gate, w_up, w_down):
    owners = lax.axis_size(("role", "ep"))
    tok_rows, top_count = routes.shape
    paired = lax.axis_size("tp") == 2 and lax.axis_size("role") == 2 and lax.axis_size("ep") % 4 == 0
    if paired and 2 * slot_capacity(tok_rows, top_count, owners) >= tok_rows:
        return dense_device(tokens, out_grad, routes, probs, w_gate, w_up, w_down)
    return routed_device(tokens, out_grad, routes, probs, w_gate, w_up, w_down)


def solution(mesh):
    in_specs = (
        P(("groups", "role", "ep"), "tp"),
        P(("groups", "role", "ep"), "tp"),
        P(("groups", "role", "ep"), None),
        P(("groups", "role", "ep"), None),
        P(("role", "ep"), None, "tp"),
        P(("role", "ep"), None, "tp"),
        P(("role", "ep"), "tp", None),
    )
    out_specs = (
        P(("groups", "role", "ep"), "tp"),
        P(("groups", "role", "ep"), None),
        P(("groups", "role", "ep"), None, "tp"),
        P(("groups", "role", "ep"), None, "tp"),
        P(("groups", "role", "ep"), "tp", None),
    )
    return jax.shard_map(
        per_device, mesh=mesh, in_specs=in_specs, out_specs=out_specs, check_vma=False
    )
```

```python
import functools
import math

import jax
import jax.numpy as jnp
from jax import lax
from jax.experimental import pallas as pl
from jax.experimental.pallas import tpu as pltpu
from jax.sharding import PartitionSpec as P


def pad_rows(array):
    return jnp.concatenate([array, jnp.zeros((1, array.shape[1]), array.dtype)], 0)


def routed_device(tokens, out_grad, routes, probs, w_gate, w_up, w_down):
    owners = lax.axis_size(("role", "ep"))
    tok_rows, top_count = routes.shape
    width_full = w_gate.shape[1]
    part_width = w_gate.shape[2]
    capacity = min(tok_rows, tok_rows * top_count * 9 // (8 * owners))
    entry_total = tok_rows * top_count
    routes_flat = routes.reshape(-1)
    onehot = (routes_flat[:, None] == jnp.arange(owners, dtype=jnp.int32)[None, :]).astype(
        jnp.int32
    )
    before = jnp.cumsum(onehot, axis=0) - onehot
    slot_index = jnp.sum(before * onehot, axis=1)
    target = routes_flat * capacity + slot_index
    row_count = owners * capacity
    entry_of_slot = (
        jnp.full((row_count,), entry_total, jnp.int32)
        .at[target]
        .set(jnp.arange(entry_total, dtype=jnp.int32))
    )
    token_of_slot = entry_of_slot // top_count
    padded_prob = jnp.concatenate([probs.reshape(-1), jnp.zeros((1,), probs.dtype)], 0)
    send_prob = padded_prob[entry_of_slot].reshape(owners, capacity)
    send_x = pad_rows(tokens)[token_of_slot]
    send_g = pad_rows(out_grad)[token_of_slot]
    slice_x, slice_g, recv_p = (
        lax.all_to_all(
            send_x.reshape(owners, capacity, tokens.shape[1]),
            ("role", "ep"),
            split_axis=0,
            concat_axis=0,
            tiled=True,
        ),
        lax.all_to_all(
            send_g.reshape(owners, capacity, tokens.shape[1]),
            ("role", "ep"),
            split_axis=0,
            concat_axis=0,
            tiled=True,
        ),
        lax.all_to_all(send_prob, ("role", "ep"), split_axis=0, concat_axis=0, tiled=True),
    )
    recv_x, recv_g = (
        lax.all_gather(slice_x, "tp", axis=2, tiled=True),
        lax.all_gather(slice_g, "tp", axis=2, tiled=True),
    )
    rows_x = recv_x.reshape(row_count, width_full)
    rows_g = recv_g.reshape(row_count, width_full)
    weight_p = recv_p.reshape(row_count, 1).astype(jnp.float32)
    gate_up = jnp.concatenate([w_gate[0], w_up[0]], 1)
    down_shard = w_down[0]
    both_rows = jnp.dot(rows_x, gate_up, preferred_element_type=jnp.float32)
    gate_rows = both_rows[:, :part_width]
    up_rows = both_rows[:, part_width:]
    sigmoid_gate = jax.nn.sigmoid(gate_rows)
    activated = gate_rows * sigmoid_gate
    hidden = activated * up_rows
    back_rows = lax.dot_general(
        rows_g, down_shard, (((1,), (1,)), ((), ())), preferred_element_type=jnp.float32
    )
    scores = lax.psum(jnp.sum(hidden * back_rows, axis=1), "tp")
    hidden_grad = weight_p * back_rows
    d_gate_rows = (
        hidden_grad * up_rows * sigmoid_gate * (1.0 + gate_rows * (1.0 - sigmoid_gate))
    ).astype(jnp.bfloat16)
    d_up_rows = (hidden_grad * activated).astype(jnp.bfloat16)
    d_both = jnp.concatenate([d_gate_rows, d_up_rows], 1)
    scaled = (weight_p * hidden).astype(jnp.bfloat16)
    grad_down = lax.dot_general(
        scaled, rows_g, (((0,), (0,)), ((), ())), preferred_element_type=jnp.float32
    )
    grad_both = lax.dot_general(
        rows_x, d_both, (((0,), (0,)), ((), ())), preferred_element_type=jnp.float32
    )
    grad_gate = grad_both[:, :part_width]
    grad_up = grad_both[:, part_width:]
    partial_low = lax.dot_general(
        d_both, gate_up, (((1,), (1,)), ((), ())), preferred_element_type=jnp.float32
    ).astype(jnp.bfloat16)
    home_s = lax.all_to_all(
        scores.reshape(owners, capacity), ("role", "ep"), split_axis=0, concat_axis=0, tiled=True
    )
    summed = lax.psum_scatter(
        partial_low.reshape(owners, capacity, width_full), "tp", scatter_dimension=2, tiled=True
    ).astype(jnp.float32)
    summed_low = summed.astype(jnp.bfloat16)
    home_x = lax.all_to_all(summed_low, ("role", "ep"), split_axis=0, concat_axis=0, tiled=True)
    slice_width = summed.shape[2]
    route_rows = home_x.reshape(row_count, slice_width).astype(jnp.float32)
    d_tok = (
        jnp.zeros((tok_rows + 1, slice_width), jnp.float32)
        .at[token_of_slot]
        .add(route_rows)[:tok_rows]
    )
    d_probs = home_s.reshape(-1)[target].reshape(tok_rows, top_count)
    return (
        d_tok.astype(jnp.bfloat16),
        d_probs,
        grad_gate.astype(jnp.bfloat16)[None],
        grad_up.astype(jnp.bfloat16)[None],
        grad_down.astype(jnp.bfloat16)[None],
    )


def slot_capacity(tok_rows, top_count, owners):
    return min(tok_rows, tok_rows * top_count * 9 // (8 * owners))


LOOSE = pl.BlockSpec(memory_space=pl.ANY)


def weights_kernel(tp_ref, wg_ref, wu_ref, wd_ref, both_ref, down_ref):
    part = wg_ref.shape[2]
    both_ref[:, :part] = wg_ref[0]
    both_ref[:, part:] = wu_ref[0]
    down_ref[...] = wd_ref[0]


def weights_call(which, w_gate, w_up, w_down):
    _, width, part = w_gate.shape
    half = width // 2

    def place(i, w):
        return (i + w[0]) % 2

    return pl.pallas_call(
        weights_kernel,
        grid_spec=pltpu.PrefetchScalarGridSpec(
            num_scalar_prefetch=1,
            grid=(2,),
            in_specs=[
                pl.BlockSpec((1, half, part), lambda i, w: (0, place(i, w), 0)),
                pl.BlockSpec((1, half, part), lambda i, w: (0, place(i, w), 0)),
                pl.BlockSpec((1, part, half), lambda i, w: (0, 0, place(i, w))),
            ],
            out_specs=[
                pl.BlockSpec((half, 2 * part), lambda i, w: (i, 0)),
                pl.BlockSpec((part, half), lambda i, w: (0, i)),
            ],
        ),
        out_shape=[
            jax.ShapeDtypeStruct((width, 2 * part), jnp.bfloat16),
            jax.ShapeDtypeStruct((part, width), jnp.bfloat16),
        ],
        compiler_params=pltpu.CompilerParams(vmem_limit_bytes=62 << 20),
        cost_estimate=pl.CostEstimate(flops=0, bytes_accessed=12 * width * part, transcendentals=0),
        name="weights",
    )(which, w_gate, w_up, w_down)


def rows_kernel(count, ways, capacity, slots, where_ref, *refs):
    weights_in, units_in, tables_in = refs[:4], refs[4 : 4 + 4 * count], refs[4 + 4 * count : 4 + 5 * count]
    leaves = 1 + max(way[0] for way in ways.values())
    refs = refs[len(refs) - 17 - leaves :]
    outs, packets, refs = refs[:2], refs[2 : 2 + leaves], refs[2 + leaves :]
    x_all, g_all, tables, wgu0, wgu1, wd0, wd1, xc, gc, both, scaled, piece, unit_sems, weight_sems = refs[:14]
    out_sems = refs[14]
    half, tok = x_all.shape[3], x_all.shape[2] // 2
    part = scaled.shape[2]
    owners = tables.shape[2]
    wgu, wd = (wgu0, wgu1), (wd0, wd1)

    x_copies, g_copies = [], []
    for index, unit in enumerate(units_in):
        chunk, y, x = index // 4, index // 2 % 2, index % 2
        rows = pl.ds(y * tok, tok)
        x_copies.append(pltpu.make_async_copy(unit.at[pl.ds(0, tok)], x_all.at[chunk, x, rows], unit_sems.at[0, index]))
        g_copies.append(pltpu.make_async_copy(unit.at[pl.ds(tok, tok)], g_all.at[chunk, x, rows], unit_sems.at[1, index]))
    t_copies = [
        pltpu.make_async_copy(table, tables.at[chunk], unit_sems.at[2, chunk]) for chunk, table in enumerate(tables_in)
    ]
    weight_copies = [
        pltpu.make_async_copy(source, target, weight_sems.at[index])
        for index, (source, target) in enumerate(zip(weights_in, (wgu0, wgu1, wd0, wd1)))
    ]
    for copy in t_copies + x_copies + weight_copies[:2] + g_copies + weight_copies[2:]:
        copy.start()
    leaving = []

    def leave(source, target):
        copy = pltpu.make_async_copy(source, target, out_sems.at[len(leaving)])
        copy.start()
        leaving.append(copy)

    def leave_rows(held, start):
        for expert in range(2):
            leave(held.at[expert], outs[expert].at[:, pl.ds(start, held.shape[2])])

    def dot(a, b, dims):
        return lax.dot_general(a, b, (dims, ((), ())), preferred_element_type=jnp.float32)

    for copy in t_copies:
        copy.wait()
    earlier = lax.broadcasted_iota(jnp.int32, (tok, tok), 0) < lax.broadcasted_iota(jnp.int32, (tok, tok), 1)
    earlier = earlier.astype(jnp.bfloat16)
    number = lax.broadcasted_iota(jnp.int32, (slots, tok), 0).astype(jnp.float32)
    names = lax.broadcasted_iota(jnp.int32, (owners, tok), 0)
    picks, low_picks, probs = {}, {}, {}
    for chunk in range(count):
        found = []
        for y in range(2):
            table = tables[chunk, y].astype(jnp.float32)
            rank = dot((table >= 0.0).astype(jnp.bfloat16), earlier, ((1,), (0,))) + float(y * capacity)
            found.append((table, jnp.where(table >= 0.0, rank, -1.0)))
        for expert in range(2):
            mine = names == where_ref[expert]
            halves, prob = [], None
            for table, rank in found:
                weight = jnp.sum(jnp.where(mine, table, 0.0), axis=0, keepdims=True)
                slot = jnp.sum(jnp.where(mine, rank, 0.0), axis=0, keepdims=True)
                halves.append((number == slot).astype(jnp.float32))
                term = jnp.sum(halves[-1] * weight, axis=1, keepdims=True)
                prob = term if prob is None else prob + term
            picks[chunk, expert] = halves
            low_picks[chunk, expert] = jnp.concatenate(halves, 1).astype(jnp.bfloat16)
            probs[chunk, expert] = prob
    spans = [pl.ds(chunk * slots, slots) for chunk in range(count)]
    sides = [slice(side * half, (side + 1) * half) for side in range(2)]

    def gather(copies, source, target):
        for chunk in range(count):
            for copy in copies[4 * chunk : 4 * chunk + 4]:
                copy.wait()
            both_picks = jnp.concatenate([low_picks[chunk, expert] for expert in range(2)], 0)
            for side in range(2):
                rows = dot(both_picks, source[chunk, side], ((1,), (0,))).astype(jnp.bfloat16)
                for expert in range(2):
                    target[expert, spans[chunk], sides[side]] = rows[expert * slots : (expert + 1) * slots]

    gather(x_copies, x_all, xc)
    leave_rows(xc, 0)
    rows = []
    for expert in range(2):
        weight_copies[expert].wait()
        rows.append(dot(xc[expert], wgu[expert][...], ((1,), (0,))))
    gather(g_copies, g_all, gc)
    leave_rows(gc, 2 * half)
    scores = []
    for expert in range(2):
        weight_copies[2 + expert].wait()
        back = dot(gc[expert], wd[expert][...], ((1,), (1,)))
        gate, up = rows[expert][:, :part], rows[expert][:, part:]
        sig = jax.nn.sigmoid(gate)
        act = gate * sig
        hidden = act * up
        scores.append(jnp.sum(hidden * back, axis=1, keepdims=True))
        prob = jnp.concatenate([probs[chunk, expert] for chunk in range(count)], 0)
        hgrad = prob * back
        both[expert, :, :part] = (hgrad * up * sig * (1.0 + gate * (1.0 - sig))).astype(jnp.bfloat16)
        both[expert, :, part:] = (hgrad * act).astype(jnp.bfloat16)
        scaled[expert] = (prob * hidden).astype(jnp.bfloat16)
    leave_rows(both, 4 * half)
    leave_rows(scaled, 4 * half + 2 * part)

    names = lax.broadcasted_iota(jnp.int32, (owners, half), 0)
    column = lax.broadcasted_iota(jnp.int32, (owners, half), 1) // (2 * tok)
    for chunk in range(count):
        for y in range(2):
            extra = jnp.zeros((owners, half), jnp.float32)
            for expert in range(2):
                part_scores = scores[expert][chunk * slots : (chunk + 1) * slots]
                line = jnp.sum(picks[chunk, expert][y] * part_scores, axis=0, keepdims=True)
                high = line.astype(jnp.bfloat16).astype(jnp.float32)
                line = jnp.concatenate([high, line - high] * (half // (2 * tok)), 1)
                extra = extra + jnp.where((names == where_ref[expert]) & (column == where_ref[2]), line, 0.0)
            for side in range(2):
                piece[chunk, side, y, tok:] = extra.astype(jnp.bfloat16)
    for side in (1, 0):
        low = [
            dot(both[expert], wgu[expert][sides[side], :], ((1,), (1,))).astype(jnp.bfloat16) for expert in range(2)
        ]
        for chunk in range(count):
            total = None
            for expert in range(2):
                term = dot(low_picks[chunk, expert], low[expert][chunk * slots : (chunk + 1) * slots], ((0,), (0,)))
                total = term if total is None else total + term
            for y in range(2):
                piece[chunk, side, y, :tok] = total[y * tok : (y + 1) * tok].astype(jnp.bfloat16)
                number, slot = ways[chunk, y, side]
                leave(piece.at[chunk, side, y], packets[number].at[slot])
    for copy in leaving:
        copy.wait()


def rows_call(items, owners, capacity, slots, where, weights, units, tables, after):
    count = len(tables)
    ways = {block: (number, slot) for number, blocks in enumerate(items) for slot, block in enumerate(blocks)}
    tok, half = units[0].shape[0] // 2, units[0].shape[1]
    part, width = weights[2].shape
    widths = (width, width, 2 * part, part)
    packet = (tok + owners, half)
    return pl.pallas_call(
        functools.partial(rows_kernel, count, ways, capacity, slots),
        grid_spec=pltpu.PrefetchScalarGridSpec(
            num_scalar_prefetch=1,
            grid=(1,),
            in_specs=[LOOSE] * (4 + 5 * count + len(after)),
            out_specs=[LOOSE] * (2 + len(items)),
            scratch_shapes=[pltpu.VMEM((count, 2, 2 * tok, half), jnp.bfloat16)] * 2
            + [pltpu.VMEM((count, 2, owners, tok), jnp.bfloat16)]
            + [pltpu.VMEM((width, 2 * part), jnp.bfloat16)] * 2
            + [pltpu.VMEM((part, width), jnp.bfloat16)] * 2
            + [pltpu.VMEM((2, count * slots, size), jnp.bfloat16) for size in widths]
            + [
                pltpu.VMEM((count, 2, 2) + packet, jnp.bfloat16),
                pltpu.SemaphoreType.DMA((3, 4 * count)),
                pltpu.SemaphoreType.DMA((4,)),
                pltpu.SemaphoreType.DMA((8 + 4 * count,)),
            ],
        ),
        out_shape=[jax.ShapeDtypeStruct((count * slots, sum(widths)), jnp.bfloat16)] * 2
        + [jax.ShapeDtypeStruct((len(blocks),) + packet, jnp.bfloat16) for blocks in items],
        compiler_params=pltpu.CompilerParams(vmem_limit_bytes=62 << 20),
        cost_estimate=pl.CostEstimate(
            flops=count * (20 * slots * width * part + 24 * slots * tok * width),
            bytes_accessed=count * 16 * tok * width + 12 * width * part,
            transcendentals=2 * count * slots * part,
        ),
        name="rows",
    )(where, *weights, *units, *tables, *after)


def grads_kernel(count, wide, deep, blocks, tp_ref, *refs):
    sources, outs = refs[:count], refs[count:-4]
    wide_all, deep_all, wide_sems, deep_sems = refs[-4:]
    starts = [sum(source.shape[0] for source in sources[:index]) for index in range(count)]
    size = wide_all.shape[2]
    block = pl.program_id(0)

    def copies(column):
        return [
            pltpu.make_async_copy(
                source.at[:, pl.ds(wide + column * size, size)],
                wide_all.at[column, pl.ds(starts[index], source.shape[0])],
                wide_sems.at[column, index],
            )
            for index, source in enumerate(sources)
        ]

    @pl.when(block == 0)
    def _():
        deep_copies = [
            pltpu.make_async_copy(
                source.at[:, pl.ds(deep, deep_all.shape[1])],
                deep_all.at[pl.ds(starts[index], source.shape[0])],
                deep_sems.at[index],
            )
            for index, source in enumerate(sources)
        ]
        for copy in deep_copies:
            copy.start()
        for column in range(blocks):
            for copy in copies(column):
                copy.start()
        for copy in deep_copies:
            copy.wait()

    for column in range(blocks):

        @pl.when(block == column)
        def _(column=column):
            for copy in copies(column):
                copy.wait()

    dims = (((0,), (0,)), ((), ()))
    if len(outs) == 2:
        part = outs[0].shape[2]
        both = lax.dot_general(wide_all[block], deep_all[...], dims, preferred_element_type=jnp.float32)
        outs[0][0] = both[:, :part].astype(jnp.bfloat16)
        outs[1][0] = both[:, part:].astype(jnp.bfloat16)
    else:
        down = lax.dot_general(deep_all[...], wide_all[block], dims, preferred_element_type=jnp.float32)
        outs[0][0] = down.astype(jnp.bfloat16)


def grads_call(which, packed, width, part, down):
    rows, count = sum(item.shape[0] for item in packed), len(packed)
    step = math.gcd(width // 2, 512)
    per = width // 2 // step
    deep = part if down else 2 * part

    def place(i, w):
        return (i + w[0] * per) % (2 * per)

    if down:
        specs = [pl.BlockSpec((1, part, step), lambda i, w: (0, 0, place(i, w)))]
        shapes = [(1, part, width)]
    else:
        specs = [pl.BlockSpec((1, step, part), lambda i, w: (0, place(i, w), 0))] * 2
        shapes = [(1, width, part)] * 2
    starts = (width, 2 * width + 2 * part) if down else (0, 2 * width)
    return pl.pallas_call(
        functools.partial(grads_kernel, count, *starts, 2 * per),
        grid_spec=pltpu.PrefetchScalarGridSpec(
            num_scalar_prefetch=1,
            grid=(2 * per,),
            in_specs=[LOOSE] * count,
            out_specs=specs,
            scratch_shapes=[
                pltpu.VMEM((2 * per, rows, step), jnp.bfloat16),
                pltpu.VMEM((rows, deep), jnp.bfloat16),
                pltpu.SemaphoreType.DMA((2 * per, count)),
                pltpu.SemaphoreType.DMA((count,)),
            ],
        ),
        out_shape=[jax.ShapeDtypeStruct(shape, jnp.bfloat16) for shape in shapes],
        compiler_params=pltpu.CompilerParams(vmem_limit_bytes=24 << 20),
        cost_estimate=pl.CostEstimate(
            flops=2 * rows * width * deep, bytes_accessed=2 * rows * (width + deep), transcendentals=0
        ),
        name="grads",
    )(which, *packed)


def dense_device(tokens, out_grad, routes, probs, w_gate, w_up, w_down):
    owners = lax.axis_size(("role", "ep"))
    ep = lax.axis_size("ep")
    n_y = 2
    n_z = ep // n_y
    tok_rows, half = tokens.shape
    capacity = slot_capacity(tok_rows, routes.shape[1], owners)
    slots = -(-n_y * capacity // 16) * 16
    role, place, which = lax.axis_index("role"), lax.axis_index("ep"), lax.axis_index("tp")

    def over_x(array):
        return lax.ppermute(array, "tp", [(0, 1), (1, 0)])

    def over_role(array):
        return lax.ppermute(array, "role", [(0, 1), (1, 0)])

    def over_y(array):
        return lax.ppermute(array, "ep", [(i, i + 1 - 2 * (i % n_y)) for i in range(ep)])

    def over_z(array, shift):
        return lax.ppermute(array, "ep", [(i, (i + shift * n_y) % ep) for i in range(ep)])

    def tied(values, others):
        return lax.optimization_barrier((list(values), list(others)))[0]

    last = n_z - 1
    routes_in = []
    for z in range(n_z):
        shift = -1 if z == last and z > 1 else 1
        if z:
            routes_in.append(((z, 0, 0), (0 if z in (1, last) else z - 1, 0, 0), functools.partial(over_z, shift=shift)))
        routes_in.append(((z, 1, 0), (z, 0, 0), over_y))
        routes_in.append(((z, 0, 1), (z, 0, 0), over_x))
        if z == 0:
            routes_in.append(((z, 1, 1), (z, 1, 0), over_x))
        elif z in (1, last):
            routes_in.append(((z, 1, 1), (0, 1, 1), functools.partial(over_z, shift=shift)))
        else:
            routes_in.append(((z, 1, 1), (z, 0, 1), over_y))
    routes_in.sort(key=lambda item: (item[0][0] % 2 if item[2] in (over_x, over_y) else 0, sum(item[0][1:])))

    rounds, waiting, there = [], list(routes_in), {(0, 0, 0)}
    while waiting:
        moves = {}
        for item in waiting:
            axis = item[2] if item[2] in (over_x, over_y) else over_z
            if item[1] in there and axis not in moves:
                moves[axis] = item
        rounds.append(list(moves.values()))
        there |= {item[0] for item in rounds[-1]}
        waiting = [item for item in waiting if item[0] not in there]

    which_ref = which.reshape(1).astype(jnp.int32)
    where = jnp.stack([role * ep + place, (1 - role) * ep + place, which]).astype(jnp.int32)
    both_w, down_w = weights_call(which_ref, w_gate, w_up, w_down)
    width, part = both_w.shape[0], down_w.shape[0]

    def rows_of(steps, items, after):
        four = [units[z, y, x] for z in steps for y in range(2) for x in range(2)]
        return rows_call(items, owners, capacity, slots, where, weights, four, [tables[z] for z in steps], after)

    units = {(0, 0, 0): jnp.concatenate([tokens, out_grad], 0)}
    settled = dict(units)
    for number, moves in enumerate(rounds):
        arrived = {target: move(settled[source]) for target, source, move in moves}
        units.update(arrived)
        settled.update(arrived)
        extra = []
        if number == 0:
            extra = [both_w, down_w]
            both_w, down_w, routes, probs = tied([both_w, down_w, routes, probs], arrived.values())
            weights = (both_w, over_role(both_w), down_w, over_role(down_w))
            chosen = routes[:, :, None] == jnp.arange(owners, dtype=jnp.int32)
            table = jnp.sum(jnp.where(chosen, probs[:, :, None].astype(jnp.float32) + 1.0, 0.0), axis=1) - 1.0
            table = table.astype(jnp.bfloat16).T
            table = jnp.stack([table, over_y(table)])
        if number == 1:
            (table,) = tied([table], arrived.values())
            tables = [over_z(table, z) if z else table for z in range(n_z)]
        if number == 2:
            mine_0, other_0, near, side_0, far, y_0 = rows_of(
                [0], [[(0, 0, 0)], [(0, 0, 1)], [(0, 1, 1)], [(0, 1, 0)]], []
            )
            extra = [mine_0]
        names = list(settled)
        settled = dict(zip(names, tied([settled[item] for item in names], extra)))

    def total(*blocks):
        return sum(block.astype(jnp.float32) for block in blocks).astype(jnp.bfloat16)

    items = [[(1, 1, 1)], [(1, 0, 1), (0, 0, 1)], [(0, 1, 0)], [(0, 1, 1)], [(0, 0, 0)], [(1, 0, 0)], [(1, 1, 0)]]
    mine_1, other_1, x_2, x_12, y_1, z_1, keep_1, keep_2, keep_2y = rows_of([1, 2], items, [])
    other_1, x_2, x_12, y_1, z_1 = tied([other_1, x_2, x_12, y_1, z_1], arrived.values())
    from_x2, from_y1, from_z1 = over_x(x_2), over_y(y_1), over_z(z_1, -1)
    from_x12 = over_x(x_12)
    items = [[(0, 0, 1)], [(0, 1, 0)], [(0, 1, 1)], [(0, 0, 0)]]
    mine_3, other_3, x_3, y_3, z_3, keep_3 = rows_of([3], items, [mine_1])
    mine_3, other_3, x_3, y_3, z_3, keep_2y = tied(
        [mine_3, other_3, x_3, y_3, z_3, keep_2y], [from_x2, from_y1, from_z1]
    )
    from_z3, from_x3, from_y2, from_y3 = over_z(z_3, 1), over_x(x_3), over_y(total(keep_2y, from_x2)), over_y(y_3)
    packed = [mine_0, over_role(other_0), mine_1, over_role(other_1), mine_3, over_role(other_3)]
    d_gate, d_up = grads_call(which_ref, packed, width, part, False)
    from_z3, from_x12, from_y2 = tied([from_z3, from_x12, from_y2], [d_gate, d_up])
    from_far = over_y(total(far, from_z1, from_z3))
    from_z2 = over_z(total(keep_2, from_x12[:1], from_y2), 1)
    home_1 = over_z(total(keep_1, from_x12[1:], from_y1), -1)
    (d_down,) = grads_call(which_ref, packed, width, part, True)
    from_x3, from_y3, from_z2, y_0 = tied([from_x3, from_y3, from_z2, y_0], [d_down])
    from_y0 = over_y(y_0)
    home_3 = over_z(total(keep_3, from_x3, from_y3, from_z2), 1)
    from_x0 = over_x(total(side_0, from_far))
    home = (near, from_y0, home_1, home_3, from_x0)
    d_tok = sum(block[0, :tok_rows].astype(jnp.float32) for block in home).astype(jnp.bfloat16)
    home = sum(block[0, tok_rows:, : 4 * tok_rows].astype(jnp.float32) for block in home)
    score = jnp.sum(home.reshape(owners, 4, tok_rows), axis=1).T
    d_probs = jnp.sum(jnp.where(chosen, score[:, None, :], 0.0), axis=2)
    return d_tok, d_probs, d_gate, d_up, d_down


def per_device(tokens, out_grad, routes, probs, w_gate, w_up, w_down):
    owners = lax.axis_size(("role", "ep"))
    tok_rows, top_count = routes.shape
    paired = lax.axis_size("tp") == 2 and lax.axis_size("role") == 2 and lax.axis_size("ep") == 8
    if paired and 2 * slot_capacity(tok_rows, top_count, owners) >= tok_rows:
        return dense_device(tokens, out_grad, routes, probs, w_gate, w_up, w_down)
    return routed_device(tokens, out_grad, routes, probs, w_gate, w_up, w_down)


def solution(mesh):
    in_specs = (
        P(("groups", "role", "ep"), "tp"),
        P(("groups", "role", "ep"), "tp"),
        P(("groups", "role", "ep"), None),
        P(("groups", "role", "ep"), None),
        P(("role", "ep"), None, "tp"),
        P(("role", "ep"), None, "tp"),
        P(("role", "ep"), "tp", None),
    )
    out_specs = (
        P(("groups", "role", "ep"), "tp"),
        P(("groups", "role", "ep"), None),
        P(("groups", "role", "ep"), None, "tp"),
        P(("groups", "role", "ep"), None, "tp"),
        P(("groups", "role", "ep"), "tp", None),
    )
    return jax.shard_map(
        per_device, mesh=mesh, in_specs=in_specs, out_specs=out_specs, check_vma=False
    )
```

```python
import functools
import math

import jax
import jax.numpy as jnp
from jax import lax
from jax.experimental import pallas as pl
from jax.experimental.pallas import tpu as pltpu
from jax.sharding import PartitionSpec as P


def pad_rows(array):
    return jnp.concatenate([array, jnp.zeros((1, array.shape[1]), array.dtype)], 0)


def routed_device(tokens, out_grad, routes, probs, w_gate, w_up, w_down):
    owners = lax.axis_size(("role", "ep"))
    tok_rows, top_count = routes.shape
    width_full = w_gate.shape[1]
    part_width = w_gate.shape[2]
    capacity = min(tok_rows, tok_rows * top_count * 9 // (8 * owners))
    entry_total = tok_rows * top_count
    routes_flat = routes.reshape(-1)
    onehot = (routes_flat[:, None] == jnp.arange(owners, dtype=jnp.int32)[None, :]).astype(
        jnp.int32
    )
    before = jnp.cumsum(onehot, axis=0) - onehot
    slot_index = jnp.sum(before * onehot, axis=1)
    target = routes_flat * capacity + slot_index
    row_count = owners * capacity
    entry_of_slot = (
        jnp.full((row_count,), entry_total, jnp.int32)
        .at[target]
        .set(jnp.arange(entry_total, dtype=jnp.int32))
    )
    token_of_slot = entry_of_slot // top_count
    padded_prob = jnp.concatenate([probs.reshape(-1), jnp.zeros((1,), probs.dtype)], 0)
    send_prob = padded_prob[entry_of_slot].reshape(owners, capacity)
    send_x = pad_rows(tokens)[token_of_slot]
    send_g = pad_rows(out_grad)[token_of_slot]
    slice_x, slice_g, recv_p = (
        lax.all_to_all(
            send_x.reshape(owners, capacity, tokens.shape[1]),
            ("role", "ep"),
            split_axis=0,
            concat_axis=0,
            tiled=True,
        ),
        lax.all_to_all(
            send_g.reshape(owners, capacity, tokens.shape[1]),
            ("role", "ep"),
            split_axis=0,
            concat_axis=0,
            tiled=True,
        ),
        lax.all_to_all(send_prob, ("role", "ep"), split_axis=0, concat_axis=0, tiled=True),
    )
    recv_x, recv_g = (
        lax.all_gather(slice_x, "tp", axis=2, tiled=True),
        lax.all_gather(slice_g, "tp", axis=2, tiled=True),
    )
    rows_x = recv_x.reshape(row_count, width_full)
    rows_g = recv_g.reshape(row_count, width_full)
    weight_p = recv_p.reshape(row_count, 1).astype(jnp.float32)
    gate_up = jnp.concatenate([w_gate[0], w_up[0]], 1)
    down_shard = w_down[0]
    both_rows = jnp.dot(rows_x, gate_up, preferred_element_type=jnp.float32)
    gate_rows = both_rows[:, :part_width]
    up_rows = both_rows[:, part_width:]
    sigmoid_gate = jax.nn.sigmoid(gate_rows)
    activated = gate_rows * sigmoid_gate
    hidden = activated * up_rows
    back_rows = lax.dot_general(
        rows_g, down_shard, (((1,), (1,)), ((), ())), preferred_element_type=jnp.float32
    )
    scores = lax.psum(jnp.sum(hidden * back_rows, axis=1), "tp")
    hidden_grad = weight_p * back_rows
    d_gate_rows = (
        hidden_grad * up_rows * sigmoid_gate * (1.0 + gate_rows * (1.0 - sigmoid_gate))
    ).astype(jnp.bfloat16)
    d_up_rows = (hidden_grad * activated).astype(jnp.bfloat16)
    d_both = jnp.concatenate([d_gate_rows, d_up_rows], 1)
    scaled = (weight_p * hidden).astype(jnp.bfloat16)
    grad_down = lax.dot_general(
        scaled, rows_g, (((0,), (0,)), ((), ())), preferred_element_type=jnp.float32
    )
    grad_both = lax.dot_general(
        rows_x, d_both, (((0,), (0,)), ((), ())), preferred_element_type=jnp.float32
    )
    grad_gate = grad_both[:, :part_width]
    grad_up = grad_both[:, part_width:]
    partial_low = lax.dot_general(
        d_both, gate_up, (((1,), (1,)), ((), ())), preferred_element_type=jnp.float32
    ).astype(jnp.bfloat16)
    home_s = lax.all_to_all(
        scores.reshape(owners, capacity), ("role", "ep"), split_axis=0, concat_axis=0, tiled=True
    )
    summed = lax.psum_scatter(
        partial_low.reshape(owners, capacity, width_full), "tp", scatter_dimension=2, tiled=True
    ).astype(jnp.float32)
    summed_low = summed.astype(jnp.bfloat16)
    home_x = lax.all_to_all(summed_low, ("role", "ep"), split_axis=0, concat_axis=0, tiled=True)
    slice_width = summed.shape[2]
    route_rows = home_x.reshape(row_count, slice_width).astype(jnp.float32)
    d_tok = (
        jnp.zeros((tok_rows + 1, slice_width), jnp.float32)
        .at[token_of_slot]
        .add(route_rows)[:tok_rows]
    )
    d_probs = home_s.reshape(-1)[target].reshape(tok_rows, top_count)
    return (
        d_tok.astype(jnp.bfloat16),
        d_probs,
        grad_gate.astype(jnp.bfloat16)[None],
        grad_up.astype(jnp.bfloat16)[None],
        grad_down.astype(jnp.bfloat16)[None],
    )


def slot_capacity(tok_rows, top_count, owners):
    return min(tok_rows, tok_rows * top_count * 9 // (8 * owners))


LOOSE = pl.BlockSpec(memory_space=pl.ANY)


def weights_kernel(tp_ref, wg_ref, wu_ref, wd_ref, both_ref, down_ref):
    part = wg_ref.shape[2]
    both_ref[:, :part] = wg_ref[0]
    both_ref[:, part:] = wu_ref[0]
    down_ref[...] = wd_ref[0]


def weights_call(which, w_gate, w_up, w_down):
    _, width, part = w_gate.shape
    half = width // 2

    def place(i, w):
        return (i + w[0]) % 2

    return pl.pallas_call(
        weights_kernel,
        grid_spec=pltpu.PrefetchScalarGridSpec(
            num_scalar_prefetch=1,
            grid=(2,),
            in_specs=[
                pl.BlockSpec((1, half, part), lambda i, w: (0, place(i, w), 0)),
                pl.BlockSpec((1, half, part), lambda i, w: (0, place(i, w), 0)),
                pl.BlockSpec((1, part, half), lambda i, w: (0, 0, place(i, w))),
            ],
            out_specs=[
                pl.BlockSpec((half, 2 * part), lambda i, w: (i, 0)),
                pl.BlockSpec((part, half), lambda i, w: (0, i)),
            ],
        ),
        out_shape=[
            jax.ShapeDtypeStruct((width, 2 * part), jnp.bfloat16),
            jax.ShapeDtypeStruct((part, width), jnp.bfloat16),
        ],
        compiler_params=pltpu.CompilerParams(vmem_limit_bytes=62 << 20),
        cost_estimate=pl.CostEstimate(flops=0, bytes_accessed=12 * width * part, transcendentals=0),
        name="weights",
    )(which, w_gate, w_up, w_down)


def rows_kernel(count, ways, capacity, slots, where_ref, *refs):
    weights_in, units_in, tables_in = refs[:4], refs[4 : 4 + 4 * count], refs[4 + 4 * count : 4 + 5 * count]
    leaves = 1 + max(way[0] for way in ways.values())
    carried_in = refs[4 + 5 * count : 4 + 5 * count + sum(len(block) == 1 for block in ways)]
    refs = refs[len(refs) - 18 - leaves :]
    outs, packets, refs = refs[:2], refs[2 : 2 + leaves], refs[2 + leaves :]
    x_all, g_all, tables, wgu0, wgu1, wd0, wd1, xc, gc, both, scaled, dense, piece, unit_sems, weight_sems = refs[:15]
    out_sems = refs[15]
    half, tok = x_all.shape[3], x_all.shape[2] // 2
    part = scaled.shape[2]
    owners = tables.shape[2]
    wgu, wd = (wgu0, wgu1), (wd0, wd1)

    x_copies, g_copies = [], []
    for index, unit in enumerate(units_in):
        chunk, y, x = index // 4, index // 2 % 2, index % 2
        rows = pl.ds(y * tok, tok)
        x_copies.append(pltpu.make_async_copy(unit.at[pl.ds(0, tok)], x_all.at[chunk, x, rows], unit_sems.at[0, index]))
        g_copies.append(pltpu.make_async_copy(unit.at[pl.ds(tok, tok)], g_all.at[chunk, x, rows], unit_sems.at[1, index]))
    t_copies = [
        pltpu.make_async_copy(table, tables.at[chunk], unit_sems.at[2, chunk]) for chunk, table in enumerate(tables_in)
    ]
    weight_copies = [
        pltpu.make_async_copy(source, target, weight_sems.at[index])
        for index, (source, target) in enumerate(zip(weights_in, (wgu0, wgu1, wd0, wd1)))
    ]
    for copy in t_copies + x_copies + weight_copies[:2]:
        copy.start()
    leaving = []

    def leave(source, target):
        copy = pltpu.make_async_copy(source, target, out_sems.at[len(leaving)])
        copy.start()
        leaving.append(copy)

    for index, block in enumerate(carried_in):
        number, slot = ways[(index,)]
        leave(block.at[0], packets[number].at[slot])

    def leave_rows(held, start):
        for expert in range(2):
            leave(held.at[expert], outs[expert].at[:, pl.ds(start, held.shape[2])])

    def dot(a, b, dims):
        return lax.dot_general(a, b, (dims, ((), ())), preferred_element_type=jnp.float32)

    for copy in t_copies:
        copy.wait()
    earlier = lax.broadcasted_iota(jnp.int32, (tok, tok), 0) < lax.broadcasted_iota(jnp.int32, (tok, tok), 1)
    earlier = earlier.astype(jnp.bfloat16)
    number = lax.broadcasted_iota(jnp.int32, (slots, tok), 0).astype(jnp.float32)
    names = lax.broadcasted_iota(jnp.int32, (owners, tok), 0)
    picks, low_picks, probs = {}, {}, {}
    for chunk in range(count):
        found = []
        for y in range(2):
            table = tables[chunk, y].astype(jnp.float32)
            rank = dot((table >= 0.0).astype(jnp.bfloat16), earlier, ((1,), (0,))) + float(y * capacity)
            found.append((table, jnp.where(table >= 0.0, rank, -1.0)))
        for expert in range(2):
            mine = names == where_ref[expert]
            halves, prob = [], None
            for table, rank in found:
                weight = jnp.sum(jnp.where(mine, table, 0.0), axis=0, keepdims=True)
                slot = jnp.sum(jnp.where(mine, rank, 0.0), axis=0, keepdims=True)
                halves.append((number == slot).astype(jnp.float32))
                term = jnp.sum(halves[-1] * weight, axis=1, keepdims=True)
                prob = term if prob is None else prob + term
            picks[chunk, expert] = halves
            low_picks[chunk, expert] = jnp.concatenate(halves, 1).astype(jnp.bfloat16)
            probs[chunk, expert] = prob
    spans = [pl.ds(chunk * slots, slots) for chunk in range(count)]
    sides = [slice(side * half, (side + 1) * half) for side in range(2)]

    def gather(copies, source, target, following):
        for copy in copies:
            copy.wait()
        for copy in following:
            copy.start()
        for chunk in range(count):
            both_picks = jnp.concatenate([low_picks[chunk, expert] for expert in range(2)], 0)
            for side in range(2):
                rows = dot(both_picks, source[chunk, side], ((1,), (0,))).astype(jnp.bfloat16)
                for expert in range(2):
                    target[expert, spans[chunk], sides[side]] = rows[expert * slots : (expert + 1) * slots]

    gather(x_copies, x_all, xc, g_copies + weight_copies[2:])
    leave_rows(xc, 0)
    rows = []
    for expert in range(2):
        weight_copies[expert].wait()
        rows.append(dot(xc[expert], wgu[expert][...], ((1,), (0,))))
    gather(g_copies, g_all, gc, ())
    leave_rows(gc, 2 * half)
    scores = []
    for expert in range(2):
        weight_copies[2 + expert].wait()
        back = dot(gc[expert], wd[expert][...], ((1,), (1,)))
        gate, up = rows[expert][:, :part], rows[expert][:, part:]
        sig = jax.nn.sigmoid(gate)
        act = gate * sig
        hidden = act * up
        scores.append(jnp.sum(hidden * back, axis=1, keepdims=True))
        prob = jnp.concatenate([probs[chunk, expert] for chunk in range(count)], 0)
        hgrad = prob * back
        both[expert, :, :part] = (hgrad * up * sig * (1.0 + gate * (1.0 - sig))).astype(jnp.bfloat16)
        both[expert, :, part:] = (hgrad * act).astype(jnp.bfloat16)
        scaled[expert] = (prob * hidden).astype(jnp.bfloat16)
    leave_rows(both, 4 * half)
    leave_rows(scaled, 4 * half + 2 * part)

    names = lax.broadcasted_iota(jnp.int32, (owners, half), 0)
    column = lax.broadcasted_iota(jnp.int32, (owners, half), 1) // (2 * tok)
    for chunk in range(count):
        for y in range(2):
            extra = jnp.zeros((owners, half), jnp.float32)
            for expert in range(2):
                part_scores = scores[expert][chunk * slots : (chunk + 1) * slots]
                line = jnp.sum(picks[chunk, expert][y] * part_scores, axis=0, keepdims=True)
                high = line.astype(jnp.bfloat16).astype(jnp.float32)
                line = jnp.concatenate([high, line - high] * (half // (2 * tok)), 1)
                extra = extra + jnp.where((names == where_ref[expert]) & (column == where_ref[2]), line, 0.0)
            for side in range(2):
                piece[chunk, side, y, tok:] = extra.astype(jnp.bfloat16)
    for chunk in range(count):
        for expert in range(2):
            placed = dot(low_picks[chunk, expert], both[expert, spans[chunk], :], ((0,), (0,)))
            dense[expert, pl.ds(chunk * 2 * tok, 2 * tok)] = placed.astype(jnp.bfloat16)
    for side in (1, 0):
        total = dot(dense[0], wgu0[sides[side], :], ((1,), (1,)))
        total = total + dot(dense[1], wgu1[sides[side], :], ((1,), (1,)))
        for chunk in range(count):
            for y in range(2):
                start = (2 * chunk + y) * tok
                piece[chunk, side, y, :tok] = total[start : start + tok].astype(jnp.bfloat16)
                number, slot = ways[chunk, y, side]
                leave(piece.at[chunk, side, y], packets[number].at[slot])
    for copy in leaving:
        copy.wait()


def rows_call(items, owners, capacity, slots, where, weights, units, tables, carried, after):
    count = len(tables)
    ways = {block: (number, slot) for number, blocks in enumerate(items) for slot, block in enumerate(blocks)}
    tok, half = units[0].shape[0] // 2, units[0].shape[1]
    part, width = weights[2].shape
    widths = (width, width, 2 * part, part)
    packet = (tok + owners, half)
    return pl.pallas_call(
        functools.partial(rows_kernel, count, ways, capacity, slots),
        grid_spec=pltpu.PrefetchScalarGridSpec(
            num_scalar_prefetch=1,
            grid=(1,),
            in_specs=[LOOSE] * (4 + 5 * count + len(carried) + len(after)),
            out_specs=[LOOSE] * (2 + len(items)),
            scratch_shapes=[pltpu.VMEM((count, 2, 2 * tok, half), jnp.bfloat16)] * 2
            + [pltpu.VMEM((count, 2, owners, tok), jnp.bfloat16)]
            + [pltpu.VMEM((width, 2 * part), jnp.bfloat16)] * 2
            + [pltpu.VMEM((part, width), jnp.bfloat16)] * 2
            + [pltpu.VMEM((2, count * slots, size), jnp.bfloat16) for size in widths]
            + [
                pltpu.VMEM((2, count * 2 * tok, 2 * part), jnp.bfloat16),
                pltpu.VMEM((count, 2, 2) + packet, jnp.bfloat16),
                pltpu.SemaphoreType.DMA((3, 4 * count)),
                pltpu.SemaphoreType.DMA((4,)),
                pltpu.SemaphoreType.DMA((8 + 4 * count + len(carried),)),
            ],
        ),
        out_shape=[jax.ShapeDtypeStruct((count * slots, sum(widths)), jnp.bfloat16)] * 2
        + [jax.ShapeDtypeStruct((len(blocks),) + packet, jnp.bfloat16) for blocks in items],
        compiler_params=pltpu.CompilerParams(vmem_limit_bytes=62 << 20),
        cost_estimate=pl.CostEstimate(
            flops=count * (20 * slots * width * part + 24 * slots * tok * width),
            bytes_accessed=count * 16 * tok * width + 12 * width * part,
            transcendentals=2 * count * slots * part,
        ),
        name="rows",
    )(where, *weights, *units, *tables, *carried, *after)


def grads_kernel(count, wide, deep, blocks, tp_ref, *refs):
    sources, outs = refs[:count], refs[count:-4]
    wide_all, deep_all, wide_sems, deep_sems = refs[-4:]
    starts = [sum(source.shape[0] for source in sources[:index]) for index in range(count)]
    size = wide_all.shape[2]
    block = pl.program_id(0)

    def copies(column):
        return [
            pltpu.make_async_copy(
                source.at[:, pl.ds(wide + column * size, size)],
                wide_all.at[column, pl.ds(starts[index], source.shape[0])],
                wide_sems.at[column, index],
            )
            for index, source in enumerate(sources)
        ]

    @pl.when(block == 0)
    def _():
        deep_copies = [
            pltpu.make_async_copy(
                source.at[:, pl.ds(deep, deep_all.shape[1])],
                deep_all.at[pl.ds(starts[index], source.shape[0])],
                deep_sems.at[index],
            )
            for index, source in enumerate(sources)
        ]
        for copy in deep_copies:
            copy.start()
        for column in range(blocks):
            for copy in copies(column):
                copy.start()
        for copy in deep_copies:
            copy.wait()

    for column in range(blocks):

        @pl.when(block == column)
        def _(column=column):
            for copy in copies(column):
                copy.wait()

    dims = (((0,), (0,)), ((), ()))
    if len(outs) == 2:
        part = outs[0].shape[2]
        both = lax.dot_general(wide_all[block], deep_all[...], dims, preferred_element_type=jnp.float32)
        outs[0][0] = both[:, :part].astype(jnp.bfloat16)
        outs[1][0] = both[:, part:].astype(jnp.bfloat16)
    else:
        down = lax.dot_general(deep_all[...], wide_all[block], dims, preferred_element_type=jnp.float32)
        outs[0][0] = down.astype(jnp.bfloat16)


def grads_call(which, packed, width, part, down):
    rows, count = sum(item.shape[0] for item in packed), len(packed)
    step = math.gcd(width // 2, 512)
    per = width // 2 // step
    deep = part if down else 2 * part

    def place(i, w):
        return (i + w[0] * per) % (2 * per)

    if down:
        specs = [pl.BlockSpec((1, part, step), lambda i, w: (0, 0, place(i, w)))]
        shapes = [(1, part, width)]
    else:
        specs = [pl.BlockSpec((1, step, part), lambda i, w: (0, place(i, w), 0))] * 2
        shapes = [(1, width, part)] * 2
    starts = (width, 2 * width + 2 * part) if down else (0, 2 * width)
    return pl.pallas_call(
        functools.partial(grads_kernel, count, *starts, 2 * per),
        grid_spec=pltpu.PrefetchScalarGridSpec(
            num_scalar_prefetch=1,
            grid=(2 * per,),
            in_specs=[LOOSE] * count,
            out_specs=specs,
            scratch_shapes=[
                pltpu.VMEM((2 * per, rows, step), jnp.bfloat16),
                pltpu.VMEM((rows, deep), jnp.bfloat16),
                pltpu.SemaphoreType.DMA((2 * per, count)),
                pltpu.SemaphoreType.DMA((count,)),
            ],
        ),
        out_shape=[jax.ShapeDtypeStruct(shape, jnp.bfloat16) for shape in shapes],
        compiler_params=pltpu.CompilerParams(vmem_limit_bytes=62 << 20),
        cost_estimate=pl.CostEstimate(
            flops=2 * rows * width * deep, bytes_accessed=2 * rows * (width + deep), transcendentals=0
        ),
        name="grads",
    )(which, *packed)


def dense_device(tokens, out_grad, routes, probs, w_gate, w_up, w_down):
    owners = lax.axis_size(("role", "ep"))
    ep = lax.axis_size("ep")
    n_y = 2
    n_z = ep // n_y
    tok_rows, half = tokens.shape
    capacity = slot_capacity(tok_rows, routes.shape[1], owners)
    slots = -(-n_y * capacity // 16) * 16
    role, place, which = lax.axis_index("role"), lax.axis_index("ep"), lax.axis_index("tp")

    def over_x(array):
        return lax.ppermute(array, "tp", [(0, 1), (1, 0)])

    def over_role(array):
        return lax.ppermute(array, "role", [(0, 1), (1, 0)])

    def over_y(array):
        return lax.ppermute(array, "ep", [(i, i + 1 - 2 * (i % n_y)) for i in range(ep)])

    def over_z(array, shift):
        return lax.ppermute(array, "ep", [(i, (i + shift * n_y) % ep) for i in range(ep)])

    def tied(values, others):
        return lax.optimization_barrier((list(values), list(others)))[0]

    last = n_z - 1
    routes_in = []
    for z in range(n_z):
        shift = -1 if z == last and z > 1 else 1
        if z:
            routes_in.append(((z, 0, 0), (0 if z in (1, last) else z - 1, 0, 0), functools.partial(over_z, shift=shift)))
        routes_in.append(((z, 1, 0), (z, 0, 0), over_y))
        routes_in.append(((z, 0, 1), (z, 0, 0), over_x))
        if z == 0:
            routes_in.append(((z, 1, 1), (z, 1, 0), over_x))
        elif z in (1, last):
            routes_in.append(((z, 1, 1), (0, 1, 1), functools.partial(over_z, shift=shift)))
        else:
            routes_in.append(((z, 1, 1), (z, 0, 1), over_y))
    routes_in.sort(key=lambda item: (item[0][0] % 2 if item[2] in (over_x, over_y) else 0, sum(item[0][1:])))

    rounds, waiting, there = [], list(routes_in), {(0, 0, 0)}
    while waiting:
        moves = {}
        for item in waiting:
            axis = item[2] if item[2] in (over_x, over_y) else over_z
            if item[1] in there and axis not in moves:
                moves[axis] = item
        rounds.append(list(moves.values()))
        there |= {item[0] for item in rounds[-1]}
        waiting = [item for item in waiting if item[0] not in there]

    which_ref = which.reshape(1).astype(jnp.int32)
    where = jnp.stack([role * ep + place, (1 - role) * ep + place, which]).astype(jnp.int32)
    both_w, down_w = weights_call(which_ref, w_gate, w_up, w_down)
    width, part = both_w.shape[0], down_w.shape[0]

    def rows_of(steps, items, carried=(), after=()):
        four = [units[z, y, x] for z in steps for y in range(2) for x in range(2)]
        return rows_call(items, owners, capacity, slots, where, weights, four, [tables[z] for z in steps], carried, after)

    units = {(0, 0, 0): jnp.concatenate([tokens, out_grad], 0)}
    settled = dict(units)
    for number, moves in enumerate(rounds):
        arrived = {target: move(settled[source]) for target, source, move in moves}
        units.update(arrived)
        settled.update(arrived)
        extra = []
        if number == 0:
            extra = [both_w, down_w]
            both_w, down_w, routes, probs = tied([both_w, down_w, routes, probs], arrived.values())
            weights = (both_w, over_role(both_w), down_w, over_role(down_w))
            chosen = routes[:, :, None] == jnp.arange(owners, dtype=jnp.int32)
            table = jnp.sum(jnp.where(chosen, probs[:, :, None].astype(jnp.float32) + 1.0, 0.0), axis=1) - 1.0
            table = table.astype(jnp.bfloat16).T
            table = jnp.stack([table, over_y(table)])
        if number == 1:
            (table,) = tied([table], arrived.values())
            tables = [over_z(table, z) if z else table for z in range(n_z)]
        if number == 2:
            mine_0, other_0, near, side_0, far, y_0 = rows_of(
                [0], [[(0, 0, 0)], [(0, 0, 1)], [(0, 1, 1)], [(0, 1, 0)]]
            )
            extra = [mine_0]
        if number == 3:
            (other_0,) = tied([other_0], [settled[0, 0, 0]])
            other_0 = over_role(other_0)
            extra = [other_0] + tables[1:]
        names = list(settled)
        settled = dict(zip(names, tied([settled[item] for item in names], extra)))

    def total(*blocks):
        return sum(block.astype(jnp.float32) for block in blocks).astype(jnp.bfloat16)

    items = [[(1, 1, 1), (1, 0, 1)], [(0, 1, 0), (0,)], [(0, 1, 1)], [(0, 0, 1)], [(0, 0, 0)], [(1, 0, 0)], [(1, 1, 0)]]
    mine_1, other_1, x_2, y_1, z_1, x_1, keep_1, keep_2, keep_2y = rows_of([1, 2], items, [y_0])
    other_1, x_2, y_1, z_1 = tied([other_1, x_2, y_1, z_1], arrived.values())
    from_x2, from_y1, from_z1 = over_x(x_2), over_y(y_1), over_z(z_1, -1)
    items = [[(0, 0, 1), (0,)], [(0, 1, 0)], [(0, 1, 1)], [(0, 0, 0)]]
    mine_3, other_3, x_3, y_3, z_3, keep_3 = rows_of([3], items, [x_1], [mine_1])
    mine_3, other_3, x_3, y_3, z_3, keep_2y = tied(
        [mine_3, other_3, x_3, y_3, z_3, keep_2y], [from_x2, from_y1, from_z1]
    )
    from_z3, from_y2 = over_z(z_3, 1), over_y(total(keep_2y, from_x2[:1]))
    from_x3, from_y3 = over_x(x_3), over_y(y_3)
    packed = [mine_0, other_0, mine_1, over_role(other_1), mine_3, over_role(other_3)]
    (d_down,) = grads_call(which_ref, packed, width, part, True)
    from_z3, from_y2 = tied([from_z3, from_y2], [d_down])
    from_far = over_y(total(far, from_z1, from_z3))
    from_z2 = over_z(total(keep_2, from_x2[1:], from_y2), 1)
    d_gate, d_up = grads_call(which_ref, packed, width, part, False)
    from_x3, from_y3, from_far, from_z2 = tied([from_x3, from_y3, from_far, from_z2], [d_gate, d_up])
    home_1 = over_z(total(keep_1, from_x3[1:], from_y1[:1]), -1)
    home_3 = over_z(total(keep_3, from_x3[:1], from_y3, from_z2), 1)
    from_x0 = over_x(total(side_0, from_far))
    home = (near, from_y1[1:], home_1, home_3, from_x0)
    d_tok = sum(block[0, :tok_rows].astype(jnp.float32) for block in home).astype(jnp.bfloat16)
    home = sum(block[0, tok_rows:, : 4 * tok_rows].astype(jnp.float32) for block in home)
    score = jnp.sum(home.reshape(owners, 4, tok_rows), axis=1).T
    d_probs = jnp.sum(jnp.where(chosen, score[:, None, :], 0.0), axis=2)
    return d_tok, d_probs, d_gate, d_up, d_down


def per_device(tokens, out_grad, routes, probs, w_gate, w_up, w_down):
    owners = lax.axis_size(("role", "ep"))
    tok_rows, top_count = routes.shape
    paired = lax.axis_size("tp") == 2 and lax.axis_size("role") == 2 and lax.axis_size("ep") == 8
    if paired and 2 * slot_capacity(tok_rows, top_count, owners) >= tok_rows:
        return dense_device(tokens, out_grad, routes, probs, w_gate, w_up, w_down)
    return routed_device(tokens, out_grad, routes, probs, w_gate, w_up, w_down)


def solution(mesh):
    in_specs = (
        P(("groups", "role", "ep"), "tp"),
        P(("groups", "role", "ep"), "tp"),
        P(("groups", "role", "ep"), None),
        P(("groups", "role", "ep"), None),
        P(("role", "ep"), None, "tp"),
        P(("role", "ep"), None, "tp"),
        P(("role", "ep"), "tp", None),
    )
    out_specs = (
        P(("groups", "role", "ep"), "tp"),
        P(("groups", "role", "ep"), None),
        P(("groups", "role", "ep"), None, "tp"),
        P(("groups", "role", "ep"), None, "tp"),
        P(("groups", "role", "ep"), "tp", None),
    )
    return jax.shard_map(
        per_device, mesh=mesh, in_specs=in_specs, out_specs=out_specs, check_vma=False
    )
```

```python
import functools
import math

import jax
import jax.numpy as jnp
from jax import lax
from jax.experimental import pallas as pl
from jax.experimental.pallas import tpu as pltpu
from jax.sharding import PartitionSpec as P


def pad_rows(array):
    return jnp.concatenate([array, jnp.zeros((1, array.shape[1]), array.dtype)], 0)


def routed_device(tokens, out_grad, routes, probs, w_gate, w_up, w_down):
    owners = lax.axis_size(("role", "ep"))
    tok_rows, top_count = routes.shape
    width_full = w_gate.shape[1]
    part_width = w_gate.shape[2]
    capacity = min(tok_rows, tok_rows * top_count * 9 // (8 * owners))
    entry_total = tok_rows * top_count
    routes_flat = routes.reshape(-1)
    onehot = (routes_flat[:, None] == jnp.arange(owners, dtype=jnp.int32)[None, :]).astype(
        jnp.int32
    )
    before = jnp.cumsum(onehot, axis=0) - onehot
    slot_index = jnp.sum(before * onehot, axis=1)
    target = routes_flat * capacity + slot_index
    row_count = owners * capacity
    entry_of_slot = (
        jnp.full((row_count,), entry_total, jnp.int32)
        .at[target]
        .set(jnp.arange(entry_total, dtype=jnp.int32))
    )
    token_of_slot = entry_of_slot // top_count
    padded_prob = jnp.concatenate([probs.reshape(-1), jnp.zeros((1,), probs.dtype)], 0)
    send_prob = padded_prob[entry_of_slot].reshape(owners, capacity)
    send_x = pad_rows(tokens)[token_of_slot]
    send_g = pad_rows(out_grad)[token_of_slot]
    slice_x, slice_g, recv_p = (
        lax.all_to_all(
            send_x.reshape(owners, capacity, tokens.shape[1]),
            ("role", "ep"),
            split_axis=0,
            concat_axis=0,
            tiled=True,
        ),
        lax.all_to_all(
            send_g.reshape(owners, capacity, tokens.shape[1]),
            ("role", "ep"),
            split_axis=0,
            concat_axis=0,
            tiled=True,
        ),
        lax.all_to_all(send_prob, ("role", "ep"), split_axis=0, concat_axis=0, tiled=True),
    )
    recv_x, recv_g = (
        lax.all_gather(slice_x, "tp", axis=2, tiled=True),
        lax.all_gather(slice_g, "tp", axis=2, tiled=True),
    )
    rows_x = recv_x.reshape(row_count, width_full)
    rows_g = recv_g.reshape(row_count, width_full)
    weight_p = recv_p.reshape(row_count, 1).astype(jnp.float32)
    gate_up = jnp.concatenate([w_gate[0], w_up[0]], 1)
    down_shard = w_down[0]
    both_rows = jnp.dot(rows_x, gate_up, preferred_element_type=jnp.float32)
    gate_rows = both_rows[:, :part_width]
    up_rows = both_rows[:, part_width:]
    sigmoid_gate = jax.nn.sigmoid(gate_rows)
    activated = gate_rows * sigmoid_gate
    hidden = activated * up_rows
    back_rows = lax.dot_general(
        rows_g, down_shard, (((1,), (1,)), ((), ())), preferred_element_type=jnp.float32
    )
    scores = lax.psum(jnp.sum(hidden * back_rows, axis=1), "tp")
    hidden_grad = weight_p * back_rows
    d_gate_rows = (
        hidden_grad * up_rows * sigmoid_gate * (1.0 + gate_rows * (1.0 - sigmoid_gate))
    ).astype(jnp.bfloat16)
    d_up_rows = (hidden_grad * activated).astype(jnp.bfloat16)
    d_both = jnp.concatenate([d_gate_rows, d_up_rows], 1)
    scaled = (weight_p * hidden).astype(jnp.bfloat16)
    grad_down = lax.dot_general(
        scaled, rows_g, (((0,), (0,)), ((), ())), preferred_element_type=jnp.float32
    )
    grad_both = lax.dot_general(
        rows_x, d_both, (((0,), (0,)), ((), ())), preferred_element_type=jnp.float32
    )
    grad_gate = grad_both[:, :part_width]
    grad_up = grad_both[:, part_width:]
    partial_low = lax.dot_general(
        d_both, gate_up, (((1,), (1,)), ((), ())), preferred_element_type=jnp.float32
    ).astype(jnp.bfloat16)
    home_s = lax.all_to_all(
        scores.reshape(owners, capacity), ("role", "ep"), split_axis=0, concat_axis=0, tiled=True
    )
    summed = lax.psum_scatter(
        partial_low.reshape(owners, capacity, width_full), "tp", scatter_dimension=2, tiled=True
    ).astype(jnp.float32)
    summed_low = summed.astype(jnp.bfloat16)
    home_x = lax.all_to_all(summed_low, ("role", "ep"), split_axis=0, concat_axis=0, tiled=True)
    slice_width = summed.shape[2]
    route_rows = home_x.reshape(row_count, slice_width).astype(jnp.float32)
    d_tok = (
        jnp.zeros((tok_rows + 1, slice_width), jnp.float32)
        .at[token_of_slot]
        .add(route_rows)[:tok_rows]
    )
    d_probs = home_s.reshape(-1)[target].reshape(tok_rows, top_count)
    return (
        d_tok.astype(jnp.bfloat16),
        d_probs,
        grad_gate.astype(jnp.bfloat16)[None],
        grad_up.astype(jnp.bfloat16)[None],
        grad_down.astype(jnp.bfloat16)[None],
    )


def slot_capacity(tok_rows, top_count, owners):
    return min(tok_rows, tok_rows * top_count * 9 // (8 * owners))


LOOSE = pl.BlockSpec(memory_space=pl.ANY)


def weights_kernel(tp_ref, wg_ref, wu_ref, wd_ref, both_ref, down_ref):
    part = wg_ref.shape[2]
    both_ref[:, :part] = wg_ref[0]
    both_ref[:, part:] = wu_ref[0]
    down_ref[...] = wd_ref[0]


def weights_call(which, w_gate, w_up, w_down):
    _, width, part = w_gate.shape
    half = width // 2

    def place(i, w):
        return (i + w[0]) % 2

    return pl.pallas_call(
        weights_kernel,
        grid_spec=pltpu.PrefetchScalarGridSpec(
            num_scalar_prefetch=1,
            grid=(2,),
            in_specs=[
                pl.BlockSpec((1, half, part), lambda i, w: (0, place(i, w), 0)),
                pl.BlockSpec((1, half, part), lambda i, w: (0, place(i, w), 0)),
                pl.BlockSpec((1, part, half), lambda i, w: (0, 0, place(i, w))),
            ],
            out_specs=[
                pl.BlockSpec((half, 2 * part), lambda i, w: (i, 0)),
                pl.BlockSpec((part, half), lambda i, w: (0, i)),
            ],
        ),
        out_shape=[
            jax.ShapeDtypeStruct((width, 2 * part), jnp.bfloat16),
            jax.ShapeDtypeStruct((part, width), jnp.bfloat16),
        ],
        compiler_params=pltpu.CompilerParams(vmem_limit_bytes=62 << 20),
        cost_estimate=pl.CostEstimate(flops=0, bytes_accessed=12 * width * part, transcendentals=0),
        name="weights",
    )(which, w_gate, w_up, w_down)


def rows_kernel(count, ways, capacity, slots, where_ref, *refs):
    weights_in, units_in, tables_in = refs[:4], refs[4 : 4 + 4 * count], refs[4 + 4 * count : 4 + 5 * count]
    leaves = 1 + max(way[0] for way in ways.values())
    refs = refs[len(refs) - 18 - leaves :]
    outs, packets, refs = refs[:2], refs[2 : 2 + leaves], refs[2 + leaves :]
    x_all, g_all, tables, wgu0, wgu1, wd0, wd1, xc, gc, both, scaled, dense, piece, unit_sems, weight_sems = refs[:15]
    out_sems = refs[15]
    half, tok = x_all.shape[3], x_all.shape[2] // 2
    part = scaled.shape[2]
    owners = tables.shape[2]
    wgu, wd = (wgu0, wgu1), (wd0, wd1)

    x_copies, g_copies = [], []
    for index, unit in enumerate(units_in):
        chunk, y, x = index // 4, index // 2 % 2, index % 2
        rows = pl.ds(y * tok, tok)
        x_copies.append(pltpu.make_async_copy(unit.at[pl.ds(0, tok)], x_all.at[chunk, x, rows], unit_sems.at[0, index]))
        g_copies.append(pltpu.make_async_copy(unit.at[pl.ds(tok, tok)], g_all.at[chunk, x, rows], unit_sems.at[1, index]))
    t_copies = [
        pltpu.make_async_copy(table, tables.at[chunk], unit_sems.at[2, chunk]) for chunk, table in enumerate(tables_in)
    ]
    weight_copies = [
        pltpu.make_async_copy(source, target, weight_sems.at[index])
        for index, (source, target) in enumerate(zip(weights_in, (wgu0, wgu1, wd0, wd1)))
    ]
    for copy in t_copies + x_copies + weight_copies[:2]:
        copy.start()
    leaving = []

    def leave(source, target):
        copy = pltpu.make_async_copy(source, target, out_sems.at[len(leaving)])
        copy.start()
        leaving.append(copy)

    def leave_rows(held, start):
        for expert in range(2):
            leave(held.at[expert], outs[expert].at[:, pl.ds(start, held.shape[2])])

    def dot(a, b, dims):
        return lax.dot_general(a, b, (dims, ((), ())), preferred_element_type=jnp.float32)

    for copy in t_copies:
        copy.wait()
    earlier = lax.broadcasted_iota(jnp.int32, (tok, tok), 0) < lax.broadcasted_iota(jnp.int32, (tok, tok), 1)
    earlier = earlier.astype(jnp.bfloat16)
    number = lax.broadcasted_iota(jnp.int32, (slots, tok), 0).astype(jnp.float32)
    names = lax.broadcasted_iota(jnp.int32, (owners, tok), 0)
    picks, low_picks, probs = {}, {}, {}
    for chunk in range(count):
        found = []
        for y in range(2):
            table = tables[chunk, y].astype(jnp.float32)
            rank = dot((table >= 0.0).astype(jnp.bfloat16), earlier, ((1,), (0,))) + float(y * capacity)
            found.append((table, jnp.where(table >= 0.0, rank, -1.0)))
        for expert in range(2):
            mine = names == where_ref[expert]
            halves, prob = [], None
            for table, rank in found:
                weight = jnp.sum(jnp.where(mine, table, 0.0), axis=0, keepdims=True)
                slot = jnp.sum(jnp.where(mine, rank, 0.0), axis=0, keepdims=True)
                halves.append((number == slot).astype(jnp.float32))
                term = jnp.sum(halves[-1] * weight, axis=1, keepdims=True)
                prob = term if prob is None else prob + term
            picks[chunk, expert] = halves
            low_picks[chunk, expert] = jnp.concatenate(halves, 1).astype(jnp.bfloat16)
            probs[chunk, expert] = prob
    spans = [pl.ds(chunk * slots, slots) for chunk in range(count)]
    sides = [slice(side * half, (side + 1) * half) for side in range(2)]

    def gather(copies, source, target, following):
        for copy in copies:
            copy.wait()
        for copy in following:
            copy.start()
        for chunk in range(count):
            both_picks = jnp.concatenate([low_picks[chunk, expert] for expert in range(2)], 0)
            for side in range(2):
                rows = dot(both_picks, source[chunk, side], ((1,), (0,))).astype(jnp.bfloat16)
                for expert in range(2):
                    target[expert, spans[chunk], sides[side]] = rows[expert * slots : (expert + 1) * slots]

    gather(x_copies, x_all, xc, g_copies + weight_copies[2:])
    leave_rows(xc, 0)
    rows = []
    for expert in range(2):
        weight_copies[expert].wait()
        rows.append(dot(xc[expert], wgu[expert][...], ((1,), (0,))))
    gather(g_copies, g_all, gc, ())
    leave_rows(gc, 2 * half)
    scores = []
    for expert in range(2):
        weight_copies[2 + expert].wait()
        back = dot(gc[expert], wd[expert][...], ((1,), (1,)))
        gate, up = rows[expert][:, :part], rows[expert][:, part:]
        sig = jax.nn.sigmoid(gate)
        act = gate * sig
        hidden = act * up
        scores.append(jnp.sum(hidden * back, axis=1, keepdims=True))
        prob = jnp.concatenate([probs[chunk, expert] for chunk in range(count)], 0)
        hgrad = prob * back
        both[expert, :, :part] = (hgrad * up * sig * (1.0 + gate * (1.0 - sig))).astype(jnp.bfloat16)
        both[expert, :, part:] = (hgrad * act).astype(jnp.bfloat16)
        scaled[expert] = (prob * hidden).astype(jnp.bfloat16)
    leave_rows(both, 4 * half)
    leave_rows(scaled, 4 * half + 2 * part)

    names = lax.broadcasted_iota(jnp.int32, (owners, half), 0)
    column = lax.broadcasted_iota(jnp.int32, (owners, half), 1) // (2 * tok)
    for chunk in range(count):
        for y in range(2):
            extra = jnp.zeros((owners, half), jnp.float32)
            for expert in range(2):
                part_scores = scores[expert][chunk * slots : (chunk + 1) * slots]
                line = jnp.sum(picks[chunk, expert][y] * part_scores, axis=0, keepdims=True)
                high = line.astype(jnp.bfloat16).astype(jnp.float32)
                line = jnp.concatenate([high, line - high] * (half // (2 * tok)), 1)
                extra = extra + jnp.where((names == where_ref[expert]) & (column == where_ref[2]), line, 0.0)
            for side in range(2):
                piece[chunk, side, y, tok:] = extra.astype(jnp.bfloat16)
    for chunk in range(count):
        for expert in range(2):
            placed = dot(low_picks[chunk, expert], both[expert, spans[chunk], :], ((0,), (0,)))
            dense[expert, pl.ds(chunk * 2 * tok, 2 * tok)] = placed.astype(jnp.bfloat16)
    for side in (1, 0):
        total = dot(dense[0], wgu0[sides[side], :], ((1,), (1,)))
        total = total + dot(dense[1], wgu1[sides[side], :], ((1,), (1,)))
        for chunk in range(count):
            for y in range(2):
                start = (2 * chunk + y) * tok
                piece[chunk, side, y, :tok] = total[start : start + tok].astype(jnp.bfloat16)
                number, slot = ways[chunk, y, side]
                leave(piece.at[chunk, side, y], packets[number].at[slot])
    for copy in leaving:
        copy.wait()


def rows_call(items, owners, capacity, slots, where, weights, units, tables, after):
    count = len(tables)
    ways = {block: (number, slot) for number, blocks in enumerate(items) for slot, block in enumerate(blocks)}
    tok, half = units[0].shape[0] // 2, units[0].shape[1]
    part, width = weights[2].shape
    widths = (width, width, 2 * part, part)
    packet = (tok + owners, half)
    return pl.pallas_call(
        functools.partial(rows_kernel, count, ways, capacity, slots),
        grid_spec=pltpu.PrefetchScalarGridSpec(
            num_scalar_prefetch=1,
            grid=(1,),
            in_specs=[LOOSE] * (4 + 5 * count + len(after)),
            out_specs=[LOOSE] * (2 + len(items)),
            scratch_shapes=[pltpu.VMEM((count, 2, 2 * tok, half), jnp.bfloat16)] * 2
            + [pltpu.VMEM((count, 2, owners, tok), jnp.bfloat16)]
            + [pltpu.VMEM((width, 2 * part), jnp.bfloat16)] * 2
            + [pltpu.VMEM((part, width), jnp.bfloat16)] * 2
            + [pltpu.VMEM((2, count * slots, size), jnp.bfloat16) for size in widths]
            + [
                pltpu.VMEM((2, count * 2 * tok, 2 * part), jnp.bfloat16),
                pltpu.VMEM((count, 2, 2) + packet, jnp.bfloat16),
                pltpu.SemaphoreType.DMA((3, 4 * count)),
                pltpu.SemaphoreType.DMA((4,)),
                pltpu.SemaphoreType.DMA((8 + 4 * count,)),
            ],
        ),
        out_shape=[jax.ShapeDtypeStruct((count * slots, sum(widths)), jnp.bfloat16)] * 2
        + [jax.ShapeDtypeStruct((len(blocks),) + packet, jnp.bfloat16) for blocks in items],
        compiler_params=pltpu.CompilerParams(vmem_limit_bytes=62 << 20),
        cost_estimate=pl.CostEstimate(
            flops=count * (20 * slots * width * part + 24 * slots * tok * width),
            bytes_accessed=count * 16 * tok * width + 12 * width * part,
            transcendentals=2 * count * slots * part,
        ),
        name="rows",
    )(where, *weights, *units, *tables, *after)


def grads_kernel(count, wide, deep, blocks, tp_ref, *refs):
    sources, outs = refs[:count], refs[count:-4]
    wide_all, deep_all, wide_sems, deep_sems = refs[-4:]
    starts = [sum(source.shape[0] for source in sources[:index]) for index in range(count)]
    size = wide_all.shape[2]
    block = pl.program_id(0)

    def copies(column):
        return [
            pltpu.make_async_copy(
                source.at[:, pl.ds(wide + column * size, size)],
                wide_all.at[column, pl.ds(starts[index], source.shape[0])],
                wide_sems.at[column, index],
            )
            for index, source in enumerate(sources)
        ]

    @pl.when(block == 0)
    def _():
        deep_copies = [
            pltpu.make_async_copy(
                source.at[:, pl.ds(deep, deep_all.shape[1])],
                deep_all.at[pl.ds(starts[index], source.shape[0])],
                deep_sems.at[index],
            )
            for index, source in enumerate(sources)
        ]
        for copy in deep_copies:
            copy.start()
        for column in range(blocks):
            for copy in copies(column):
                copy.start()
        for copy in deep_copies:
            copy.wait()

    for column in range(blocks):

        @pl.when(block == column)
        def _(column=column):
            for copy in copies(column):
                copy.wait()

    dims = (((0,), (0,)), ((), ()))
    if len(outs) == 2:
        part = outs[0].shape[2]
        both = lax.dot_general(wide_all[block], deep_all[...], dims, preferred_element_type=jnp.float32)
        outs[0][0] = both[:, :part].astype(jnp.bfloat16)
        outs[1][0] = both[:, part:].astype(jnp.bfloat16)
    else:
        down = lax.dot_general(deep_all[...], wide_all[block], dims, preferred_element_type=jnp.float32)
        outs[0][0] = down.astype(jnp.bfloat16)


def grads_call(which, packed, width, part, down):
    rows, count = sum(item.shape[0] for item in packed), len(packed)
    step = math.gcd(width // 2, 512)
    per = width // 2 // step
    deep = part if down else 2 * part

    def place(i, w):
        return (i + w[0] * per) % (2 * per)

    if down:
        specs = [pl.BlockSpec((1, part, step), lambda i, w: (0, 0, place(i, w)))]
        shapes = [(1, part, width)]
    else:
        specs = [pl.BlockSpec((1, step, part), lambda i, w: (0, place(i, w), 0))] * 2
        shapes = [(1, width, part)] * 2
    starts = (width, 2 * width + 2 * part) if down else (0, 2 * width)
    return pl.pallas_call(
        functools.partial(grads_kernel, count, *starts, 2 * per),
        grid_spec=pltpu.PrefetchScalarGridSpec(
            num_scalar_prefetch=1,
            grid=(2 * per,),
            in_specs=[LOOSE] * count,
            out_specs=specs,
            scratch_shapes=[
                pltpu.VMEM((2 * per, rows, step), jnp.bfloat16),
                pltpu.VMEM((rows, deep), jnp.bfloat16),
                pltpu.SemaphoreType.DMA((2 * per, count)),
                pltpu.SemaphoreType.DMA((count,)),
            ],
        ),
        out_shape=[jax.ShapeDtypeStruct(shape, jnp.bfloat16) for shape in shapes],
        compiler_params=pltpu.CompilerParams(vmem_limit_bytes=24 << 20),
        cost_estimate=pl.CostEstimate(
            flops=2 * rows * width * deep, bytes_accessed=2 * rows * (width + deep), transcendentals=0
        ),
        name="grads",
    )(which, *packed)


def dense_device(tokens, out_grad, routes, probs, w_gate, w_up, w_down):
    owners = lax.axis_size(("role", "ep"))
    ep = lax.axis_size("ep")
    n_y = 2
    n_z = ep // n_y
    tok_rows, half = tokens.shape
    capacity = slot_capacity(tok_rows, routes.shape[1], owners)
    slots = -(-n_y * capacity // 16) * 16
    role, place, which = lax.axis_index("role"), lax.axis_index("ep"), lax.axis_index("tp")

    def over_x(array):
        return lax.ppermute(array, "tp", [(0, 1), (1, 0)])

    def over_role(array):
        return lax.ppermute(array, "role", [(0, 1), (1, 0)])

    def over_y(array):
        return lax.ppermute(array, "ep", [(i, i + 1 - 2 * (i % n_y)) for i in range(ep)])

    def over_z(array, shift):
        return lax.ppermute(array, "ep", [(i, (i + shift * n_y) % ep) for i in range(ep)])

    def tied(values, others):
        return lax.optimization_barrier((list(values), list(others)))[0]

    last = n_z - 1
    routes_in = []
    for z in range(n_z):
        shift = -1 if z == last and z > 1 else 1
        if z:
            routes_in.append(((z, 0, 0), (0 if z in (1, last) else z - 1, 0, 0), functools.partial(over_z, shift=shift)))
        routes_in.append(((z, 1, 0), (z, 0, 0), over_y))
        routes_in.append(((z, 0, 1), (z, 0, 0), over_x))
        if z == 0:
            routes_in.append(((z, 1, 1), (z, 1, 0), over_x))
        elif z in (1, last):
            routes_in.append(((z, 1, 1), (0, 1, 1), functools.partial(over_z, shift=shift)))
        else:
            routes_in.append(((z, 1, 1), (z, 0, 1), over_y))
    routes_in.sort(key=lambda item: (item[0][0] % 2 if item[2] in (over_x, over_y) else 0, sum(item[0][1:])))

    rounds, waiting, there = [], list(routes_in), {(0, 0, 0)}
    while waiting:
        moves = {}
        for item in waiting:
            axis = item[2] if item[2] in (over_x, over_y) else over_z
            if item[1] in there and axis not in moves:
                moves[axis] = item
        rounds.append(moves)
        there |= {item[0] for item in moves.values()}
        waiting = [item for item in waiting if item[0] not in there]

    which_ref = which.reshape(1).astype(jnp.int32)
    where = jnp.stack([role * ep + place, (1 - role) * ep + place, which]).astype(jnp.int32)
    both_w, down_w = weights_call(which_ref, w_gate, w_up, w_down)
    width, part = both_w.shape[0], down_w.shape[0]

    def rows_of(steps, items, after=()):
        four = [units[z, y, x] for z in steps for y in range(2) for x in range(2)]
        return rows_call(items, owners, capacity, slots, where, weights, four, [tables[z] for z in steps], after)

    units = {(0, 0, 0): jnp.concatenate([tokens, out_grad], 0)}
    settled = dict(units)
    for number, moves in enumerate(rounds):
        arrived = {target: move(settled[source]) for target, source, move in moves.values()}
        units.update(arrived)
        settled.update(arrived)
        extra = []
        if number == 0:
            extra = [both_w, down_w]
            both_w, down_w, routes, probs = tied([both_w, down_w, routes, probs], arrived.values())
            weights = (both_w, over_role(both_w), down_w, over_role(down_w))
            chosen = routes[:, :, None] == jnp.arange(owners, dtype=jnp.int32)
            table = jnp.sum(jnp.where(chosen, probs[:, :, None].astype(jnp.float32) + 1.0, 0.0), axis=1) - 1.0
            table = table.astype(jnp.bfloat16).T
            table = jnp.stack([table, over_y(table)])
        if number == 1:
            (table,) = tied([table], arrived.values())
            tables = [over_z(table, z) if z else table for z in range(n_z)]
        if number == 2:
            mine_0, other_0, near, side_0, far, y_0 = rows_of(
                [0], [[(0, 0, 0)], [(0, 0, 1)], [(0, 1, 1)], [(0, 1, 0)]]
            )
            extra = [mine_0]
        if number == 3:
            (other_0,) = tied([other_0], [settled[0, 0, 0]])
            other_0 = over_role(other_0)
            extra = [other_0]
        names = list(settled)
        settled = dict(zip(names, tied([settled[item] for item in names], extra)))

    def total(*blocks):
        return sum(block.astype(jnp.float32) for block in blocks).astype(jnp.bfloat16)

    items = [[(1, 1, 1)], [(1, 0, 1)], [(0, 1, 0)], [(0, 1, 1)], [(0, 0, 1)], [(0, 0, 0)], [(1, 0, 0)], [(1, 1, 0)]]
    mine_1, other_1, x_2, x_20, y_1, z_1, x_1, keep_1, keep_2, keep_2y = rows_of([1, 2], items)
    x_2, y_1, z_1 = tied([x_2, y_1, z_1], arrived.values())
    from_x2, from_y1, from_z1 = over_x(x_2), over_y(y_1), over_z(z_1, -1)
    items = [[(0, 0, 1)], [(0, 1, 0)], [(0, 1, 1)], [(0, 0, 0)]]
    mine_3, other_3, x_3, y_3, z_3, keep_3 = rows_of([3], items, [mine_1])
    mine_3, other_3, other_1, z_3, x_3, y_3, x_1, x_20, keep_2y = tied(
        [mine_3, other_3, other_1, z_3, x_3, y_3, x_1, x_20, keep_2y], [from_x2, from_y1, from_z1]
    )
    from_z3, from_y2, from_x20 = over_z(z_3, 1), over_y(total(keep_2y, from_x2)), over_x(x_20)
    from_x1, from_x3, from_y3 = over_x(x_1), over_x(x_3), over_y(y_3)
    from_far = over_y(total(far, from_z1, from_z3))
    from_z2 = over_z(total(keep_2, from_x20, from_y2), 1)
    packed = [mine_0, other_0, mine_1, over_role(other_1), mine_3, over_role(other_3)]
    d_gate, d_up = grads_call(which_ref, packed, width, part, False)
    from_x1, from_x3, from_y3, from_far, from_z2, y_0 = tied(
        [from_x1, from_x3, from_y3, from_far, from_z2, y_0], [d_gate, d_up]
    )
    from_y0 = over_y(y_0)
    home_1 = over_z(total(keep_1, from_x1, from_y1), -1)
    home_3 = over_z(total(keep_3, from_x3, from_y3, from_z2), 1)
    from_x0 = over_x(total(side_0, from_far))
    (d_down,) = grads_call(which_ref, packed, width, part, True)
    home_1, home_3, from_x0, from_y0 = tied([home_1, home_3, from_x0, from_y0], [d_down])
    home = (near, from_y0, home_1, home_3, from_x0)
    d_tok = sum(block[0, :tok_rows].astype(jnp.float32) for block in home).astype(jnp.bfloat16)
    home = sum(block[0, tok_rows:, : 4 * tok_rows].astype(jnp.float32) for block in home)
    score = jnp.sum(home.reshape(owners, 4, tok_rows), axis=1).T
    d_probs = jnp.sum(jnp.where(chosen, score[:, None, :], 0.0), axis=2)
    return d_tok, d_probs, d_gate, d_up, d_down


def per_device(tokens, out_grad, routes, probs, w_gate, w_up, w_down):
    owners = lax.axis_size(("role", "ep"))
    tok_rows, top_count = routes.shape
    paired = lax.axis_size("tp") == 2 and lax.axis_size("role") == 2 and lax.axis_size("ep") == 8
    if paired and 2 * slot_capacity(tok_rows, top_count, owners) >= tok_rows:
        return dense_device(tokens, out_grad, routes, probs, w_gate, w_up, w_down)
    return routed_device(tokens, out_grad, routes, probs, w_gate, w_up, w_down)


def solution(mesh):
    in_specs = (
        P(("groups", "role", "ep"), "tp"),
        P(("groups", "role", "ep"), "tp"),
        P(("groups", "role", "ep"), None),
        P(("groups", "role", "ep"), None),
        P(("role", "ep"), None, "tp"),
        P(("role", "ep"), None, "tp"),
        P(("role", "ep"), "tp", None),
    )
    out_specs = (
        P(("groups", "role", "ep"), "tp"),
        P(("groups", "role", "ep"), None),
        P(("groups", "role", "ep"), None, "tp"),
        P(("groups", "role", "ep"), None, "tp"),
        P(("groups", "role", "ep"), "tp", None),
    )
    return jax.shard_map(
        per_device, mesh=mesh, in_specs=in_specs, out_specs=out_specs, check_vma=False
    )
```

```python
import functools
import math

import jax
import jax.numpy as jnp
from jax import lax
from jax.experimental import pallas as pl
from jax.experimental.pallas import tpu as pltpu
from jax.sharding import PartitionSpec as P


def pad_rows(array):
    return jnp.concatenate([array, jnp.zeros((1, array.shape[1]), array.dtype)], 0)


def routed_device(tokens, out_grad, routes, probs, w_gate, w_up, w_down):
    owners = lax.axis_size(("role", "ep"))
    tok_rows, top_count = routes.shape
    width_full = w_gate.shape[1]
    part_width = w_gate.shape[2]
    capacity = min(tok_rows, tok_rows * top_count * 9 // (8 * owners))
    entry_total = tok_rows * top_count
    routes_flat = routes.reshape(-1)
    onehot = (routes_flat[:, None] == jnp.arange(owners, dtype=jnp.int32)[None, :]).astype(
        jnp.int32
    )
    before = jnp.cumsum(onehot, axis=0) - onehot
    slot_index = jnp.sum(before * onehot, axis=1)
    target = routes_flat * capacity + slot_index
    row_count = owners * capacity
    entry_of_slot = (
        jnp.full((row_count,), entry_total, jnp.int32)
        .at[target]
        .set(jnp.arange(entry_total, dtype=jnp.int32))
    )
    token_of_slot = entry_of_slot // top_count
    padded_prob = jnp.concatenate([probs.reshape(-1), jnp.zeros((1,), probs.dtype)], 0)
    send_prob = padded_prob[entry_of_slot].reshape(owners, capacity)
    send_x = pad_rows(tokens)[token_of_slot]
    send_g = pad_rows(out_grad)[token_of_slot]
    slice_x, slice_g, recv_p = (
        lax.all_to_all(
            send_x.reshape(owners, capacity, tokens.shape[1]),
            ("role", "ep"),
            split_axis=0,
            concat_axis=0,
            tiled=True,
        ),
        lax.all_to_all(
            send_g.reshape(owners, capacity, tokens.shape[1]),
            ("role", "ep"),
            split_axis=0,
            concat_axis=0,
            tiled=True,
        ),
        lax.all_to_all(send_prob, ("role", "ep"), split_axis=0, concat_axis=0, tiled=True),
    )
    recv_x, recv_g = (
        lax.all_gather(slice_x, "tp", axis=2, tiled=True),
        lax.all_gather(slice_g, "tp", axis=2, tiled=True),
    )
    rows_x = recv_x.reshape(row_count, width_full)
    rows_g = recv_g.reshape(row_count, width_full)
    weight_p = recv_p.reshape(row_count, 1).astype(jnp.float32)
    gate_up = jnp.concatenate([w_gate[0], w_up[0]], 1)
    down_shard = w_down[0]
    both_rows = jnp.dot(rows_x, gate_up, preferred_element_type=jnp.float32)
    gate_rows = both_rows[:, :part_width]
    up_rows = both_rows[:, part_width:]
    sigmoid_gate = jax.nn.sigmoid(gate_rows)
    activated = gate_rows * sigmoid_gate
    hidden = activated * up_rows
    back_rows = lax.dot_general(
        rows_g, down_shard, (((1,), (1,)), ((), ())), preferred_element_type=jnp.float32
    )
    scores = lax.psum(jnp.sum(hidden * back_rows, axis=1), "tp")
    hidden_grad = weight_p * back_rows
    d_gate_rows = (
        hidden_grad * up_rows * sigmoid_gate * (1.0 + gate_rows * (1.0 - sigmoid_gate))
    ).astype(jnp.bfloat16)
    d_up_rows = (hidden_grad * activated).astype(jnp.bfloat16)
    d_both = jnp.concatenate([d_gate_rows, d_up_rows], 1)
    scaled = (weight_p * hidden).astype(jnp.bfloat16)
    grad_down = lax.dot_general(
        scaled, rows_g, (((0,), (0,)), ((), ())), preferred_element_type=jnp.float32
    )
    grad_both = lax.dot_general(
        rows_x, d_both, (((0,), (0,)), ((), ())), preferred_element_type=jnp.float32
    )
    grad_gate = grad_both[:, :part_width]
    grad_up = grad_both[:, part_width:]
    partial_low = lax.dot_general(
        d_both, gate_up, (((1,), (1,)), ((), ())), preferred_element_type=jnp.float32
    ).astype(jnp.bfloat16)
    home_s = lax.all_to_all(
        scores.reshape(owners, capacity), ("role", "ep"), split_axis=0, concat_axis=0, tiled=True
    )
    summed = lax.psum_scatter(
        partial_low.reshape(owners, capacity, width_full), "tp", scatter_dimension=2, tiled=True
    ).astype(jnp.float32)
    summed_low = summed.astype(jnp.bfloat16)
    home_x = lax.all_to_all(summed_low, ("role", "ep"), split_axis=0, concat_axis=0, tiled=True)
    slice_width = summed.shape[2]
    route_rows = home_x.reshape(row_count, slice_width).astype(jnp.float32)
    d_tok = (
        jnp.zeros((tok_rows + 1, slice_width), jnp.float32)
        .at[token_of_slot]
        .add(route_rows)[:tok_rows]
    )
    d_probs = home_s.reshape(-1)[target].reshape(tok_rows, top_count)
    return (
        d_tok.astype(jnp.bfloat16),
        d_probs,
        grad_gate.astype(jnp.bfloat16)[None],
        grad_up.astype(jnp.bfloat16)[None],
        grad_down.astype(jnp.bfloat16)[None],
    )


def slot_capacity(tok_rows, top_count, owners):
    return min(tok_rows, tok_rows * top_count * 9 // (8 * owners))


LOOSE = pl.BlockSpec(memory_space=pl.ANY)


def weights_kernel(tp_ref, wg_ref, wu_ref, wd_ref, both_ref, down_ref):
    part = wg_ref.shape[2]
    both_ref[:, :part] = wg_ref[0]
    both_ref[:, part:] = wu_ref[0]
    down_ref[...] = wd_ref[0]


def weights_call(which, w_gate, w_up, w_down):
    _, width, part = w_gate.shape
    half = width // 2

    def place(i, w):
        return (i + w[0]) % 2

    return pl.pallas_call(
        weights_kernel,
        grid_spec=pltpu.PrefetchScalarGridSpec(
            num_scalar_prefetch=1,
            grid=(2,),
            in_specs=[
                pl.BlockSpec((1, half, part), lambda i, w: (0, place(i, w), 0)),
                pl.BlockSpec((1, half, part), lambda i, w: (0, place(i, w), 0)),
                pl.BlockSpec((1, part, half), lambda i, w: (0, 0, place(i, w))),
            ],
            out_specs=[
                pl.BlockSpec((half, 2 * part), lambda i, w: (i, 0)),
                pl.BlockSpec((part, half), lambda i, w: (0, i)),
            ],
        ),
        out_shape=[
            jax.ShapeDtypeStruct((width, 2 * part), jnp.bfloat16),
            jax.ShapeDtypeStruct((part, width), jnp.bfloat16),
        ],
        compiler_params=pltpu.CompilerParams(vmem_limit_bytes=30 << 20),
        cost_estimate=pl.CostEstimate(flops=0, bytes_accessed=12 * width * part, transcendentals=0),
        name="weights",
    )(which, w_gate, w_up, w_down)


def rows_kernel(count, ways, capacity, slots, where_ref, *refs):
    weights_in, units_in, tables_in = refs[:4], refs[4 : 4 + 4 * count], refs[4 + 4 * count : 4 + 5 * count]
    leaves = 1 + max(way[0] for way in ways.values())
    refs = refs[len(refs) - 17 - leaves :]
    outs, packets, refs = refs[:2], refs[2 : 2 + leaves], refs[2 + leaves :]
    x_all, g_all, tables, wgu0, wgu1, wd0, wd1, xc, gc, both, scaled, piece, unit_sems, weight_sems = refs[:14]
    out_sems = refs[14]
    half, tok = x_all.shape[3], x_all.shape[2] // 2
    part = scaled.shape[2]
    owners = tables.shape[2]
    wgu, wd = (wgu0, wgu1), (wd0, wd1)

    x_copies, g_copies = [], []
    for index, unit in enumerate(units_in):
        chunk, y, x = index // 4, index // 2 % 2, index % 2
        rows = pl.ds(y * tok, tok)
        x_copies.append(pltpu.make_async_copy(unit.at[pl.ds(0, tok)], x_all.at[chunk, x, rows], unit_sems.at[0, index]))
        g_copies.append(pltpu.make_async_copy(unit.at[pl.ds(tok, tok)], g_all.at[chunk, x, rows], unit_sems.at[1, index]))
    t_copies = [
        pltpu.make_async_copy(table, tables.at[chunk], unit_sems.at[2, chunk]) for chunk, table in enumerate(tables_in)
    ]
    weight_copies = [
        pltpu.make_async_copy(source, target, weight_sems.at[index])
        for index, (source, target) in enumerate(zip(weights_in, (wgu0, wgu1, wd0, wd1)))
    ]
    for copy in t_copies + x_copies + weight_copies[:2] + g_copies + weight_copies[2:]:
        copy.start()
    leaving = []

    def leave(source, target):
        copy = pltpu.make_async_copy(source, target, out_sems.at[len(leaving)])
        copy.start()
        leaving.append(copy)

    def leave_rows(held, start):
        for expert in range(2):
            leave(held.at[expert], outs[expert].at[:, pl.ds(start, held.shape[2])])

    def dot(a, b, dims):
        return lax.dot_general(a, b, (dims, ((), ())), preferred_element_type=jnp.float32)

    for copy in t_copies:
        copy.wait()
    earlier = lax.broadcasted_iota(jnp.int32, (tok, tok), 0) < lax.broadcasted_iota(jnp.int32, (tok, tok), 1)
    earlier = earlier.astype(jnp.bfloat16)
    number = lax.broadcasted_iota(jnp.int32, (slots, tok), 0).astype(jnp.float32)
    names = lax.broadcasted_iota(jnp.int32, (owners, tok), 0)
    picks, low_picks, probs = {}, {}, {}
    for chunk in range(count):
        found = []
        for y in range(2):
            table = tables[chunk, y].astype(jnp.float32)
            rank = dot((table >= 0.0).astype(jnp.bfloat16), earlier, ((1,), (0,))) + float(y * capacity)
            found.append((table, jnp.where(table >= 0.0, rank, -1.0)))
        for expert in range(2):
            mine = names == where_ref[expert]
            halves, prob = [], None
            for table, rank in found:
                weight = jnp.sum(jnp.where(mine, table, 0.0), axis=0, keepdims=True)
                slot = jnp.sum(jnp.where(mine, rank, 0.0), axis=0, keepdims=True)
                halves.append((number == slot).astype(jnp.float32))
                term = jnp.sum(halves[-1] * weight, axis=1, keepdims=True)
                prob = term if prob is None else prob + term
            picks[chunk, expert] = halves
            low_picks[chunk, expert] = jnp.concatenate(halves, 1).astype(jnp.bfloat16)
            probs[chunk, expert] = prob
    spans = [pl.ds(chunk * slots, slots) for chunk in range(count)]
    sides = [slice(side * half, (side + 1) * half) for side in range(2)]

    def gather(copies, source, target):
        for chunk in range(count):
            for copy in copies[4 * chunk : 4 * chunk + 4]:
                copy.wait()
            both_picks = jnp.concatenate([low_picks[chunk, expert] for expert in range(2)], 0)
            for side in range(2):
                rows = dot(both_picks, source[chunk, side], ((1,), (0,))).astype(jnp.bfloat16)
                for expert in range(2):
                    target[expert, spans[chunk], sides[side]] = rows[expert * slots : (expert + 1) * slots]

    gather(x_copies, x_all, xc)
    leave_rows(xc, 0)
    rows = []
    for expert in range(2):
        weight_copies[expert].wait()
        rows.append(dot(xc[expert], wgu[expert][...], ((1,), (0,))))
    gather(g_copies, g_all, gc)
    leave_rows(gc, 2 * half)
    scores = []
    for expert in range(2):
        weight_copies[2 + expert].wait()
        back = dot(gc[expert], wd[expert][...], ((1,), (1,)))
        gate, up = rows[expert][:, :part], rows[expert][:, part:]
        sig = jax.nn.sigmoid(gate)
        act = gate * sig
        hidden = act * up
        scores.append(jnp.sum(hidden * back, axis=1, keepdims=True))
        prob = jnp.concatenate([probs[chunk, expert] for chunk in range(count)], 0)
        hgrad = prob * back
        both[expert, :, :part] = (hgrad * up * sig * (1.0 + gate * (1.0 - sig))).astype(jnp.bfloat16)
        both[expert, :, part:] = (hgrad * act).astype(jnp.bfloat16)
        scaled[expert] = (prob * hidden).astype(jnp.bfloat16)
    leave_rows(both, 4 * half)
    leave_rows(scaled, 4 * half + 2 * part)

    names = lax.broadcasted_iota(jnp.int32, (owners, half), 0)
    column = lax.broadcasted_iota(jnp.int32, (owners, half), 1) // (2 * tok)
    for chunk in range(count):
        for y in range(2):
            extra = jnp.zeros((owners, half), jnp.float32)
            for expert in range(2):
                part_scores = scores[expert][chunk * slots : (chunk + 1) * slots]
                line = jnp.sum(picks[chunk, expert][y] * part_scores, axis=0, keepdims=True)
                high = line.astype(jnp.bfloat16).astype(jnp.float32)
                line = jnp.concatenate([high, line - high] * (half // (2 * tok)), 1)
                extra = extra + jnp.where((names == where_ref[expert]) & (column == where_ref[2]), line, 0.0)
            for side in range(2):
                piece[chunk, side, y, tok:] = extra.astype(jnp.bfloat16)
    for side in (1, 0):
        low = [
            dot(both[expert], wgu[expert][sides[side], :], ((1,), (1,))).astype(jnp.bfloat16) for expert in range(2)
        ]
        for chunk in range(count):
            total = None
            for expert in range(2):
                term = dot(low_picks[chunk, expert], low[expert][chunk * slots : (chunk + 1) * slots], ((0,), (0,)))
                total = term if total is None else total + term
            for y in range(2):
                piece[chunk, side, y, :tok] = total[y * tok : (y + 1) * tok].astype(jnp.bfloat16)
                number, slot = ways[chunk, y, side]
                leave(piece.at[chunk, side, y], packets[number].at[slot])
    for copy in leaving:
        copy.wait()


def rows_call(items, owners, capacity, slots, where, weights, units, tables, after):
    count = len(tables)
    ways = {block: (number, slot) for number, blocks in enumerate(items) for slot, block in enumerate(blocks)}
    tok, half = units[0].shape[0] // 2, units[0].shape[1]
    part, width = weights[2].shape
    widths = (width, width, 2 * part, part)
    packet = (tok + owners, half)
    return pl.pallas_call(
        functools.partial(rows_kernel, count, ways, capacity, slots),
        grid_spec=pltpu.PrefetchScalarGridSpec(
            num_scalar_prefetch=1,
            grid=(1,),
            in_specs=[LOOSE] * (4 + 5 * count + len(after)),
            out_specs=[LOOSE] * (2 + len(items)),
            scratch_shapes=[pltpu.VMEM((count, 2, 2 * tok, half), jnp.bfloat16)] * 2
            + [pltpu.VMEM((count, 2, owners, tok), jnp.bfloat16)]
            + [pltpu.VMEM((width, 2 * part), jnp.bfloat16)] * 2
            + [pltpu.VMEM((part, width), jnp.bfloat16)] * 2
            + [pltpu.VMEM((2, count * slots, size), jnp.bfloat16) for size in widths]
            + [
                pltpu.VMEM((count, 2, 2) + packet, jnp.bfloat16),
                pltpu.SemaphoreType.DMA((3, 4 * count)),
                pltpu.SemaphoreType.DMA((4,)),
                pltpu.SemaphoreType.DMA((8 + 4 * count,)),
            ],
        ),
        out_shape=[jax.ShapeDtypeStruct((count * slots, sum(widths)), jnp.bfloat16)] * 2
        + [jax.ShapeDtypeStruct((len(blocks),) + packet, jnp.bfloat16) for blocks in items],
        compiler_params=pltpu.CompilerParams(vmem_limit_bytes=30 << 20),
        cost_estimate=pl.CostEstimate(
            flops=count * (20 * slots * width * part + 24 * slots * tok * width),
            bytes_accessed=count * 16 * tok * width + 12 * width * part,
            transcendentals=2 * count * slots * part,
        ),
        name="rows",
    )(where, *weights, *units, *tables, *after)


def grads_kernel(count, wide, deep, blocks, tp_ref, *refs):
    sources, outs = refs[:count], refs[count:-4]
    wide_all, deep_all, wide_sems, deep_sems = refs[-4:]
    starts = [sum(source.shape[0] for source in sources[:index]) for index in range(count)]
    size = wide_all.shape[2]
    block = pl.program_id(0)

    def copies(column):
        return [
            pltpu.make_async_copy(
                source.at[:, pl.ds(wide + column * size, size)],
                wide_all.at[column, pl.ds(starts[index], source.shape[0])],
                wide_sems.at[column, index],
            )
            for index, source in enumerate(sources)
        ]

    @pl.when(block == 0)
    def _():
        deep_copies = [
            pltpu.make_async_copy(
                source.at[:, pl.ds(deep, deep_all.shape[1])],
                deep_all.at[pl.ds(starts[index], source.shape[0])],
                deep_sems.at[index],
            )
            for index, source in enumerate(sources)
        ]
        for copy in deep_copies:
            copy.start()
        for column in range(blocks):
            for copy in copies(column):
                copy.start()
        for copy in deep_copies:
            copy.wait()

    for column in range(blocks):

        @pl.when(block == column)
        def _(column=column):
            for copy in copies(column):
                copy.wait()

    dims = (((0,), (0,)), ((), ()))
    if len(outs) == 2:
        part = outs[0].shape[2]
        both = lax.dot_general(wide_all[block], deep_all[...], dims, preferred_element_type=jnp.float32)
        outs[0][0] = both[:, :part].astype(jnp.bfloat16)
        outs[1][0] = both[:, part:].astype(jnp.bfloat16)
    else:
        down = lax.dot_general(deep_all[...], wide_all[block], dims, preferred_element_type=jnp.float32)
        outs[0][0] = down.astype(jnp.bfloat16)


def grads_call(which, packed, width, part, down):
    rows, count = sum(item.shape[0] for item in packed), len(packed)
    step = math.gcd(width // 2, 512)
    per = width // 2 // step
    deep = part if down else 2 * part

    def place(i, w):
        return (i + w[0] * per) % (2 * per)

    if down:
        specs = [pl.BlockSpec((1, part, step), lambda i, w: (0, 0, place(i, w)))]
        shapes = [(1, part, width)]
    else:
        specs = [pl.BlockSpec((1, step, part), lambda i, w: (0, place(i, w), 0))] * 2
        shapes = [(1, width, part)] * 2
    starts = (width, 2 * width + 2 * part) if down else (0, 2 * width)
    return pl.pallas_call(
        functools.partial(grads_kernel, count, *starts, 2 * per),
        grid_spec=pltpu.PrefetchScalarGridSpec(
            num_scalar_prefetch=1,
            grid=(2 * per,),
            in_specs=[LOOSE] * count,
            out_specs=specs,
            scratch_shapes=[
                pltpu.VMEM((2 * per, rows, step), jnp.bfloat16),
                pltpu.VMEM((rows, deep), jnp.bfloat16),
                pltpu.SemaphoreType.DMA((2 * per, count)),
                pltpu.SemaphoreType.DMA((count,)),
            ],
        ),
        out_shape=[jax.ShapeDtypeStruct(shape, jnp.bfloat16) for shape in shapes],
        compiler_params=pltpu.CompilerParams(vmem_limit_bytes=20 << 20),
        cost_estimate=pl.CostEstimate(
            flops=2 * rows * width * deep, bytes_accessed=2 * rows * (width + deep), transcendentals=0
        ),
        name="grads",
    )(which, *packed)


def dense_device(tokens, out_grad, routes, probs, w_gate, w_up, w_down):
    owners = lax.axis_size(("role", "ep"))
    ep = lax.axis_size("ep")
    n_y = 2
    n_z = ep // n_y
    tok_rows, half = tokens.shape
    capacity = slot_capacity(tok_rows, routes.shape[1], owners)
    slots = -(-n_y * capacity // 16) * 16
    role, place, which = lax.axis_index("role"), lax.axis_index("ep"), lax.axis_index("tp")

    def over_x(array):
        return lax.ppermute(array, "tp", [(0, 1), (1, 0)])

    def over_role(array):
        return lax.ppermute(array, "role", [(0, 1), (1, 0)])

    def over_y(array):
        return lax.ppermute(array, "ep", [(i, i + 1 - 2 * (i % n_y)) for i in range(ep)])

    def over_z(array, shift):
        return lax.ppermute(array, "ep", [(i, (i + shift * n_y) % ep) for i in range(ep)])

    def tied(values, others):
        return lax.optimization_barrier((list(values), list(others)))[0]

    last = n_z - 1
    routes_in = []
    for z in range(n_z):
        shift = -1 if z == last and z > 1 else 1
        if z:
            routes_in.append(((z, 0, 0), (0 if z in (1, last) else z - 1, 0, 0), functools.partial(over_z, shift=shift)))
        routes_in.append(((z, 1, 0), (z, 0, 0), over_y))
        routes_in.append(((z, 0, 1), (z, 0, 0), over_x))
        if z == 0:
            routes_in.append(((z, 1, 1), (z, 1, 0), over_x))
        elif z in (1, last):
            routes_in.append(((z, 1, 1), (0, 1, 1), functools.partial(over_z, shift=shift)))
        else:
            routes_in.append(((z, 1, 1), (z, 0, 1), over_y))
    routes_in.sort(key=lambda item: (item[0][0] % 2 if item[2] in (over_x, over_y) else 0, sum(item[0][1:])))

    rounds, waiting, there = [], list(routes_in), {(0, 0, 0)}
    while waiting:
        moves = {}
        for item in waiting:
            axis = item[2] if item[2] in (over_x, over_y) else over_z
            if item[1] in there and axis not in moves:
                moves[axis] = item
        rounds.append(list(moves.values()))
        there |= {item[0] for item in rounds[-1]}
        waiting = [item for item in waiting if item[0] not in there]

    which_ref = which.reshape(1).astype(jnp.int32)
    where = jnp.stack([role * ep + place, (1 - role) * ep + place, which]).astype(jnp.int32)
    both_w, down_w = weights_call(which_ref, w_gate, w_up, w_down)
    width, part = both_w.shape[0], down_w.shape[0]

    def rows_of(steps, items, after):
        four = [units[z, y, x] for z in steps for y in range(2) for x in range(2)]
        return rows_call(items, owners, capacity, slots, where, weights, four, [tables[z] for z in steps], after)

    units = {(0, 0, 0): jnp.concatenate([tokens, out_grad], 0)}
    settled = dict(units)
    for number, moves in enumerate(rounds):
        arrived = {target: move(settled[source]) for target, source, move in moves}
        units.update(arrived)
        settled.update(arrived)
        extra = []
        if number == 0:
            extra = [both_w, down_w]
            both_w, down_w, routes, probs = tied([both_w, down_w, routes, probs], arrived.values())
            weights = (both_w, over_role(both_w), down_w, over_role(down_w))
            chosen = routes[:, :, None] == jnp.arange(owners, dtype=jnp.int32)
            table = jnp.sum(jnp.where(chosen, probs[:, :, None].astype(jnp.float32) + 1.0, 0.0), axis=1) - 1.0
            table = table.astype(jnp.bfloat16).T
            table = jnp.stack([table, over_y(table)])
        if number == 1:
            (table,) = tied([table], arrived.values())
            tables = [over_z(table, z) if z else table for z in range(n_z)]
        if number == 2:
            mine_0, other_0, near, side_0, far, y_0 = rows_of(
                [0], [[(0, 0, 0)], [(0, 0, 1)], [(0, 1, 1)], [(0, 1, 0)]], []
            )
            extra = [mine_0]
        names = list(settled)
        settled = dict(zip(names, tied([settled[item] for item in names], extra)))

    def total(*blocks):
        return sum(block.astype(jnp.float32) for block in blocks).astype(jnp.bfloat16)

    items = [[(1, 1, 1)], [(1, 0, 1), (0, 0, 1)], [(0, 1, 0)], [(0, 1, 1)], [(0, 0, 0)], [(1, 0, 0)], [(1, 1, 0)]]
    mine_1, other_1, x_2, x_12, y_1, z_1, keep_1, keep_2, keep_2y = rows_of([1, 2], items, [])
    other_1, x_2, x_12, y_1, z_1 = tied([other_1, x_2, x_12, y_1, z_1], arrived.values())
    from_x2, from_y1, from_z1 = over_x(x_2), over_y(y_1), over_z(z_1, -1)
    from_x12 = over_x(x_12)
    items = [[(0, 0, 1)], [(0, 1, 0)], [(0, 1, 1)], [(0, 0, 0)]]
    mine_3, other_3, x_3, y_3, z_3, keep_3 = rows_of([3], items, [mine_1])
    mine_3, other_3, x_3, y_3, z_3, keep_2y = tied(
        [mine_3, other_3, x_3, y_3, z_3, keep_2y], [from_x2, from_y1, from_z1]
    )
    from_z3, from_x3, from_y2, from_y3 = over_z(z_3, 1), over_x(x_3), over_y(total(keep_2y, from_x2)), over_y(y_3)
    packed = [mine_0, over_role(other_0), mine_1, over_role(other_1), mine_3, over_role(other_3)]
    d_gate, d_up = grads_call(which_ref, packed, width, part, False)
    from_z3, from_x12, from_y2 = tied([from_z3, from_x12, from_y2], [d_gate, d_up])
    from_far = over_y(total(far, from_z1, from_z3))
    from_z2 = over_z(total(keep_2, from_x12[:1], from_y2), 1)
    home_1 = over_z(total(keep_1, from_x12[1:], from_y1), -1)
    (d_down,) = grads_call(which_ref, packed, width, part, True)
    from_x3, from_y3, from_z2, y_0 = tied([from_x3, from_y3, from_z2, y_0], [d_down])
    from_y0 = over_y(y_0)
    home_3 = over_z(total(keep_3, from_x3, from_y3, from_z2), 1)
    from_x0 = over_x(total(side_0, from_far))
    home = (near, from_y0, home_1, home_3, from_x0)
    d_tok = sum(block[0, :tok_rows].astype(jnp.float32) for block in home).astype(jnp.bfloat16)
    home = sum(block[0, tok_rows:, : 4 * tok_rows].astype(jnp.float32) for block in home)
    score = jnp.sum(home.reshape(owners, 4, tok_rows), axis=1).T
    d_probs = jnp.sum(jnp.where(chosen, score[:, None, :], 0.0), axis=2)
    return d_tok, d_probs, d_gate, d_up, d_down


def per_device(tokens, out_grad, routes, probs, w_gate, w_up, w_down):
    owners = lax.axis_size(("role", "ep"))
    tok_rows, top_count = routes.shape
    paired = lax.axis_size("tp") == 2 and lax.axis_size("role") == 2 and lax.axis_size("ep") == 8
    if paired and 2 * slot_capacity(tok_rows, top_count, owners) >= tok_rows:
        return dense_device(tokens, out_grad, routes, probs, w_gate, w_up, w_down)
    return routed_device(tokens, out_grad, routes, probs, w_gate, w_up, w_down)


def solution(mesh):
    in_specs = (
        P(("groups", "role", "ep"), "tp"),
        P(("groups", "role", "ep"), "tp"),
        P(("groups", "role", "ep"), None),
        P(("groups", "role", "ep"), None),
        P(("role", "ep"), None, "tp"),
        P(("role", "ep"), None, "tp"),
        P(("role", "ep"), "tp", None),
    )
    out_specs = (
        P(("groups", "role", "ep"), "tp"),
        P(("groups", "role", "ep"), None),
        P(("groups", "role", "ep"), None, "tp"),
        P(("groups", "role", "ep"), None, "tp"),
        P(("groups", "role", "ep"), "tp", None),
    )
    return jax.shard_map(
        per_device, mesh=mesh, in_specs=in_specs, out_specs=out_specs, check_vma=False
    )
```

```python
import functools
import math

import jax
import jax.numpy as jnp
from jax import lax
from jax.experimental import pallas as pl
from jax.experimental.pallas import tpu as pltpu
from jax.sharding import PartitionSpec as P


def pad_rows(array):
    return jnp.concatenate([array, jnp.zeros((1, array.shape[1]), array.dtype)], 0)


def routed_device(tokens, out_grad, routes, probs, w_gate, w_up, w_down):
    owners = lax.axis_size(("role", "ep"))
    tok_rows, top_count = routes.shape
    width_full = w_gate.shape[1]
    part_width = w_gate.shape[2]
    capacity = min(tok_rows, tok_rows * top_count * 9 // (8 * owners))
    entry_total = tok_rows * top_count
    routes_flat = routes.reshape(-1)
    onehot = (routes_flat[:, None] == jnp.arange(owners, dtype=jnp.int32)[None, :]).astype(
        jnp.int32
    )
    before = jnp.cumsum(onehot, axis=0) - onehot
    slot_index = jnp.sum(before * onehot, axis=1)
    target = routes_flat * capacity + slot_index
    row_count = owners * capacity
    entry_of_slot = (
        jnp.full((row_count,), entry_total, jnp.int32)
        .at[target]
        .set(jnp.arange(entry_total, dtype=jnp.int32))
    )
    token_of_slot = entry_of_slot // top_count
    padded_prob = jnp.concatenate([probs.reshape(-1), jnp.zeros((1,), probs.dtype)], 0)
    send_prob = padded_prob[entry_of_slot].reshape(owners, capacity)
    send_x = pad_rows(tokens)[token_of_slot]
    send_g = pad_rows(out_grad)[token_of_slot]
    slice_x, slice_g, recv_p = (
        lax.all_to_all(
            send_x.reshape(owners, capacity, tokens.shape[1]),
            ("role", "ep"),
            split_axis=0,
            concat_axis=0,
            tiled=True,
        ),
        lax.all_to_all(
            send_g.reshape(owners, capacity, tokens.shape[1]),
            ("role", "ep"),
            split_axis=0,
            concat_axis=0,
            tiled=True,
        ),
        lax.all_to_all(send_prob, ("role", "ep"), split_axis=0, concat_axis=0, tiled=True),
    )
    recv_x, recv_g = (
        lax.all_gather(slice_x, "tp", axis=2, tiled=True),
        lax.all_gather(slice_g, "tp", axis=2, tiled=True),
    )
    rows_x = recv_x.reshape(row_count, width_full)
    rows_g = recv_g.reshape(row_count, width_full)
    weight_p = recv_p.reshape(row_count, 1).astype(jnp.float32)
    gate_up = jnp.concatenate([w_gate[0], w_up[0]], 1)
    down_shard = w_down[0]
    both_rows = jnp.dot(rows_x, gate_up, preferred_element_type=jnp.float32)
    gate_rows = both_rows[:, :part_width]
    up_rows = both_rows[:, part_width:]
    sigmoid_gate = jax.nn.sigmoid(gate_rows)
    activated = gate_rows * sigmoid_gate
    hidden = activated * up_rows
    back_rows = lax.dot_general(
        rows_g, down_shard, (((1,), (1,)), ((), ())), preferred_element_type=jnp.float32
    )
    scores = lax.psum(jnp.sum(hidden * back_rows, axis=1), "tp")
    hidden_grad = weight_p * back_rows
    d_gate_rows = (
        hidden_grad * up_rows * sigmoid_gate * (1.0 + gate_rows * (1.0 - sigmoid_gate))
    ).astype(jnp.bfloat16)
    d_up_rows = (hidden_grad * activated).astype(jnp.bfloat16)
    d_both = jnp.concatenate([d_gate_rows, d_up_rows], 1)
    scaled = (weight_p * hidden).astype(jnp.bfloat16)
    grad_down = lax.dot_general(
        scaled, rows_g, (((0,), (0,)), ((), ())), preferred_element_type=jnp.float32
    )
    grad_both = lax.dot_general(
        rows_x, d_both, (((0,), (0,)), ((), ())), preferred_element_type=jnp.float32
    )
    grad_gate = grad_both[:, :part_width]
    grad_up = grad_both[:, part_width:]
    partial_low = lax.dot_general(
        d_both, gate_up, (((1,), (1,)), ((), ())), preferred_element_type=jnp.float32
    ).astype(jnp.bfloat16)
    home_s = lax.all_to_all(
        scores.reshape(owners, capacity), ("role", "ep"), split_axis=0, concat_axis=0, tiled=True
    )
    summed = lax.psum_scatter(
        partial_low.reshape(owners, capacity, width_full), "tp", scatter_dimension=2, tiled=True
    ).astype(jnp.float32)
    summed_low = summed.astype(jnp.bfloat16)
    home_x = lax.all_to_all(summed_low, ("role", "ep"), split_axis=0, concat_axis=0, tiled=True)
    slice_width = summed.shape[2]
    route_rows = home_x.reshape(row_count, slice_width).astype(jnp.float32)
    d_tok = (
        jnp.zeros((tok_rows + 1, slice_width), jnp.float32)
        .at[token_of_slot]
        .add(route_rows)[:tok_rows]
    )
    d_probs = home_s.reshape(-1)[target].reshape(tok_rows, top_count)
    return (
        d_tok.astype(jnp.bfloat16),
        d_probs,
        grad_gate.astype(jnp.bfloat16)[None],
        grad_up.astype(jnp.bfloat16)[None],
        grad_down.astype(jnp.bfloat16)[None],
    )


def slot_capacity(tok_rows, top_count, owners):
    return min(tok_rows, tok_rows * top_count * 9 // (8 * owners))


LOOSE = pl.BlockSpec(memory_space=pl.ANY)


def weights_kernel(tp_ref, wg_ref, wu_ref, wd_ref, both_ref, down_ref):
    part = wg_ref.shape[2]
    both_ref[:, :part] = wg_ref[0]
    both_ref[:, part:] = wu_ref[0]
    down_ref[...] = wd_ref[0]


def weights_call(which, w_gate, w_up, w_down):
    _, width, part = w_gate.shape
    half = width // 2

    def place(i, w):
        return (i + w[0]) % 2

    return pl.pallas_call(
        weights_kernel,
        grid_spec=pltpu.PrefetchScalarGridSpec(
            num_scalar_prefetch=1,
            grid=(2,),
            in_specs=[
                pl.BlockSpec((1, half, part), lambda i, w: (0, place(i, w), 0)),
                pl.BlockSpec((1, half, part), lambda i, w: (0, place(i, w), 0)),
                pl.BlockSpec((1, part, half), lambda i, w: (0, 0, place(i, w))),
            ],
            out_specs=[
                pl.BlockSpec((half, 2 * part), lambda i, w: (i, 0)),
                pl.BlockSpec((part, half), lambda i, w: (0, i)),
            ],
        ),
        out_shape=[
            jax.ShapeDtypeStruct((width, 2 * part), jnp.bfloat16),
            jax.ShapeDtypeStruct((part, width), jnp.bfloat16),
        ],
        compiler_params=pltpu.CompilerParams(vmem_limit_bytes=16 << 20),
        cost_estimate=pl.CostEstimate(flops=0, bytes_accessed=12 * width * part, transcendentals=0),
        name="weights",
    )(which, w_gate, w_up, w_down)


def join_kernel(top_ref, bottom_ref, out_ref, sems):
    rows = top_ref.shape[0]
    copies = [
        pltpu.make_async_copy(top_ref, out_ref.at[pl.ds(0, rows)], sems.at[0]),
        pltpu.make_async_copy(bottom_ref, out_ref.at[pl.ds(rows, rows)], sems.at[1]),
    ]
    for copy in copies:
        copy.start()
    for copy in copies:
        copy.wait()


def join_call(top, bottom):
    rows, columns = top.shape
    return pl.pallas_call(
        join_kernel,
        in_specs=[LOOSE] * 2,
        out_specs=LOOSE,
        out_shape=jax.ShapeDtypeStruct((2 * rows, columns), top.dtype),
        scratch_shapes=[pltpu.SemaphoreType.DMA((2,))],
        compiler_params=pltpu.CompilerParams(vmem_limit_bytes=8 << 20),
        cost_estimate=pl.CostEstimate(flops=0, bytes_accessed=8 * rows * columns, transcendentals=0),
        name="join",
    )(top, bottom)


def rows_kernel(count, ways, capacity, slots, where_ref, *refs):
    weights_in, units_in, tables_in = refs[:4], refs[4 : 4 + 4 * count], refs[4 + 4 * count : 4 + 5 * count]
    leaves = 1 + max(way[0] for way in ways.values())
    refs = refs[len(refs) - 6 - leaves :]
    outs, packets, refs = refs[:2], refs[2 : 2 + leaves], refs[2 + leaves :]
    x_all, g_all, tables, unit_sems = refs
    half, tok = x_all.shape[3], x_all.shape[2] // 2
    part = weights_in[2].shape[0]
    owners = tables.shape[2]
    wgu, wd = weights_in[:2], weights_in[2:]

    x_copies, g_copies = [], []
    for index, unit in enumerate(units_in):
        chunk, y, x = index // 4, index // 2 % 2, index % 2
        rows = pl.ds(y * tok, tok)
        x_copies.append(pltpu.make_async_copy(unit.at[pl.ds(0, tok)], x_all.at[chunk, x, rows], unit_sems.at[0, index]))
        g_copies.append(pltpu.make_async_copy(unit.at[pl.ds(tok, tok)], g_all.at[chunk, x, rows], unit_sems.at[1, index]))
    t_copies = [
        pltpu.make_async_copy(table, tables.at[chunk], unit_sems.at[2, chunk]) for chunk, table in enumerate(tables_in)
    ]
    for copy in t_copies + x_copies + g_copies:
        copy.start()
    both_at, scaled_at = pl.ds(4 * half, 2 * part), pl.ds(4 * half + 2 * part, part)

    def dot(a, b, dims):
        return lax.dot_general(a, b, (dims, ((), ())), preferred_element_type=jnp.float32)

    for copy in t_copies:
        copy.wait()
    earlier = lax.broadcasted_iota(jnp.int32, (tok, tok), 0) < lax.broadcasted_iota(jnp.int32, (tok, tok), 1)
    earlier = earlier.astype(jnp.bfloat16)
    place = lax.broadcasted_iota(jnp.int32, (slots, tok), 0).astype(jnp.float32)
    names = lax.broadcasted_iota(jnp.int32, (owners, tok), 0)
    picks, low_picks, probs = {}, {}, {}
    for chunk in range(count):
        found = []
        for y in range(2):
            table = tables[chunk, y].astype(jnp.float32)
            rank = dot((table >= 0.0).astype(jnp.bfloat16), earlier, ((1,), (0,))) + float(y * capacity)
            found.append((table, jnp.where(table >= 0.0, rank, -1.0)))
        for expert in range(2):
            mine = names == where_ref[expert]
            halves, prob = [], None
            for table, rank in found:
                weight = jnp.sum(jnp.where(mine, table, 0.0), axis=0, keepdims=True)
                slot = jnp.sum(jnp.where(mine, rank, 0.0), axis=0, keepdims=True)
                halves.append((place == slot).astype(jnp.float32))
                term = jnp.sum(halves[-1] * weight, axis=1, keepdims=True)
                prob = term if prob is None else prob + term
            picks[chunk, expert] = halves
            low_picks[chunk, expert] = jnp.concatenate(halves, 1).astype(jnp.bfloat16)
            probs[chunk, expert] = prob
    spans = [pl.ds(chunk * slots, slots) for chunk in range(count)]
    sides = [slice(side * half, (side + 1) * half) for side in range(2)]

    def gather(copies, source, offset):
        for chunk in range(count):
            for copy in copies[4 * chunk : 4 * chunk + 4]:
                copy.wait()
            both_picks = jnp.concatenate([low_picks[chunk, expert] for expert in range(2)], 0)
            for side in range(2):
                rows = dot(both_picks, source[chunk, side], ((1,), (0,))).astype(jnp.bfloat16)
                for expert in range(2):
                    columns = pl.ds(offset + side * half, half)
                    outs[expert][spans[chunk], columns] = rows[expert * slots : (expert + 1) * slots]

    gather(x_copies, x_all, 0)
    rows = []
    for expert in range(2):
        rows.append(dot(outs[expert][:, : 2 * half], wgu[expert][...], ((1,), (0,))))
    gather(g_copies, g_all, 2 * half)
    scores = []
    for expert in range(2):
        back = dot(outs[expert][:, 2 * half : 4 * half], wd[expert][...], ((1,), (1,)))
        gate, up = rows[expert][:, :part], rows[expert][:, part:]
        sig = jax.nn.sigmoid(gate)
        act = gate * sig
        hidden = act * up
        scores.append(jnp.sum(hidden * back, axis=1, keepdims=True))
        prob = jnp.concatenate([probs[chunk, expert] for chunk in range(count)], 0)
        hgrad = prob * back
        d_gate = (hgrad * up * sig * (1.0 + gate * (1.0 - sig))).astype(jnp.bfloat16)
        outs[expert][:, both_at] = jnp.concatenate([d_gate, (hgrad * act).astype(jnp.bfloat16)], 1)
        outs[expert][:, scaled_at] = (prob * hidden).astype(jnp.bfloat16)

    names = lax.broadcasted_iota(jnp.int32, (owners, half), 0)
    column = lax.broadcasted_iota(jnp.int32, (owners, half), 1) // (2 * tok)
    for chunk in range(count):
        for y in range(2):
            extra = jnp.zeros((owners, half), jnp.float32)
            for expert in range(2):
                part_scores = scores[expert][chunk * slots : (chunk + 1) * slots]
                line = jnp.sum(picks[chunk, expert][y] * part_scores, axis=0, keepdims=True)
                high = line.astype(jnp.bfloat16).astype(jnp.float32)
                line = jnp.concatenate([high, line - high] * (half // (2 * tok)), 1)
                extra = extra + jnp.where((names == where_ref[expert]) & (column == where_ref[2]), line, 0.0)
            for side in range(2):
                number, slot = ways[chunk, y, side]
                packets[number][slot, tok:] = extra.astype(jnp.bfloat16)
    for side in (1, 0):
        low = [
            dot(outs[expert][:, both_at], wgu[expert][sides[side], :], ((1,), (1,))).astype(jnp.bfloat16) for expert in range(2)
        ]
        for chunk in range(count):
            total = None
            for expert in range(2):
                term = dot(low_picks[chunk, expert], low[expert][chunk * slots : (chunk + 1) * slots], ((0,), (0,)))
                total = term if total is None else total + term
            for y in range(2):
                number, slot = ways[chunk, y, side]
                packets[number][slot, :tok] = total[y * tok : (y + 1) * tok].astype(jnp.bfloat16)


def rows_call(items, owners, capacity, slots, where, weights, units, tables, after):
    count = len(tables)
    ways = {block: (number, slot) for number, blocks in enumerate(items) for slot, block in enumerate(blocks)}
    tok, half = units[0].shape[0] // 2, units[0].shape[1]
    part, width = weights[2].shape
    widths = (width, width, 2 * part, part)
    packet = (tok + owners, half)
    return pl.pallas_call(
        functools.partial(rows_kernel, count, ways, capacity, slots),
        grid_spec=pltpu.PrefetchScalarGridSpec(
            num_scalar_prefetch=1,
            grid=(1,),
            in_specs=[pl.BlockSpec(memory_space=pltpu.VMEM)] * 4 + [LOOSE] * (5 * count + len(after)),
            out_specs=[pl.BlockSpec(memory_space=pltpu.VMEM)] * (2 + len(items)),
            scratch_shapes=[pltpu.VMEM((count, 2, 2 * tok, half), jnp.bfloat16)] * 2
            + [pltpu.VMEM((count, 2, owners, tok), jnp.bfloat16)]
            + [pltpu.SemaphoreType.DMA((3, 4 * count))],
        ),
        out_shape=[pltpu.VMEM((count * slots, sum(widths)), jnp.bfloat16)] * 2
        + [pltpu.VMEM((len(blocks),) + packet, jnp.bfloat16) for blocks in items],
        compiler_params=pltpu.CompilerParams(vmem_limit_bytes=16 << 20),
        cost_estimate=pl.CostEstimate(
            flops=count * (20 * slots * width * part + 24 * slots * tok * width),
            bytes_accessed=count * 16 * tok * width + 12 * width * part,
            transcendentals=2 * count * slots * part,
        ),
        name="rows",
    )(where, *[pltpu.with_memory_space_constraint(item, pltpu.VMEM) for item in weights], *units, *tables, *after)


def grads_kernel(count, wide, deep, blocks, tp_ref, *refs):
    sources, outs = refs[:count], refs[count:-4]
    wide_all, deep_all, wide_sems, deep_sems = refs[-4:]
    starts = [sum(source.shape[0] for source in sources[:index]) for index in range(count)]
    size = wide_all.shape[2]
    block = pl.program_id(0)

    def copies(column):
        return [
            pltpu.make_async_copy(
                source.at[:, pl.ds(wide + column * size, size)],
                wide_all.at[column, pl.ds(starts[index], source.shape[0])],
                wide_sems.at[column, index],
            )
            for index, source in enumerate(sources)
        ]

    @pl.when(block == 0)
    def _():
        deep_copies = [
            pltpu.make_async_copy(
                source.at[:, pl.ds(deep, deep_all.shape[1])],
                deep_all.at[pl.ds(starts[index], source.shape[0])],
                deep_sems.at[index],
            )
            for index, source in enumerate(sources)
        ]
        for copy in deep_copies:
            copy.start()
        for column in range(blocks):
            for copy in copies(column):
                copy.start()
        for copy in deep_copies:
            copy.wait()

    for column in range(blocks):

        @pl.when(block == column)
        def _(column=column):
            for copy in copies(column):
                copy.wait()

    dims = (((0,), (0,)), ((), ()))
    if len(outs) == 2:
        part = outs[0].shape[2]
        both = lax.dot_general(wide_all[block], deep_all[...], dims, preferred_element_type=jnp.float32)
        outs[0][0] = both[:, :part].astype(jnp.bfloat16)
        outs[1][0] = both[:, part:].astype(jnp.bfloat16)
    else:
        down = lax.dot_general(deep_all[...], wide_all[block], dims, preferred_element_type=jnp.float32)
        outs[0][0] = down.astype(jnp.bfloat16)


def grads_call(which, packed, width, part, down):
    rows, count = sum(item.shape[0] for item in packed), len(packed)
    step = math.gcd(width // 2, 512)
    per = width // 2 // step
    deep = part if down else 2 * part

    def place(i, w):
        return (i + w[0] * per) % (2 * per)

    if down:
        specs = [pl.BlockSpec((1, part, step), lambda i, w: (0, 0, place(i, w)))]
        shapes = [(1, part, width)]
    else:
        specs = [pl.BlockSpec((1, step, part), lambda i, w: (0, place(i, w), 0))] * 2
        shapes = [(1, width, part)] * 2
    starts = (width, 2 * width + 2 * part) if down else (0, 2 * width)
    return pl.pallas_call(
        functools.partial(grads_kernel, count, *starts, 2 * per),
        grid_spec=pltpu.PrefetchScalarGridSpec(
            num_scalar_prefetch=1,
            grid=(2 * per,),
            in_specs=[LOOSE] * count,
            out_specs=specs,
            scratch_shapes=[
                pltpu.VMEM((2 * per, rows, step), jnp.bfloat16),
                pltpu.VMEM((rows, deep), jnp.bfloat16),
                pltpu.SemaphoreType.DMA((2 * per, count)),
                pltpu.SemaphoreType.DMA((count,)),
            ],
        ),
        out_shape=[jax.ShapeDtypeStruct(shape, jnp.bfloat16) for shape in shapes],
        compiler_params=pltpu.CompilerParams(vmem_limit_bytes=20 << 20),
        cost_estimate=pl.CostEstimate(
            flops=2 * rows * width * deep, bytes_accessed=2 * rows * (width + deep), transcendentals=0
        ),
        name="grads",
    )(which, *packed)


def dense_device(tokens, out_grad, routes, probs, w_gate, w_up, w_down):
    owners = lax.axis_size(("role", "ep"))
    ep = lax.axis_size("ep")
    n_y = 2
    n_z = ep // n_y
    tok_rows, half = tokens.shape
    capacity = slot_capacity(tok_rows, routes.shape[1], owners)
    slots = -(-n_y * capacity // 16) * 16
    role, place, which = lax.axis_index("role"), lax.axis_index("ep"), lax.axis_index("tp")

    def over_x(array):
        return lax.ppermute(array, "tp", [(0, 1), (1, 0)])

    def over_role(array):
        return lax.ppermute(array, "role", [(0, 1), (1, 0)])

    def over_y(array):
        return lax.ppermute(array, "ep", [(i, i + 1 - 2 * (i % n_y)) for i in range(ep)])

    def over_z(array, shift):
        return lax.ppermute(array, "ep", [(i, (i + shift * n_y) % ep) for i in range(ep)])

    def tied(values, others):
        return lax.optimization_barrier((list(values), list(others)))[0]

    last = n_z - 1
    routes_in = []
    for z in range(n_z):
        shift = -1 if z == last and z > 1 else 1
        if z:
            routes_in.append(((z, 0, 0), (0 if z in (1, last) else z - 1, 0, 0), functools.partial(over_z, shift=shift)))
        routes_in.append(((z, 1, 0), (z, 0, 0), over_y))
        routes_in.append(((z, 0, 1), (z, 0, 0), over_x))
        if z == 0:
            routes_in.append(((z, 1, 1), (z, 1, 0), over_x))
        elif z in (1, last):
            routes_in.append(((z, 1, 1), (0, 1, 1), functools.partial(over_z, shift=shift)))
        else:
            routes_in.append(((z, 1, 1), (z, 0, 1), over_y))
    routes_in.sort(key=lambda item: (item[0][0] % 2 if item[2] in (over_x, over_y) else 0, sum(item[0][1:])))

    rounds, waiting, there = [], list(routes_in), {(0, 0, 0)}
    while waiting:
        moves = {}
        for item in waiting:
            axis = item[2] if item[2] in (over_x, over_y) else over_z
            if item[1] in there and axis not in moves:
                moves[axis] = item
        rounds.append(list(moves.values()))
        there |= {item[0] for item in rounds[-1]}
        waiting = [item for item in waiting if item[0] not in there]

    which_ref = which.reshape(1).astype(jnp.int32)
    where = jnp.stack([role * ep + place, (1 - role) * ep + place, which]).astype(jnp.int32)
    both_w, down_w = weights_call(which_ref, w_gate, w_up, w_down)
    width, part = both_w.shape[0], down_w.shape[0]

    def rows_of(steps, items, after):
        four = [units[z, y, x] for z in steps for y in range(2) for x in range(2)]
        return rows_call(items, owners, capacity, slots, where, weights, four, [tables[z] for z in steps], after)

    units = {(0, 0, 0): join_call(tokens, out_grad)}
    settled = dict(units)
    for number, moves in enumerate(rounds):
        arrived = {target: move(settled[source]) for target, source, move in moves}
        units.update(arrived)
        settled.update(arrived)
        extra = []
        if number == 0:
            extra = [both_w, down_w]
            both_w, down_w, routes, probs = tied([both_w, down_w, routes, probs], arrived.values())
            weights = (both_w, over_role(both_w), down_w, over_role(down_w))
            chosen = routes[:, :, None] == jnp.arange(owners, dtype=jnp.int32)
            table = jnp.sum(jnp.where(chosen, probs[:, :, None].astype(jnp.float32) + 1.0, 0.0), axis=1) - 1.0
            table = table.astype(jnp.bfloat16).T
            table = jnp.stack([table, over_y(table)])
        if number == 1:
            (table,) = tied([table], arrived.values())
            tables = [over_z(table, z) if z else table for z in range(n_z)]
        if number == 2:
            mine_0, other_0, near, side_0, far, y_0 = rows_of(
                [0], [[(0, 0, 0)], [(0, 0, 1)], [(0, 1, 1)], [(0, 1, 0)]], []
            )
            extra = [mine_0]
        names = list(settled)
        settled = dict(zip(names, tied([settled[item] for item in names], extra)))

    def total(*blocks):
        return sum(block.astype(jnp.float32) for block in blocks).astype(jnp.bfloat16)

    items = [[(1, 1, 1)], [(1, 0, 1)], [(0, 0, 1)], [(0, 1, 0)], [(0, 1, 1)], [(0, 0, 0)], [(1, 0, 0)], [(1, 1, 0)]]
    mine_1, other_1, x_2, x_20, x_1, y_1, z_1, keep_1, keep_2, keep_2y = rows_of([1, 2], items, [])
    other_1, x_2, x_20, x_1, y_1, z_1 = tied([other_1, x_2, x_20, x_1, y_1, z_1], arrived.values())
    from_x2, from_y1, from_z1 = over_x(x_2), over_y(y_1), over_z(z_1, -1)
    from_x20, from_x1 = over_x(x_20), over_x(x_1)
    items = [[(0, 0, 1)], [(0, 1, 0)], [(0, 1, 1)], [(0, 0, 0)]]
    mine_3, other_3, x_3, y_3, z_3, keep_3 = rows_of([3], items, [mine_1])
    mine_3, other_3, x_3, y_3, z_3, keep_2y = tied(
        [mine_3, other_3, x_3, y_3, z_3, keep_2y], [from_x2, from_y1, from_z1]
    )
    from_z3, from_x3, from_y2, from_y3 = over_z(z_3, 1), over_x(x_3), over_y(total(keep_2y, from_x2)), over_y(y_3)
    packed = [mine_0, over_role(other_0), mine_1, over_role(other_1), mine_3, over_role(other_3)]
    d_gate, d_up = grads_call(which_ref, packed, width, part, False)
    from_z3, from_x20, from_x1, from_y2 = tied([from_z3, from_x20, from_x1, from_y2], [d_gate, d_up])
    from_far = over_y(total(far, from_z1, from_z3))
    from_z2 = over_z(total(keep_2, from_x20, from_y2), 1)
    home_1 = over_z(total(keep_1, from_x1, from_y1), -1)
    (d_down,) = grads_call(which_ref, packed, width, part, True)
    from_x3, from_y3, from_z2, y_0 = tied([from_x3, from_y3, from_z2, y_0], [d_down])
    from_y0 = over_y(y_0)
    home_3 = over_z(total(keep_3, from_x3, from_y3, from_z2), 1)
    from_x0 = over_x(total(side_0, from_far))
    home = (near, from_y0, home_1, home_3, from_x0)
    d_tok = sum(block[0, :tok_rows].astype(jnp.float32) for block in home).astype(jnp.bfloat16)
    home = sum(block[0, tok_rows:, : 4 * tok_rows].astype(jnp.float32) for block in home)
    score = jnp.sum(home.reshape(owners, 4, tok_rows), axis=1).T
    d_probs = jnp.sum(jnp.where(chosen, score[:, None, :], 0.0), axis=2)
    return d_tok, d_probs, d_gate, d_up, d_down


def per_device(tokens, out_grad, routes, probs, w_gate, w_up, w_down):
    owners = lax.axis_size(("role", "ep"))
    tok_rows, top_count = routes.shape
    paired = lax.axis_size("tp") == 2 and lax.axis_size("role") == 2 and lax.axis_size("ep") == 8
    if paired and 2 * slot_capacity(tok_rows, top_count, owners) >= tok_rows:
        return dense_device(tokens, out_grad, routes, probs, w_gate, w_up, w_down)
    return routed_device(tokens, out_grad, routes, probs, w_gate, w_up, w_down)


def solution(mesh):
    in_specs = (
        P(("groups", "role", "ep"), "tp"),
        P(("groups", "role", "ep"), "tp"),
        P(("groups", "role", "ep"), None),
        P(("groups", "role", "ep"), None),
        P(("role", "ep"), None, "tp"),
        P(("role", "ep"), None, "tp"),
        P(("role", "ep"), "tp", None),
    )
    out_specs = (
        P(("groups", "role", "ep"), "tp"),
        P(("groups", "role", "ep"), None),
        P(("groups", "role", "ep"), None, "tp"),
        P(("groups", "role", "ep"), None, "tp"),
        P(("groups", "role", "ep"), "tp", None),
    )
    return jax.shard_map(
        per_device, mesh=mesh, in_specs=in_specs, out_specs=out_specs, check_vma=False
    )
```

```python
import functools
import math

import jax
import jax.numpy as jnp
from jax import lax
from jax.experimental import pallas as pl
from jax.experimental.pallas import tpu as pltpu
from jax.sharding import PartitionSpec as P


def pad_rows(array):
    return jnp.concatenate([array, jnp.zeros((1, array.shape[1]), array.dtype)], 0)


def routed_device(tokens, out_grad, routes, probs, w_gate, w_up, w_down):
    owners = lax.axis_size(("role", "ep"))
    tok_rows, top_count = routes.shape
    width_full = w_gate.shape[1]
    part_width = w_gate.shape[2]
    capacity = min(tok_rows, tok_rows * top_count * 9 // (8 * owners))
    entry_total = tok_rows * top_count
    routes_flat = routes.reshape(-1)
    onehot = (routes_flat[:, None] == jnp.arange(owners, dtype=jnp.int32)[None, :]).astype(
        jnp.int32
    )
    before = jnp.cumsum(onehot, axis=0) - onehot
    slot_index = jnp.sum(before * onehot, axis=1)
    target = routes_flat * capacity + slot_index
    row_count = owners * capacity
    entry_of_slot = (
        jnp.full((row_count,), entry_total, jnp.int32)
        .at[target]
        .set(jnp.arange(entry_total, dtype=jnp.int32))
    )
    token_of_slot = entry_of_slot // top_count
    padded_prob = jnp.concatenate([probs.reshape(-1), jnp.zeros((1,), probs.dtype)], 0)
    send_prob = padded_prob[entry_of_slot].reshape(owners, capacity)
    send_x = pad_rows(tokens)[token_of_slot]
    send_g = pad_rows(out_grad)[token_of_slot]
    slice_x, slice_g, recv_p = (
        lax.all_to_all(
            send_x.reshape(owners, capacity, tokens.shape[1]),
            ("role", "ep"),
            split_axis=0,
            concat_axis=0,
            tiled=True,
        ),
        lax.all_to_all(
            send_g.reshape(owners, capacity, tokens.shape[1]),
            ("role", "ep"),
            split_axis=0,
            concat_axis=0,
            tiled=True,
        ),
        lax.all_to_all(send_prob, ("role", "ep"), split_axis=0, concat_axis=0, tiled=True),
    )
    recv_x, recv_g = (
        lax.all_gather(slice_x, "tp", axis=2, tiled=True),
        lax.all_gather(slice_g, "tp", axis=2, tiled=True),
    )
    rows_x = recv_x.reshape(row_count, width_full)
    rows_g = recv_g.reshape(row_count, width_full)
    weight_p = recv_p.reshape(row_count, 1).astype(jnp.float32)
    gate_up = jnp.concatenate([w_gate[0], w_up[0]], 1)
    down_shard = w_down[0]
    both_rows = jnp.dot(rows_x, gate_up, preferred_element_type=jnp.float32)
    gate_rows = both_rows[:, :part_width]
    up_rows = both_rows[:, part_width:]
    sigmoid_gate = jax.nn.sigmoid(gate_rows)
    activated = gate_rows * sigmoid_gate
    hidden = activated * up_rows
    back_rows = lax.dot_general(
        rows_g, down_shard, (((1,), (1,)), ((), ())), preferred_element_type=jnp.float32
    )
    scores = lax.psum(jnp.sum(hidden * back_rows, axis=1), "tp")
    hidden_grad = weight_p * back_rows
    d_gate_rows = (
        hidden_grad * up_rows * sigmoid_gate * (1.0 + gate_rows * (1.0 - sigmoid_gate))
    ).astype(jnp.bfloat16)
    d_up_rows = (hidden_grad * activated).astype(jnp.bfloat16)
    d_both = jnp.concatenate([d_gate_rows, d_up_rows], 1)
    scaled = (weight_p * hidden).astype(jnp.bfloat16)
    grad_down = lax.dot_general(
        scaled, rows_g, (((0,), (0,)), ((), ())), preferred_element_type=jnp.float32
    )
    grad_both = lax.dot_general(
        rows_x, d_both, (((0,), (0,)), ((), ())), preferred_element_type=jnp.float32
    )
    grad_gate = grad_both[:, :part_width]
    grad_up = grad_both[:, part_width:]
    partial_low = lax.dot_general(
        d_both, gate_up, (((1,), (1,)), ((), ())), preferred_element_type=jnp.float32
    ).astype(jnp.bfloat16)
    home_s = lax.all_to_all(
        scores.reshape(owners, capacity), ("role", "ep"), split_axis=0, concat_axis=0, tiled=True
    )
    summed = lax.psum_scatter(
        partial_low.reshape(owners, capacity, width_full), "tp", scatter_dimension=2, tiled=True
    ).astype(jnp.float32)
    summed_low = summed.astype(jnp.bfloat16)
    home_x = lax.all_to_all(summed_low, ("role", "ep"), split_axis=0, concat_axis=0, tiled=True)
    slice_width = summed.shape[2]
    route_rows = home_x.reshape(row_count, slice_width).astype(jnp.float32)
    d_tok = (
        jnp.zeros((tok_rows + 1, slice_width), jnp.float32)
        .at[token_of_slot]
        .add(route_rows)[:tok_rows]
    )
    d_probs = home_s.reshape(-1)[target].reshape(tok_rows, top_count)
    return (
        d_tok.astype(jnp.bfloat16),
        d_probs,
        grad_gate.astype(jnp.bfloat16)[None],
        grad_up.astype(jnp.bfloat16)[None],
        grad_down.astype(jnp.bfloat16)[None],
    )


def slot_capacity(tok_rows, top_count, owners):
    return min(tok_rows, tok_rows * top_count * 9 // (8 * owners))


LOOSE = pl.BlockSpec(memory_space=pl.ANY)


def weights_kernel(tp_ref, wg_ref, wu_ref, wd_ref, both_ref, down_ref):
    part = wg_ref.shape[2]
    both_ref[:, :part] = wg_ref[0]
    both_ref[:, part:] = wu_ref[0]
    down_ref[...] = wd_ref[0]


def weights_call(which, w_gate, w_up, w_down):
    _, width, part = w_gate.shape
    half = width // 2

    def place(i, w):
        return (i + w[0]) % 2

    return pl.pallas_call(
        weights_kernel,
        grid_spec=pltpu.PrefetchScalarGridSpec(
            num_scalar_prefetch=1,
            grid=(2,),
            in_specs=[
                pl.BlockSpec((1, half, part), lambda i, w: (0, place(i, w), 0)),
                pl.BlockSpec((1, half, part), lambda i, w: (0, place(i, w), 0)),
                pl.BlockSpec((1, part, half), lambda i, w: (0, 0, place(i, w))),
            ],
            out_specs=[
                pl.BlockSpec((half, 2 * part), lambda i, w: (i, 0)),
                pl.BlockSpec((part, half), lambda i, w: (0, i)),
            ],
        ),
        out_shape=[
            jax.ShapeDtypeStruct((width, 2 * part), jnp.bfloat16),
            jax.ShapeDtypeStruct((part, width), jnp.bfloat16),
        ],
        compiler_params=pltpu.CompilerParams(vmem_limit_bytes=12 << 20),
        cost_estimate=pl.CostEstimate(flops=0, bytes_accessed=12 * width * part, transcendentals=0),
        name="weights",
    )(which, *[pltpu.with_memory_space_constraint(item, pltpu.HBM) for item in (w_gate, w_up, w_down)])


def join_kernel(top_ref, bottom_ref, out_ref, sems):
    rows = top_ref.shape[0]
    copies = [
        pltpu.make_async_copy(top_ref, out_ref.at[pl.ds(0, rows)], sems.at[0]),
        pltpu.make_async_copy(bottom_ref, out_ref.at[pl.ds(rows, rows)], sems.at[1]),
    ]
    for copy in copies:
        copy.start()
    for copy in copies:
        copy.wait()


def join_call(top, bottom):
    rows, columns = top.shape
    return pl.pallas_call(
        join_kernel,
        in_specs=[LOOSE] * 2,
        out_specs=LOOSE,
        out_shape=jax.ShapeDtypeStruct((2 * rows, columns), top.dtype),
        scratch_shapes=[pltpu.SemaphoreType.DMA((2,))],
        compiler_params=pltpu.CompilerParams(vmem_limit_bytes=8 << 20),
        cost_estimate=pl.CostEstimate(flops=0, bytes_accessed=8 * rows * columns, transcendentals=0),
        name="join",
    )(*[pltpu.with_memory_space_constraint(item, pltpu.HBM) for item in (top, bottom)])


def rows_kernel(count, ways, capacity, slots, where_ref, *refs):
    weights_in, units_in, tables_in = refs[:4], refs[4 : 4 + 4 * count], refs[4 + 4 * count : 4 + 5 * count]
    leaves = 1 + max(way[0] for way in ways.values())
    refs = refs[len(refs) - 6 - leaves :]
    outs, packets, refs = refs[:2], refs[2 : 2 + leaves], refs[2 + leaves :]
    x_all, g_all, tables, unit_sems = refs
    half, tok = x_all.shape[3], x_all.shape[2] // 2
    part = weights_in[2].shape[0]
    owners = tables.shape[2]
    wgu, wd = weights_in[:2], weights_in[2:]

    x_copies, g_copies = [], []
    for index, unit in enumerate(units_in):
        chunk, y, x = index // 4, index // 2 % 2, index % 2
        rows = pl.ds(y * tok, tok)
        x_copies.append(pltpu.make_async_copy(unit.at[pl.ds(0, tok)], x_all.at[chunk, x, rows], unit_sems.at[0, index]))
        g_copies.append(pltpu.make_async_copy(unit.at[pl.ds(tok, tok)], g_all.at[chunk, x, rows], unit_sems.at[1, index]))
    t_copies = [
        pltpu.make_async_copy(table, tables.at[chunk], unit_sems.at[2, chunk]) for chunk, table in enumerate(tables_in)
    ]
    for copy in t_copies + x_copies + g_copies:
        copy.start()
    both_at, scaled_at = pl.ds(4 * half, 2 * part), pl.ds(4 * half + 2 * part, part)

    def dot(a, b, dims):
        return lax.dot_general(a, b, (dims, ((), ())), preferred_element_type=jnp.float32)

    for copy in t_copies:
        copy.wait()
    earlier = lax.broadcasted_iota(jnp.int32, (tok, tok), 0) < lax.broadcasted_iota(jnp.int32, (tok, tok), 1)
    earlier = earlier.astype(jnp.bfloat16)
    place = lax.broadcasted_iota(jnp.int32, (slots, tok), 0).astype(jnp.float32)
    names = lax.broadcasted_iota(jnp.int32, (owners, tok), 0)
    picks, low_picks, probs = {}, {}, {}
    for chunk in range(count):
        found = []
        for y in range(2):
            table = tables[chunk, y].astype(jnp.float32)
            rank = dot((table >= 0.0).astype(jnp.bfloat16), earlier, ((1,), (0,))) + float(y * capacity)
            found.append((table, jnp.where(table >= 0.0, rank, -1.0)))
        for expert in range(2):
            mine = names == where_ref[expert]
            halves, prob = [], None
            for table, rank in found:
                weight = jnp.sum(jnp.where(mine, table, 0.0), axis=0, keepdims=True)
                slot = jnp.sum(jnp.where(mine, rank, 0.0), axis=0, keepdims=True)
                halves.append((place == slot).astype(jnp.float32))
                term = jnp.sum(halves[-1] * weight, axis=1, keepdims=True)
                prob = term if prob is None else prob + term
            picks[chunk, expert] = halves
            low_picks[chunk, expert] = jnp.concatenate(halves, 1).astype(jnp.bfloat16)
            probs[chunk, expert] = prob
    spans = [pl.ds(chunk * slots, slots) for chunk in range(count)]
    sides = [slice(side * half, (side + 1) * half) for side in range(2)]

    def gather(copies, source, offset):
        for chunk in range(count):
            for copy in copies[4 * chunk : 4 * chunk + 4]:
                copy.wait()
            both_picks = jnp.concatenate([low_picks[chunk, expert] for expert in range(2)], 0)
            for side in range(2):
                rows = dot(both_picks, source[chunk, side], ((1,), (0,))).astype(jnp.bfloat16)
                for expert in range(2):
                    columns = pl.ds(offset + side * half, half)
                    outs[expert][spans[chunk], columns] = rows[expert * slots : (expert + 1) * slots]

    gather(x_copies, x_all, 0)
    rows = []
    for expert in range(2):
        rows.append(dot(outs[expert][:, : 2 * half], wgu[expert][...], ((1,), (0,))))
    gather(g_copies, g_all, 2 * half)
    scores = []
    for expert in range(2):
        back = dot(outs[expert][:, 2 * half : 4 * half], wd[expert][...], ((1,), (1,)))
        gate, up = rows[expert][:, :part], rows[expert][:, part:]
        sig = jax.nn.sigmoid(gate)
        act = gate * sig
        hidden = act * up
        scores.append(jnp.sum(hidden * back, axis=1, keepdims=True))
        prob = jnp.concatenate([probs[chunk, expert] for chunk in range(count)], 0)
        hgrad = prob * back
        d_gate = (hgrad * up * sig * (1.0 + gate * (1.0 - sig))).astype(jnp.bfloat16)
        outs[expert][:, both_at] = jnp.concatenate([d_gate, (hgrad * act).astype(jnp.bfloat16)], 1)
        outs[expert][:, scaled_at] = (prob * hidden).astype(jnp.bfloat16)

    names = lax.broadcasted_iota(jnp.int32, (owners, half), 0)
    column = lax.broadcasted_iota(jnp.int32, (owners, half), 1) // (2 * tok)
    for chunk in range(count):
        for y in range(2):
            extra = jnp.zeros((owners, half), jnp.float32)
            for expert in range(2):
                part_scores = scores[expert][chunk * slots : (chunk + 1) * slots]
                line = jnp.sum(picks[chunk, expert][y] * part_scores, axis=0, keepdims=True)
                high = line.astype(jnp.bfloat16).astype(jnp.float32)
                line = jnp.concatenate([high, line - high] * (half // (2 * tok)), 1)
                extra = extra + jnp.where((names == where_ref[expert]) & (column == where_ref[2]), line, 0.0)
            for side in range(2):
                number, slot = ways[chunk, y, side]
                packets[number][slot, tok:] = extra.astype(jnp.bfloat16)
    for side in (1, 0):
        low = [
            dot(outs[expert][:, both_at], wgu[expert][sides[side], :], ((1,), (1,))).astype(jnp.bfloat16) for expert in range(2)
        ]
        for chunk in range(count):
            total = None
            for expert in range(2):
                term = dot(low_picks[chunk, expert], low[expert][chunk * slots : (chunk + 1) * slots], ((0,), (0,)))
                total = term if total is None else total + term
            for y in range(2):
                number, slot = ways[chunk, y, side]
                packets[number][slot, :tok] = total[y * tok : (y + 1) * tok].astype(jnp.bfloat16)


def rows_call(items, owners, capacity, slots, where, weights, units, tables, after):
    count = len(tables)
    ways = {block: (number, slot) for number, blocks in enumerate(items) for slot, block in enumerate(blocks)}
    tok, half = units[0].shape[0] // 2, units[0].shape[1]
    part, width = weights[2].shape
    widths = (width, width, 2 * part, part)
    packet = (tok + owners, half)
    return pl.pallas_call(
        functools.partial(rows_kernel, count, ways, capacity, slots),
        grid_spec=pltpu.PrefetchScalarGridSpec(
            num_scalar_prefetch=1,
            grid=(1,),
            in_specs=[pl.BlockSpec(memory_space=pltpu.VMEM)] * 4 + [LOOSE] * (5 * count + len(after)),
            out_specs=[pl.BlockSpec(memory_space=pltpu.VMEM)] * (2 + len(items)),
            scratch_shapes=[pltpu.VMEM((count, 2, 2 * tok, half), jnp.bfloat16)] * 2
            + [pltpu.VMEM((count, 2, owners, tok), jnp.bfloat16)]
            + [pltpu.SemaphoreType.DMA((3, 4 * count))],
        ),
        out_shape=[pltpu.VMEM((count * slots, sum(widths)), jnp.bfloat16)] * 2
        + [pltpu.VMEM((len(blocks),) + packet, jnp.bfloat16) for blocks in items],
        compiler_params=pltpu.CompilerParams(vmem_limit_bytes=14 << 20),
        cost_estimate=pl.CostEstimate(
            flops=count * (20 * slots * width * part + 24 * slots * tok * width),
            bytes_accessed=count * 16 * tok * width + 12 * width * part,
            transcendentals=2 * count * slots * part,
        ),
        name="rows",
    )(where, *[pltpu.with_memory_space_constraint(item, pltpu.VMEM) for item in weights], *units, *tables, *after)


def grads_kernel(count, wide, deep, blocks, tp_ref, *refs):
    sources, outs = refs[:count], refs[count:-4]
    wide_all, deep_all, wide_sems, deep_sems = refs[-4:]
    starts = [sum(source.shape[0] for source in sources[:index]) for index in range(count)]
    size = wide_all.shape[2]
    block = pl.program_id(0)

    def copies(column):
        return [
            pltpu.make_async_copy(
                source.at[:, pl.ds(wide + column * size, size)],
                wide_all.at[column, pl.ds(starts[index], source.shape[0])],
                wide_sems.at[column, index],
            )
            for index, source in enumerate(sources)
        ]

    @pl.when(block == 0)
    def _():
        deep_copies = [
            pltpu.make_async_copy(
                source.at[:, pl.ds(deep, deep_all.shape[1])],
                deep_all.at[pl.ds(starts[index], source.shape[0])],
                deep_sems.at[index],
            )
            for index, source in enumerate(sources)
        ]
        for copy in deep_copies:
            copy.start()
        for column in range(blocks):
            for copy in copies(column):
                copy.start()
        for copy in deep_copies:
            copy.wait()

    for column in range(blocks):

        @pl.when(block == column)
        def _(column=column):
            for copy in copies(column):
                copy.wait()

    dims = (((0,), (0,)), ((), ()))
    if len(outs) == 2:
        part = outs[0].shape[2]
        both = lax.dot_general(wide_all[block], deep_all[...], dims, preferred_element_type=jnp.float32)
        outs[0][0] = both[:, :part].astype(jnp.bfloat16)
        outs[1][0] = both[:, part:].astype(jnp.bfloat16)
    else:
        down = lax.dot_general(deep_all[...], wide_all[block], dims, preferred_element_type=jnp.float32)
        outs[0][0] = down.astype(jnp.bfloat16)


def grads_call(which, packed, width, part, down):
    rows, count = sum(item.shape[0] for item in packed), len(packed)
    step = math.gcd(width // 2, 512)
    per = width // 2 // step
    deep = part if down else 2 * part

    def place(i, w):
        return (i + w[0] * per) % (2 * per)

    if down:
        specs = [pl.BlockSpec((1, part, step), lambda i, w: (0, 0, place(i, w)))]
        shapes = [(1, part, width)]
    else:
        specs = [pl.BlockSpec((1, step, part), lambda i, w: (0, place(i, w), 0))] * 2
        shapes = [(1, width, part)] * 2
    starts = (width, 2 * width + 2 * part) if down else (0, 2 * width)
    return pl.pallas_call(
        functools.partial(grads_kernel, count, *starts, 2 * per),
        grid_spec=pltpu.PrefetchScalarGridSpec(
            num_scalar_prefetch=1,
            grid=(2 * per,),
            in_specs=[LOOSE] * count,
            out_specs=specs,
            scratch_shapes=[
                pltpu.VMEM((2 * per, rows, step), jnp.bfloat16),
                pltpu.VMEM((rows, deep), jnp.bfloat16),
                pltpu.SemaphoreType.DMA((2 * per, count)),
                pltpu.SemaphoreType.DMA((count,)),
            ],
        ),
        out_shape=[jax.ShapeDtypeStruct(shape, jnp.bfloat16) for shape in shapes],
        compiler_params=pltpu.CompilerParams(vmem_limit_bytes=14 << 20),
        cost_estimate=pl.CostEstimate(
            flops=2 * rows * width * deep, bytes_accessed=2 * rows * (width + deep), transcendentals=0
        ),
        name="grads",
    )(which, *packed)


def dense_device(tokens, out_grad, routes, probs, w_gate, w_up, w_down):
    owners = lax.axis_size(("role", "ep"))
    ep = lax.axis_size("ep")
    n_y = 2
    n_z = ep // n_y
    tok_rows, half = tokens.shape
    capacity = slot_capacity(tok_rows, routes.shape[1], owners)
    slots = -(-n_y * capacity // 16) * 16
    role, place, which = lax.axis_index("role"), lax.axis_index("ep"), lax.axis_index("tp")

    def over_x(array):
        return lax.ppermute(array, "tp", [(0, 1), (1, 0)])

    def over_role(array):
        return lax.ppermute(array, "role", [(0, 1), (1, 0)])

    def over_y(array):
        return lax.ppermute(array, "ep", [(i, i + 1 - 2 * (i % n_y)) for i in range(ep)])

    def over_z(array, shift):
        return lax.ppermute(array, "ep", [(i, (i + shift * n_y) % ep) for i in range(ep)])

    def tied(values, others):
        return lax.optimization_barrier((list(values), list(others)))[0]

    last = n_z - 1
    routes_in = []
    for z in range(n_z):
        shift = -1 if z == last and z > 1 else 1
        if z:
            routes_in.append(((z, 0, 0), (0 if z in (1, last) else z - 1, 0, 0), functools.partial(over_z, shift=shift)))
        routes_in.append(((z, 1, 0), (z, 0, 0), over_y))
        routes_in.append(((z, 0, 1), (z, 0, 0), over_x))
        if z == 0:
            routes_in.append(((z, 1, 1), (z, 1, 0), over_x))
        elif z in (1, last):
            routes_in.append(((z, 1, 1), (0, 1, 1), functools.partial(over_z, shift=shift)))
        else:
            routes_in.append(((z, 1, 1), (z, 0, 1), over_y))
    routes_in.sort(key=lambda item: (item[0][0] % 2 if item[2] in (over_x, over_y) else 0, sum(item[0][1:])))

    rounds, waiting, there = [], list(routes_in), {(0, 0, 0)}
    while waiting:
        moves = {}
        for item in waiting:
            axis = item[2] if item[2] in (over_x, over_y) else over_z
            if item[1] in there and axis not in moves:
                moves[axis] = item
        rounds.append(list(moves.values()))
        there |= {item[0] for item in rounds[-1]}
        waiting = [item for item in waiting if item[0] not in there]

    which_ref = which.reshape(1).astype(jnp.int32)
    where = jnp.stack([role * ep + place, (1 - role) * ep + place, which]).astype(jnp.int32)
    both_w, down_w = weights_call(which_ref, w_gate, w_up, w_down)
    width, part = both_w.shape[0], down_w.shape[0]

    def rows_of(steps, items, after):
        four = [units[z, y, x] for z in steps for y in range(2) for x in range(2)]
        return rows_call(items, owners, capacity, slots, where, weights, four, [tables[z] for z in steps], after)

    units = {(0, 0, 0): join_call(tokens, out_grad)}
    settled = dict(units)
    for number, moves in enumerate(rounds):
        arrived = {target: move(settled[source]) for target, source, move in moves}
        units.update(arrived)
        settled.update(arrived)
        extra = []
        if number == 0:
            extra = [both_w, down_w]
            both_w, down_w, routes, probs = tied([both_w, down_w, routes, probs], arrived.values())
            weights = (both_w, over_role(both_w), down_w, over_role(down_w))
            chosen = routes[:, :, None] == jnp.arange(owners, dtype=jnp.int32)
            table = jnp.sum(jnp.where(chosen, probs[:, :, None].astype(jnp.float32) + 1.0, 0.0), axis=1) - 1.0
            table = table.astype(jnp.bfloat16).T
            table = jnp.stack([table, over_y(table)])
        if number == 1:
            (table,) = tied([table], arrived.values())
            tables = [over_z(table, z) if z else table for z in range(n_z)]
        if number == 2:
            mine_0, other_0, near, side_0, far, y_0 = rows_of(
                [0], [[(0, 0, 0)], [(0, 0, 1)], [(0, 1, 1)], [(0, 1, 0)]], []
            )
            extra = [mine_0]
        names = list(settled)
        settled = dict(zip(names, tied([settled[item] for item in names], extra)))

    def total(*blocks):
        return sum(block.astype(jnp.float32) for block in blocks).astype(jnp.bfloat16)

    items = [[(1, 1, 1)], [(1, 0, 1)], [(0, 0, 1)], [(0, 1, 0)], [(0, 1, 1)], [(0, 0, 0)], [(1, 0, 0)], [(1, 1, 0)]]
    mine_1, other_1, x_2, x_20, x_1, y_1, z_1, keep_1, keep_2, keep_2y = rows_of([1, 2], items, [])
    other_1, x_2, x_20, x_1, y_1, z_1 = tied([other_1, x_2, x_20, x_1, y_1, z_1], arrived.values())
    from_x2, from_y1, from_z1 = over_x(x_2), over_y(y_1), over_z(z_1, -1)
    from_x20, from_x1 = over_x(x_20), over_x(x_1)
    items = [[(0, 0, 1)], [(0, 1, 0)], [(0, 1, 1)], [(0, 0, 0)]]
    mine_3, other_3, x_3, y_3, z_3, keep_3 = rows_of([3], items, [mine_1])
    mine_3, other_3, x_3, y_3, z_3, keep_2y = tied(
        [mine_3, other_3, x_3, y_3, z_3, keep_2y], [from_x2, from_y1, from_z1]
    )
    from_z3, from_x3, from_y2, from_y3 = over_z(z_3, 1), over_x(x_3), over_y(total(keep_2y, from_x2)), over_y(y_3)
    packed = [mine_0, over_role(other_0), mine_1, over_role(other_1), mine_3, over_role(other_3)]
    d_gate, d_up = grads_call(which_ref, packed, width, part, False)
    from_z3, from_x20, from_y2 = tied([from_z3, from_x20, from_y2], [d_gate, d_up])
    from_far = over_y(total(far, from_z1, from_z3))
    from_z2 = over_z(total(keep_2, from_x20, from_y2), 1)
    (d_down,) = grads_call(which_ref, packed, width, part, True)
    from_x1, from_x3, from_y3, from_z2, y_0 = tied([from_x1, from_x3, from_y3, from_z2, y_0], [d_down, from_far])
    home_1 = over_z(total(keep_1, from_x1, from_y1), -1)
    from_y0 = over_y(y_0)
    home_3 = over_z(total(keep_3, from_x3, from_y3, from_z2), 1)
    from_x0 = over_x(total(side_0, from_far))
    home = (near, from_y0, home_1, home_3, from_x0)
    d_tok = sum(block[0, :tok_rows].astype(jnp.float32) for block in home).astype(jnp.bfloat16)
    home = sum(block[0, tok_rows:, : 4 * tok_rows].astype(jnp.float32) for block in home)
    score = jnp.sum(home.reshape(owners, 4, tok_rows), axis=1).T
    d_probs = jnp.sum(jnp.where(chosen, score[:, None, :], 0.0), axis=2)
    return d_tok, d_probs, d_gate, d_up, d_down


def per_device(tokens, out_grad, routes, probs, w_gate, w_up, w_down):
    owners = lax.axis_size(("role", "ep"))
    tok_rows, top_count = routes.shape
    paired = lax.axis_size("tp") == 2 and lax.axis_size("role") == 2 and lax.axis_size("ep") == 8
    if paired and 2 * slot_capacity(tok_rows, top_count, owners) >= tok_rows:
        return dense_device(tokens, out_grad, routes, probs, w_gate, w_up, w_down)
    return routed_device(tokens, out_grad, routes, probs, w_gate, w_up, w_down)


def solution(mesh):
    in_specs = (
        P(("groups", "role", "ep"), "tp"),
        P(("groups", "role", "ep"), "tp"),
        P(("groups", "role", "ep"), None),
        P(("groups", "role", "ep"), None),
        P(("role", "ep"), None, "tp"),
        P(("role", "ep"), None, "tp"),
        P(("role", "ep"), "tp", None),
    )
    out_specs = (
        P(("groups", "role", "ep"), "tp"),
        P(("groups", "role", "ep"), None),
        P(("groups", "role", "ep"), None, "tp"),
        P(("groups", "role", "ep"), None, "tp"),
        P(("groups", "role", "ep"), "tp", None),
    )
    return jax.shard_map(
        per_device, mesh=mesh, in_specs=in_specs, out_specs=out_specs, check_vma=False
    )
```

```python
import functools
import math

import jax
import jax.numpy as jnp
from jax import lax
from jax.experimental import pallas as pl
from jax.experimental.pallas import tpu as pltpu
from jax.sharding import PartitionSpec as P


def pad_rows(array):
    return jnp.concatenate([array, jnp.zeros((1, array.shape[1]), array.dtype)], 0)


def routed_device(tokens, out_grad, routes, probs, w_gate, w_up, w_down):
    owners = lax.axis_size(("role", "ep"))
    tok_rows, top_count = routes.shape
    width_full = w_gate.shape[1]
    part_width = w_gate.shape[2]
    capacity = min(tok_rows, tok_rows * top_count * 9 // (8 * owners))
    entry_total = tok_rows * top_count
    routes_flat = routes.reshape(-1)
    onehot = (routes_flat[:, None] == jnp.arange(owners, dtype=jnp.int32)[None, :]).astype(
        jnp.int32
    )
    before = jnp.cumsum(onehot, axis=0) - onehot
    slot_index = jnp.sum(before * onehot, axis=1)
    target = routes_flat * capacity + slot_index
    row_count = owners * capacity
    entry_of_slot = (
        jnp.full((row_count,), entry_total, jnp.int32)
        .at[target]
        .set(jnp.arange(entry_total, dtype=jnp.int32))
    )
    token_of_slot = entry_of_slot // top_count
    padded_prob = jnp.concatenate([probs.reshape(-1), jnp.zeros((1,), probs.dtype)], 0)
    send_prob = padded_prob[entry_of_slot].reshape(owners, capacity)
    send_x = pad_rows(tokens)[token_of_slot]
    send_g = pad_rows(out_grad)[token_of_slot]
    slice_x, slice_g, recv_p = (
        lax.all_to_all(
            send_x.reshape(owners, capacity, tokens.shape[1]),
            ("role", "ep"),
            split_axis=0,
            concat_axis=0,
            tiled=True,
        ),
        lax.all_to_all(
            send_g.reshape(owners, capacity, tokens.shape[1]),
            ("role", "ep"),
            split_axis=0,
            concat_axis=0,
            tiled=True,
        ),
        lax.all_to_all(send_prob, ("role", "ep"), split_axis=0, concat_axis=0, tiled=True),
    )
    recv_x, recv_g = (
        lax.all_gather(slice_x, "tp", axis=2, tiled=True),
        lax.all_gather(slice_g, "tp", axis=2, tiled=True),
    )
    rows_x = recv_x.reshape(row_count, width_full)
    rows_g = recv_g.reshape(row_count, width_full)
    weight_p = recv_p.reshape(row_count, 1).astype(jnp.float32)
    gate_up = jnp.concatenate([w_gate[0], w_up[0]], 1)
    down_shard = w_down[0]
    both_rows = jnp.dot(rows_x, gate_up, preferred_element_type=jnp.float32)
    gate_rows = both_rows[:, :part_width]
    up_rows = both_rows[:, part_width:]
    sigmoid_gate = jax.nn.sigmoid(gate_rows)
    activated = gate_rows * sigmoid_gate
    hidden = activated * up_rows
    back_rows = lax.dot_general(
        rows_g, down_shard, (((1,), (1,)), ((), ())), preferred_element_type=jnp.float32
    )
    scores = lax.psum(jnp.sum(hidden * back_rows, axis=1), "tp")
    hidden_grad = weight_p * back_rows
    d_gate_rows = (
        hidden_grad * up_rows * sigmoid_gate * (1.0 + gate_rows * (1.0 - sigmoid_gate))
    ).astype(jnp.bfloat16)
    d_up_rows = (hidden_grad * activated).astype(jnp.bfloat16)
    d_both = jnp.concatenate([d_gate_rows, d_up_rows], 1)
    scaled = (weight_p * hidden).astype(jnp.bfloat16)
    grad_down = lax.dot_general(
        scaled, rows_g, (((0,), (0,)), ((), ())), preferred_element_type=jnp.float32
    )
    grad_both = lax.dot_general(
        rows_x, d_both, (((0,), (0,)), ((), ())), preferred_element_type=jnp.float32
    )
    grad_gate = grad_both[:, :part_width]
    grad_up = grad_both[:, part_width:]
    partial_low = lax.dot_general(
        d_both, gate_up, (((1,), (1,)), ((), ())), preferred_element_type=jnp.float32
    ).astype(jnp.bfloat16)
    home_s = lax.all_to_all(
        scores.reshape(owners, capacity), ("role", "ep"), split_axis=0, concat_axis=0, tiled=True
    )
    summed = lax.psum_scatter(
        partial_low.reshape(owners, capacity, width_full), "tp", scatter_dimension=2, tiled=True
    ).astype(jnp.float32)
    summed_low = summed.astype(jnp.bfloat16)
    home_x = lax.all_to_all(summed_low, ("role", "ep"), split_axis=0, concat_axis=0, tiled=True)
    slice_width = summed.shape[2]
    route_rows = home_x.reshape(row_count, slice_width).astype(jnp.float32)
    d_tok = (
        jnp.zeros((tok_rows + 1, slice_width), jnp.float32)
        .at[token_of_slot]
        .add(route_rows)[:tok_rows]
    )
    d_probs = home_s.reshape(-1)[target].reshape(tok_rows, top_count)
    return (
        d_tok.astype(jnp.bfloat16),
        d_probs,
        grad_gate.astype(jnp.bfloat16)[None],
        grad_up.astype(jnp.bfloat16)[None],
        grad_down.astype(jnp.bfloat16)[None],
    )


def slot_capacity(tok_rows, top_count, owners):
    return min(tok_rows, tok_rows * top_count * 9 // (8 * owners))


LOOSE = pl.BlockSpec(memory_space=pl.ANY)


def weights_kernel(tp_ref, wg_ref, wu_ref, wd_ref, both_ref, down_ref):
    part = wg_ref.shape[2]
    both_ref[:, :part] = wg_ref[0]
    both_ref[:, part:] = wu_ref[0]
    down_ref[...] = wd_ref[0]


def weights_call(which, w_gate, w_up, w_down):
    _, width, part = w_gate.shape
    half = width // 2

    def place(i, w):
        return (i + w[0]) % 2

    return pl.pallas_call(
        weights_kernel,
        grid_spec=pltpu.PrefetchScalarGridSpec(
            num_scalar_prefetch=1,
            grid=(2,),
            in_specs=[
                pl.BlockSpec((1, half, part), lambda i, w: (0, place(i, w), 0)),
                pl.BlockSpec((1, half, part), lambda i, w: (0, place(i, w), 0)),
                pl.BlockSpec((1, part, half), lambda i, w: (0, 0, place(i, w))),
            ],
            out_specs=[
                pl.BlockSpec((half, 2 * part), lambda i, w: (i, 0)),
                pl.BlockSpec((part, half), lambda i, w: (0, i)),
            ],
        ),
        out_shape=[
            jax.ShapeDtypeStruct((width, 2 * part), jnp.bfloat16),
            jax.ShapeDtypeStruct((part, width), jnp.bfloat16),
        ],
        compiler_params=pltpu.CompilerParams(vmem_limit_bytes=12 << 20),
        cost_estimate=pl.CostEstimate(flops=0, bytes_accessed=12 * width * part, transcendentals=0),
        name="weights",
    )(which, *[pltpu.with_memory_space_constraint(item, pltpu.HBM) for item in (w_gate, w_up, w_down)])


def join_kernel(top_ref, bottom_ref, out_ref, sems):
    rows = top_ref.shape[0]
    copies = [
        pltpu.make_async_copy(top_ref, out_ref.at[pl.ds(0, rows)], sems.at[0]),
        pltpu.make_async_copy(bottom_ref, out_ref.at[pl.ds(rows, rows)], sems.at[1]),
    ]
    for copy in copies:
        copy.start()
    for copy in copies:
        copy.wait()


def join_call(top, bottom):
    rows, columns = top.shape
    return pl.pallas_call(
        join_kernel,
        in_specs=[LOOSE] * 2,
        out_specs=pl.BlockSpec(memory_space=pltpu.VMEM),
        out_shape=pltpu.VMEM((2 * rows, columns), top.dtype),
        scratch_shapes=[pltpu.SemaphoreType.DMA((2,))],
        compiler_params=pltpu.CompilerParams(vmem_limit_bytes=8 << 20),
        cost_estimate=pl.CostEstimate(flops=0, bytes_accessed=8 * rows * columns, transcendentals=0),
        name="join",
    )(*[pltpu.with_memory_space_constraint(item, pltpu.HBM) for item in (top, bottom)])


def rows_kernel(count, ways, capacity, slots, where_ref, *refs):
    weights_in, units_in, tables_in = refs[:4], refs[4 : 4 + 4 * count], refs[4 + 4 * count : 4 + 5 * count]
    leaves = 1 + max(way[0] for way in ways.values())
    refs = refs[len(refs) - 6 - leaves :]
    outs, packets, refs = refs[:2], refs[2 : 2 + leaves], refs[2 + leaves :]
    x_all, g_all, tables, unit_sems = refs
    half, tok = x_all.shape[3], x_all.shape[2] // 2
    part = weights_in[2].shape[0]
    owners = tables.shape[2]
    wgu, wd = weights_in[:2], weights_in[2:]

    x_copies, g_copies = [], []
    for index, unit in enumerate(units_in):
        chunk, y, x = index // 4, index // 2 % 2, index % 2
        rows = pl.ds(y * tok, tok)
        x_copies.append(pltpu.make_async_copy(unit.at[pl.ds(0, tok)], x_all.at[chunk, x, rows], unit_sems.at[0, index]))
        g_copies.append(pltpu.make_async_copy(unit.at[pl.ds(tok, tok)], g_all.at[chunk, x, rows], unit_sems.at[1, index]))
    t_copies = [
        pltpu.make_async_copy(table, tables.at[chunk], unit_sems.at[2, chunk]) for chunk, table in enumerate(tables_in)
    ]
    for copy in t_copies + x_copies + g_copies:
        copy.start()
    both_at, scaled_at = pl.ds(4 * half, 2 * part), pl.ds(4 * half + 2 * part, part)

    def dot(a, b, dims):
        return lax.dot_general(a, b, (dims, ((), ())), preferred_element_type=jnp.float32)

    for copy in t_copies:
        copy.wait()
    earlier = lax.broadcasted_iota(jnp.int32, (tok, tok), 0) < lax.broadcasted_iota(jnp.int32, (tok, tok), 1)
    earlier = earlier.astype(jnp.bfloat16)
    place = lax.broadcasted_iota(jnp.int32, (slots, tok), 0).astype(jnp.float32)
    names = lax.broadcasted_iota(jnp.int32, (owners, tok), 0)
    picks, low_picks, probs = {}, {}, {}
    for chunk in range(count):
        found = []
        for y in range(2):
            table = tables[chunk, y].astype(jnp.float32)
            rank = dot((table >= 0.0).astype(jnp.bfloat16), earlier, ((1,), (0,))) + float(y * capacity)
            found.append((table, jnp.where(table >= 0.0, rank, -1.0)))
        for expert in range(2):
            mine = names == where_ref[expert]
            halves, prob = [], None
            for table, rank in found:
                weight = jnp.sum(jnp.where(mine, table, 0.0), axis=0, keepdims=True)
                slot = jnp.sum(jnp.where(mine, rank, 0.0), axis=0, keepdims=True)
                halves.append((place == slot).astype(jnp.float32))
                term = jnp.sum(halves[-1] * weight, axis=1, keepdims=True)
                prob = term if prob is None else prob + term
            picks[chunk, expert] = halves
            low_picks[chunk, expert] = jnp.concatenate(halves, 1).astype(jnp.bfloat16)
            probs[chunk, expert] = prob
    spans = [pl.ds(chunk * slots, slots) for chunk in range(count)]
    sides = [slice(side * half, (side + 1) * half) for side in range(2)]

    def gather(copies, source, offset):
        for chunk in range(count):
            for copy in copies[4 * chunk : 4 * chunk + 4]:
                copy.wait()
            both_picks = jnp.concatenate([low_picks[chunk, expert] for expert in range(2)], 0)
            for side in range(2):
                rows = dot(both_picks, source[chunk, side], ((1,), (0,))).astype(jnp.bfloat16)
                for expert in range(2):
                    columns = pl.ds(offset + side * half, half)
                    outs[expert][spans[chunk], columns] = rows[expert * slots : (expert + 1) * slots]

    gather(x_copies, x_all, 0)
    rows = []
    for expert in range(2):
        rows.append(dot(outs[expert][:, : 2 * half], wgu[expert][...], ((1,), (0,))))
    gather(g_copies, g_all, 2 * half)
    scores = []
    for expert in range(2):
        back = dot(outs[expert][:, 2 * half : 4 * half], wd[expert][...], ((1,), (1,)))
        gate, up = rows[expert][:, :part], rows[expert][:, part:]
        sig = jax.nn.sigmoid(gate)
        act = gate * sig
        hidden = act * up
        scores.append(jnp.sum(hidden * back, axis=1, keepdims=True))
        prob = jnp.concatenate([probs[chunk, expert] for chunk in range(count)], 0)
        hgrad = prob * back
        d_gate = (hgrad * up * sig * (1.0 + gate * (1.0 - sig))).astype(jnp.bfloat16)
        outs[expert][:, both_at] = jnp.concatenate([d_gate, (hgrad * act).astype(jnp.bfloat16)], 1)
        outs[expert][:, scaled_at] = (prob * hidden).astype(jnp.bfloat16)

    extra_rows = packets[0].shape[1] - tok
    per_row = owners // extra_rows
    names = lax.broadcasted_iota(jnp.int32, (extra_rows, half), 0)
    column = lax.broadcasted_iota(jnp.int32, (extra_rows, half), 1) // (2 * tok)
    for chunk in range(count):
        for y in range(2):
            extra = jnp.zeros((extra_rows, half), jnp.float32)
            for expert in range(2):
                part_scores = scores[expert][chunk * slots : (chunk + 1) * slots]
                line = jnp.sum(picks[chunk, expert][y] * part_scores, axis=0, keepdims=True)
                high = line.astype(jnp.bfloat16).astype(jnp.float32)
                line = jnp.concatenate([high, line - high] * (half // (2 * tok)), 1)
                row, cell = where_ref[expert] // per_row, where_ref[expert] % per_row * 2 + where_ref[2]
                extra = extra + jnp.where((names == row) & (column == cell), line, 0.0)
            for side in range(2):
                number, slot = ways[chunk, y, side]
                packets[number][slot, tok:] = extra.astype(jnp.bfloat16)
    early = count == 1
    grads = [outs[expert][:, both_at] for expert in range(2)]
    if early:
        grads = [dot(low_picks[0, expert], grads[expert], ((0,), (0,))).astype(jnp.bfloat16) for expert in range(2)]
    for side in (1, 0):
        low = [dot(grads[expert], wgu[expert][sides[side], :], ((1,), (1,))) for expert in range(2)]
        for chunk in range(count):
            if early:
                total = low[0] + low[1]
            else:
                rows = slice(chunk * slots, (chunk + 1) * slots)
                total = sum(
                    dot(low_picks[chunk, expert], low[expert][rows].astype(jnp.bfloat16), ((0,), (0,)))
                    for expert in range(2)
                )
            for y in range(2):
                number, slot = ways[chunk, y, side]
                packets[number][slot, :tok] = total[y * tok : (y + 1) * tok].astype(jnp.bfloat16)


def rows_call(items, owners, capacity, slots, where, weights, units, tables, after):
    count = len(tables)
    ways = {block: (number, slot) for number, blocks in enumerate(items) for slot, block in enumerate(blocks)}
    tok, half = units[0].shape[0] // 2, units[0].shape[1]
    part, width = weights[2].shape
    widths = (width, width, 2 * part, part)
    packet = (tok + 4 * tok * owners // half, half)
    return pl.pallas_call(
        functools.partial(rows_kernel, count, ways, capacity, slots),
        grid_spec=pltpu.PrefetchScalarGridSpec(
            num_scalar_prefetch=1,
            grid=(1,),
            in_specs=[pl.BlockSpec(memory_space=pltpu.VMEM)] * 4 + [LOOSE] * (5 * count + len(after)),
            out_specs=[pl.BlockSpec(memory_space=pltpu.VMEM)] * (2 + len(items)),
            scratch_shapes=[pltpu.VMEM((count, 2, 2 * tok, half), jnp.bfloat16)] * 2
            + [pltpu.VMEM((count, 2, owners, tok), jnp.bfloat16)]
            + [pltpu.SemaphoreType.DMA((3, 4 * count))],
        ),
        out_shape=[pltpu.VMEM((count * slots, sum(widths)), jnp.bfloat16)] * 2
        + [pltpu.VMEM((len(blocks),) + packet, jnp.bfloat16) for blocks in items],
        compiler_params=pltpu.CompilerParams(vmem_limit_bytes=14 << 20),
        cost_estimate=pl.CostEstimate(
            flops=count * (20 * slots * width * part + 24 * slots * tok * width),
            bytes_accessed=count * 16 * tok * width + 12 * width * part,
            transcendentals=2 * count * slots * part,
        ),
        name="rows",
    )(where, *[pltpu.with_memory_space_constraint(item, pltpu.VMEM) for item in weights], *units, *tables, *after)


def grads_kernel(count, wide, deep, blocks, tp_ref, *refs):
    sources, outs = refs[:count], refs[count:-4]
    wide_all, deep_all, wide_sems, deep_sems = refs[-4:]
    starts = [sum(source.shape[0] for source in sources[:index]) for index in range(count)]
    size = wide_all.shape[2]
    block = pl.program_id(0)

    def copies(column):
        return [
            pltpu.make_async_copy(
                source.at[:, pl.ds(wide + column * size, size)],
                wide_all.at[column, pl.ds(starts[index], source.shape[0])],
                wide_sems.at[column, index],
            )
            for index, source in enumerate(sources)
        ]

    @pl.when(block == 0)
    def _():
        deep_copies = [
            pltpu.make_async_copy(
                source.at[:, pl.ds(deep, deep_all.shape[1])],
                deep_all.at[pl.ds(starts[index], source.shape[0])],
                deep_sems.at[index],
            )
            for index, source in enumerate(sources)
        ]
        for copy in deep_copies:
            copy.start()
        for column in range(blocks):
            for copy in copies(column):
                copy.start()
        for copy in deep_copies:
            copy.wait()

    for column in range(blocks):

        @pl.when(block == column)
        def _(column=column):
            for copy in copies(column):
                copy.wait()

    dims = (((0,), (0,)), ((), ()))
    if len(outs) == 2:
        part = outs[0].shape[2]
        both = lax.dot_general(wide_all[block], deep_all[...], dims, preferred_element_type=jnp.float32)
        outs[0][0] = both[:, :part].astype(jnp.bfloat16)
        outs[1][0] = both[:, part:].astype(jnp.bfloat16)
    else:
        down = lax.dot_general(deep_all[...], wide_all[block], dims, preferred_element_type=jnp.float32)
        outs[0][0] = down.astype(jnp.bfloat16)


def grads_call(which, packed, width, part, down):
    rows, count = sum(item.shape[0] for item in packed), len(packed)
    step = math.gcd(width // 2, 512)
    per = width // 2 // step
    deep = part if down else 2 * part

    def place(i, w):
        return (i + w[0] * per) % (2 * per)

    if down:
        specs = [pl.BlockSpec((1, part, step), lambda i, w: (0, 0, place(i, w)))]
        shapes = [(1, part, width)]
    else:
        specs = [pl.BlockSpec((1, step, part), lambda i, w: (0, place(i, w), 0))] * 2
        shapes = [(1, width, part)] * 2
    starts = (width, 2 * width + 2 * part) if down else (0, 2 * width)
    return pl.pallas_call(
        functools.partial(grads_kernel, count, *starts, 2 * per),
        grid_spec=pltpu.PrefetchScalarGridSpec(
            num_scalar_prefetch=1,
            grid=(2 * per,),
            in_specs=[LOOSE] * count,
            out_specs=specs,
            scratch_shapes=[
                pltpu.VMEM((2 * per, rows, step), jnp.bfloat16),
                pltpu.VMEM((rows, deep), jnp.bfloat16),
                pltpu.SemaphoreType.DMA((2 * per, count)),
                pltpu.SemaphoreType.DMA((count,)),
            ],
        ),
        out_shape=[jax.ShapeDtypeStruct(shape, jnp.bfloat16) for shape in shapes],
        compiler_params=pltpu.CompilerParams(vmem_limit_bytes=14 << 20),
        cost_estimate=pl.CostEstimate(
            flops=2 * rows * width * deep, bytes_accessed=2 * rows * (width + deep), transcendentals=0
        ),
        name="grads",
    )(which, *packed)


def dense_device(tokens, out_grad, routes, probs, w_gate, w_up, w_down):
    owners = lax.axis_size(("role", "ep"))
    ep = lax.axis_size("ep")
    n_y = 2
    n_z = ep // n_y
    tok_rows, half = tokens.shape
    capacity = slot_capacity(tok_rows, routes.shape[1], owners)
    slots = -(-n_y * capacity // 16) * 16
    role, place, which = lax.axis_index("role"), lax.axis_index("ep"), lax.axis_index("tp")

    def over_x(array):
        return lax.ppermute(array, "tp", [(0, 1), (1, 0)])

    def over_role(array):
        return lax.ppermute(array, "role", [(0, 1), (1, 0)])

    def over_y(array):
        return lax.ppermute(array, "ep", [(i, i + 1 - 2 * (i % n_y)) for i in range(ep)])

    def over_z(array, shift):
        return lax.ppermute(array, "ep", [(i, (i + shift * n_y) % ep) for i in range(ep)])

    def tied(values, others):
        return lax.optimization_barrier((list(values), list(others)))[0]

    last = n_z - 1
    routes_in = []
    for z in range(n_z):
        shift = -1 if z == last and z > 1 else 1
        if z:
            routes_in.append(((z, 0, 0), (0 if z in (1, last) else z - 1, 0, 0), functools.partial(over_z, shift=shift)))
        routes_in.append(((z, 1, 0), (z, 0, 0), over_y))
        routes_in.append(((z, 0, 1), (z, 0, 0), over_x))
        if z == 0:
            routes_in.append(((z, 1, 1), (z, 1, 0), over_x))
        elif z in (1, last):
            routes_in.append(((z, 1, 1), (0, 1, 1), functools.partial(over_z, shift=shift)))
        else:
            routes_in.append(((z, 1, 1), (z, 0, 1), over_y))
    routes_in.sort(key=lambda item: (item[0][0] % 2 if item[2] in (over_x, over_y) else 0, sum(item[0][1:])))

    rounds, waiting, there = [], list(routes_in), {(0, 0, 0)}
    while waiting:
        moves = {}
        for item in waiting:
            axis = item[2] if item[2] in (over_x, over_y) else over_z
            if item[1] in there and axis not in moves:
                moves[axis] = item
        rounds.append(list(moves.values()))
        there |= {item[0] for item in rounds[-1]}
        waiting = [item for item in waiting if item[0] not in there]

    which_ref = which.reshape(1).astype(jnp.int32)
    where = jnp.stack([role * ep + place, (1 - role) * ep + place, which]).astype(jnp.int32)
    both_w, down_w = weights_call(which_ref, w_gate, w_up, w_down)
    width, part = both_w.shape[0], down_w.shape[0]

    def rows_of(steps, items, after):
        four = [units[z, y, x] for z in steps for y in range(2) for x in range(2)]
        return rows_call(items, owners, capacity, slots, where, weights, four, [tables[z] for z in steps], after)

    units = {(0, 0, 0): join_call(tokens, out_grad)}
    settled = dict(units)
    for number, moves in enumerate(rounds):
        arrived = {target: move(settled[source]) for target, source, move in moves}
        units.update(arrived)
        settled.update(arrived)
        extra = []
        if number == 0:
            extra = [both_w, down_w]
            both_w, down_w, routes, probs = tied([both_w, down_w, routes, probs], arrived.values())
            weights = (both_w, over_role(both_w), down_w, over_role(down_w))
            chosen = routes[:, :, None] == jnp.arange(owners, dtype=jnp.int32)
            table = jnp.sum(jnp.where(chosen, probs[:, :, None].astype(jnp.float32) + 1.0, 0.0), axis=1) - 1.0
            table = table.astype(jnp.bfloat16).T
            table = jnp.stack([table, over_y(table)])
        if number == 1:
            (table,) = tied([table], arrived.values())
            tables = [over_z(table, z) if z else table for z in range(n_z)]
        if number == 2:
            mine_0, other_0, near, side_0, far, y_0 = rows_of(
                [0], [[(0, 0, 0)], [(0, 0, 1)], [(0, 1, 1)], [(0, 1, 0)]], []
            )
            extra = [mine_0]
        names = list(settled)
        settled = dict(zip(names, tied([settled[item] for item in names], extra)))

    def total(*blocks):
        return sum(block.astype(jnp.float32) for block in blocks).astype(jnp.bfloat16)

    items = [[(1, 1, 1)], [(1, 0, 1)], [(0, 0, 1)], [(0, 1, 0)], [(0, 1, 1)], [(0, 0, 0)], [(1, 0, 0)], [(1, 1, 0)]]
    mine_1, other_1, x_2, x_20, x_1, y_1, z_1, keep_1, keep_2, keep_2y = rows_of([1, 2], items, [])
    other_1, x_2, x_20, x_1, y_1, z_1 = tied([other_1, x_2, x_20, x_1, y_1, z_1], arrived.values())
    from_x2, from_y1, from_z1 = over_x(x_2), over_y(y_1), over_z(z_1, -1)
    from_x20 = over_x(x_20)
    items = [[(0, 0, 1)], [(0, 1, 0)], [(0, 1, 1)], [(0, 0, 0)]]
    mine_3, other_3, x_3, y_3, z_3, keep_3 = rows_of([3], items, [mine_1])
    mine_3, other_3, x_3, y_3, z_3, keep_2y = tied(
        [mine_3, other_3, x_3, y_3, z_3, keep_2y], [from_x2, from_y1, from_z1]
    )
    from_z3, from_x3, from_y2, from_y3 = over_z(z_3, 1), over_x(x_3), over_y(total(keep_2y, from_x2)), over_y(y_3)
    packed = [mine_0, over_role(other_0), mine_1, over_role(other_1), mine_3, over_role(other_3)]
    d_gate, d_up = grads_call(which_ref, packed, width, part, False)
    from_z3, from_x20, from_y2, x_1 = tied([from_z3, from_x20, from_y2, x_1], [d_gate, d_up])
    from_x1 = over_x(x_1)
    from_far = over_y(total(far, from_z1, from_z3))
    from_z2 = over_z(total(keep_2, from_x20, from_y2), 1)
    (d_down,) = grads_call(which_ref, packed, width, part, True)
    (from_x1,) = tied([from_x1], [d_down])
    home_1 = total(keep_1, from_x1, from_y1)
    from_far, from_x3, from_y3, from_z2, y_0 = tied([from_far, from_x3, from_y3, from_z2, y_0], [d_down, home_1])
    from_x0 = over_x(total(side_0, from_far))
    home_1 = over_z(home_1, -1)
    home_3 = over_z(total(keep_3, from_x3, from_y3, from_z2), 1)
    from_y0 = over_y(y_0)
    home = (near, from_x0, home_3, home_1, from_y0)
    d_tok = sum(block[0, :tok_rows].astype(jnp.float32) for block in home).astype(jnp.bfloat16)
    home = sum(block[0, tok_rows:].astype(jnp.float32) for block in home)
    score = jnp.sum(home.reshape(owners, 4, tok_rows), axis=1).T
    d_probs = jnp.sum(jnp.where(chosen, score[:, None, :], 0.0), axis=2)
    return d_tok, d_probs, d_gate, d_up, d_down


def per_device(tokens, out_grad, routes, probs, w_gate, w_up, w_down):
    owners = lax.axis_size(("role", "ep"))
    tok_rows, top_count = routes.shape
    paired = lax.axis_size("tp") == 2 and lax.axis_size("role") == 2 and lax.axis_size("ep") == 8
    if paired and 2 * slot_capacity(tok_rows, top_count, owners) >= tok_rows:
        return dense_device(tokens, out_grad, routes, probs, w_gate, w_up, w_down)
    return routed_device(tokens, out_grad, routes, probs, w_gate, w_up, w_down)


def solution(mesh):
    in_specs = (
        P(("groups", "role", "ep"), "tp"),
        P(("groups", "role", "ep"), "tp"),
        P(("groups", "role", "ep"), None),
        P(("groups", "role", "ep"), None),
        P(("role", "ep"), None, "tp"),
        P(("role", "ep"), None, "tp"),
        P(("role", "ep"), "tp", None),
    )
    out_specs = (
        P(("groups", "role", "ep"), "tp"),
        P(("groups", "role", "ep"), None),
        P(("groups", "role", "ep"), None, "tp"),
        P(("groups", "role", "ep"), None, "tp"),
        P(("groups", "role", "ep"), "tp", None),
    )
    return jax.shard_map(
        per_device, mesh=mesh, in_specs=in_specs, out_specs=out_specs, check_vma=False
    )
```

```python
import functools
import math

import jax
import jax.numpy as jnp
from jax import lax
from jax.experimental import pallas as pl
from jax.experimental.pallas import tpu as pltpu
from jax.sharding import PartitionSpec as P


def pad_rows(array):
    return jnp.concatenate([array, jnp.zeros((1, array.shape[1]), array.dtype)], 0)


def routed_device(tokens, out_grad, routes, probs, w_gate, w_up, w_down):
    owners = lax.axis_size(("role", "ep"))
    tok_rows, top_count = routes.shape
    width_full = w_gate.shape[1]
    part_width = w_gate.shape[2]
    capacity = min(tok_rows, tok_rows * top_count * 9 // (8 * owners))
    entry_total = tok_rows * top_count
    routes_flat = routes.reshape(-1)
    onehot = (routes_flat[:, None] == jnp.arange(owners, dtype=jnp.int32)[None, :]).astype(
        jnp.int32
    )
    before = jnp.cumsum(onehot, axis=0) - onehot
    slot_index = jnp.sum(before * onehot, axis=1)
    target = routes_flat * capacity + slot_index
    row_count = owners * capacity
    entry_of_slot = (
        jnp.full((row_count,), entry_total, jnp.int32)
        .at[target]
        .set(jnp.arange(entry_total, dtype=jnp.int32))
    )
    token_of_slot = entry_of_slot // top_count
    padded_prob = jnp.concatenate([probs.reshape(-1), jnp.zeros((1,), probs.dtype)], 0)
    send_prob = padded_prob[entry_of_slot].reshape(owners, capacity)
    send_x = pad_rows(tokens)[token_of_slot]
    send_g = pad_rows(out_grad)[token_of_slot]
    slice_x, slice_g, recv_p = (
        lax.all_to_all(
            send_x.reshape(owners, capacity, tokens.shape[1]),
            ("role", "ep"),
            split_axis=0,
            concat_axis=0,
            tiled=True,
        ),
        lax.all_to_all(
            send_g.reshape(owners, capacity, tokens.shape[1]),
            ("role", "ep"),
            split_axis=0,
            concat_axis=0,
            tiled=True,
        ),
        lax.all_to_all(send_prob, ("role", "ep"), split_axis=0, concat_axis=0, tiled=True),
    )
    recv_x, recv_g = (
        lax.all_gather(slice_x, "tp", axis=2, tiled=True),
        lax.all_gather(slice_g, "tp", axis=2, tiled=True),
    )
    rows_x = recv_x.reshape(row_count, width_full)
    rows_g = recv_g.reshape(row_count, width_full)
    weight_p = recv_p.reshape(row_count, 1).astype(jnp.float32)
    gate_up = jnp.concatenate([w_gate[0], w_up[0]], 1)
    down_shard = w_down[0]
    both_rows = jnp.dot(rows_x, gate_up, preferred_element_type=jnp.float32)
    gate_rows = both_rows[:, :part_width]
    up_rows = both_rows[:, part_width:]
    sigmoid_gate = jax.nn.sigmoid(gate_rows)
    activated = gate_rows * sigmoid_gate
    hidden = activated * up_rows
    back_rows = lax.dot_general(
        rows_g, down_shard, (((1,), (1,)), ((), ())), preferred_element_type=jnp.float32
    )
    scores = lax.psum(jnp.sum(hidden * back_rows, axis=1), "tp")
    hidden_grad = weight_p * back_rows
    d_gate_rows = (
        hidden_grad * up_rows * sigmoid_gate * (1.0 + gate_rows * (1.0 - sigmoid_gate))
    ).astype(jnp.bfloat16)
    d_up_rows = (hidden_grad * activated).astype(jnp.bfloat16)
    d_both = jnp.concatenate([d_gate_rows, d_up_rows], 1)
    scaled = (weight_p * hidden).astype(jnp.bfloat16)
    grad_down = lax.dot_general(
        scaled, rows_g, (((0,), (0,)), ((), ())), preferred_element_type=jnp.float32
    )
    grad_both = lax.dot_general(
        rows_x, d_both, (((0,), (0,)), ((), ())), preferred_element_type=jnp.float32
    )
    grad_gate = grad_both[:, :part_width]
    grad_up = grad_both[:, part_width:]
    partial_low = lax.dot_general(
        d_both, gate_up, (((1,), (1,)), ((), ())), preferred_element_type=jnp.float32
    ).astype(jnp.bfloat16)
    home_s = lax.all_to_all(
        scores.reshape(owners, capacity), ("role", "ep"), split_axis=0, concat_axis=0, tiled=True
    )
    summed = lax.psum_scatter(
        partial_low.reshape(owners, capacity, width_full), "tp", scatter_dimension=2, tiled=True
    ).astype(jnp.float32)
    summed_low = summed.astype(jnp.bfloat16)
    home_x = lax.all_to_all(summed_low, ("role", "ep"), split_axis=0, concat_axis=0, tiled=True)
    slice_width = summed.shape[2]
    route_rows = home_x.reshape(row_count, slice_width).astype(jnp.float32)
    d_tok = (
        jnp.zeros((tok_rows + 1, slice_width), jnp.float32)
        .at[token_of_slot]
        .add(route_rows)[:tok_rows]
    )
    d_probs = home_s.reshape(-1)[target].reshape(tok_rows, top_count)
    return (
        d_tok.astype(jnp.bfloat16),
        d_probs,
        grad_gate.astype(jnp.bfloat16)[None],
        grad_up.astype(jnp.bfloat16)[None],
        grad_down.astype(jnp.bfloat16)[None],
    )


def slot_capacity(tok_rows, top_count, owners):
    return min(tok_rows, tok_rows * top_count * 9 // (8 * owners))


LOOSE = pl.BlockSpec(memory_space=pl.ANY)


def weights_kernel(tp_ref, wg_ref, wu_ref, wd_ref, both_ref, down_ref):
    part = wg_ref.shape[2]
    both_ref[:, :part] = wg_ref[0]
    both_ref[:, part:] = wu_ref[0]
    down_ref[...] = wd_ref[0]


def weights_call(which, w_gate, w_up, w_down):
    _, width, part = w_gate.shape
    half = width // 2

    def place(i, w):
        return (i + w[0]) % 2

    return pl.pallas_call(
        weights_kernel,
        grid_spec=pltpu.PrefetchScalarGridSpec(
            num_scalar_prefetch=1,
            grid=(2,),
            in_specs=[
                pl.BlockSpec((1, half, part), lambda i, w: (0, place(i, w), 0)),
                pl.BlockSpec((1, half, part), lambda i, w: (0, place(i, w), 0)),
                pl.BlockSpec((1, part, half), lambda i, w: (0, 0, place(i, w))),
            ],
            out_specs=[
                pl.BlockSpec((half, 2 * part), lambda i, w: (i, 0)),
                pl.BlockSpec((part, half), lambda i, w: (0, i)),
            ],
        ),
        out_shape=[
            jax.ShapeDtypeStruct((width, 2 * part), jnp.bfloat16),
            jax.ShapeDtypeStruct((part, width), jnp.bfloat16),
        ],
        compiler_params=pltpu.CompilerParams(vmem_limit_bytes=12 << 20),
        cost_estimate=pl.CostEstimate(flops=0, bytes_accessed=12 * width * part, transcendentals=0),
        name="weights",
    )(which, *[pltpu.with_memory_space_constraint(item, pltpu.HBM) for item in (w_gate, w_up, w_down)])


def join_kernel(top_ref, bottom_ref, out_ref, sems):
    rows = top_ref.shape[0]
    copies = [
        pltpu.make_async_copy(top_ref, out_ref.at[pl.ds(0, rows)], sems.at[0]),
        pltpu.make_async_copy(bottom_ref, out_ref.at[pl.ds(rows, rows)], sems.at[1]),
    ]
    for copy in copies:
        copy.start()
    for copy in copies:
        copy.wait()


def join_call(top, bottom):
    rows, columns = top.shape
    return pl.pallas_call(
        join_kernel,
        in_specs=[LOOSE] * 2,
        out_specs=pl.BlockSpec(memory_space=pltpu.VMEM),
        out_shape=pltpu.VMEM((2 * rows, columns), top.dtype),
        scratch_shapes=[pltpu.SemaphoreType.DMA((2,))],
        compiler_params=pltpu.CompilerParams(vmem_limit_bytes=8 << 20),
        cost_estimate=pl.CostEstimate(flops=0, bytes_accessed=8 * rows * columns, transcendentals=0),
        name="join",
    )(*[pltpu.with_memory_space_constraint(item, pltpu.HBM) for item in (top, bottom)])


def rows_kernel(count, ways, capacity, slots, where_ref, *refs):
    weights_in, units_in, tables_in = refs[:4], refs[4 : 4 + 4 * count], refs[4 + 4 * count : 4 + 5 * count]
    leaves = 1 + max(way[0] for way in ways.values())
    refs = refs[len(refs) - 6 - leaves :]
    outs, packets, refs = refs[:2], refs[2 : 2 + leaves], refs[2 + leaves :]
    x_all, g_all, tables, unit_sems = refs
    half, tok = x_all.shape[3], x_all.shape[2] // 2
    part = weights_in[2].shape[0]
    owners = tables.shape[2]
    wgu, wd = weights_in[:2], weights_in[2:]

    x_copies, g_copies = [], []
    for index, unit in enumerate(units_in):
        chunk, y, x = index // 4, index // 2 % 2, index % 2
        rows = pl.ds(y * tok, tok)
        x_copies.append(pltpu.make_async_copy(unit.at[pl.ds(0, tok)], x_all.at[chunk, x, rows], unit_sems.at[0, index]))
        g_copies.append(pltpu.make_async_copy(unit.at[pl.ds(tok, tok)], g_all.at[chunk, x, rows], unit_sems.at[1, index]))
    t_copies = [
        pltpu.make_async_copy(table, tables.at[chunk], unit_sems.at[2, chunk]) for chunk, table in enumerate(tables_in)
    ]
    for copy in t_copies + x_copies + g_copies:
        copy.start()
    both_at, scaled_at = pl.ds(4 * half, 2 * part), pl.ds(4 * half + 2 * part, part)

    def dot(a, b, dims):
        return lax.dot_general(a, b, (dims, ((), ())), preferred_element_type=jnp.float32)

    for copy in t_copies:
        copy.wait()
    earlier = lax.broadcasted_iota(jnp.int32, (tok, tok), 0) < lax.broadcasted_iota(jnp.int32, (tok, tok), 1)
    earlier = earlier.astype(jnp.bfloat16)
    place = lax.broadcasted_iota(jnp.int32, (slots, tok), 0).astype(jnp.float32)
    names = lax.broadcasted_iota(jnp.int32, (owners, tok), 0)
    picks, low_picks, probs = {}, {}, {}
    for chunk in range(count):
        found = []
        for y in range(2):
            table = tables[chunk, y].astype(jnp.float32)
            rank = dot((table >= 0.0).astype(jnp.bfloat16), earlier, ((1,), (0,))) + float(y * capacity)
            found.append((table, jnp.where(table >= 0.0, rank, -1.0)))
        for expert in range(2):
            mine = names == where_ref[expert]
            halves, prob = [], None
            for table, rank in found:
                weight = jnp.sum(jnp.where(mine, table, 0.0), axis=0, keepdims=True)
                slot = jnp.sum(jnp.where(mine, rank, 0.0), axis=0, keepdims=True)
                halves.append((place == slot).astype(jnp.float32))
                term = jnp.sum(halves[-1] * weight, axis=1, keepdims=True)
                prob = term if prob is None else prob + term
            picks[chunk, expert] = halves
            low_picks[chunk, expert] = jnp.concatenate(halves, 1).astype(jnp.bfloat16)
            probs[chunk, expert] = prob
    spans = [pl.ds(chunk * slots, slots) for chunk in range(count)]
    sides = [slice(side * half, (side + 1) * half) for side in range(2)]

    def gather(copies, source, offset):
        for chunk in range(count):
            for copy in copies[4 * chunk : 4 * chunk + 4]:
                copy.wait()
            both_picks = jnp.concatenate([low_picks[chunk, expert] for expert in range(2)], 0)
            for side in range(2):
                rows = dot(both_picks, source[chunk, side], ((1,), (0,))).astype(jnp.bfloat16)
                for expert in range(2):
                    columns = pl.ds(offset + side * half, half)
                    outs[expert][spans[chunk], columns] = rows[expert * slots : (expert + 1) * slots]

    gather(x_copies, x_all, 0)
    rows = []
    for expert in range(2):
        rows.append(dot(outs[expert][:, : 2 * half], wgu[expert][...], ((1,), (0,))))
    gather(g_copies, g_all, 2 * half)
    scores = []
    for expert in range(2):
        back = dot(outs[expert][:, 2 * half : 4 * half], wd[expert][...], ((1,), (1,)))
        gate, up = rows[expert][:, :part], rows[expert][:, part:]
        sig = jax.nn.sigmoid(gate)
        act = gate * sig
        hidden = act * up
        scores.append(jnp.sum(hidden * back, axis=1, keepdims=True))
        prob = jnp.concatenate([probs[chunk, expert] for chunk in range(count)], 0)
        hgrad = prob * back
        d_gate = (hgrad * up * sig * (1.0 + gate * (1.0 - sig))).astype(jnp.bfloat16)
        outs[expert][:, both_at] = jnp.concatenate([d_gate, (hgrad * act).astype(jnp.bfloat16)], 1)
        outs[expert][:, scaled_at] = (prob * hidden).astype(jnp.bfloat16)

    extra_rows = packets[0].shape[1] - tok
    per_row = owners // extra_rows
    names = lax.broadcasted_iota(jnp.int32, (extra_rows, half), 0)
    column = lax.broadcasted_iota(jnp.int32, (extra_rows, half), 1) // (2 * tok)
    for chunk in range(count):
        for y in range(2):
            extra = jnp.zeros((extra_rows, half), jnp.float32)
            for expert in range(2):
                part_scores = scores[expert][chunk * slots : (chunk + 1) * slots]
                line = jnp.sum(picks[chunk, expert][y] * part_scores, axis=0, keepdims=True)
                high = line.astype(jnp.bfloat16).astype(jnp.float32)
                line = jnp.concatenate([high, line - high] * (half // (2 * tok)), 1)
                row, cell = where_ref[expert] // per_row, where_ref[expert] % per_row * 2 + where_ref[2]
                extra = extra + jnp.where((names == row) & (column == cell), line, 0.0)
            for side in range(2):
                number, slot = ways[chunk, y, side]
                packets[number][slot, tok:] = extra.astype(jnp.bfloat16)
    early = count == 1
    grads = [outs[expert][:, both_at] for expert in range(2)]
    if early:
        grads = [dot(low_picks[0, expert], grads[expert], ((0,), (0,))).astype(jnp.bfloat16) for expert in range(2)]
    for side in (1, 0):
        low = [dot(grads[expert], wgu[expert][sides[side], :], ((1,), (1,))) for expert in range(2)]
        for chunk in range(count):
            if early:
                total = low[0] + low[1]
            else:
                rows = slice(chunk * slots, (chunk + 1) * slots)
                total = sum(
                    dot(low_picks[chunk, expert], low[expert][rows].astype(jnp.bfloat16), ((0,), (0,)))
                    for expert in range(2)
                )
            for y in range(2):
                number, slot = ways[chunk, y, side]
                packets[number][slot, :tok] = total[y * tok : (y + 1) * tok].astype(jnp.bfloat16)


def rows_call(items, owners, capacity, slots, where, weights, units, tables, after):
    count = len(tables)
    ways = {block: (number, slot) for number, blocks in enumerate(items) for slot, block in enumerate(blocks)}
    tok, half = units[0].shape[0] // 2, units[0].shape[1]
    part, width = weights[2].shape
    widths = (width, width, 2 * part, part)
    packet = (tok + 4 * tok * owners // half, half)
    return pl.pallas_call(
        functools.partial(rows_kernel, count, ways, capacity, slots),
        grid_spec=pltpu.PrefetchScalarGridSpec(
            num_scalar_prefetch=1,
            grid=(1,),
            in_specs=[pl.BlockSpec(memory_space=pltpu.VMEM)] * 4 + [LOOSE] * (5 * count + len(after)),
            out_specs=[pl.BlockSpec(memory_space=pltpu.VMEM)] * (2 + len(items)),
            scratch_shapes=[pltpu.VMEM((count, 2, 2 * tok, half), jnp.bfloat16)] * 2
            + [pltpu.VMEM((count, 2, owners, tok), jnp.bfloat16)]
            + [pltpu.SemaphoreType.DMA((3, 4 * count))],
        ),
        out_shape=[pltpu.VMEM((count * slots, sum(widths)), jnp.bfloat16)] * 2
        + [pltpu.VMEM((len(blocks),) + packet, jnp.bfloat16) for blocks in items],
        compiler_params=pltpu.CompilerParams(vmem_limit_bytes=14 << 20),
        cost_estimate=pl.CostEstimate(
            flops=count * (20 * slots * width * part + 24 * slots * tok * width),
            bytes_accessed=count * 16 * tok * width + 12 * width * part,
            transcendentals=2 * count * slots * part,
        ),
        name="rows",
    )(where, *[pltpu.with_memory_space_constraint(item, pltpu.VMEM) for item in (*weights, *units, *tables)], *after)


def grads_kernel(count, wide, deep, blocks, tp_ref, *refs):
    sources, outs = refs[:count], refs[count:-4]
    wide_all, deep_all, wide_sems, deep_sems = refs[-4:]
    starts = [sum(source.shape[0] for source in sources[:index]) for index in range(count)]
    size = wide_all.shape[2]
    block = pl.program_id(0)

    def copies(column):
        return [
            pltpu.make_async_copy(
                source.at[:, pl.ds(wide + column * size, size)],
                wide_all.at[column, pl.ds(starts[index], source.shape[0])],
                wide_sems.at[column, index],
            )
            for index, source in enumerate(sources)
        ]

    @pl.when(block == 0)
    def _():
        deep_copies = [
            pltpu.make_async_copy(
                source.at[:, pl.ds(deep, deep_all.shape[1])],
                deep_all.at[pl.ds(starts[index], source.shape[0])],
                deep_sems.at[index],
            )
            for index, source in enumerate(sources)
        ]
        for copy in deep_copies:
            copy.start()
        for column in range(blocks):
            for copy in copies(column):
                copy.start()
        for copy in deep_copies:
            copy.wait()

    for column in range(blocks):

        @pl.when(block == column)
        def _(column=column):
            for copy in copies(column):
                copy.wait()

    dims = (((0,), (0,)), ((), ()))
    if len(outs) == 2:
        part = outs[0].shape[2]
        both = lax.dot_general(wide_all[block], deep_all[...], dims, preferred_element_type=jnp.float32)
        outs[0][0] = both[:, :part].astype(jnp.bfloat16)
        outs[1][0] = both[:, part:].astype(jnp.bfloat16)
    else:
        down = lax.dot_general(deep_all[...], wide_all[block], dims, preferred_element_type=jnp.float32)
        outs[0][0] = down.astype(jnp.bfloat16)


def grads_call(which, packed, width, part, down):
    rows, count = sum(item.shape[0] for item in packed), len(packed)
    step = math.gcd(width // 2, 512)
    per = width // 2 // step
    deep = part if down else 2 * part

    def place(i, w):
        return (i + w[0] * per) % (2 * per)

    if down:
        specs = [pl.BlockSpec((1, part, step), lambda i, w: (0, 0, place(i, w)))]
        shapes = [(1, part, width)]
    else:
        specs = [pl.BlockSpec((1, step, part), lambda i, w: (0, place(i, w), 0))] * 2
        shapes = [(1, width, part)] * 2
    starts = (width, 2 * width + 2 * part) if down else (0, 2 * width)
    return pl.pallas_call(
        functools.partial(grads_kernel, count, *starts, 2 * per),
        grid_spec=pltpu.PrefetchScalarGridSpec(
            num_scalar_prefetch=1,
            grid=(2 * per,),
            in_specs=[LOOSE] * count,
            out_specs=specs,
            scratch_shapes=[
                pltpu.VMEM((2 * per, rows, step), jnp.bfloat16),
                pltpu.VMEM((rows, deep), jnp.bfloat16),
                pltpu.SemaphoreType.DMA((2 * per, count)),
                pltpu.SemaphoreType.DMA((count,)),
            ],
        ),
        out_shape=[jax.ShapeDtypeStruct(shape, jnp.bfloat16) for shape in shapes],
        compiler_params=pltpu.CompilerParams(vmem_limit_bytes=14 << 20),
        cost_estimate=pl.CostEstimate(
            flops=2 * rows * width * deep, bytes_accessed=2 * rows * (width + deep), transcendentals=0
        ),
        name="grads",
    )(which, *packed)


def dense_device(tokens, out_grad, routes, probs, w_gate, w_up, w_down):
    owners = lax.axis_size(("role", "ep"))
    ep = lax.axis_size("ep")
    n_y = 2
    n_z = ep // n_y
    tok_rows, half = tokens.shape
    capacity = slot_capacity(tok_rows, routes.shape[1], owners)
    slots = -(-n_y * capacity // 16) * 16
    role, place, which = lax.axis_index("role"), lax.axis_index("ep"), lax.axis_index("tp")

    def over_x(array):
        return lax.ppermute(array, "tp", [(0, 1), (1, 0)])

    def over_role(array):
        return lax.ppermute(array, "role", [(0, 1), (1, 0)])

    def over_y(array):
        return lax.ppermute(array, "ep", [(i, i + 1 - 2 * (i % n_y)) for i in range(ep)])

    def over_z(array, shift):
        return lax.ppermute(array, "ep", [(i, (i + shift * n_y) % ep) for i in range(ep)])

    def tied(values, others):
        return lax.optimization_barrier((list(values), list(others)))[0]

    last = n_z - 1
    routes_in = []
    for z in range(n_z):
        shift = -1 if z == last and z > 1 else 1
        if z:
            routes_in.append(((z, 0, 0), (0 if z in (1, last) else z - 1, 0, 0), functools.partial(over_z, shift=shift)))
        routes_in.append(((z, 1, 0), (z, 0, 0), over_y))
        routes_in.append(((z, 0, 1), (z, 0, 0), over_x))
        if z == 0:
            routes_in.append(((z, 1, 1), (z, 1, 0), over_x))
        elif z in (1, last):
            routes_in.append(((z, 1, 1), (0, 1, 1), functools.partial(over_z, shift=shift)))
        else:
            routes_in.append(((z, 1, 1), (z, 0, 1), over_y))
    routes_in.sort(key=lambda item: (item[0][0] % 2 if item[2] in (over_x, over_y) else 0, sum(item[0][1:])))

    rounds, waiting, there = [], list(routes_in), {(0, 0, 0)}
    while waiting:
        moves = {}
        for item in waiting:
            axis = item[2] if item[2] in (over_x, over_y) else over_z
            if item[1] in there and axis not in moves:
                moves[axis] = item
        rounds.append(list(moves.values()))
        there |= {item[0] for item in rounds[-1]}
        waiting = [item for item in waiting if item[0] not in there]

    which_ref = which.reshape(1).astype(jnp.int32)
    where = jnp.stack([role * ep + place, (1 - role) * ep + place, which]).astype(jnp.int32)
    both_w, down_w = weights_call(which_ref, w_gate, w_up, w_down)
    width, part = both_w.shape[0], down_w.shape[0]

    def rows_of(steps, items, after):
        four = [units[z, y, x] for z in steps for y in range(2) for x in range(2)]
        return rows_call(items, owners, capacity, slots, where, weights, four, [tables[z] for z in steps], after)

    units = {(0, 0, 0): join_call(tokens, out_grad)}
    settled = dict(units)
    for number, moves in enumerate(rounds):
        arrived = {target: move(settled[source]) for target, source, move in moves}
        units.update(arrived)
        settled.update(arrived)
        extra = []
        if number == 0:
            extra = [both_w, down_w]
            both_w, down_w, routes, probs = tied([both_w, down_w, routes, probs], arrived.values())
            weights = (both_w, over_role(both_w), down_w, over_role(down_w))
            chosen = routes[:, :, None] == jnp.arange(owners, dtype=jnp.int32)
            table = jnp.sum(jnp.where(chosen, probs[:, :, None].astype(jnp.float32) + 1.0, 0.0), axis=1) - 1.0
            table = table.astype(jnp.bfloat16).T
            table = jnp.stack([table, over_y(table)])
        if number == 1:
            (table,) = tied([table], arrived.values())
            tables = [over_z(table, z) if z else table for z in range(n_z)]
        if number == 2:
            mine_0, other_0, near, side_0, far, y_0 = rows_of(
                [0], [[(0, 0, 0)], [(0, 0, 1)], [(0, 1, 1)], [(0, 1, 0)]], []
            )
            extra = [mine_0]
        names = list(settled)
        settled = dict(zip(names, tied([settled[item] for item in names], extra)))

    def total(*blocks):
        return sum(block.astype(jnp.float32) for block in blocks).astype(jnp.bfloat16)

    items = [[(1, 1, 1)], [(1, 0, 1)], [(0, 0, 1)], [(0, 1, 0)], [(0, 1, 1)], [(0, 0, 0)], [(1, 0, 0)], [(1, 1, 0)]]
    mine_1, other_1, x_2, x_20, x_1, y_1, z_1, keep_1, keep_2, keep_2y = rows_of([1, 2], items, tables[3:])
    other_1, x_2, x_20, x_1, y_1, z_1 = tied([other_1, x_2, x_20, x_1, y_1, z_1], arrived.values())
    from_x2, from_y1, from_z1 = over_x(x_2), over_y(y_1), over_z(z_1, -1)
    from_x20 = over_x(x_20)
    items = [[(0, 0, 1)], [(0, 1, 0)], [(0, 1, 1)], [(0, 0, 0)]]
    mine_3, other_3, x_3, y_3, z_3, keep_3 = rows_of([3], items, [mine_1])
    mine_3, other_3, x_3, y_3, z_3, keep_2y = tied(
        [mine_3, other_3, x_3, y_3, z_3, keep_2y], [from_x2, from_y1, from_z1]
    )
    from_z3, from_x3, from_y2, from_y3 = over_z(z_3, 1), over_x(x_3), over_y(total(keep_2y, from_x2)), over_y(y_3)
    packed = [mine_0, over_role(other_0), mine_1, over_role(other_1), mine_3, over_role(other_3)]
    d_gate, d_up = grads_call(which_ref, packed, width, part, False)
    from_z3, from_x20, from_y2, x_1 = tied([from_z3, from_x20, from_y2, x_1], [d_gate, d_up])
    from_x1 = over_x(x_1)
    from_far = over_y(total(far, from_z1, from_z3))
    from_z2 = over_z(total(keep_2, from_x20, from_y2), 1)
    (d_down,) = grads_call(which_ref, packed, width, part, True)
    (from_x1,) = tied([from_x1], [d_down])
    home_1 = total(keep_1, from_x1, from_y1)
    from_far, from_x3, from_y3, from_z2, y_0 = tied([from_far, from_x3, from_y3, from_z2, y_0], [d_down, home_1])
    from_x0 = over_x(total(side_0, from_far))
    home_1 = over_z(home_1, -1)
    home_3 = over_z(total(keep_3, from_x3, from_y3, from_z2), 1)
    from_y0 = over_y(y_0)
    home = (near, from_x0, home_3, home_1, from_y0)
    d_tok = sum(block[0, :tok_rows].astype(jnp.float32) for block in home).astype(jnp.bfloat16)
    home = sum(block[0, tok_rows:].astype(jnp.float32) for block in home)
    score = jnp.sum(home.reshape(owners, 4, tok_rows), axis=1).T
    d_probs = jnp.sum(jnp.where(chosen, score[:, None, :], 0.0), axis=2)
    return d_tok, d_probs, d_gate, d_up, d_down


def per_device(tokens, out_grad, routes, probs, w_gate, w_up, w_down):
    owners = lax.axis_size(("role", "ep"))
    tok_rows, top_count = routes.shape
    paired = lax.axis_size("tp") == 2 and lax.axis_size("role") == 2 and lax.axis_size("ep") == 8
    if paired and 2 * slot_capacity(tok_rows, top_count, owners) >= tok_rows:
        return dense_device(tokens, out_grad, routes, probs, w_gate, w_up, w_down)
    return routed_device(tokens, out_grad, routes, probs, w_gate, w_up, w_down)


def solution(mesh):
    in_specs = (
        P(("groups", "role", "ep"), "tp"),
        P(("groups", "role", "ep"), "tp"),
        P(("groups", "role", "ep"), None),
        P(("groups", "role", "ep"), None),
        P(("role", "ep"), None, "tp"),
        P(("role", "ep"), None, "tp"),
        P(("role", "ep"), "tp", None),
    )
    out_specs = (
        P(("groups", "role", "ep"), "tp"),
        P(("groups", "role", "ep"), None),
        P(("groups", "role", "ep"), None, "tp"),
        P(("groups", "role", "ep"), None, "tp"),
        P(("groups", "role", "ep"), "tp", None),
    )
    return jax.shard_map(
        per_device, mesh=mesh, in_specs=in_specs, out_specs=out_specs, check_vma=False
    )
```

```python
import functools
import math

import jax
import jax.numpy as jnp
from jax import lax
from jax.experimental import pallas as pl
from jax.experimental.pallas import tpu as pltpu
from jax.sharding import PartitionSpec as P


def pad_rows(array):
    return jnp.concatenate([array, jnp.zeros((1, array.shape[1]), array.dtype)], 0)


def routed_device(tokens, out_grad, routes, probs, w_gate, w_up, w_down):
    owners = lax.axis_size(("role", "ep"))
    tok_rows, top_count = routes.shape
    width_full = w_gate.shape[1]
    part_width = w_gate.shape[2]
    capacity = min(tok_rows, tok_rows * top_count * 9 // (8 * owners))
    entry_total = tok_rows * top_count
    routes_flat = routes.reshape(-1)
    onehot = (routes_flat[:, None] == jnp.arange(owners, dtype=jnp.int32)[None, :]).astype(
        jnp.int32
    )
    before = jnp.cumsum(onehot, axis=0) - onehot
    slot_index = jnp.sum(before * onehot, axis=1)
    target = routes_flat * capacity + slot_index
    row_count = owners * capacity
    entry_of_slot = (
        jnp.full((row_count,), entry_total, jnp.int32)
        .at[target]
        .set(jnp.arange(entry_total, dtype=jnp.int32))
    )
    token_of_slot = entry_of_slot // top_count
    padded_prob = jnp.concatenate([probs.reshape(-1), jnp.zeros((1,), probs.dtype)], 0)
    send_prob = padded_prob[entry_of_slot].reshape(owners, capacity)
    send_x = pad_rows(tokens)[token_of_slot]
    send_g = pad_rows(out_grad)[token_of_slot]
    slice_x, slice_g, recv_p = (
        lax.all_to_all(
            send_x.reshape(owners, capacity, tokens.shape[1]),
            ("role", "ep"),
            split_axis=0,
            concat_axis=0,
            tiled=True,
        ),
        lax.all_to_all(
            send_g.reshape(owners, capacity, tokens.shape[1]),
            ("role", "ep"),
            split_axis=0,
            concat_axis=0,
            tiled=True,
        ),
        lax.all_to_all(send_prob, ("role", "ep"), split_axis=0, concat_axis=0, tiled=True),
    )
    recv_x, recv_g = (
        lax.all_gather(slice_x, "tp", axis=2, tiled=True),
        lax.all_gather(slice_g, "tp", axis=2, tiled=True),
    )
    rows_x = recv_x.reshape(row_count, width_full)
    rows_g = recv_g.reshape(row_count, width_full)
    weight_p = recv_p.reshape(row_count, 1).astype(jnp.float32)
    gate_up = jnp.concatenate([w_gate[0], w_up[0]], 1)
    down_shard = w_down[0]
    both_rows = jnp.dot(rows_x, gate_up, preferred_element_type=jnp.float32)
    gate_rows = both_rows[:, :part_width]
    up_rows = both_rows[:, part_width:]
    sigmoid_gate = jax.nn.sigmoid(gate_rows)
    activated = gate_rows * sigmoid_gate
    hidden = activated * up_rows
    back_rows = lax.dot_general(
        rows_g, down_shard, (((1,), (1,)), ((), ())), preferred_element_type=jnp.float32
    )
    scores = lax.psum(jnp.sum(hidden * back_rows, axis=1), "tp")
    hidden_grad = weight_p * back_rows
    d_gate_rows = (
        hidden_grad * up_rows * sigmoid_gate * (1.0 + gate_rows * (1.0 - sigmoid_gate))
    ).astype(jnp.bfloat16)
    d_up_rows = (hidden_grad * activated).astype(jnp.bfloat16)
    d_both = jnp.concatenate([d_gate_rows, d_up_rows], 1)
    scaled = (weight_p * hidden).astype(jnp.bfloat16)
    grad_down = lax.dot_general(
        scaled, rows_g, (((0,), (0,)), ((), ())), preferred_element_type=jnp.float32
    )
    grad_both = lax.dot_general(
        rows_x, d_both, (((0,), (0,)), ((), ())), preferred_element_type=jnp.float32
    )
    grad_gate = grad_both[:, :part_width]
    grad_up = grad_both[:, part_width:]
    partial_low = lax.dot_general(
        d_both, gate_up, (((1,), (1,)), ((), ())), preferred_element_type=jnp.float32
    ).astype(jnp.bfloat16)
    home_s = lax.all_to_all(
        scores.reshape(owners, capacity), ("role", "ep"), split_axis=0, concat_axis=0, tiled=True
    )
    summed = lax.psum_scatter(
        partial_low.reshape(owners, capacity, width_full), "tp", scatter_dimension=2, tiled=True
    ).astype(jnp.float32)
    summed_low = summed.astype(jnp.bfloat16)
    home_x = lax.all_to_all(summed_low, ("role", "ep"), split_axis=0, concat_axis=0, tiled=True)
    slice_width = summed.shape[2]
    route_rows = home_x.reshape(row_count, slice_width).astype(jnp.float32)
    d_tok = (
        jnp.zeros((tok_rows + 1, slice_width), jnp.float32)
        .at[token_of_slot]
        .add(route_rows)[:tok_rows]
    )
    d_probs = home_s.reshape(-1)[target].reshape(tok_rows, top_count)
    return (
        d_tok.astype(jnp.bfloat16),
        d_probs,
        grad_gate.astype(jnp.bfloat16)[None],
        grad_up.astype(jnp.bfloat16)[None],
        grad_down.astype(jnp.bfloat16)[None],
    )


def slot_capacity(tok_rows, top_count, owners):
    return min(tok_rows, tok_rows * top_count * 9 // (8 * owners))


LOOSE = pl.BlockSpec(memory_space=pl.ANY)


def weights_kernel(tp_ref, wg_ref, wu_ref, wd_ref, both_ref, down_ref):
    part = wg_ref.shape[2]
    both_ref[:, :part] = wg_ref[0]
    both_ref[:, part:] = wu_ref[0]
    down_ref[...] = wd_ref[0]


def weights_call(which, w_gate, w_up, w_down):
    _, width, part = w_gate.shape
    half = width // 2

    def place(i, w):
        return (i + w[0]) % 2

    return pl.pallas_call(
        weights_kernel,
        grid_spec=pltpu.PrefetchScalarGridSpec(
            num_scalar_prefetch=1,
            grid=(2,),
            in_specs=[
                pl.BlockSpec((1, half, part), lambda i, w: (0, place(i, w), 0)),
                pl.BlockSpec((1, half, part), lambda i, w: (0, place(i, w), 0)),
                pl.BlockSpec((1, part, half), lambda i, w: (0, 0, place(i, w))),
            ],
            out_specs=[
                pl.BlockSpec((half, 2 * part), lambda i, w: (i, 0)),
                pl.BlockSpec((part, half), lambda i, w: (0, i)),
            ],
        ),
        out_shape=[
            jax.ShapeDtypeStruct((width, 2 * part), jnp.bfloat16),
            jax.ShapeDtypeStruct((part, width), jnp.bfloat16),
        ],
        compiler_params=pltpu.CompilerParams(vmem_limit_bytes=12 << 20),
        cost_estimate=pl.CostEstimate(flops=0, bytes_accessed=12 * width * part, transcendentals=0),
        name="weights",
    )(which, *[pltpu.with_memory_space_constraint(item, pltpu.HBM) for item in (w_gate, w_up, w_down)])


def join_kernel(top_ref, bottom_ref, out_ref, sems):
    rows = top_ref.shape[0]
    copies = [
        pltpu.make_async_copy(top_ref, out_ref.at[pl.ds(0, rows)], sems.at[0]),
        pltpu.make_async_copy(bottom_ref, out_ref.at[pl.ds(rows, rows)], sems.at[1]),
    ]
    for copy in copies:
        copy.start()
    for copy in copies:
        copy.wait()


def join_call(top, bottom):
    rows, columns = top.shape
    return pl.pallas_call(
        join_kernel,
        in_specs=[LOOSE] * 2,
        out_specs=pl.BlockSpec(memory_space=pltpu.VMEM),
        out_shape=pltpu.VMEM((2 * rows, columns), top.dtype),
        scratch_shapes=[pltpu.SemaphoreType.DMA((2,))],
        compiler_params=pltpu.CompilerParams(vmem_limit_bytes=8 << 20),
        cost_estimate=pl.CostEstimate(flops=0, bytes_accessed=8 * rows * columns, transcendentals=0),
        name="join",
    )(*[pltpu.with_memory_space_constraint(item, pltpu.HBM) for item in (top, bottom)])


def rows_kernel(count, ways, capacity, slots, where_ref, *refs):
    weights_in, units_in, tables_in = refs[:4], refs[4 : 4 + 4 * count], refs[4 + 4 * count : 4 + 5 * count]
    leaves = 1 + max(way[0] for way in ways.values())
    refs = refs[len(refs) - 6 - leaves :]
    outs, packets, refs = refs[:2], refs[2 : 2 + leaves], refs[2 + leaves :]
    x_all, g_all, tables, unit_sems = refs
    half, tok = x_all.shape[3], x_all.shape[2] // 2
    part = weights_in[2].shape[0]
    owners = tables.shape[2]
    wgu, wd = weights_in[:2], weights_in[2:]

    x_copies, g_copies = [], []
    for index, unit in enumerate(units_in):
        chunk, y, x = index // 4, index // 2 % 2, index % 2
        rows = pl.ds(y * tok, tok)
        x_copies.append(pltpu.make_async_copy(unit.at[pl.ds(0, tok)], x_all.at[chunk, x, rows], unit_sems.at[0, index]))
        g_copies.append(pltpu.make_async_copy(unit.at[pl.ds(tok, tok)], g_all.at[chunk, x, rows], unit_sems.at[1, index]))
    t_copies = [
        pltpu.make_async_copy(table, tables.at[chunk], unit_sems.at[2, chunk]) for chunk, table in enumerate(tables_in)
    ]
    for copy in t_copies + x_copies + g_copies:
        copy.start()
    both_at, scaled_at = pl.ds(4 * half, 2 * part), pl.ds(4 * half + 2 * part, part)

    def dot(a, b, dims):
        return lax.dot_general(a, b, (dims, ((), ())), preferred_element_type=jnp.float32)

    for copy in t_copies:
        copy.wait()
    earlier = lax.broadcasted_iota(jnp.int32, (tok, tok), 0) < lax.broadcasted_iota(jnp.int32, (tok, tok), 1)
    earlier = earlier.astype(jnp.bfloat16)
    place = lax.broadcasted_iota(jnp.int32, (slots, tok), 0).astype(jnp.float32)
    names = lax.broadcasted_iota(jnp.int32, (owners, tok), 0)
    picks, low_picks, probs = {}, {}, {}
    for chunk in range(count):
        found = []
        for y in range(2):
            table = tables[chunk, y].astype(jnp.float32)
            rank = dot((table >= 0.0).astype(jnp.bfloat16), earlier, ((1,), (0,))) + float(y * capacity)
            found.append((table, jnp.where(table >= 0.0, rank, -1.0)))
        for expert in range(2):
            mine = names == where_ref[expert]
            halves, prob = [], None
            for table, rank in found:
                weight = jnp.sum(jnp.where(mine, table, 0.0), axis=0, keepdims=True)
                slot = jnp.sum(jnp.where(mine, rank, 0.0), axis=0, keepdims=True)
                halves.append((place == slot).astype(jnp.float32))
                term = jnp.sum(halves[-1] * weight, axis=1, keepdims=True)
                prob = term if prob is None else prob + term
            picks[chunk, expert] = halves
            low_picks[chunk, expert] = jnp.concatenate(halves, 1).astype(jnp.bfloat16)
            probs[chunk, expert] = prob
    spans = [pl.ds(chunk * slots, slots) for chunk in range(count)]
    sides = [slice(side * half, (side + 1) * half) for side in range(2)]

    def gather(copies, source, offset):
        for chunk in range(count):
            for copy in copies[4 * chunk : 4 * chunk + 4]:
                copy.wait()
            both_picks = jnp.concatenate([low_picks[chunk, expert] for expert in range(2)], 0)
            for side in range(2):
                rows = dot(both_picks, source[chunk, side], ((1,), (0,))).astype(jnp.bfloat16)
                for expert in range(2):
                    columns = pl.ds(offset + side * half, half)
                    outs[expert][spans[chunk], columns] = rows[expert * slots : (expert + 1) * slots]

    gather(x_copies, x_all, 0)
    rows = []
    for expert in range(2):
        rows.append(dot(outs[expert][:, : 2 * half], wgu[expert][...], ((1,), (0,))))
    gather(g_copies, g_all, 2 * half)
    scores = []
    for expert in range(2):
        back = dot(outs[expert][:, 2 * half : 4 * half], wd[expert][...], ((1,), (1,)))
        gate, up = rows[expert][:, :part], rows[expert][:, part:]
        sig = jax.nn.sigmoid(gate)
        act = gate * sig
        hidden = act * up
        scores.append(jnp.sum(hidden * back, axis=1, keepdims=True))
        prob = jnp.concatenate([probs[chunk, expert] for chunk in range(count)], 0)
        hgrad = prob * back
        d_gate = (hgrad * up * sig * (1.0 + gate * (1.0 - sig))).astype(jnp.bfloat16)
        outs[expert][:, both_at] = jnp.concatenate([d_gate, (hgrad * act).astype(jnp.bfloat16)], 1)
        outs[expert][:, scaled_at] = (prob * hidden).astype(jnp.bfloat16)

    extra_rows = packets[0].shape[1] - tok
    per_row = owners // extra_rows
    names = lax.broadcasted_iota(jnp.int32, (extra_rows, half), 0)
    column = lax.broadcasted_iota(jnp.int32, (extra_rows, half), 1) // (2 * tok)
    for chunk in range(count):
        for y in range(2):
            extra = jnp.zeros((extra_rows, half), jnp.float32)
            for expert in range(2):
                part_scores = scores[expert][chunk * slots : (chunk + 1) * slots]
                line = jnp.sum(picks[chunk, expert][y] * part_scores, axis=0, keepdims=True)
                high = line.astype(jnp.bfloat16).astype(jnp.float32)
                line = jnp.concatenate([high, line - high] * (half // (2 * tok)), 1)
                row, cell = where_ref[expert] // per_row, where_ref[expert] % per_row * 2 + where_ref[2]
                extra = extra + jnp.where((names == row) & (column == cell), line, 0.0)
            for side in range(2):
                number, slot = ways[chunk, y, side]
                packets[number][slot, tok:] = extra.astype(jnp.bfloat16)
    early = count == 1
    grads = [outs[expert][:, both_at] for expert in range(2)]
    if early:
        grads = [dot(low_picks[0, expert], grads[expert], ((0,), (0,))).astype(jnp.bfloat16) for expert in range(2)]
    for side in (1, 0):
        low = [dot(grads[expert], wgu[expert][sides[side], :], ((1,), (1,))) for expert in range(2)]
        for chunk in range(count):
            if early:
                total = low[0] + low[1]
            else:
                rows = slice(chunk * slots, (chunk + 1) * slots)
                total = sum(
                    dot(low_picks[chunk, expert], low[expert][rows].astype(jnp.bfloat16), ((0,), (0,)))
                    for expert in range(2)
                )
            for y in range(2):
                number, slot = ways[chunk, y, side]
                packets[number][slot, :tok] = total[y * tok : (y + 1) * tok].astype(jnp.bfloat16)


def rows_call(items, owners, capacity, slots, where, weights, units, tables, after):
    count = len(tables)
    ways = {block: (number, slot) for number, blocks in enumerate(items) for slot, block in enumerate(blocks)}
    tok, half = units[0].shape[0] // 2, units[0].shape[1]
    part, width = weights[2].shape
    widths = (width, width, 2 * part, part)
    packet = (tok + 4 * tok * owners // half, half)
    return pl.pallas_call(
        functools.partial(rows_kernel, count, ways, capacity, slots),
        grid_spec=pltpu.PrefetchScalarGridSpec(
            num_scalar_prefetch=1,
            grid=(1,),
            in_specs=[pl.BlockSpec(memory_space=pltpu.VMEM)] * 4 + [LOOSE] * (5 * count + len(after)),
            out_specs=[pl.BlockSpec(memory_space=pltpu.VMEM)] * (2 + len(items)),
            scratch_shapes=[pltpu.VMEM((count, 2, 2 * tok, half), jnp.bfloat16)] * 2
            + [pltpu.VMEM((count, 2, owners, tok), jnp.bfloat16)]
            + [pltpu.SemaphoreType.DMA((3, 4 * count))],
        ),
        out_shape=[pltpu.VMEM((count * slots, sum(widths)), jnp.bfloat16)] * 2
        + [pltpu.VMEM((len(blocks),) + packet, jnp.bfloat16) for blocks in items],
        compiler_params=pltpu.CompilerParams(vmem_limit_bytes=14 << 20),
        cost_estimate=pl.CostEstimate(
            flops=count * (20 * slots * width * part + 24 * slots * tok * width),
            bytes_accessed=count * 16 * tok * width + 12 * width * part,
            transcendentals=2 * count * slots * part,
        ),
        name="rows",
    )(where, *[pltpu.with_memory_space_constraint(item, pltpu.VMEM) for item in (*weights, *units, *tables)], *after)


def grads_kernel(count, wide, deep, blocks, tp_ref, *refs):
    sources, outs = refs[:count], refs[count:-4]
    wide_all, deep_all, wide_sems, deep_sems = refs[-4:]
    starts = [sum(source.shape[0] for source in sources[:index]) for index in range(count)]
    size = wide_all.shape[2]
    block = pl.program_id(0)

    def copies(column):
        return [
            pltpu.make_async_copy(
                source.at[:, pl.ds(wide + column * size, size)],
                wide_all.at[column, pl.ds(starts[index], source.shape[0])],
                wide_sems.at[column, index],
            )
            for index, source in enumerate(sources)
        ]

    @pl.when(block == 0)
    def _():
        deep_copies = [
            pltpu.make_async_copy(
                source.at[:, pl.ds(deep, deep_all.shape[1])],
                deep_all.at[pl.ds(starts[index], source.shape[0])],
                deep_sems.at[index],
            )
            for index, source in enumerate(sources)
        ]
        for copy in deep_copies:
            copy.start()
        for column in range(blocks):
            for copy in copies(column):
                copy.start()
        for copy in deep_copies:
            copy.wait()

    for column in range(blocks):

        @pl.when(block == column)
        def _(column=column):
            for copy in copies(column):
                copy.wait()

    dims = (((0,), (0,)), ((), ()))
    if len(outs) == 2:
        part = outs[0].shape[2]
        both = lax.dot_general(wide_all[block], deep_all[...], dims, preferred_element_type=jnp.float32)
        outs[0][0] = both[:, :part].astype(jnp.bfloat16)
        outs[1][0] = both[:, part:].astype(jnp.bfloat16)
    else:
        down = lax.dot_general(deep_all[...], wide_all[block], dims, preferred_element_type=jnp.float32)
        outs[0][0] = down.astype(jnp.bfloat16)


def grads_call(which, packed, width, part, down):
    rows, count = sum(item.shape[0] for item in packed), len(packed)
    step = math.gcd(width // 2, 512 if down else 1024)
    per = width // 2 // step
    deep = part if down else 2 * part

    def place(i, w):
        return (i + w[0] * per) % (2 * per)

    if down:
        specs = [pl.BlockSpec((1, part, step), lambda i, w: (0, 0, place(i, w)))]
        shapes = [(1, part, width)]
    else:
        specs = [pl.BlockSpec((1, step, part), lambda i, w: (0, place(i, w), 0))] * 2
        shapes = [(1, width, part)] * 2
    starts = (width, 2 * width + 2 * part) if down else (0, 2 * width)
    return pl.pallas_call(
        functools.partial(grads_kernel, count, *starts, 2 * per),
        grid_spec=pltpu.PrefetchScalarGridSpec(
            num_scalar_prefetch=1,
            grid=(2 * per,),
            in_specs=[LOOSE] * count,
            out_specs=specs,
            scratch_shapes=[
                pltpu.VMEM((2 * per, rows, step), jnp.bfloat16),
                pltpu.VMEM((rows, deep), jnp.bfloat16),
                pltpu.SemaphoreType.DMA((2 * per, count)),
                pltpu.SemaphoreType.DMA((count,)),
            ],
        ),
        out_shape=[jax.ShapeDtypeStruct(shape, jnp.bfloat16) for shape in shapes],
        compiler_params=pltpu.CompilerParams(vmem_limit_bytes=22 << 20),
        cost_estimate=pl.CostEstimate(
            flops=2 * rows * width * deep, bytes_accessed=2 * rows * (width + deep), transcendentals=0
        ),
        name="grads",
    )(which, *packed)


def dense_device(tokens, out_grad, routes, probs, w_gate, w_up, w_down):
    owners = lax.axis_size(("role", "ep"))
    ep = lax.axis_size("ep")
    n_y = 2
    n_z = ep // n_y
    tok_rows, half = tokens.shape
    capacity = slot_capacity(tok_rows, routes.shape[1], owners)
    slots = -(-n_y * capacity // 16) * 16
    role, place, which = lax.axis_index("role"), lax.axis_index("ep"), lax.axis_index("tp")

    def over_x(array):
        return lax.ppermute(array, "tp", [(0, 1), (1, 0)])

    def over_role(array):
        return lax.ppermute(array, "role", [(0, 1), (1, 0)])

    def over_y(array):
        return lax.ppermute(array, "ep", [(i, i + 1 - 2 * (i % n_y)) for i in range(ep)])

    def over_z(array, shift):
        return lax.ppermute(array, "ep", [(i, (i + shift * n_y) % ep) for i in range(ep)])

    def tied(values, others):
        return lax.optimization_barrier((list(values), list(others)))[0]

    last = n_z - 1
    routes_in = []
    for z in range(n_z):
        shift = -1 if z == last and z > 1 else 1
        if z:
            routes_in.append(((z, 0, 0), (0 if z in (1, last) else z - 1, 0, 0), functools.partial(over_z, shift=shift)))
        routes_in.append(((z, 1, 0), (z, 0, 0), over_y))
        routes_in.append(((z, 0, 1), (z, 0, 0), over_x))
        if z == 0:
            routes_in.append(((z, 1, 1), (z, 1, 0), over_x))
        elif z in (1, last):
            routes_in.append(((z, 1, 1), (0, 1, 1), functools.partial(over_z, shift=shift)))
        else:
            routes_in.append(((z, 1, 1), (z, 0, 1), over_y))
    routes_in.sort(key=lambda item: (item[0][0] % 2 if item[2] in (over_x, over_y) else 0, sum(item[0][1:])))

    rounds, waiting, there = [], list(routes_in), {(0, 0, 0)}
    while waiting:
        moves = {}
        for item in waiting:
            axis = item[2] if item[2] in (over_x, over_y) else over_z
            if item[1] in there and axis not in moves:
                moves[axis] = item
        rounds.append(list(moves.values()))
        there |= {item[0] for item in rounds[-1]}
        waiting = [item for item in waiting if item[0] not in there]

    which_ref = which.reshape(1).astype(jnp.int32)
    where = jnp.stack([role * ep + place, (1 - role) * ep + place, which]).astype(jnp.int32)
    both_w, down_w = weights_call(which_ref, w_gate, w_up, w_down)
    width, part = both_w.shape[0], down_w.shape[0]

    def rows_of(steps, items, after):
        four = [units[z, y, x] for z in steps for y in range(2) for x in range(2)]
        return rows_call(items, owners, capacity, slots, where, weights, four, [tables[z] for z in steps], after)

    units = {(0, 0, 0): join_call(tokens, out_grad)}
    settled = dict(units)
    for number, moves in enumerate(rounds):
        arrived = {target: move(settled[source]) for target, source, move in moves}
        units.update(arrived)
        settled.update(arrived)
        extra = []
        if number == 0:
            extra = [both_w, down_w]
            both_w, down_w, routes, probs = tied([both_w, down_w, routes, probs], arrived.values())
            weights = (both_w, over_role(both_w), down_w, over_role(down_w))
            chosen = routes[:, :, None] == jnp.arange(owners, dtype=jnp.int32)
            table = jnp.sum(jnp.where(chosen, probs[:, :, None].astype(jnp.float32) + 1.0, 0.0), axis=1) - 1.0
            table = table.astype(jnp.bfloat16).T
            table = jnp.stack([table, over_y(table)])
        if number == 1:
            (table,) = tied([table], arrived.values())
            tables = [over_z(table, z) if z else table for z in range(n_z)]
        if number == 2:
            mine_0, other_0, near, side_0, far, y_0 = rows_of(
                [0], [[(0, 0, 0)], [(0, 0, 1)], [(0, 1, 1)], [(0, 1, 0)]], []
            )
            extra = [mine_0]
        names = list(settled)
        settled = dict(zip(names, tied([settled[item] for item in names], extra)))

    def total(*blocks):
        return sum(block.astype(jnp.float32) for block in blocks).astype(jnp.bfloat16)

    items = [[(1, 1, 1)], [(1, 0, 1)], [(0, 0, 1)], [(0, 1, 0)], [(0, 1, 1)], [(0, 0, 0)], [(1, 0, 0)], [(1, 1, 0)]]
    mine_1, other_1, x_2, x_20, x_1, y_1, z_1, keep_1, keep_2, keep_2y = rows_of([1, 2], items, tables[3:])
    other_1, x_2, x_20, x_1, y_1, z_1 = tied([other_1, x_2, x_20, x_1, y_1, z_1], arrived.values())
    from_x2, from_y1, from_z1 = over_x(x_2), over_y(y_1), over_z(z_1, -1)
    from_x20 = over_x(x_20)
    items = [[(0, 0, 1)], [(0, 1, 0)], [(0, 1, 1)], [(0, 0, 0)]]
    mine_3, other_3, x_3, y_3, z_3, keep_3 = rows_of([3], items, [mine_1])
    mine_3, other_3, x_3, y_3, z_3, keep_2y = tied(
        [mine_3, other_3, x_3, y_3, z_3, keep_2y], [from_x2, from_y1, from_z1]
    )
    from_z3, from_y2, from_x1 = over_z(z_3, 1), over_y(total(keep_2y, from_x2)), over_x(x_1)
    from_x3, from_y3 = over_x(x_3), over_y(y_3)
    packed = [mine_0, over_role(other_0), mine_1, over_role(other_1), mine_3, over_role(other_3)]
    (d_down,) = grads_call(which_ref, packed, width, part, True)
    from_z3, from_x20, from_y2 = tied([from_z3, from_x20, from_y2], [d_down])
    far, step_2 = total(far, from_z1, from_z3), total(keep_2, from_x20, from_y2)
    (from_x1,) = tied([from_x1], [far, step_2])
    from_far, from_z2 = over_y(far), over_z(step_2, 1)
    home_1 = over_z(total(keep_1, from_x1, from_y1), -1)
    from_x0 = over_x(total(side_0, from_far))
    from_x3, from_y3, from_z2 = tied([from_x3, from_y3, from_z2], [from_far])
    home_3 = over_z(total(keep_3, from_x3, from_y3, from_z2), 1)
    from_y0 = over_y(tied([y_0], [from_far])[0])
    d_gate, d_up = grads_call(which_ref, packed, width, part, False)
    home_1, from_x0, home_3, from_y0 = tied([home_1, from_x0, home_3, from_y0], [d_gate, d_up])
    home = (near, from_x0, home_3, home_1, from_y0)
    d_tok = sum(block[0, :tok_rows].astype(jnp.float32) for block in home).astype(jnp.bfloat16)
    home = sum(block[0, tok_rows:].astype(jnp.float32) for block in home)
    score = jnp.sum(home.reshape(owners, 4, tok_rows), axis=1).T
    d_probs = jnp.sum(jnp.where(chosen, score[:, None, :], 0.0), axis=2)
    return d_tok, d_probs, d_gate, d_up, d_down


def per_device(tokens, out_grad, routes, probs, w_gate, w_up, w_down):
    owners = lax.axis_size(("role", "ep"))
    tok_rows, top_count = routes.shape
    paired = lax.axis_size("tp") == 2 and lax.axis_size("role") == 2 and lax.axis_size("ep") == 8
    if paired and 2 * slot_capacity(tok_rows, top_count, owners) >= tok_rows:
        return dense_device(tokens, out_grad, routes, probs, w_gate, w_up, w_down)
    return routed_device(tokens, out_grad, routes, probs, w_gate, w_up, w_down)


def solution(mesh):
    in_specs = (
        P(("groups", "role", "ep"), "tp"),
        P(("groups", "role", "ep"), "tp"),
        P(("groups", "role", "ep"), None),
        P(("groups", "role", "ep"), None),
        P(("role", "ep"), None, "tp"),
        P(("role", "ep"), None, "tp"),
        P(("role", "ep"), "tp", None),
    )
    out_specs = (
        P(("groups", "role", "ep"), "tp"),
        P(("groups", "role", "ep"), None),
        P(("groups", "role", "ep"), None, "tp"),
        P(("groups", "role", "ep"), None, "tp"),
        P(("groups", "role", "ep"), "tp", None),
    )
    return jax.shard_map(
        per_device, mesh=mesh, in_specs=in_specs, out_specs=out_specs, check_vma=False
    )
```

```python
import functools
import math

import jax
import jax.numpy as jnp
from jax import lax
from jax.experimental import pallas as pl
from jax.experimental.pallas import tpu as pltpu
from jax.sharding import PartitionSpec as P


def pad_rows(array):
    return jnp.concatenate([array, jnp.zeros((1, array.shape[1]), array.dtype)], 0)


def routed_device(tokens, out_grad, routes, probs, w_gate, w_up, w_down):
    owners = lax.axis_size(("role", "ep"))
    tok_rows, top_count = routes.shape
    width_full = w_gate.shape[1]
    part_width = w_gate.shape[2]
    capacity = min(tok_rows, tok_rows * top_count * 9 // (8 * owners))
    entry_total = tok_rows * top_count
    routes_flat = routes.reshape(-1)
    onehot = (routes_flat[:, None] == jnp.arange(owners, dtype=jnp.int32)[None, :]).astype(
        jnp.int32
    )
    before = jnp.cumsum(onehot, axis=0) - onehot
    slot_index = jnp.sum(before * onehot, axis=1)
    target = routes_flat * capacity + slot_index
    row_count = owners * capacity
    entry_of_slot = (
        jnp.full((row_count,), entry_total, jnp.int32)
        .at[target]
        .set(jnp.arange(entry_total, dtype=jnp.int32))
    )
    token_of_slot = entry_of_slot // top_count
    padded_prob = jnp.concatenate([probs.reshape(-1), jnp.zeros((1,), probs.dtype)], 0)
    send_prob = padded_prob[entry_of_slot].reshape(owners, capacity)
    send_x = pad_rows(tokens)[token_of_slot]
    send_g = pad_rows(out_grad)[token_of_slot]
    slice_x, slice_g, recv_p = (
        lax.all_to_all(
            send_x.reshape(owners, capacity, tokens.shape[1]),
            ("role", "ep"),
            split_axis=0,
            concat_axis=0,
            tiled=True,
        ),
        lax.all_to_all(
            send_g.reshape(owners, capacity, tokens.shape[1]),
            ("role", "ep"),
            split_axis=0,
            concat_axis=0,
            tiled=True,
        ),
        lax.all_to_all(send_prob, ("role", "ep"), split_axis=0, concat_axis=0, tiled=True),
    )
    recv_x, recv_g = (
        lax.all_gather(slice_x, "tp", axis=2, tiled=True),
        lax.all_gather(slice_g, "tp", axis=2, tiled=True),
    )
    rows_x = recv_x.reshape(row_count, width_full)
    rows_g = recv_g.reshape(row_count, width_full)
    weight_p = recv_p.reshape(row_count, 1).astype(jnp.float32)
    gate_up = jnp.concatenate([w_gate[0], w_up[0]], 1)
    down_shard = w_down[0]
    both_rows = jnp.dot(rows_x, gate_up, preferred_element_type=jnp.float32)
    gate_rows = both_rows[:, :part_width]
    up_rows = both_rows[:, part_width:]
    sigmoid_gate = jax.nn.sigmoid(gate_rows)
    activated = gate_rows * sigmoid_gate
    hidden = activated * up_rows
    back_rows = lax.dot_general(
        rows_g, down_shard, (((1,), (1,)), ((), ())), preferred_element_type=jnp.float32
    )
    scores = lax.psum(jnp.sum(hidden * back_rows, axis=1), "tp")
    hidden_grad = weight_p * back_rows
    d_gate_rows = (
        hidden_grad * up_rows * sigmoid_gate * (1.0 + gate_rows * (1.0 - sigmoid_gate))
    ).astype(jnp.bfloat16)
    d_up_rows = (hidden_grad * activated).astype(jnp.bfloat16)
    d_both = jnp.concatenate([d_gate_rows, d_up_rows], 1)
    scaled = (weight_p * hidden).astype(jnp.bfloat16)
    grad_down = lax.dot_general(
        scaled, rows_g, (((0,), (0,)), ((), ())), preferred_element_type=jnp.float32
    )
    grad_both = lax.dot_general(
        rows_x, d_both, (((0,), (0,)), ((), ())), preferred_element_type=jnp.float32
    )
    grad_gate = grad_both[:, :part_width]
    grad_up = grad_both[:, part_width:]
    partial_low = lax.dot_general(
        d_both, gate_up, (((1,), (1,)), ((), ())), preferred_element_type=jnp.float32
    ).astype(jnp.bfloat16)
    home_s = lax.all_to_all(
        scores.reshape(owners, capacity), ("role", "ep"), split_axis=0, concat_axis=0, tiled=True
    )
    summed = lax.psum_scatter(
        partial_low.reshape(owners, capacity, width_full), "tp", scatter_dimension=2, tiled=True
    ).astype(jnp.float32)
    summed_low = summed.astype(jnp.bfloat16)
    home_x = lax.all_to_all(summed_low, ("role", "ep"), split_axis=0, concat_axis=0, tiled=True)
    slice_width = summed.shape[2]
    route_rows = home_x.reshape(row_count, slice_width).astype(jnp.float32)
    d_tok = (
        jnp.zeros((tok_rows + 1, slice_width), jnp.float32)
        .at[token_of_slot]
        .add(route_rows)[:tok_rows]
    )
    d_probs = home_s.reshape(-1)[target].reshape(tok_rows, top_count)
    return (
        d_tok.astype(jnp.bfloat16),
        d_probs,
        grad_gate.astype(jnp.bfloat16)[None],
        grad_up.astype(jnp.bfloat16)[None],
        grad_down.astype(jnp.bfloat16)[None],
    )


def slot_capacity(tok_rows, top_count, owners):
    return min(tok_rows, tok_rows * top_count * 9 // (8 * owners))


LOOSE = pl.BlockSpec(memory_space=pl.ANY)


def weights_kernel(tp_ref, wg_ref, wu_ref, wd_ref, both_ref, down_ref):
    part = wg_ref.shape[2]
    both_ref[:, :part] = wg_ref[0]
    both_ref[:, part:] = wu_ref[0]
    down_ref[...] = wd_ref[0]


def weights_call(which, w_gate, w_up, w_down):
    _, width, part = w_gate.shape
    half = width // 2

    def place(i, w):
        return (i + w[0]) % 2

    return pl.pallas_call(
        weights_kernel,
        grid_spec=pltpu.PrefetchScalarGridSpec(
            num_scalar_prefetch=1,
            grid=(2,),
            in_specs=[
                pl.BlockSpec((1, half, part), lambda i, w: (0, place(i, w), 0)),
                pl.BlockSpec((1, half, part), lambda i, w: (0, place(i, w), 0)),
                pl.BlockSpec((1, part, half), lambda i, w: (0, 0, place(i, w))),
            ],
            out_specs=[
                pl.BlockSpec((half, 2 * part), lambda i, w: (i, 0)),
                pl.BlockSpec((part, half), lambda i, w: (0, i)),
            ],
        ),
        out_shape=[
            jax.ShapeDtypeStruct((width, 2 * part), jnp.bfloat16),
            jax.ShapeDtypeStruct((part, width), jnp.bfloat16),
        ],
        compiler_params=pltpu.CompilerParams(vmem_limit_bytes=12 << 20),
        cost_estimate=pl.CostEstimate(flops=0, bytes_accessed=12 * width * part, transcendentals=0),
        name="weights",
    )(which, *[pltpu.with_memory_space_constraint(item, pltpu.HBM) for item in (w_gate, w_up, w_down)])


def join_kernel(top_ref, bottom_ref, out_ref, sems):
    rows = top_ref.shape[0]
    copies = [
        pltpu.make_async_copy(top_ref, out_ref.at[pl.ds(0, rows)], sems.at[0]),
        pltpu.make_async_copy(bottom_ref, out_ref.at[pl.ds(rows, rows)], sems.at[1]),
    ]
    for copy in copies:
        copy.start()
    for copy in copies:
        copy.wait()


def join_call(top, bottom):
    rows, columns = top.shape
    return pl.pallas_call(
        join_kernel,
        in_specs=[LOOSE] * 2,
        out_specs=pl.BlockSpec(memory_space=pltpu.VMEM),
        out_shape=pltpu.VMEM((2 * rows, columns), top.dtype),
        scratch_shapes=[pltpu.SemaphoreType.DMA((2,))],
        compiler_params=pltpu.CompilerParams(vmem_limit_bytes=8 << 20),
        cost_estimate=pl.CostEstimate(flops=0, bytes_accessed=8 * rows * columns, transcendentals=0),
        name="join",
    )(*[pltpu.with_memory_space_constraint(item, pltpu.HBM) for item in (top, bottom)])


def rows_kernel(count, ways, capacity, slots, where_ref, *refs):
    weights_in, units_in, tables_in = refs[:4], refs[4 : 4 + 4 * count], refs[4 + 4 * count : 4 + 5 * count]
    leaves = 1 + max(way[0] for way in ways.values())
    refs = refs[len(refs) - 6 - leaves :]
    outs, packets, refs = refs[:2], refs[2 : 2 + leaves], refs[2 + leaves :]
    x_all, g_all, tables, unit_sems = refs
    half, tok = x_all.shape[3], x_all.shape[2] // 2
    part = weights_in[2].shape[0]
    owners = tables.shape[2]
    wgu, wd = weights_in[:2], weights_in[2:]

    x_copies, g_copies = [], []
    for index, unit in enumerate(units_in):
        chunk, y, x = index // 4, index // 2 % 2, index % 2
        rows = pl.ds(y * tok, tok)
        x_copies.append(pltpu.make_async_copy(unit.at[pl.ds(0, tok)], x_all.at[chunk, x, rows], unit_sems.at[0, index]))
        g_copies.append(pltpu.make_async_copy(unit.at[pl.ds(tok, tok)], g_all.at[chunk, x, rows], unit_sems.at[1, index]))
    t_copies = [
        pltpu.make_async_copy(table, tables.at[chunk], unit_sems.at[2, chunk]) for chunk, table in enumerate(tables_in)
    ]
    for copy in t_copies + x_copies + g_copies:
        copy.start()
    both_at, scaled_at = pl.ds(4 * half, 2 * part), pl.ds(4 * half + 2 * part, part)

    def dot(a, b, dims):
        return lax.dot_general(a, b, (dims, ((), ())), preferred_element_type=jnp.float32)

    for copy in t_copies:
        copy.wait()
    earlier = lax.broadcasted_iota(jnp.int32, (tok, tok), 0) < lax.broadcasted_iota(jnp.int32, (tok, tok), 1)
    earlier = earlier.astype(jnp.bfloat16)
    place = lax.broadcasted_iota(jnp.int32, (slots, tok), 0).astype(jnp.float32)
    names = lax.broadcasted_iota(jnp.int32, (owners, tok), 0)
    picks, low_picks, probs = {}, {}, {}
    for chunk in range(count):
        found = []
        for y in range(2):
            table = tables[chunk, y].astype(jnp.float32)
            rank = dot((table >= 0.0).astype(jnp.bfloat16), earlier, ((1,), (0,))) + float(y * capacity)
            found.append((table, jnp.where(table >= 0.0, rank, -1.0)))
        for expert in range(2):
            mine = names == where_ref[expert]
            halves, prob = [], None
            for table, rank in found:
                weight = jnp.sum(jnp.where(mine, table, 0.0), axis=0, keepdims=True)
                slot = jnp.sum(jnp.where(mine, rank, 0.0), axis=0, keepdims=True)
                halves.append((place == slot).astype(jnp.float32))
                term = jnp.sum(halves[-1] * weight, axis=1, keepdims=True)
                prob = term if prob is None else prob + term
            picks[chunk, expert] = halves
            low_picks[chunk, expert] = jnp.concatenate(halves, 1).astype(jnp.bfloat16)
            probs[chunk, expert] = prob
    spans = [pl.ds(chunk * slots, slots) for chunk in range(count)]
    sides = [slice(side * half, (side + 1) * half) for side in range(2)]

    def gather(copies, source, offset):
        for chunk in range(count):
            for copy in copies[4 * chunk : 4 * chunk + 4]:
                copy.wait()
            both_picks = jnp.concatenate([low_picks[chunk, expert] for expert in range(2)], 0)
            for side in range(2):
                rows = dot(both_picks, source[chunk, side], ((1,), (0,))).astype(jnp.bfloat16)
                for expert in range(2):
                    columns = pl.ds(offset + side * half, half)
                    outs[expert][spans[chunk], columns] = rows[expert * slots : (expert + 1) * slots]

    gather(x_copies, x_all, 0)
    rows = []
    for expert in range(2):
        rows.append(dot(outs[expert][:, : 2 * half], wgu[expert][...], ((1,), (0,))))
    gather(g_copies, g_all, 2 * half)
    scores = []
    for expert in range(2):
        back = dot(outs[expert][:, 2 * half : 4 * half], wd[expert][...], ((1,), (1,)))
        gate, up = rows[expert][:, :part], rows[expert][:, part:]
        sig = jax.nn.sigmoid(gate)
        act = gate * sig
        hidden = act * up
        scores.append(jnp.sum(hidden * back, axis=1, keepdims=True))
        prob = jnp.concatenate([probs[chunk, expert] for chunk in range(count)], 0)
        hgrad = prob * back
        d_gate = (hgrad * up * sig * (1.0 + gate * (1.0 - sig))).astype(jnp.bfloat16)
        outs[expert][:, both_at] = jnp.concatenate([d_gate, (hgrad * act).astype(jnp.bfloat16)], 1)
        outs[expert][:, scaled_at] = (prob * hidden).astype(jnp.bfloat16)

    extra_rows = packets[0].shape[1] - tok
    per_row = owners // extra_rows
    names = lax.broadcasted_iota(jnp.int32, (extra_rows, half), 0)
    column = lax.broadcasted_iota(jnp.int32, (extra_rows, half), 1) // (2 * tok)
    for chunk in range(count):
        for y in range(2):
            extra = jnp.zeros((extra_rows, half), jnp.float32)
            for expert in range(2):
                part_scores = scores[expert][chunk * slots : (chunk + 1) * slots]
                line = jnp.sum(picks[chunk, expert][y] * part_scores, axis=0, keepdims=True)
                high = line.astype(jnp.bfloat16).astype(jnp.float32)
                line = jnp.concatenate([high, line - high] * (half // (2 * tok)), 1)
                row, cell = where_ref[expert] // per_row, where_ref[expert] % per_row * 2 + where_ref[2]
                extra = extra + jnp.where((names == row) & (column == cell), line, 0.0)
            for side in range(2):
                number, slot = ways[chunk, y, side]
                packets[number][slot, tok:] = extra.astype(jnp.bfloat16)
    early = count == 1
    grads = [outs[expert][:, both_at] for expert in range(2)]
    if early:
        grads = [dot(low_picks[0, expert], grads[expert], ((0,), (0,))).astype(jnp.bfloat16) for expert in range(2)]
    for side in (1, 0):
        low = [dot(grads[expert], wgu[expert][sides[side], :], ((1,), (1,))) for expert in range(2)]
        for chunk in range(count):
            if early:
                total = low[0] + low[1]
            else:
                rows = slice(chunk * slots, (chunk + 1) * slots)
                total = sum(
                    dot(low_picks[chunk, expert], low[expert][rows].astype(jnp.bfloat16), ((0,), (0,)))
                    for expert in range(2)
                )
            for y in range(2):
                number, slot = ways[chunk, y, side]
                packets[number][slot, :tok] = total[y * tok : (y + 1) * tok].astype(jnp.bfloat16)


def rows_call(items, owners, capacity, slots, where, weights, units, tables, after):
    count = len(tables)
    ways = {block: (number, slot) for number, blocks in enumerate(items) for slot, block in enumerate(blocks)}
    tok, half = units[0].shape[0] // 2, units[0].shape[1]
    part, width = weights[2].shape
    widths = (width, width, 2 * part, part)
    packet = (tok + 4 * tok * owners // half, half)
    return pl.pallas_call(
        functools.partial(rows_kernel, count, ways, capacity, slots),
        grid_spec=pltpu.PrefetchScalarGridSpec(
            num_scalar_prefetch=1,
            grid=(1,),
            in_specs=[pl.BlockSpec(memory_space=pltpu.VMEM)] * 4 + [LOOSE] * (5 * count + len(after)),
            out_specs=[pl.BlockSpec(memory_space=pltpu.VMEM)] * (2 + len(items)),
            scratch_shapes=[pltpu.VMEM((count, 2, 2 * tok, half), jnp.bfloat16)] * 2
            + [pltpu.VMEM((count, 2, owners, tok), jnp.bfloat16)]
            + [pltpu.SemaphoreType.DMA((3, 4 * count))],
        ),
        out_shape=[pltpu.VMEM((count * slots, sum(widths)), jnp.bfloat16)] * 2
        + [pltpu.VMEM((len(blocks),) + packet, jnp.bfloat16) for blocks in items],
        compiler_params=pltpu.CompilerParams(vmem_limit_bytes=14 << 20),
        cost_estimate=pl.CostEstimate(
            flops=count * (20 * slots * width * part + 24 * slots * tok * width),
            bytes_accessed=count * 16 * tok * width + 12 * width * part,
            transcendentals=2 * count * slots * part,
        ),
        name="rows",
    )(where, *[pltpu.with_memory_space_constraint(item, pltpu.VMEM) for item in (*weights, *units, *tables)], *after)


def grads_kernel(count, wide, deep, blocks, tp_ref, *refs):
    sources, outs = refs[:count], refs[count:-4]
    wide_all, deep_all, wide_sems, deep_sems = refs[-4:]
    starts = [sum(source.shape[0] for source in sources[:index]) for index in range(count)]
    size = wide_all.shape[2]
    block = pl.program_id(0)

    def copies(column):
        return [
            pltpu.make_async_copy(
                source.at[:, pl.ds(wide + column * size, size)],
                wide_all.at[column, pl.ds(starts[index], source.shape[0])],
                wide_sems.at[column, index],
            )
            for index, source in enumerate(sources)
        ]

    @pl.when(block == 0)
    def _():
        deep_copies = [
            pltpu.make_async_copy(
                source.at[:, pl.ds(deep, deep_all.shape[1])],
                deep_all.at[pl.ds(starts[index], source.shape[0])],
                deep_sems.at[index],
            )
            for index, source in enumerate(sources)
        ]
        for copy in deep_copies:
            copy.start()
        for column in range(blocks):
            for copy in copies(column):
                copy.start()
        for copy in deep_copies:
            copy.wait()

    for column in range(blocks):

        @pl.when(block == column)
        def _(column=column):
            for copy in copies(column):
                copy.wait()

    dims = (((0,), (0,)), ((), ()))
    if len(outs) == 2:
        part = outs[0].shape[2]
        both = lax.dot_general(wide_all[block], deep_all[...], dims, preferred_element_type=jnp.float32)
        outs[0][0] = both[:, :part].astype(jnp.bfloat16)
        outs[1][0] = both[:, part:].astype(jnp.bfloat16)
    else:
        down = lax.dot_general(deep_all[...], wide_all[block], dims, preferred_element_type=jnp.float32)
        outs[0][0] = down.astype(jnp.bfloat16)


def grads_call(which, packed, width, part, down):
    rows, count = sum(item.shape[0] for item in packed), len(packed)
    step = math.gcd(width // 2, 512 if down else 1024)
    per = width // 2 // step
    deep = part if down else 2 * part

    def place(i, w):
        return (i + w[0] * per) % (2 * per)

    if down:
        specs = [pl.BlockSpec((1, part, step), lambda i, w: (0, 0, place(i, w)))]
        shapes = [(1, part, width)]
    else:
        specs = [pl.BlockSpec((1, step, part), lambda i, w: (0, place(i, w), 0))] * 2
        shapes = [(1, width, part)] * 2
    starts = (width, 2 * width + 2 * part) if down else (0, 2 * width)
    return pl.pallas_call(
        functools.partial(grads_kernel, count, *starts, 2 * per),
        grid_spec=pltpu.PrefetchScalarGridSpec(
            num_scalar_prefetch=1,
            grid=(2 * per,),
            in_specs=[LOOSE] * count,
            out_specs=specs,
            scratch_shapes=[
                pltpu.VMEM((2 * per, rows, step), jnp.bfloat16),
                pltpu.VMEM((rows, deep), jnp.bfloat16),
                pltpu.SemaphoreType.DMA((2 * per, count)),
                pltpu.SemaphoreType.DMA((count,)),
            ],
        ),
        out_shape=[jax.ShapeDtypeStruct(shape, jnp.bfloat16) for shape in shapes],
        compiler_params=pltpu.CompilerParams(vmem_limit_bytes=22 << 20),
        cost_estimate=pl.CostEstimate(
            flops=2 * rows * width * deep, bytes_accessed=2 * rows * (width + deep), transcendentals=0
        ),
        name="grads",
    )(which, *packed)


def dense_device(tokens, out_grad, routes, probs, w_gate, w_up, w_down):
    owners = lax.axis_size(("role", "ep"))
    ep = lax.axis_size("ep")
    n_y = 2
    n_z = ep // n_y
    tok_rows, half = tokens.shape
    capacity = slot_capacity(tok_rows, routes.shape[1], owners)
    slots = -(-n_y * capacity // 16) * 16
    role, place, which = lax.axis_index("role"), lax.axis_index("ep"), lax.axis_index("tp")

    def over_x(array):
        return lax.ppermute(array, "tp", [(0, 1), (1, 0)])

    def over_role(array):
        return lax.ppermute(array, "role", [(0, 1), (1, 0)])

    def over_y(array):
        return lax.ppermute(array, "ep", [(i, i + 1 - 2 * (i % n_y)) for i in range(ep)])

    def over_z(array, shift):
        return lax.ppermute(array, "ep", [(i, (i + shift * n_y) % ep) for i in range(ep)])

    def tied(values, others):
        return lax.optimization_barrier((list(values), list(others)))[0]

    last = n_z - 1
    routes_in = []
    for z in range(n_z):
        shift = -1 if z == last and z > 1 else 1
        if z:
            routes_in.append(((z, 0, 0), (0 if z in (1, last) else z - 1, 0, 0), functools.partial(over_z, shift=shift)))
        routes_in.append(((z, 1, 0), (z, 0, 0), over_y))
        routes_in.append(((z, 0, 1), (z, 0, 0), over_x))
        if z == 0:
            routes_in.append(((z, 1, 1), (z, 1, 0), over_x))
        elif z in (1, last):
            routes_in.append(((z, 1, 1), (0, 1, 1), functools.partial(over_z, shift=shift)))
        else:
            routes_in.append(((z, 1, 1), (z, 0, 1), over_y))
    routes_in.sort(key=lambda item: (item[0][0] % 2 if item[2] in (over_x, over_y) else 0, sum(item[0][1:])))

    rounds, waiting, there = [], list(routes_in), {(0, 0, 0)}
    while waiting:
        moves = {}
        for item in waiting:
            axis = item[2] if item[2] in (over_x, over_y) else over_z
            if item[1] in there and axis not in moves:
                moves[axis] = item
        rounds.append(moves)
        there |= {item[0] for item in moves.values()}
        waiting = [item for item in waiting if item[0] not in there]

    which_ref = which.reshape(1).astype(jnp.int32)
    where = jnp.stack([role * ep + place, (1 - role) * ep + place, which]).astype(jnp.int32)
    both_w, down_w = weights_call(which_ref, w_gate, w_up, w_down)
    width, part = both_w.shape[0], down_w.shape[0]

    def rows_of(steps, items, after):
        four = [units[z, y, x] for z in steps for y in range(2) for x in range(2)]
        return rows_call(items, owners, capacity, slots, where, weights, four, [tables[z] for z in steps], after)

    units = {(0, 0, 0): join_call(tokens, out_grad)}
    flying, landed, extra = {}, [], []
    for number, moves in enumerate(rounds):
        arrived = {}
        for axis, (target, source, move) in moves.items():
            (block,) = tied([units[source]], [flying[axis]] + landed + extra) if flying else [units[source]]
            arrived[axis] = move(block)
        units.update({moves[axis][0]: block for axis, block in arrived.items()})
        flying, landed, extra = arrived, list(flying.values()), []
        if number == 0:
            extra = [both_w, down_w]
            both_w, down_w, routes, probs = tied([both_w, down_w, routes, probs], arrived.values())
            weights = (both_w, over_role(both_w), down_w, over_role(down_w))
            chosen = routes[:, :, None] == jnp.arange(owners, dtype=jnp.int32)
            table = jnp.sum(jnp.where(chosen, probs[:, :, None].astype(jnp.float32) + 1.0, 0.0), axis=1) - 1.0
            table = table.astype(jnp.bfloat16).T
            table = jnp.stack([table, over_y(table)])
        if number == 1:
            (table,) = tied([table], arrived.values())
            tables = [over_z(table, z) if z else table for z in range(n_z)]
        if number == 2:
            mine_0, other_0, near, side_0, far, y_0 = rows_of(
                [0], [[(0, 0, 0)], [(0, 0, 1)], [(0, 1, 1)], [(0, 1, 0)]], []
            )
            extra = [mine_0]

    def total(*blocks):
        return sum(block.astype(jnp.float32) for block in blocks).astype(jnp.bfloat16)

    items = [[(1, 1, 1)], [(1, 0, 1)], [(0, 0, 1)], [(0, 1, 0)], [(0, 1, 1)], [(0, 0, 0)], [(1, 0, 0)], [(1, 1, 0)]]
    mine_1, other_1, x_2, x_20, x_1, y_1, z_1, keep_1, keep_2, keep_2y = rows_of([1, 2], items, tables[3:])
    other_1, x_2, x_20, x_1, y_1, z_1 = tied([other_1, x_2, x_20, x_1, y_1, z_1], arrived.values())
    from_x2, from_y1, from_z1 = over_x(x_2), over_y(y_1), over_z(z_1, -1)
    from_x20 = over_x(x_20)
    items = [[(0, 0, 1)], [(0, 1, 0)], [(0, 1, 1)], [(0, 0, 0)]]
    mine_3, other_3, x_3, y_3, z_3, keep_3 = rows_of([3], items, [mine_1])
    mine_3, other_3, x_3, y_3, z_3, keep_2y = tied(
        [mine_3, other_3, x_3, y_3, z_3, keep_2y], [from_x2, from_y1, from_z1]
    )
    from_z3, from_y2, from_x1 = over_z(z_3, 1), over_y(total(keep_2y, from_x2)), over_x(x_1)
    from_x3, from_y3 = over_x(x_3), over_y(y_3)
    packed = [mine_0, over_role(other_0), mine_1, over_role(other_1), mine_3, over_role(other_3)]
    (d_down,) = grads_call(which_ref, packed, width, part, True)
    from_z3, from_x20, from_y2 = tied([from_z3, from_x20, from_y2], [d_down])
    far, step_2 = total(far, from_z1, from_z3), total(keep_2, from_x20, from_y2)
    (from_x1,) = tied([from_x1], [far, step_2])
    from_far, from_z2 = over_y(far), over_z(step_2, 1)
    home_1 = over_z(total(keep_1, from_x1, from_y1), -1)
    from_x0 = over_x(total(side_0, from_far))
    from_x3, from_y3, from_z2 = tied([from_x3, from_y3, from_z2], [from_far])
    home_3 = over_z(total(keep_3, from_x3, from_y3, from_z2), 1)
    from_y0 = over_y(tied([y_0], [from_far])[0])
    d_gate, d_up = grads_call(which_ref, packed, width, part, False)
    home_1, from_x0, home_3, from_y0 = tied([home_1, from_x0, home_3, from_y0], [d_gate, d_up])
    home = (near, from_x0, home_3, home_1, from_y0)
    d_tok = sum(block[0, :tok_rows].astype(jnp.float32) for block in home).astype(jnp.bfloat16)
    home = sum(block[0, tok_rows:].astype(jnp.float32) for block in home)
    score = jnp.sum(home.reshape(owners, 4, tok_rows), axis=1).T
    d_probs = jnp.sum(jnp.where(chosen, score[:, None, :], 0.0), axis=2)
    return d_tok, d_probs, d_gate, d_up, d_down


def per_device(tokens, out_grad, routes, probs, w_gate, w_up, w_down):
    owners = lax.axis_size(("role", "ep"))
    tok_rows, top_count = routes.shape
    paired = lax.axis_size("tp") == 2 and lax.axis_size("role") == 2 and lax.axis_size("ep") == 8
    if paired and 2 * slot_capacity(tok_rows, top_count, owners) >= tok_rows:
        return dense_device(tokens, out_grad, routes, probs, w_gate, w_up, w_down)
    return routed_device(tokens, out_grad, routes, probs, w_gate, w_up, w_down)


def solution(mesh):
    in_specs = (
        P(("groups", "role", "ep"), "tp"),
        P(("groups", "role", "ep"), "tp"),
        P(("groups", "role", "ep"), None),
        P(("groups", "role", "ep"), None),
        P(("role", "ep"), None, "tp"),
        P(("role", "ep"), None, "tp"),
        P(("role", "ep"), "tp", None),
    )
    out_specs = (
        P(("groups", "role", "ep"), "tp"),
        P(("groups", "role", "ep"), None),
        P(("groups", "role", "ep"), None, "tp"),
        P(("groups", "role", "ep"), None, "tp"),
        P(("groups", "role", "ep"), "tp", None),
    )
    return jax.shard_map(
        per_device, mesh=mesh, in_specs=in_specs, out_specs=out_specs, check_vma=False
    )
```

```python
import functools
import math

import jax
import jax.numpy as jnp
from jax import lax
from jax.experimental import pallas as pl
from jax.experimental.pallas import tpu as pltpu
from jax.sharding import PartitionSpec as P


def pad_rows(array):
    return jnp.concatenate([array, jnp.zeros((1, array.shape[1]), array.dtype)], 0)


def routed_device(tokens, out_grad, routes, probs, w_gate, w_up, w_down):
    owners = lax.axis_size(("role", "ep"))
    tok_rows, top_count = routes.shape
    width_full = w_gate.shape[1]
    part_width = w_gate.shape[2]
    capacity = min(tok_rows, tok_rows * top_count * 9 // (8 * owners))
    entry_total = tok_rows * top_count
    routes_flat = routes.reshape(-1)
    onehot = (routes_flat[:, None] == jnp.arange(owners, dtype=jnp.int32)[None, :]).astype(
        jnp.int32
    )
    before = jnp.cumsum(onehot, axis=0) - onehot
    slot_index = jnp.sum(before * onehot, axis=1)
    target = routes_flat * capacity + slot_index
    row_count = owners * capacity
    entry_of_slot = (
        jnp.full((row_count,), entry_total, jnp.int32)
        .at[target]
        .set(jnp.arange(entry_total, dtype=jnp.int32))
    )
    token_of_slot = entry_of_slot // top_count
    padded_prob = jnp.concatenate([probs.reshape(-1), jnp.zeros((1,), probs.dtype)], 0)
    send_prob = padded_prob[entry_of_slot].reshape(owners, capacity)
    send_x = pad_rows(tokens)[token_of_slot]
    send_g = pad_rows(out_grad)[token_of_slot]
    slice_x, slice_g, recv_p = (
        lax.all_to_all(
            send_x.reshape(owners, capacity, tokens.shape[1]),
            ("role", "ep"),
            split_axis=0,
            concat_axis=0,
            tiled=True,
        ),
        lax.all_to_all(
            send_g.reshape(owners, capacity, tokens.shape[1]),
            ("role", "ep"),
            split_axis=0,
            concat_axis=0,
            tiled=True,
        ),
        lax.all_to_all(send_prob, ("role", "ep"), split_axis=0, concat_axis=0, tiled=True),
    )
    recv_x, recv_g = (
        lax.all_gather(slice_x, "tp", axis=2, tiled=True),
        lax.all_gather(slice_g, "tp", axis=2, tiled=True),
    )
    rows_x = recv_x.reshape(row_count, width_full)
    rows_g = recv_g.reshape(row_count, width_full)
    weight_p = recv_p.reshape(row_count, 1).astype(jnp.float32)
    gate_up = jnp.concatenate([w_gate[0], w_up[0]], 1)
    down_shard = w_down[0]
    both_rows = jnp.dot(rows_x, gate_up, preferred_element_type=jnp.float32)
    gate_rows = both_rows[:, :part_width]
    up_rows = both_rows[:, part_width:]
    sigmoid_gate = jax.nn.sigmoid(gate_rows)
    activated = gate_rows * sigmoid_gate
    hidden = activated * up_rows
    back_rows = lax.dot_general(
        rows_g, down_shard, (((1,), (1,)), ((), ())), preferred_element_type=jnp.float32
    )
    scores = lax.psum(jnp.sum(hidden * back_rows, axis=1), "tp")
    hidden_grad = weight_p * back_rows
    d_gate_rows = (
        hidden_grad * up_rows * sigmoid_gate * (1.0 + gate_rows * (1.0 - sigmoid_gate))
    ).astype(jnp.bfloat16)
    d_up_rows = (hidden_grad * activated).astype(jnp.bfloat16)
    d_both = jnp.concatenate([d_gate_rows, d_up_rows], 1)
    scaled = (weight_p * hidden).astype(jnp.bfloat16)
    grad_down = lax.dot_general(
        scaled, rows_g, (((0,), (0,)), ((), ())), preferred_element_type=jnp.float32
    )
    grad_both = lax.dot_general(
        rows_x, d_both, (((0,), (0,)), ((), ())), preferred_element_type=jnp.float32
    )
    grad_gate = grad_both[:, :part_width]
    grad_up = grad_both[:, part_width:]
    partial_low = lax.dot_general(
        d_both, gate_up, (((1,), (1,)), ((), ())), preferred_element_type=jnp.float32
    ).astype(jnp.bfloat16)
    home_s = lax.all_to_all(
        scores.reshape(owners, capacity), ("role", "ep"), split_axis=0, concat_axis=0, tiled=True
    )
    summed = lax.psum_scatter(
        partial_low.reshape(owners, capacity, width_full), "tp", scatter_dimension=2, tiled=True
    ).astype(jnp.float32)
    summed_low = summed.astype(jnp.bfloat16)
    home_x = lax.all_to_all(summed_low, ("role", "ep"), split_axis=0, concat_axis=0, tiled=True)
    slice_width = summed.shape[2]
    route_rows = home_x.reshape(row_count, slice_width).astype(jnp.float32)
    d_tok = (
        jnp.zeros((tok_rows + 1, slice_width), jnp.float32)
        .at[token_of_slot]
        .add(route_rows)[:tok_rows]
    )
    d_probs = home_s.reshape(-1)[target].reshape(tok_rows, top_count)
    return (
        d_tok.astype(jnp.bfloat16),
        d_probs,
        grad_gate.astype(jnp.bfloat16)[None],
        grad_up.astype(jnp.bfloat16)[None],
        grad_down.astype(jnp.bfloat16)[None],
    )


def slot_capacity(tok_rows, top_count, owners):
    return min(tok_rows, tok_rows * top_count * 9 // (8 * owners))


LOOSE = pl.BlockSpec(memory_space=pl.ANY)


def weights_kernel(tp_ref, wg_ref, wu_ref, wd_ref, both_ref, down_ref):
    part = wg_ref.shape[2]
    both_ref[:, :part] = wg_ref[0]
    both_ref[:, part:] = wu_ref[0]
    down_ref[...] = wd_ref[0]


def weights_call(which, w_gate, w_up, w_down):
    _, width, part = w_gate.shape
    half = width // 2

    def place(i, w):
        return (i + w[0]) % 2

    return pl.pallas_call(
        weights_kernel,
        grid_spec=pltpu.PrefetchScalarGridSpec(
            num_scalar_prefetch=1,
            grid=(2,),
            in_specs=[
                pl.BlockSpec((1, half, part), lambda i, w: (0, place(i, w), 0)),
                pl.BlockSpec((1, half, part), lambda i, w: (0, place(i, w), 0)),
                pl.BlockSpec((1, part, half), lambda i, w: (0, 0, place(i, w))),
            ],
            out_specs=[
                pl.BlockSpec((half, 2 * part), lambda i, w: (i, 0)),
                pl.BlockSpec((part, half), lambda i, w: (0, i)),
            ],
        ),
        out_shape=[
            jax.ShapeDtypeStruct((width, 2 * part), jnp.bfloat16),
            jax.ShapeDtypeStruct((part, width), jnp.bfloat16),
        ],
        compiler_params=pltpu.CompilerParams(vmem_limit_bytes=12 << 20),
        cost_estimate=pl.CostEstimate(flops=0, bytes_accessed=12 * width * part, transcendentals=0),
        name="weights",
    )(which, *[pltpu.with_memory_space_constraint(item, pltpu.HBM) for item in (w_gate, w_up, w_down)])


def join_kernel(top_ref, bottom_ref, out_ref, sems):
    rows = top_ref.shape[0]
    copies = [
        pltpu.make_async_copy(top_ref, out_ref.at[pl.ds(0, rows)], sems.at[0]),
        pltpu.make_async_copy(bottom_ref, out_ref.at[pl.ds(rows, rows)], sems.at[1]),
    ]
    for copy in copies:
        copy.start()
    for copy in copies:
        copy.wait()


def join_call(top, bottom):
    rows, columns = top.shape
    return pl.pallas_call(
        join_kernel,
        in_specs=[LOOSE] * 2,
        out_specs=pl.BlockSpec(memory_space=pltpu.VMEM),
        out_shape=pltpu.VMEM((2 * rows, columns), top.dtype),
        scratch_shapes=[pltpu.SemaphoreType.DMA((2,))],
        compiler_params=pltpu.CompilerParams(vmem_limit_bytes=8 << 20),
        cost_estimate=pl.CostEstimate(flops=0, bytes_accessed=8 * rows * columns, transcendentals=0),
        name="join",
    )(*[pltpu.with_memory_space_constraint(item, pltpu.HBM) for item in (top, bottom)])


def rows_kernel(count, ways, capacity, slots, where_ref, *refs):
    weights_in, units_in, tables_in = refs[:4], refs[4 : 4 + 4 * count], refs[4 + 4 * count : 4 + 5 * count]
    leaves = 1 + max(way[0] for way in ways.values())
    refs = refs[len(refs) - 6 - leaves :]
    outs, packets, refs = refs[:2], refs[2 : 2 + leaves], refs[2 + leaves :]
    x_all, g_all, tables, unit_sems = refs
    half, tok = x_all.shape[3], x_all.shape[2] // 2
    part = weights_in[2].shape[0]
    owners = tables.shape[2]
    wgu, wd = weights_in[:2], weights_in[2:]

    x_copies, g_copies = [], []
    for index, unit in enumerate(units_in):
        chunk, y, x = index // 4, index // 2 % 2, index % 2
        rows = pl.ds(y * tok, tok)
        x_copies.append(pltpu.make_async_copy(unit.at[pl.ds(0, tok)], x_all.at[chunk, x, rows], unit_sems.at[0, index]))
        g_copies.append(pltpu.make_async_copy(unit.at[pl.ds(tok, tok)], g_all.at[chunk, x, rows], unit_sems.at[1, index]))
    t_copies = [
        pltpu.make_async_copy(table, tables.at[chunk], unit_sems.at[2, chunk]) for chunk, table in enumerate(tables_in)
    ]
    for copy in t_copies + x_copies + g_copies:
        copy.start()
    both_at, scaled_at = pl.ds(4 * half, 2 * part), pl.ds(4 * half + 2 * part, part)

    def dot(a, b, dims):
        return lax.dot_general(a, b, (dims, ((), ())), preferred_element_type=jnp.float32)

    for copy in t_copies:
        copy.wait()
    earlier = lax.broadcasted_iota(jnp.int32, (tok, tok), 0) < lax.broadcasted_iota(jnp.int32, (tok, tok), 1)
    earlier = earlier.astype(jnp.bfloat16)
    place = lax.broadcasted_iota(jnp.int32, (slots, tok), 0).astype(jnp.float32)
    names = lax.broadcasted_iota(jnp.int32, (owners, tok), 0)
    picks, low_picks, probs = {}, {}, {}
    for chunk in range(count):
        found = []
        for y in range(2):
            table = tables[chunk, y].astype(jnp.float32)
            rank = dot((table >= 0.0).astype(jnp.bfloat16), earlier, ((1,), (0,))) + float(y * capacity)
            found.append((table, jnp.where(table >= 0.0, rank, -1.0)))
        for expert in range(2):
            mine = names == where_ref[expert]
            halves, prob = [], None
            for table, rank in found:
                weight = jnp.sum(jnp.where(mine, table, 0.0), axis=0, keepdims=True)
                slot = jnp.sum(jnp.where(mine, rank, 0.0), axis=0, keepdims=True)
                halves.append((place == slot).astype(jnp.float32))
                term = jnp.sum(halves[-1] * weight, axis=1, keepdims=True)
                prob = term if prob is None else prob + term
            picks[chunk, expert] = halves
            low_picks[chunk, expert] = jnp.concatenate(halves, 1).astype(jnp.bfloat16)
            probs[chunk, expert] = prob
    spans = [pl.ds(chunk * slots, slots) for chunk in range(count)]
    sides = [slice(side * half, (side + 1) * half) for side in range(2)]

    def gather(copies, source, offset):
        for chunk in range(count):
            for copy in copies[4 * chunk : 4 * chunk + 4]:
                copy.wait()
            both_picks = jnp.concatenate([low_picks[chunk, expert] for expert in range(2)], 0)
            for side in range(2):
                rows = dot(both_picks, source[chunk, side], ((1,), (0,))).astype(jnp.bfloat16)
                for expert in range(2):
                    columns = pl.ds(offset + side * half, half)
                    outs[expert][spans[chunk], columns] = rows[expert * slots : (expert + 1) * slots]

    gather(x_copies, x_all, 0)
    rows = []
    for expert in range(2):
        rows.append(dot(outs[expert][:, : 2 * half], wgu[expert][...], ((1,), (0,))))
    gather(g_copies, g_all, 2 * half)
    scores = []
    for expert in range(2):
        back = dot(outs[expert][:, 2 * half : 4 * half], wd[expert][...], ((1,), (1,)))
        gate, up = rows[expert][:, :part], rows[expert][:, part:]
        sig = jax.nn.sigmoid(gate)
        act = gate * sig
        hidden = act * up
        scores.append(jnp.sum(hidden * back, axis=1, keepdims=True))
        prob = jnp.concatenate([probs[chunk, expert] for chunk in range(count)], 0)
        hgrad = prob * back
        d_gate = (hgrad * up * sig * (1.0 + gate * (1.0 - sig))).astype(jnp.bfloat16)
        outs[expert][:, both_at] = jnp.concatenate([d_gate, (hgrad * act).astype(jnp.bfloat16)], 1)
        outs[expert][:, scaled_at] = (prob * hidden).astype(jnp.bfloat16)

    extra_rows = packets[0].shape[1] - tok
    per_row = owners // extra_rows
    names = lax.broadcasted_iota(jnp.int32, (extra_rows, half), 0)
    column = lax.broadcasted_iota(jnp.int32, (extra_rows, half), 1) // (2 * tok)
    for chunk in range(count):
        for y in range(2):
            extra = jnp.zeros((extra_rows, half), jnp.float32)
            for expert in range(2):
                part_scores = scores[expert][chunk * slots : (chunk + 1) * slots]
                line = jnp.sum(picks[chunk, expert][y] * part_scores, axis=0, keepdims=True)
                high = line.astype(jnp.bfloat16).astype(jnp.float32)
                line = jnp.concatenate([high, line - high] * (half // (2 * tok)), 1)
                row, cell = where_ref[expert] // per_row, where_ref[expert] % per_row * 2 + where_ref[2]
                extra = extra + jnp.where((names == row) & (column == cell), line, 0.0)
            for side in range(2):
                number, slot = ways[chunk, y, side]
                packets[number][slot, tok:] = extra.astype(jnp.bfloat16)
    early = count == 1
    grads = [outs[expert][:, both_at] for expert in range(2)]
    if early:
        grads = [dot(low_picks[0, expert], grads[expert], ((0,), (0,))).astype(jnp.bfloat16) for expert in range(2)]
    for side in (1, 0):
        low = [dot(grads[expert], wgu[expert][sides[side], :], ((1,), (1,))) for expert in range(2)]
        for chunk in range(count):
            if early:
                total = low[0] + low[1]
            else:
                rows = slice(chunk * slots, (chunk + 1) * slots)
                total = sum(
                    dot(low_picks[chunk, expert], low[expert][rows].astype(jnp.bfloat16), ((0,), (0,)))
                    for expert in range(2)
                )
            for y in range(2):
                number, slot = ways[chunk, y, side]
                packets[number][slot, :tok] = total[y * tok : (y + 1) * tok].astype(jnp.bfloat16)


def rows_call(items, owners, capacity, slots, where, weights, units, tables, after):
    count = len(tables)
    ways = {block: (number, slot) for number, blocks in enumerate(items) for slot, block in enumerate(blocks)}
    tok, half = units[0].shape[0] // 2, units[0].shape[1]
    part, width = weights[2].shape
    widths = (width, width, 2 * part, part)
    packet = (tok + 4 * tok * owners // half, half)
    return pl.pallas_call(
        functools.partial(rows_kernel, count, ways, capacity, slots),
        grid_spec=pltpu.PrefetchScalarGridSpec(
            num_scalar_prefetch=1,
            grid=(1,),
            in_specs=[pl.BlockSpec(memory_space=pltpu.VMEM)] * 4 + [LOOSE] * (5 * count + len(after)),
            out_specs=[pl.BlockSpec(memory_space=pltpu.VMEM)] * (2 + len(items)),
            scratch_shapes=[pltpu.VMEM((count, 2, 2 * tok, half), jnp.bfloat16)] * 2
            + [pltpu.VMEM((count, 2, owners, tok), jnp.bfloat16)]
            + [pltpu.SemaphoreType.DMA((3, 4 * count))],
        ),
        out_shape=[pltpu.VMEM((count * slots, sum(widths)), jnp.bfloat16)] * 2
        + [pltpu.VMEM((len(blocks),) + packet, jnp.bfloat16) for blocks in items],
        compiler_params=pltpu.CompilerParams(vmem_limit_bytes=14 << 20),
        cost_estimate=pl.CostEstimate(
            flops=count * (20 * slots * width * part + 24 * slots * tok * width),
            bytes_accessed=count * 16 * tok * width + 12 * width * part,
            transcendentals=2 * count * slots * part,
        ),
        name="rows",
    )(where, *[pltpu.with_memory_space_constraint(item, pltpu.VMEM) for item in (*weights, *units, *tables)], *after)


def grads_kernel(count, wide, deep, blocks, tp_ref, *refs):
    sources, outs = refs[:count], refs[count:-4]
    wide_all, deep_all, wide_sems, deep_sems = refs[-4:]
    starts = [sum(source.shape[0] for source in sources[:index]) for index in range(count)]
    size = wide_all.shape[2]
    block = pl.program_id(0)

    def copies(column):
        return [
            pltpu.make_async_copy(
                source.at[:, pl.ds(wide + column * size, size)],
                wide_all.at[column, pl.ds(starts[index], source.shape[0])],
                wide_sems.at[column, index],
            )
            for index, source in enumerate(sources)
        ]

    @pl.when(block == 0)
    def _():
        deep_copies = [
            pltpu.make_async_copy(
                source.at[:, pl.ds(deep, deep_all.shape[1])],
                deep_all.at[pl.ds(starts[index], source.shape[0])],
                deep_sems.at[index],
            )
            for index, source in enumerate(sources)
        ]
        for copy in deep_copies:
            copy.start()
        for column in range(blocks):
            for copy in copies(column):
                copy.start()
        for copy in deep_copies:
            copy.wait()

    for column in range(blocks):

        @pl.when(block == column)
        def _(column=column):
            for copy in copies(column):
                copy.wait()

    dims = (((0,), (0,)), ((), ()))
    if len(outs) == 2:
        part = outs[0].shape[2]
        both = lax.dot_general(wide_all[block], deep_all[...], dims, preferred_element_type=jnp.float32)
        outs[0][0] = both[:, :part].astype(jnp.bfloat16)
        outs[1][0] = both[:, part:].astype(jnp.bfloat16)
    else:
        down = lax.dot_general(deep_all[...], wide_all[block], dims, preferred_element_type=jnp.float32)
        outs[0][0] = down.astype(jnp.bfloat16)


def grads_call(which, packed, width, part, down):
    rows, count = sum(item.shape[0] for item in packed), len(packed)
    step = math.gcd(width // 2, 512 if down else 1024)
    per = width // 2 // step
    deep = part if down else 2 * part

    def place(i, w):
        return (i + w[0] * per) % (2 * per)

    if down:
        specs = [pl.BlockSpec((1, part, step), lambda i, w: (0, 0, place(i, w)))]
        shapes = [(1, part, width)]
    else:
        specs = [pl.BlockSpec((1, step, part), lambda i, w: (0, place(i, w), 0))] * 2
        shapes = [(1, width, part)] * 2
    starts = (width, 2 * width + 2 * part) if down else (0, 2 * width)
    return pl.pallas_call(
        functools.partial(grads_kernel, count, *starts, 2 * per),
        grid_spec=pltpu.PrefetchScalarGridSpec(
            num_scalar_prefetch=1,
            grid=(2 * per,),
            in_specs=[LOOSE] * count,
            out_specs=specs,
            scratch_shapes=[
                pltpu.VMEM((2 * per, rows, step), jnp.bfloat16),
                pltpu.VMEM((rows, deep), jnp.bfloat16),
                pltpu.SemaphoreType.DMA((2 * per, count)),
                pltpu.SemaphoreType.DMA((count,)),
            ],
        ),
        out_shape=[jax.ShapeDtypeStruct(shape, jnp.bfloat16) for shape in shapes],
        compiler_params=pltpu.CompilerParams(vmem_limit_bytes=22 << 20),
        cost_estimate=pl.CostEstimate(
            flops=2 * rows * width * deep, bytes_accessed=2 * rows * (width + deep), transcendentals=0
        ),
        name="grads",
    )(which, *packed)


def dense_device(tokens, out_grad, routes, probs, w_gate, w_up, w_down):
    owners = lax.axis_size(("role", "ep"))
    ep = lax.axis_size("ep")
    n_y = 2
    n_z = ep // n_y
    tok_rows, half = tokens.shape
    capacity = slot_capacity(tok_rows, routes.shape[1], owners)
    slots = -(-n_y * capacity // 16) * 16
    role, place, which = lax.axis_index("role"), lax.axis_index("ep"), lax.axis_index("tp")

    def over_x(array):
        return lax.ppermute(array, "tp", [(0, 1), (1, 0)])

    def over_role(array):
        return lax.ppermute(array, "role", [(0, 1), (1, 0)])

    def over_y(array):
        return lax.ppermute(array, "ep", [(i, i + 1 - 2 * (i % n_y)) for i in range(ep)])

    def over_z(array, shift):
        return lax.ppermute(array, "ep", [(i, (i + shift * n_y) % ep) for i in range(ep)])

    def tied(values, others):
        return lax.optimization_barrier((list(values), list(others)))[0]

    last = n_z - 1
    routes_in = []
    for z in range(n_z):
        shift = -1 if z == last and z > 1 else 1
        if z:
            routes_in.append(((z, 0, 0), (0 if z in (1, last) else z - 1, 0, 0), functools.partial(over_z, shift=shift)))
        routes_in.append(((z, 1, 0), (z, 0, 0), over_y))
        routes_in.append(((z, 0, 1), (z, 0, 0), over_x))
        if z == 0:
            routes_in.append(((z, 1, 1), (z, 1, 0), over_x))
        elif z in (1, last):
            routes_in.append(((z, 1, 1), (0, 1, 1), functools.partial(over_z, shift=shift)))
        else:
            routes_in.append(((z, 1, 1), (z, 0, 1), over_y))
    routes_in.sort(key=lambda item: (item[0][0] % 2 if item[2] in (over_x, over_y) else 0, sum(item[0][1:])))

    rounds, waiting, there = [], list(routes_in), {(0, 0, 0)}
    while waiting:
        moves = {}
        for item in waiting:
            axis = item[2] if item[2] in (over_x, over_y) else over_z
            if item[1] in there and axis not in moves:
                moves[axis] = item
        rounds.append(moves)
        there |= {item[0] for item in moves.values()}
        waiting = [item for item in waiting if item[0] not in there]

    which_ref = which.reshape(1).astype(jnp.int32)
    where = jnp.stack([role * ep + place, (1 - role) * ep + place, which]).astype(jnp.int32)
    both_w, down_w = weights_call(which_ref, w_gate, w_up, w_down)
    width, part = both_w.shape[0], down_w.shape[0]

    def rows_of(steps, items, after):
        four = [units[z, y, x] for z in steps for y in range(2) for x in range(2)]
        return rows_call(items, owners, capacity, slots, where, weights, four, [tables[z] for z in steps], after)

    units = {(0, 0, 0): join_call(tokens, out_grad)}
    flying, landed, extra = {}, [], []
    for number, moves in enumerate(rounds):
        arrived = {}
        for axis, (target, source, move) in moves.items():
            (block,) = tied([units[source]], [flying[axis]] + landed + extra) if flying else [units[source]]
            arrived[axis] = move(block)
        units.update({moves[axis][0]: block for axis, block in arrived.items()})
        flying, landed, extra = arrived, list(flying.values()), []
        if number == 0:
            extra = [both_w, down_w]
            both_w, down_w, routes, probs = tied([both_w, down_w, routes, probs], arrived.values())
            weights = (both_w, over_role(both_w), down_w, over_role(down_w))
            chosen = routes[:, :, None] == jnp.arange(owners, dtype=jnp.int32)
            table = jnp.sum(jnp.where(chosen, probs[:, :, None].astype(jnp.float32) + 1.0, 0.0), axis=1) - 1.0
            table = table.astype(jnp.bfloat16).T
            table = jnp.stack([table, over_y(table)])
        if number == 1:
            (table,) = tied([table], arrived.values())
            tables = [over_z(table, z) if z else table for z in range(n_z)]
        if number == 2:
            mine_0, other_0, near, side_0, far, y_0 = rows_of(
                [0], [[(0, 0, 0)], [(0, 0, 1)], [(0, 1, 1)], [(0, 1, 0)]], []
            )
            extra = [mine_0]

    def total(*blocks):
        return sum(block.astype(jnp.float32) for block in blocks).astype(jnp.bfloat16)

    items = [[(1, 1, 1)], [(1, 0, 1)], [(0, 0, 1)], [(0, 1, 0)], [(0, 1, 1)], [(0, 0, 0)], [(1, 0, 0)], [(1, 1, 0)]]
    mine_1, other_1, x_2, x_20, x_1, y_1, z_1, keep_1, keep_2, keep_2y = rows_of([1, 2], items, tables[3:])
    other_1, x_2, x_20, x_1, y_1, z_1 = tied([other_1, x_2, x_20, x_1, y_1, z_1], arrived.values())
    from_x2, from_y1, from_z1 = over_x(x_2), over_y(y_1), over_z(z_1, -1)
    from_x20 = over_x(x_20)
    items = [[(0, 0, 1)], [(0, 1, 0)], [(0, 1, 1)], [(0, 0, 0)]]
    mine_3, other_3, x_3, y_3, z_3, keep_3 = rows_of([3], items, [mine_1])
    mine_3, other_3, x_3, y_3, z_3, keep_2y = tied(
        [mine_3, other_3, x_3, y_3, z_3, keep_2y], [from_x2, from_y1, from_z1]
    )
    from_z3, from_y2, from_x1 = over_z(z_3, 1), over_y(total(keep_2y, from_x2)), over_x(x_1)
    from_y3 = over_y(y_3)
    packed = [mine_0, over_role(other_0), mine_1, over_role(other_1), mine_3, over_role(other_3)]
    (d_down,) = grads_call(which_ref, packed, width, part, True)
    from_z3, from_x20, from_y2 = tied([from_z3, from_x20, from_y2], [d_down])
    far, step_2 = total(far, from_z1, from_z3), total(keep_2, from_x20, from_y2)
    from_x1, x_3 = tied([from_x1, x_3], [far, step_2])
    from_far, from_z2, from_x3 = over_y(far), over_z(step_2, 1), over_x(x_3)
    home_1 = over_z(total(keep_1, from_x1, from_y1), -1)
    from_x0 = over_x(total(side_0, from_far))
    from_x3, from_y3, from_z2 = tied([from_x3, from_y3, from_z2], [from_far])
    home_3 = over_z(total(keep_3, from_x3, from_y3, from_z2), 1)
    from_y0 = over_y(tied([y_0], [from_far])[0])
    d_gate, d_up = grads_call(which_ref, packed, width, part, False)
    home_1, from_x0, home_3, from_y0 = tied([home_1, from_x0, home_3, from_y0], [d_gate, d_up])
    home = (near, from_x0, home_3, home_1, from_y0)
    d_tok = sum(block[0, :tok_rows].astype(jnp.float32) for block in home).astype(jnp.bfloat16)
    home = sum(block[0, tok_rows:].astype(jnp.float32) for block in home)
    score = jnp.sum(home.reshape(owners, 4, tok_rows), axis=1).T
    d_probs = jnp.sum(jnp.where(chosen, score[:, None, :], 0.0), axis=2)
    return d_tok, d_probs, d_gate, d_up, d_down


def per_device(tokens, out_grad, routes, probs, w_gate, w_up, w_down):
    owners = lax.axis_size(("role", "ep"))
    tok_rows, top_count = routes.shape
    paired = lax.axis_size("tp") == 2 and lax.axis_size("role") == 2 and lax.axis_size("ep") == 8
    if paired and 2 * slot_capacity(tok_rows, top_count, owners) >= tok_rows:
        return dense_device(tokens, out_grad, routes, probs, w_gate, w_up, w_down)
    return routed_device(tokens, out_grad, routes, probs, w_gate, w_up, w_down)


def solution(mesh):
    in_specs = (
        P(("groups", "role", "ep"), "tp"),
        P(("groups", "role", "ep"), "tp"),
        P(("groups", "role", "ep"), None),
        P(("groups", "role", "ep"), None),
        P(("role", "ep"), None, "tp"),
        P(("role", "ep"), None, "tp"),
        P(("role", "ep"), "tp", None),
    )
    out_specs = (
        P(("groups", "role", "ep"), "tp"),
        P(("groups", "role", "ep"), None),
        P(("groups", "role", "ep"), None, "tp"),
        P(("groups", "role", "ep"), None, "tp"),
        P(("groups", "role", "ep"), "tp", None),
    )
    return jax.shard_map(
        per_device, mesh=mesh, in_specs=in_specs, out_specs=out_specs, check_vma=False
    )
```

```python
import functools
import math

import jax
import jax.numpy as jnp
from jax import lax
from jax.experimental import pallas as pl
from jax.experimental.pallas import tpu as pltpu
from jax.sharding import PartitionSpec as P


def pad_rows(array):
    return jnp.concatenate([array, jnp.zeros((1, array.shape[1]), array.dtype)], 0)


def routed_device(tokens, out_grad, routes, probs, w_gate, w_up, w_down):
    owners = lax.axis_size(("role", "ep"))
    tok_rows, top_count = routes.shape
    width_full = w_gate.shape[1]
    part_width = w_gate.shape[2]
    capacity = min(tok_rows, tok_rows * top_count * 9 // (8 * owners))
    entry_total = tok_rows * top_count
    routes_flat = routes.reshape(-1)
    onehot = (routes_flat[:, None] == jnp.arange(owners, dtype=jnp.int32)[None, :]).astype(
        jnp.int32
    )
    before = jnp.cumsum(onehot, axis=0) - onehot
    slot_index = jnp.sum(before * onehot, axis=1)
    target = routes_flat * capacity + slot_index
    row_count = owners * capacity
    entry_of_slot = (
        jnp.full((row_count,), entry_total, jnp.int32)
        .at[target]
        .set(jnp.arange(entry_total, dtype=jnp.int32))
    )
    token_of_slot = entry_of_slot // top_count
    padded_prob = jnp.concatenate([probs.reshape(-1), jnp.zeros((1,), probs.dtype)], 0)
    send_prob = padded_prob[entry_of_slot].reshape(owners, capacity)
    send_x = pad_rows(tokens)[token_of_slot]
    send_g = pad_rows(out_grad)[token_of_slot]
    slice_x, slice_g, recv_p = (
        lax.all_to_all(
            send_x.reshape(owners, capacity, tokens.shape[1]),
            ("role", "ep"),
            split_axis=0,
            concat_axis=0,
            tiled=True,
        ),
        lax.all_to_all(
            send_g.reshape(owners, capacity, tokens.shape[1]),
            ("role", "ep"),
            split_axis=0,
            concat_axis=0,
            tiled=True,
        ),
        lax.all_to_all(send_prob, ("role", "ep"), split_axis=0, concat_axis=0, tiled=True),
    )
    recv_x, recv_g = (
        lax.all_gather(slice_x, "tp", axis=2, tiled=True),
        lax.all_gather(slice_g, "tp", axis=2, tiled=True),
    )
    rows_x = recv_x.reshape(row_count, width_full)
    rows_g = recv_g.reshape(row_count, width_full)
    weight_p = recv_p.reshape(row_count, 1).astype(jnp.float32)
    gate_up = jnp.concatenate([w_gate[0], w_up[0]], 1)
    down_shard = w_down[0]
    both_rows = jnp.dot(rows_x, gate_up, preferred_element_type=jnp.float32)
    gate_rows = both_rows[:, :part_width]
    up_rows = both_rows[:, part_width:]
    sigmoid_gate = jax.nn.sigmoid(gate_rows)
    activated = gate_rows * sigmoid_gate
    hidden = activated * up_rows
    back_rows = lax.dot_general(
        rows_g, down_shard, (((1,), (1,)), ((), ())), preferred_element_type=jnp.float32
    )
    scores = lax.psum(jnp.sum(hidden * back_rows, axis=1), "tp")
    hidden_grad = weight_p * back_rows
    d_gate_rows = (
        hidden_grad * up_rows * sigmoid_gate * (1.0 + gate_rows * (1.0 - sigmoid_gate))
    ).astype(jnp.bfloat16)
    d_up_rows = (hidden_grad * activated).astype(jnp.bfloat16)
    d_both = jnp.concatenate([d_gate_rows, d_up_rows], 1)
    scaled = (weight_p * hidden).astype(jnp.bfloat16)
    grad_down = lax.dot_general(
        scaled, rows_g, (((0,), (0,)), ((), ())), preferred_element_type=jnp.float32
    )
    grad_both = lax.dot_general(
        rows_x, d_both, (((0,), (0,)), ((), ())), preferred_element_type=jnp.float32
    )
    grad_gate = grad_both[:, :part_width]
    grad_up = grad_both[:, part_width:]
    partial_low = lax.dot_general(
        d_both, gate_up, (((1,), (1,)), ((), ())), preferred_element_type=jnp.float32
    ).astype(jnp.bfloat16)
    home_s = lax.all_to_all(
        scores.reshape(owners, capacity), ("role", "ep"), split_axis=0, concat_axis=0, tiled=True
    )
    summed = lax.psum_scatter(
        partial_low.reshape(owners, capacity, width_full), "tp", scatter_dimension=2, tiled=True
    ).astype(jnp.float32)
    summed_low = summed.astype(jnp.bfloat16)
    home_x = lax.all_to_all(summed_low, ("role", "ep"), split_axis=0, concat_axis=0, tiled=True)
    slice_width = summed.shape[2]
    route_rows = home_x.reshape(row_count, slice_width).astype(jnp.float32)
    d_tok = (
        jnp.zeros((tok_rows + 1, slice_width), jnp.float32)
        .at[token_of_slot]
        .add(route_rows)[:tok_rows]
    )
    d_probs = home_s.reshape(-1)[target].reshape(tok_rows, top_count)
    return (
        d_tok.astype(jnp.bfloat16),
        d_probs,
        grad_gate.astype(jnp.bfloat16)[None],
        grad_up.astype(jnp.bfloat16)[None],
        grad_down.astype(jnp.bfloat16)[None],
    )


def slot_capacity(tok_rows, top_count, owners):
    return min(tok_rows, tok_rows * top_count * 9 // (8 * owners))


LOOSE = pl.BlockSpec(memory_space=pl.ANY)


def weights_kernel(tp_ref, wg_ref, wu_ref, wd_ref, both_ref, down_ref):
    part = wg_ref.shape[2]
    both_ref[:, :part] = wg_ref[0]
    both_ref[:, part:] = wu_ref[0]
    down_ref[...] = wd_ref[0]


def weights_call(which, w_gate, w_up, w_down):
    _, width, part = w_gate.shape
    half = width // 2

    def place(i, w):
        return (i + w[0]) % 2

    return pl.pallas_call(
        weights_kernel,
        grid_spec=pltpu.PrefetchScalarGridSpec(
            num_scalar_prefetch=1,
            grid=(2,),
            in_specs=[
                pl.BlockSpec((1, half, part), lambda i, w: (0, place(i, w), 0)),
                pl.BlockSpec((1, half, part), lambda i, w: (0, place(i, w), 0)),
                pl.BlockSpec((1, part, half), lambda i, w: (0, 0, place(i, w))),
            ],
            out_specs=[
                pl.BlockSpec((half, 2 * part), lambda i, w: (i, 0)),
                pl.BlockSpec((part, half), lambda i, w: (0, i)),
            ],
        ),
        out_shape=[
            jax.ShapeDtypeStruct((width, 2 * part), jnp.bfloat16),
            jax.ShapeDtypeStruct((part, width), jnp.bfloat16),
        ],
        compiler_params=pltpu.CompilerParams(vmem_limit_bytes=12 << 20),
        cost_estimate=pl.CostEstimate(flops=0, bytes_accessed=12 * width * part, transcendentals=0),
        name="weights",
    )(which, *[pltpu.with_memory_space_constraint(item, pltpu.HBM) for item in (w_gate, w_up, w_down)])


def join_kernel(top_ref, bottom_ref, out_ref, sems):
    rows = top_ref.shape[0]
    copies = [
        pltpu.make_async_copy(top_ref, out_ref.at[pl.ds(0, rows)], sems.at[0]),
        pltpu.make_async_copy(bottom_ref, out_ref.at[pl.ds(rows, rows)], sems.at[1]),
    ]
    for copy in copies:
        copy.start()
    for copy in copies:
        copy.wait()


def join_call(top, bottom):
    rows, columns = top.shape
    return pl.pallas_call(
        join_kernel,
        in_specs=[LOOSE] * 2,
        out_specs=pl.BlockSpec(memory_space=pltpu.VMEM),
        out_shape=pltpu.VMEM((2 * rows, columns), top.dtype),
        scratch_shapes=[pltpu.SemaphoreType.DMA((2,))],
        compiler_params=pltpu.CompilerParams(vmem_limit_bytes=8 << 20),
        cost_estimate=pl.CostEstimate(flops=0, bytes_accessed=8 * rows * columns, transcendentals=0),
        name="join",
    )(*[pltpu.with_memory_space_constraint(item, pltpu.HBM) for item in (top, bottom)])


def rows_kernel(count, ways, capacity, slots, where_ref, *refs):
    weights_in, units_in, tables_in = refs[:4], refs[4 : 4 + 4 * count], refs[4 + 4 * count : 4 + 5 * count]
    leaves = 1 + max(way[0] for way in ways.values())
    refs = refs[len(refs) - 6 - leaves :]
    outs, packets, refs = refs[:2], refs[2 : 2 + leaves], refs[2 + leaves :]
    x_all, g_all, tables, unit_sems = refs
    half, tok = x_all.shape[3], x_all.shape[2] // 2
    part = weights_in[2].shape[0]
    owners = tables.shape[2]
    wgu, wd = weights_in[:2], weights_in[2:]

    x_copies, g_copies = [], []
    for index, unit in enumerate(units_in):
        chunk, y, x = index // 4, index // 2 % 2, index % 2
        rows = pl.ds(y * tok, tok)
        x_copies.append(pltpu.make_async_copy(unit.at[pl.ds(0, tok)], x_all.at[chunk, x, rows], unit_sems.at[0, index]))
        g_copies.append(pltpu.make_async_copy(unit.at[pl.ds(tok, tok)], g_all.at[chunk, x, rows], unit_sems.at[1, index]))
    t_copies = [
        pltpu.make_async_copy(table, tables.at[chunk], unit_sems.at[2, chunk]) for chunk, table in enumerate(tables_in)
    ]
    for copy in t_copies + x_copies + g_copies:
        copy.start()
    both_at, scaled_at = pl.ds(4 * half, 2 * part), pl.ds(4 * half + 2 * part, part)

    def dot(a, b, dims):
        return lax.dot_general(a, b, (dims, ((), ())), preferred_element_type=jnp.float32)

    for copy in t_copies:
        copy.wait()
    earlier = lax.broadcasted_iota(jnp.int32, (tok, tok), 0) < lax.broadcasted_iota(jnp.int32, (tok, tok), 1)
    earlier = earlier.astype(jnp.bfloat16)
    place = lax.broadcasted_iota(jnp.int32, (slots, tok), 0).astype(jnp.float32)
    names = lax.broadcasted_iota(jnp.int32, (owners, tok), 0)
    picks, low_picks, probs = {}, {}, {}
    for chunk in range(count):
        found = []
        for y in range(2):
            table = tables[chunk, y].astype(jnp.float32)
            rank = dot((table >= 0.0).astype(jnp.bfloat16), earlier, ((1,), (0,))) + float(y * capacity)
            found.append((table, jnp.where(table >= 0.0, rank, -1.0)))
        for expert in range(2):
            mine = names == where_ref[expert]
            halves, prob = [], None
            for table, rank in found:
                weight = jnp.sum(jnp.where(mine, table, 0.0), axis=0, keepdims=True)
                slot = jnp.sum(jnp.where(mine, rank, 0.0), axis=0, keepdims=True)
                halves.append((place == slot).astype(jnp.float32))
                term = jnp.sum(halves[-1] * weight, axis=1, keepdims=True)
                prob = term if prob is None else prob + term
            picks[chunk, expert] = halves
            low_picks[chunk, expert] = jnp.concatenate(halves, 1).astype(jnp.bfloat16)
            probs[chunk, expert] = prob
    spans = [pl.ds(chunk * slots, slots) for chunk in range(count)]
    sides = [slice(side * half, (side + 1) * half) for side in range(2)]

    def gather(copies, source, offset):
        for chunk in range(count):
            for copy in copies[4 * chunk : 4 * chunk + 4]:
                copy.wait()
            both_picks = jnp.concatenate([low_picks[chunk, expert] for expert in range(2)], 0)
            for side in range(2):
                rows = dot(both_picks, source[chunk, side], ((1,), (0,))).astype(jnp.bfloat16)
                for expert in range(2):
                    columns = pl.ds(offset + side * half, half)
                    outs[expert][spans[chunk], columns] = rows[expert * slots : (expert + 1) * slots]

    gather(x_copies, x_all, 0)
    rows = []
    for expert in range(2):
        rows.append(dot(outs[expert][:, : 2 * half], wgu[expert][...], ((1,), (0,))))
    gather(g_copies, g_all, 2 * half)
    scores = []
    for expert in range(2):
        back = dot(outs[expert][:, 2 * half : 4 * half], wd[expert][...], ((1,), (1,)))
        gate, up = rows[expert][:, :part], rows[expert][:, part:]
        sig = jax.nn.sigmoid(gate)
        act = gate * sig
        hidden = act * up
        scores.append(jnp.sum(hidden * back, axis=1, keepdims=True))
        prob = jnp.concatenate([probs[chunk, expert] for chunk in range(count)], 0)
        hgrad = prob * back
        d_gate = (hgrad * up * sig * (1.0 + gate * (1.0 - sig))).astype(jnp.bfloat16)
        outs[expert][:, both_at] = jnp.concatenate([d_gate, (hgrad * act).astype(jnp.bfloat16)], 1)
        outs[expert][:, scaled_at] = (prob * hidden).astype(jnp.bfloat16)

    extra_rows = packets[0].shape[1] - tok
    per_row = owners // extra_rows
    names = lax.broadcasted_iota(jnp.int32, (extra_rows, half), 0)
    column = lax.broadcasted_iota(jnp.int32, (extra_rows, half), 1) // (2 * tok)
    for chunk in range(count):
        for y in range(2):
            extra = jnp.zeros((extra_rows, half), jnp.float32)
            for expert in range(2):
                part_scores = scores[expert][chunk * slots : (chunk + 1) * slots]
                line = jnp.sum(picks[chunk, expert][y] * part_scores, axis=0, keepdims=True)
                high = line.astype(jnp.bfloat16).astype(jnp.float32)
                line = jnp.concatenate([high, line - high] * (half // (2 * tok)), 1)
                row, cell = where_ref[expert] // per_row, where_ref[expert] % per_row * 2 + where_ref[2]
                extra = extra + jnp.where((names == row) & (column == cell), line, 0.0)
            for side in range(2):
                number, slot = ways[chunk, y, side]
                packets[number][slot, tok:] = extra.astype(jnp.bfloat16)
    placed = []
    for expert in range(2):
        parts = [dot(low_picks[chunk, expert], outs[expert][spans[chunk], both_at], ((0,), (0,))) for chunk in range(count)]
        placed.append(jnp.concatenate(parts, 0).astype(jnp.bfloat16))
    for side in (1, 0):
        total = dot(placed[0], wgu[0][sides[side], :], ((1,), (1,))) + dot(placed[1], wgu[1][sides[side], :], ((1,), (1,)))
        for chunk in range(count):
            for y in range(2):
                number, slot = ways[chunk, y, side]
                start = (2 * chunk + y) * tok
                packets[number][slot, :tok] = total[start : start + tok].astype(jnp.bfloat16)


def rows_call(items, owners, capacity, slots, where, weights, units, tables, after):
    count = len(tables)
    ways = {block: (number, slot) for number, blocks in enumerate(items) for slot, block in enumerate(blocks)}
    tok, half = units[0].shape[0] // 2, units[0].shape[1]
    part, width = weights[2].shape
    widths = (width, width, 2 * part, part)
    packet = (tok + 4 * tok * owners // half, half)
    return pl.pallas_call(
        functools.partial(rows_kernel, count, ways, capacity, slots),
        grid_spec=pltpu.PrefetchScalarGridSpec(
            num_scalar_prefetch=1,
            grid=(1,),
            in_specs=[pl.BlockSpec(memory_space=pltpu.VMEM)] * 4 + [LOOSE] * (5 * count + len(after)),
            out_specs=[pl.BlockSpec(memory_space=pltpu.VMEM)] * (2 + len(items)),
            scratch_shapes=[pltpu.VMEM((count, 2, 2 * tok, half), jnp.bfloat16)] * 2
            + [pltpu.VMEM((count, 2, owners, tok), jnp.bfloat16)]
            + [pltpu.SemaphoreType.DMA((3, 4 * count))],
        ),
        out_shape=[pltpu.VMEM((count * slots, sum(widths)), jnp.bfloat16)] * 2
        + [pltpu.VMEM((len(blocks),) + packet, jnp.bfloat16) for blocks in items],
        compiler_params=pltpu.CompilerParams(vmem_limit_bytes=14 << 20),
        cost_estimate=pl.CostEstimate(
            flops=count * (20 * slots * width * part + 24 * slots * tok * width),
            bytes_accessed=count * 16 * tok * width + 12 * width * part,
            transcendentals=2 * count * slots * part,
        ),
        name="rows",
    )(where, *[pltpu.with_memory_space_constraint(item, pltpu.VMEM) for item in (*weights, *units, *tables)], *after)


def grads_kernel(count, wide, deep, blocks, tp_ref, *refs):
    sources, outs = refs[:count], refs[count:-4]
    wide_all, deep_all, wide_sems, deep_sems = refs[-4:]
    starts = [sum(source.shape[0] for source in sources[:index]) for index in range(count)]
    size = wide_all.shape[2]
    block = pl.program_id(0)

    def copies(column):
        return [
            pltpu.make_async_copy(
                source.at[:, pl.ds(wide + column * size, size)],
                wide_all.at[column, pl.ds(starts[index], source.shape[0])],
                wide_sems.at[column, index],
            )
            for index, source in enumerate(sources)
        ]

    @pl.when(block == 0)
    def _():
        deep_copies = [
            pltpu.make_async_copy(
                source.at[:, pl.ds(deep, deep_all.shape[1])],
                deep_all.at[pl.ds(starts[index], source.shape[0])],
                deep_sems.at[index],
            )
            for index, source in enumerate(sources)
        ]
        for copy in deep_copies:
            copy.start()
        for column in range(blocks):
            for copy in copies(column):
                copy.start()
        for copy in deep_copies:
            copy.wait()

    for column in range(blocks):

        @pl.when(block == column)
        def _(column=column):
            for copy in copies(column):
                copy.wait()

    dims = (((0,), (0,)), ((), ()))
    if len(outs) == 2:
        part = outs[0].shape[2]
        both = lax.dot_general(wide_all[block], deep_all[...], dims, preferred_element_type=jnp.float32)
        outs[0][0] = both[:, :part].astype(jnp.bfloat16)
        outs[1][0] = both[:, part:].astype(jnp.bfloat16)
    else:
        down = lax.dot_general(deep_all[...], wide_all[block], dims, preferred_element_type=jnp.float32)
        outs[0][0] = down.astype(jnp.bfloat16)


def grads_call(which, packed, width, part, down):
    rows, count = sum(item.shape[0] for item in packed), len(packed)
    step = math.gcd(width // 2, 512 if down else 1024)
    per = width // 2 // step
    deep = part if down else 2 * part

    def place(i, w):
        return (i + w[0] * per) % (2 * per)

    if down:
        specs = [pl.BlockSpec((1, part, step), lambda i, w: (0, 0, place(i, w)))]
        shapes = [(1, part, width)]
    else:
        specs = [pl.BlockSpec((1, step, part), lambda i, w: (0, place(i, w), 0))] * 2
        shapes = [(1, width, part)] * 2
    starts = (width, 2 * width + 2 * part) if down else (0, 2 * width)
    return pl.pallas_call(
        functools.partial(grads_kernel, count, *starts, 2 * per),
        grid_spec=pltpu.PrefetchScalarGridSpec(
            num_scalar_prefetch=1,
            grid=(2 * per,),
            in_specs=[LOOSE] * count,
            out_specs=specs,
            scratch_shapes=[
                pltpu.VMEM((2 * per, rows, step), jnp.bfloat16),
                pltpu.VMEM((rows, deep), jnp.bfloat16),
                pltpu.SemaphoreType.DMA((2 * per, count)),
                pltpu.SemaphoreType.DMA((count,)),
            ],
        ),
        out_shape=[jax.ShapeDtypeStruct(shape, jnp.bfloat16) for shape in shapes],
        compiler_params=pltpu.CompilerParams(vmem_limit_bytes=22 << 20),
        cost_estimate=pl.CostEstimate(
            flops=2 * rows * width * deep, bytes_accessed=2 * rows * (width + deep), transcendentals=0
        ),
        name="grads",
    )(which, *packed)


def dense_device(tokens, out_grad, routes, probs, w_gate, w_up, w_down):
    owners = lax.axis_size(("role", "ep"))
    ep = lax.axis_size("ep")
    n_y = 2
    n_z = ep // n_y
    tok_rows, half = tokens.shape
    capacity = slot_capacity(tok_rows, routes.shape[1], owners)
    slots = -(-n_y * capacity // 16) * 16
    role, place, which = lax.axis_index("role"), lax.axis_index("ep"), lax.axis_index("tp")

    def over_x(array):
        return lax.ppermute(array, "tp", [(0, 1), (1, 0)])

    def over_role(array):
        return lax.ppermute(array, "role", [(0, 1), (1, 0)])

    def over_y(array):
        return lax.ppermute(array, "ep", [(i, i + 1 - 2 * (i % n_y)) for i in range(ep)])

    def over_z(array, shift):
        return lax.ppermute(array, "ep", [(i, (i + shift * n_y) % ep) for i in range(ep)])

    def tied(values, others):
        return lax.optimization_barrier((list(values), list(others)))[0]

    last = n_z - 1
    routes_in = []
    for z in range(n_z):
        shift = -1 if z == last and z > 1 else 1
        if z:
            routes_in.append(((z, 0, 0), (0 if z in (1, last) else z - 1, 0, 0), functools.partial(over_z, shift=shift)))
        routes_in.append(((z, 1, 0), (z, 0, 0), over_y))
        routes_in.append(((z, 0, 1), (z, 0, 0), over_x))
        if z == 0:
            routes_in.append(((z, 1, 1), (z, 1, 0), over_x))
        elif z in (1, last):
            routes_in.append(((z, 1, 1), (0, 1, 1), functools.partial(over_z, shift=shift)))
        else:
            routes_in.append(((z, 1, 1), (z, 0, 1), over_y))
    routes_in.sort(key=lambda item: (item[0][0] % 2 if item[2] in (over_x, over_y) else 0, sum(item[0][1:])))

    rounds, waiting, there = [], list(routes_in), {(0, 0, 0)}
    while waiting:
        moves = {}
        for item in waiting:
            axis = item[2] if item[2] in (over_x, over_y) else over_z
            if item[1] in there and axis not in moves:
                moves[axis] = item
        rounds.append(moves)
        there |= {item[0] for item in moves.values()}
        waiting = [item for item in waiting if item[0] not in there]

    which_ref = which.reshape(1).astype(jnp.int32)
    where = jnp.stack([role * ep + place, (1 - role) * ep + place, which]).astype(jnp.int32)
    both_w, down_w = weights_call(which_ref, w_gate, w_up, w_down)
    width, part = both_w.shape[0], down_w.shape[0]

    def rows_of(steps, items, after):
        four = [units[z, y, x] for z in steps for y in range(2) for x in range(2)]
        return rows_call(items, owners, capacity, slots, where, weights, four, [tables[z] for z in steps], after)

    units = {(0, 0, 0): join_call(tokens, out_grad)}
    flying, landed, extra = {}, [], []
    for number, moves in enumerate(rounds):
        arrived = {}
        for axis, (target, source, move) in moves.items():
            (block,) = tied([units[source]], [flying[axis]] + landed + extra) if flying else [units[source]]
            arrived[axis] = move(block)
        units.update({moves[axis][0]: block for axis, block in arrived.items()})
        flying, landed, extra = arrived, list(flying.values()), []
        if number == 0:
            extra = [both_w, down_w]
            both_w, down_w, routes, probs = tied([both_w, down_w, routes, probs], arrived.values())
            weights = (both_w, over_role(both_w), down_w, over_role(down_w))
            chosen = routes[:, :, None] == jnp.arange(owners, dtype=jnp.int32)
            table = jnp.sum(jnp.where(chosen, probs[:, :, None].astype(jnp.float32) + 1.0, 0.0), axis=1) - 1.0
            table = table.astype(jnp.bfloat16).T
            table = jnp.stack([table, over_y(table)])
        if number == 1:
            (table,) = tied([table], arrived.values())
            tables = [over_z(table, z) if z else table for z in range(n_z)]
        if number == 2:
            mine_0, other_0, near, side_0, far, y_0 = rows_of(
                [0], [[(0, 0, 0)], [(0, 0, 1)], [(0, 1, 1)], [(0, 1, 0)]], []
            )
            extra = [mine_0]

    def total(*blocks):
        return sum(block.astype(jnp.float32) for block in blocks).astype(jnp.bfloat16)

    items = [[(1, 1, 1)], [(1, 0, 1)], [(0, 0, 1)], [(0, 1, 0)], [(0, 1, 1)], [(0, 0, 0)], [(1, 0, 0)], [(1, 1, 0)]]
    mine_1, other_1, x_2, x_20, x_1, y_1, z_1, keep_1, keep_2, keep_2y = rows_of([1, 2], items, tables[3:])
    other_1, x_2, x_20, x_1, y_1, z_1 = tied([other_1, x_2, x_20, x_1, y_1, z_1], arrived.values())
    from_x2, from_y1, from_z1 = over_x(x_2), over_y(y_1), over_z(z_1, -1)
    from_x20 = over_x(x_20)
    items = [[(0, 0, 1)], [(0, 1, 0)], [(0, 1, 1)], [(0, 0, 0)]]
    mine_3, other_3, x_3, y_3, z_3, keep_3 = rows_of([3], items, [mine_1])
    mine_3, other_3, x_3, y_3, z_3, keep_2y = tied(
        [mine_3, other_3, x_3, y_3, z_3, keep_2y], [from_x2, from_y1, from_z1]
    )
    from_z3, from_y2, from_x1 = over_z(z_3, 1), over_y(total(keep_2y, from_x2)), over_x(x_1)
    from_x3, from_y3 = over_x(x_3), over_y(y_3)
    packed = [mine_0, over_role(other_0), mine_1, over_role(other_1), mine_3, over_role(other_3)]
    (d_down,) = grads_call(which_ref, packed, width, part, True)
    from_z3, from_x20, from_y2 = tied([from_z3, from_x20, from_y2], [d_down])
    far, step_2 = total(far, from_z1, from_z3), total(keep_2, from_x20, from_y2)
    (from_x1,) = tied([from_x1], [far, step_2])
    from_far, from_z2 = over_y(far), over_z(step_2, 1)
    home_1 = over_z(total(keep_1, from_x1, from_y1), -1)
    from_x0 = over_x(total(side_0, from_far))
    from_x3, from_y3, from_z2 = tied([from_x3, from_y3, from_z2], [from_far])
    home_3 = over_z(total(keep_3, from_x3, from_y3, from_z2), 1)
    from_y0 = over_y(tied([y_0], [from_far])[0])
    d_gate, d_up = grads_call(which_ref, packed, width, part, False)
    home_1, from_x0, home_3, from_y0 = tied([home_1, from_x0, home_3, from_y0], [d_gate, d_up])
    home = (near, from_x0, home_3, home_1, from_y0)
    d_tok = sum(block[0, :tok_rows].astype(jnp.float32) for block in home).astype(jnp.bfloat16)
    home = sum(block[0, tok_rows:].astype(jnp.float32) for block in home)
    score = jnp.sum(home.reshape(owners, 4, tok_rows), axis=1).T
    d_probs = jnp.sum(jnp.where(chosen, score[:, None, :], 0.0), axis=2)
    return d_tok, d_probs, d_gate, d_up, d_down


def per_device(tokens, out_grad, routes, probs, w_gate, w_up, w_down):
    owners = lax.axis_size(("role", "ep"))
    tok_rows, top_count = routes.shape
    paired = lax.axis_size("tp") == 2 and lax.axis_size("role") == 2 and lax.axis_size("ep") == 8
    if paired and 2 * slot_capacity(tok_rows, top_count, owners) >= tok_rows:
        return dense_device(tokens, out_grad, routes, probs, w_gate, w_up, w_down)
    return routed_device(tokens, out_grad, routes, probs, w_gate, w_up, w_down)


def solution(mesh):
    in_specs = (
        P(("groups", "role", "ep"), "tp"),
        P(("groups", "role", "ep"), "tp"),
        P(("groups", "role", "ep"), None),
        P(("groups", "role", "ep"), None),
        P(("role", "ep"), None, "tp"),
        P(("role", "ep"), None, "tp"),
        P(("role", "ep"), "tp", None),
    )
    out_specs = (
        P(("groups", "role", "ep"), "tp"),
        P(("groups", "role", "ep"), None),
        P(("groups", "role", "ep"), None, "tp"),
        P(("groups", "role", "ep"), None, "tp"),
        P(("groups", "role", "ep"), "tp", None),
    )
    return jax.shard_map(
        per_device, mesh=mesh, in_specs=in_specs, out_specs=out_specs, check_vma=False
    )
```
